32 devices in a mesh: obs: 2 (over x), sub: 16 (over z, y, core).
Axes of the slice: x: 2, y: 2, z: 4, core: 2. Of those that a mesh axis runs over, the one named last changes fastest.
Arguments:
- visibilities: bfloat16 [2, 4, 4, 703, 3072], P(None, 'obs', None, None, 'sub'), parts along dimension 1, may hold values from -16 to 16
- delays: float32 [2, 4, 703], P(None, 'obs'), parts along dimension 1, may hold values from -1 to 1
- flags: int32 [4, 3072], P('obs', 'sub'), parts along dimension 0, may hold values 0 or 1
- windows: int32 [32], replicated, may hold values from 1 to 768, 3072 in all
- tracks: int32 [2, 4], P(None, 'obs'), parts along dimension 1, may hold values 0 or 1
Outputs:
- cleaned: bfloat16 [2, 4, 4, 703, 3072], P(None, 'obs', None, None, 'sub'), parts along dimension 1
- gains: float32 [2, 2, 4, 4, 38], P(None, None, 'obs'), parts along dimension 2
The draws below stay inside these ranges and needn't reach their ends.
There are 2 independent parts, one for each index of `obs`. The reference program is written for one: setup_inputs(seed, part) draws one part's arguments, and reference() takes and returns one part's arrays. A program takes and returns all parts, laid end to end along the dimension named above; an argument that names none is the same for every part. Nothing has to cross between parts.
Inputs may be any that keep to these rules, and one draw needn't show every extreme that they name: The windows cover all 3072 channels.
All inputs are finite; a program needn't handle non-finite values. No bound on the sum of `flags` on one device may be relied on, other than what follows from the above.
Results may differ from the reference program's by a relative error of at most 0.001.
Values sent between devices are 32-bit elements; how exact they have to be, the bound alone decides.
No kernel may reach another device: no remote copies, remote signals or barrier semaphores. Data moves between devices by JAX's collectives and lax.ppermute only.
A program may use at most 128 MiB of HBM per device.

```python
import math
import jax
import jax.numpy as jnp
import numpy as np
from jax import lax

STATIONS = 38
STATION_PAIRS = 703
CORRELATIONS = 4
BRIGHT_SOURCES = 2
TIME_SAMPLES = 2
GITERS = 8
CH_DEV = 192
CHANNEL_COUNT = 3072
WINDOW_COUNT = 32


TWO_PI_STEP = 2.0 * 3.141592653589793 / 64.0


def station_offsets(key):
    return jax.random.uniform(key, (BRIGHT_SOURCES, TIME_SAMPLES, STATIONS), jnp.float32, -0.5, 0.5)


def baseline_delays(key):
    offsets = station_offsets(key)
    first, second = np.triu_indices(STATIONS, 1)
    return offsets[:, :, first] - offsets[:, :, second]


def draw_delays(key, part):
    shared = baseline_delays(key)
    key = jax.random.fold_in(key, 3)
    return shared


def draw_visibilities(key, part):
    shared = baseline_delays(key)
    key = jax.random.fold_in(key, 5)
    keys = jax.random.split(key, 4)
    gain_shape = (2, BRIGHT_SOURCES, TIME_SAMPLES, CORRELATIONS, STATIONS)
    visibility_shape = (2, TIME_SAMPLES, CORRELATIONS, STATION_PAIRS, CHANNEL_COUNT)
    position = jnp.arange(CHANNEL_COUNT, dtype=jnp.int32).astype(jnp.float32) / float(CHANNEL_COUNT)
    spread = 0.35 * jax.random.truncated_normal(keys[0], -3.0, 3.0, gain_shape, jnp.float32)
    noise = 0.5 * jax.random.truncated_normal(keys[1], -4.0, 4.0, visibility_shape, jnp.float32)
    bright = (1.0, 0.7)
    offset = jax.random.uniform(keys[2], (BRIGHT_SOURCES,), jnp.float32, 0.0, 6.28)
    rough = jax.random.uniform(keys[3], (BRIGHT_SOURCES, CHANNEL_COUNT), jnp.float32, 0.75, 1.25)
    depth = 0.6
    first, second = np.triu_indices(STATIONS, 1)
    gain_re = 1.0 + spread[0]
    gain_im = spread[1]
    channel = jnp.arange(CHANNEL_COUNT, dtype=jnp.int32).astype(jnp.float32) * TWO_PI_STEP
    total_re = noise[0]
    total_im = noise[1]
    for source in range(BRIGHT_SOURCES):
        band = (1.0 + depth * jnp.sin(18.85 * position + offset[source])) * rough[source]
        left_re = gain_re[source][:, :, first]
        left_im = gain_im[source][:, :, first]
        right_re = gain_re[source][:, :, second]
        right_im = gain_im[source][:, :, second]
        model_re = (left_re * right_re + left_im * right_im)[..., None]
        model_im = (left_im * right_re - left_re * right_im)[..., None]
        angles = shared[source][:, None, :, None] * channel[None, None, None, :]
        cosine = jnp.cos(angles) * band
        sinus_part = jnp.sin(angles) * band
        total_re = total_re + bright[source] * (model_re * cosine - model_im * sinus_part)
        total_im = total_im + bright[source] * (model_re * sinus_part + model_im * cosine)
    return jnp.stack([total_re, total_im]).astype(jnp.bfloat16)


def set_ends(entries, key, least, high):
    place = [jax.random.randint(jax.random.fold_in(key, axis), (), 0, length) for axis, length in enumerate(entries.shape)]
    main_axis = entries.shape.index(max(entries.shape))
    beside = place[:main_axis] + [(place[main_axis] + 1) % entries.shape[main_axis]] + place[main_axis + 1:]
    return entries.at[tuple(place)].set(least).at[tuple(beside)].set(high)


def split_up(count, total, reach, lean):
    portions = [(1 << 20) // math.isqrt(rank ** lean) + 1 for rank in range(2, count + 1)]
    surplus, holding = total - reach - (count - 1), [1] * (count - 1)
    while surplus > 0:
        movable = [i for i in range(count - 1) if holding[i] < reach]
        pool, remaining = sum([portions[i] for i in movable]), surplus
        for i in movable:
            addition = min(reach - holding[i], max(1, remaining * portions[i] // pool), surplus)
            holding[i] = holding[i] + addition
            surplus = surplus - addition
    return np.array([reach] + holding)


def ragged_sizes(rng, number_of, total, reach, skew):
    if number_of == 2:
        one = jax.random.randint(rng, (), max(1, total - reach), min(reach, total - 1) + 1)
        return jnp.stack([one, total - one])
    tallies = jnp.asarray(split_up(number_of, total, reach, skew), jnp.int32)
    twos = (number_of - 1) // 2
    giver, receiver = tallies[1:1 + 2 * twos:2], tallies[2:2 + 2 * twos:2]
    room = jnp.minimum(giver - 1, reach - receiver)
    moved = jax.random.randint(jax.random.fold_in(rng, 1), (twos,), 0, 1 << 20) % (room + 1)
    tallies = tallies.at[1:1 + 2 * twos:2].set(giver - moved).at[2:2 + 2 * twos:2].set(receiver + moved)
    return tallies[jax.random.permutation(jax.random.fold_in(rng, 2), number_of)]


def setup_inputs(seed: int = 0, part: int = 0) -> dict:
    key_list = jax.random.split(jax.random.key(seed), 6)
    part_keys = jax.random.split(jax.random.fold_in(key_list[5], part), 6)
    return {
        "visibilities": draw_visibilities(jax.random.fold_in(jax.random.fold_in(key_list[5], part), 71), part),
        "delays": draw_delays(jax.random.fold_in(jax.random.fold_in(key_list[5], part), 71), part),
        "flags": set_ends((jax.random.randint(part_keys[2], (TIME_SAMPLES, CHANNEL_COUNT), 0, 5) < 1).astype(jnp.int32), jax.random.fold_in(part_keys[2], 1), 0, 1),
        "windows": ragged_sizes(key_list[3], WINDOW_COUNT, CHANNEL_COUNT, CHANNEL_COUNT // 4, 2).astype(jnp.int32),
        "tracks": set_ends((jax.random.randint(part_keys[4], (BRIGHT_SOURCES, TIME_SAMPLES), 0, 4) < 3).astype(jnp.int32), jax.random.fold_in(part_keys[4], 1), 0, 1),
    }


TWO_PI_STEP = 2.0 * 3.141592653589793 / 64.0
DAMPING = 1.0


def station_tables(count):
    first, second = np.triu_indices(count, 1)
    eye = np.eye(count, dtype=np.float32)
    return jnp.asarray(eye[first]), jnp.asarray(eye[second])


def phases(delays, channel):
    angles = delays[:, :, :, None] * (channel * TWO_PI_STEP)[None, None, None, :]
    return jnp.cos(angles), jnp.sin(angles)


def rotate(block, cos_part, sin_part, flag_block):
    weight = (1 - flag_block).astype(jnp.float32)
    vis_re = block[0].astype(jnp.float32)
    vis_im = block[1].astype(jnp.float32)
    weight_four = weight[:, None, None, :]
    window_parts = []
    for source in range(cos_part.shape[0]):
        cosine = cos_part[source][:, None]
        sinus_part = sin_part[source][:, None]
        window_parts.append(jnp.stack([(vis_re * cosine + vis_im * sinus_part) * weight_four,
                                 (vis_im * cosine - vis_re * sinus_part) * weight_four]))
    rotated = jnp.stack(window_parts, axis=1)
    weight_three = weight[:, None, :]
    mixing_re = (cos_part[1] * cos_part[0] + sin_part[1] * sin_part[0]) * weight_three
    mixing_im = (sin_part[1] * cos_part[0] - cos_part[1] * sin_part[0]) * weight_three
    return rotated, jnp.stack([mixing_re, mixing_im]), weight


def unmix(rot_sums, mix_sums, counts):
    scale = 1.0 / jnp.maximum(counts, 1.0)
    average = rot_sums * scale[None, None, :, None, None, :]
    mixing = mix_sums * scale[None, :, None, :]
    mix_re = mixing[0][:, None]
    mix_im = mixing[1][:, None]
    one_re, one_im = average[0, 0], average[1, 0]
    two_re, two_im = average[0, 1], average[1, 1]
    first_re = one_re - (mix_re * two_re - mix_im * two_im)
    first_im = one_im - (mix_re * two_im + mix_im * two_re)
    second_re = two_re - (mix_re * one_re + mix_im * one_im)
    second_im = two_im - (mix_re * one_im - mix_im * one_re)
    return jnp.stack([jnp.stack([first_re, second_re]), jnp.stack([first_im, second_im])])


def solve_gains(totals, tracks, window_count, first_tab, second_tab):
    highest = lax.Precision.HIGHEST
    half_re = jnp.einsum('bp,stkb,bq->stkpq', first_tab, totals[0], second_tab, precision=highest)
    half_im = jnp.einsum('bp,stkb,bq->stkpq', first_tab, totals[1], second_tab, precision=highest)
    full_re = half_re + jnp.swapaxes(half_re, -1, -2)
    full_im = half_im - jnp.swapaxes(half_im, -1, -2)
    gain_re = jnp.ones(full_re.shape[:-1], jnp.float32)
    gain_im = jnp.zeros(full_re.shape[:-1], jnp.float32)
    for iteration in range(GITERS):
        pull_re = (jnp.einsum('stkpq,stkq->stkp', full_re, gain_re, precision=highest)
                   - jnp.einsum('stkpq,stkq->stkp', full_im, gain_im, precision=highest))
        pull_im = (jnp.einsum('stkpq,stkq->stkp', full_re, gain_im, precision=highest)
                   + jnp.einsum('stkpq,stkq->stkp', full_im, gain_re, precision=highest))
        powers = gain_re * gain_re + gain_im * gain_im
        denominator = window_count * (jnp.sum(powers, axis=-1, keepdims=True) - powers) + DAMPING
        gain_re = 0.5 * (gain_re + pull_re / denominator)
        gain_im = 0.5 * (gain_im + pull_im / denominator)
    visible = tracks.astype(jnp.float32)[:, :, None, None]
    return gain_re * visible, gain_im * visible


def subtract(block, cos_part, sin_part, gain_re, gain_im, first_tab, second_tab):
    highest = lax.Precision.HIGHEST
    left_re = jnp.einsum('stkp,bp->stkb', gain_re, first_tab, precision=highest)
    left_im = jnp.einsum('stkp,bp->stkb', gain_im, first_tab, precision=highest)
    right_re = jnp.einsum('stkp,bp->stkb', gain_re, second_tab, precision=highest)
    right_im = jnp.einsum('stkp,bp->stkb', gain_im, second_tab, precision=highest)
    model_re = (left_re * right_re + left_im * right_im)[..., None]
    model_im = (left_im * right_re - left_re * right_im)[..., None]
    cosine = cos_part[:, :, None]
    sinus_part = sin_part[:, :, None]
    wave_re = jnp.sum(model_re * cosine - model_im * sinus_part, axis=0)
    wave_im = jnp.sum(model_re * sinus_part + model_im * cosine, axis=0)
    return jnp.stack([block[0].astype(jnp.float32) - wave_re,
                      block[1].astype(jnp.float32) - wave_im]).astype(jnp.bfloat16)


def reference(visibilities, delays, flags, windows, tracks):
    first_tab, second_tab = station_tables(STATIONS)
    highest = lax.Precision.HIGHEST
    window_ends = jnp.cumsum(windows).astype(jnp.int32)
    channel = jnp.arange(CHANNEL_COUNT, dtype=jnp.int32)
    window_of = jnp.sum((window_ends[None, :] <= channel[:, None]).astype(jnp.int32), axis=1).astype(jnp.int32)
    window_ids = jnp.arange(WINDOW_COUNT, dtype=jnp.int32)
    blocks = CHANNEL_COUNT // CH_DEV

    def accumulate(carry, index):
        start = (index * CH_DEV).astype(jnp.int32)
        block = lax.dynamic_slice_in_dim(visibilities, start, CH_DEV, 4)
        flag_block = lax.dynamic_slice_in_dim(flags, start, CH_DEV, 1)
        seg_block = lax.dynamic_slice_in_dim(window_of, start, CH_DEV, 0)
        freq_block = (start + jnp.arange(CH_DEV, dtype=jnp.int32)).astype(jnp.float32)
        cos_part, sin_part = phases(delays, freq_block)
        rotated, mixing, weight = rotate(block, cos_part, sin_part, flag_block)
        member = (seg_block[:, None] == window_ids[None, :]).astype(jnp.float32)
        return (carry[0] + jnp.einsum('astkbc,cw->astkbw', rotated, member, precision=highest),
                carry[1] + jnp.einsum('atbc,cw->atbw', mixing, member, precision=highest),
                carry[2] + jnp.dot(weight, member, precision=highest)), None

    starting_gains = (jnp.zeros((2, BRIGHT_SOURCES, TIME_SAMPLES, CORRELATIONS, STATION_PAIRS, WINDOW_COUNT), jnp.float32),
               jnp.zeros((2, TIME_SAMPLES, STATION_PAIRS, WINDOW_COUNT), jnp.float32),
               jnp.zeros((TIME_SAMPLES, WINDOW_COUNT), jnp.float32))
    sums, unused = lax.scan(accumulate, starting_gains, jnp.arange(blocks, dtype=jnp.int32))
    totals = jnp.sum(unmix(sums[0], sums[1], sums[2]), axis=-1)
    gain_re, gain_im = solve_gains(totals, tracks, float(WINDOW_COUNT), first_tab, second_tab)

    def clean(index):
        start = (index * CH_DEV).astype(jnp.int32)
        block = lax.dynamic_slice_in_dim(visibilities, start, CH_DEV, 4)
        freq_block = (start + jnp.arange(CH_DEV, dtype=jnp.int32)).astype(jnp.float32)
        cos_part, sin_part = phases(delays, freq_block)
        return subtract(block, cos_part, sin_part, gain_re, gain_im, first_tab, second_tab)

    window_parts = lax.map(clean, jnp.arange(blocks, dtype=jnp.int32))
    cleaned = jnp.moveaxis(window_parts, 0, 4).reshape(2, TIME_SAMPLES, CORRELATIONS, STATION_PAIRS, CHANNEL_COUNT)
    return cleaned, jnp.stack([gain_re, gain_im])
```

```python
import jax
import jax.numpy as jnp
import numpy as np
from jax import lax
from jax.experimental import pallas as pl
from jax.experimental.pallas import tpu as pltpu
from jax.sharding import PartitionSpec as P

STATIONS = 38
GITERS = 8
DAMPING = 1.0
STEPS_PER_TURN = 64.0
ROWS = 40
LANES = 384

F32 = jnp.float32
BF16 = jnp.bfloat16


def iota(shape, dim):
    return lax.broadcasted_iota(jnp.int32, shape, dim).astype(F32)


def sincos_turns(turns):
    half = (turns - jnp.floor(turns + 0.5)) * np.float32(np.pi)
    sq = half * half
    sin = np.float32(-1.0 / 39916800)
    for term in (1.0 / 362880, -1.0 / 5040, 1.0 / 120, -1.0 / 6, 1.0):
        sin = sin * sq + np.float32(term)
    sin = sin * half
    cos = np.float32(1.0 / 479001600)
    for term in (-1.0 / 3628800, 1.0 / 40320, -1.0 / 720, 1.0 / 24, -0.5, 1.0):
        cos = cos * sq + np.float32(term)
    return 1.0 - 2.0 * (sin * sin), 2.0 * (sin * cos)


def split_two(value):
    high = value.astype(BF16)
    low = (value - high.astype(F32)).astype(BF16)
    return high, low


def split_three(value):
    high = value.astype(BF16)
    rest = value - high.astype(F32)
    mid = rest.astype(BF16)
    low = (rest - mid.astype(F32)).astype(BF16)
    return high, mid, low


def dot(left, right):
    return jnp.dot(left, right, preferred_element_type=F32)


def phase_rows(delay, anchor, width):
    base = anchor + 8.0 * iota((width // 8, 1), 0)
    fine = iota((8, 1), 0)
    coarse_re, coarse_im = sincos_turns(delay * (base * np.float32(1.0 / STEPS_PER_TURN)))
    fine_re, fine_im = sincos_turns(delay * (fine * np.float32(1.0 / STEPS_PER_TURN)))
    return coarse_re, coarse_im, fine_re, fine_im


def spread(rows_ref, source, real, imag):
    for row in range(real.shape[0]):
        rows_ref[row, 2 * source:2 * source + 1, :] = real[row:row + 1]
        rows_ref[row, 2 * source + 1:2 * source + 2, :] = imag[row:row + 1]


def sums_kernel(width, me_ref, win_ref, flags_ref, delay_ref, vis_ref, y_ref,
                rows_s, member_s, alpha_s, window_s, coarse_s, fine_s, wave_s, mix_s, mexp_s, wt_s):
    time, part = pl.program_id(0), pl.program_id(1)
    me = me_ref[0]
    groups = flags_ref.shape[0]
    windows = win_ref.shape[1]
    anchor = me.astype(F32) * float(width)

    @pl.when((time == 0) & (part == 0))
    def prepare():
        win_row = win_ref[...].astype(F32)
        sub, lane = iota((windows, windows), 0), iota((windows, windows), 1)
        end_c = jnp.sum(jnp.where(lane <= sub, win_row, 0.0), axis=1, keepdims=True)
        start_c = jnp.sum(jnp.where(lane < sub, win_row, 0.0), axis=1, keepdims=True)
        win_c = end_c - start_c
        end_r = jnp.sum(jnp.where(sub <= lane, win_c, 0.0), axis=0, keepdims=True)
        start_r = jnp.sum(jnp.where(sub < lane, win_c, 0.0), axis=0, keepdims=True)
        group = iota((windows, groups), 1)
        low = group * float(width)
        first_hot = jnp.where((low <= start_c) & (start_c < low + float(width)), 1.0, 0.0)
        last_hot = jnp.where((low < end_c) & (end_c <= low + float(width)), 1.0, 0.0)
        first_g = jnp.sum(first_hot * group, axis=1, keepdims=True)
        last_g = jnp.sum(last_hot * group, axis=1, keepdims=True)
        full = jnp.where((group > first_g) & (group < last_g), 1.0, 0.0)
        pick = jnp.concatenate([first_hot, last_hot, full], axis=0).astype(BF16)
        place = iota((windows, width), 1)
        head_at = first_g * float(width) + place
        head_in = (head_at >= start_c) & (head_at < end_c)
        tail_in = (last_g > first_g) & (last_g * float(width) + place < end_c)
        channel = anchor + iota((width, windows), 0)
        member = (channel >= start_r) & (channel < end_r)
        diagonal = iota((width, width), 0) == iota((width, width), 1)
        window_s[0] = jnp.broadcast_to(first_g, (windows, 128))
        window_s[1] = jnp.broadcast_to(last_g, (windows, 128))
        for t in range(2):
            for g in range(groups):
                wt_s[t, g:g + 1, :] = 1.0 - flags_ref[lax.bitwise_xor(me, g), t:t + 1, :].astype(F32)
            weights = wt_s[t].astype(BF16)
            picked = dot(pick, weights)
            head = jnp.where(head_in, picked[:windows], 0.0)
            tail = jnp.where(tail_in, picked[windows:2 * windows], 0.0)
            count = jnp.sum(head + tail + picked[2 * windows:], axis=1, keepdims=True)
            scale = 1.0 / jnp.maximum(count, 1.0)
            rows_s[t] = jnp.concatenate([head, tail, wt_s[t]], axis=0).astype(BF16)
            window_s[2 + t] = jnp.broadcast_to(scale, (windows, 128))
            scale_r = jnp.sum(jnp.where(sub == lane, scale, 0.0), axis=0, keepdims=True)
            own = 1.0 - flags_ref[0, t:t + 1, :].astype(F32)
            own_c = jnp.sum(jnp.where(diagonal, own, 0.0), axis=1, keepdims=True)
            chosen = jnp.where(member, own_c, 0.0)
            member_s[t] = chosen.astype(BF16)
            alpha = jnp.sum(chosen * scale_r, axis=1, keepdims=True)
            alpha_s[t] = jnp.broadcast_to(alpha, (width, 128))
        pick_full = full.astype(BF16)
        window_s[4, :, :groups] = pick_full.astype(F32)

    size = y_ref.shape[3]
    delay = [delay_ref[s, pl.ds(time, 1), :] for s in range(2)]
    for s in range(2):
        cr, ci, fr, fi = phase_rows(delay[s], anchor, width)
        spread(coarse_s, s, cr, ci)
        fine_s[s, 0], fine_s[s, 1] = fr, fi

    def waves(block, carry):
        out = []
        for s in range(2):
            fr, fi = fine_s[s, 0], fine_s[s, 1]
            re, im = [], []
            for half in range(2):
                cr = coarse_s[block * 2 + half, 2 * s:2 * s + 1, :]
                ci = coarse_s[block * 2 + half, 2 * s + 1:2 * s + 2, :]
                re.append(cr * fr - ci * fi)
                im.append(cr * fi + ci * fr)
            out.append((jnp.concatenate(re, axis=0), jnp.concatenate(im, axis=0)))
        rows = pl.ds(pl.multiple_of(block * 16, 16), 16)
        (r0, i0), (r1, i1) = out
        for s in range(2):
            wave_s[s, 0, rows, :] = out[s][0]
            wave_s[s, 1, rows, :] = out[s][1]
        for slot, value in enumerate((r1 * r0 + i1 * i0, i1 * r0 - r1 * i0)):
            high, low = split_two(value)
            mix_s[slot, 0, rows, :] = high
            mix_s[slot, 1, rows, :] = low
        return carry

    lax.fori_loop(0, width // 16, waves, 0)

    rows = rows_s[time]
    sums = [dot(rows, mix_s[slot, 0]) + dot(rows, mix_s[slot, 1]) for slot in range(2)]
    gap = delay[1] - delay[0]
    per_group = np.float32(width / STEPS_PER_TURN)
    me_f = me.astype(F32)
    total_re, total_im = 0.0, 0.0
    for which in range(2):
        block = window_s[which][:, :1]
        pr, pi = sincos_turns(gap * ((block - me_f) * per_group))
        hr, hi = (part_sum[which * windows:(which + 1) * windows] for part_sum in sums)
        total_re = total_re + (pr * hr - pi * hi)
        total_im = total_im + (pr * hi + pi * hr)
    pr, pi = sincos_turns(gap * ((iota((groups, 1), 0) - me_f) * per_group))
    gr, gi = (part_sum[2 * windows:] for part_sum in sums)
    pick_full = window_s[4][:, :groups].astype(BF16)
    for slot, value in enumerate((pr * gr - pi * gi, pr * gi + pi * gr)):
        high, low = split_two(value)
        term = dot(pick_full, high) + dot(pick_full, low)
        if slot == 0:
            total_re = total_re + term
        else:
            total_im = total_im + term
    scale = window_s[2 + time][:, :1]
    chosen = member_s[time]
    for slot, value in enumerate((total_re, total_im)):
        high, low = split_two(value * (scale * scale))
        mexp_s[slot] = dot(chosen, high) + dot(chosen, low)

    for tile in range(size // 128):
        lanes = pl.ds(tile * 128, 128)

        def step(block, sums):
            rows = pl.ds(pl.multiple_of(block * 16, 16), 16)
            alpha = alpha_s[time, rows, :]
            mr, mi = mexp_s[0, rows, lanes], mexp_s[1, rows, lanes]
            r0, i0 = wave_s[0, 0, rows, lanes], wave_s[0, 1, rows, lanes]
            r1, i1 = wave_s[1, 0, rows, lanes], wave_s[1, 1, rows, lanes]
            factors = (
                (alpha * r0 - (mr * r1 + mi * i1), (mr * i1 - mi * r1) - alpha * i0),
                (alpha * r1 - (mr * r0 - mi * i0), (mr * i0 + mi * r0) - alpha * i1),
            )
            new = []
            for k in range(4):
                vr = vis_ref[0, 0, k, rows, lanes].astype(F32)
                vi = vis_ref[1, 0, k, rows, lanes].astype(F32)
                for s in range(2):
                    fr, fi = factors[s]
                    re = vr * fr - vi * fi
                    im = vr * fi + vi * fr
                    new.append(sums[len(new)] + (re[:8] + re[8:]))
                    new.append(sums[len(new)] + (im[:8] + im[8:]))
            return tuple(new)

        zero = jnp.zeros((8, 128), F32)
        sums = lax.fori_loop(0, width // 16, step, (zero,) * 16)
        for k in range(4):
            for s in range(2):
                for ri in range(2):
                    y_ref[ri, 0, s * 4 + k:s * 4 + k + 1, lanes] = jnp.sum(
                        sums[(k * 2 + s) * 2 + ri], axis=0, keepdims=True)


def solve_kernel(window_count, tracks_ref, hot_ref, first_ref, second_ref, *refs):
    parts, (gain_ref, model_ref, matrix_s, state_s) = refs[:-4], refs[-4:]
    total = [part[...] for part in parts]
    while len(total) > 1:
        total = [total[i] + total[i + 1] for i in range(0, len(total), 2)]
    total = total[0]
    re, im = total[:16], total[16:]
    wide = jnp.concatenate([re, im, -im, re] * 2, axis=0)
    matrix = 0.0
    for piece in split_three(wide):
        matrix = matrix + lax.dot_general(
            hot_ref[...], piece, (((1,), (1,)), ((), ())), preferred_element_type=F32)
    matrix_s[...] = matrix
    lane = lax.broadcasted_iota(jnp.int32, (ROWS, 128), 1)
    row = lax.broadcasted_iota(jnp.int32, (ROWS, 128), 0)
    quarter = lax.rem(lax.div(lane, 16), 4)
    inner = (quarter == 1) | (quarter == 2)
    for q in range(STATIONS):
        sign = jnp.where(inner & (row > q), -1.0, 1.0)
        matrix_s[q * ROWS:(q + 1) * ROWS, :] = matrix_s[q * ROWS:(q + 1) * ROWS, :] * sign

    def iterate(turn, state):
        state_s[...] = state
        pull = [jnp.zeros((ROWS, 128), F32) for _ in range(2)]
        for q in range(STATIONS):
            pull[q % 2] = pull[q % 2] + matrix_s[q * ROWS:(q + 1) * ROWS, :] * state_s[q:q + 1, :]
        pull = pull[0] + pull[1]
        pull = pull + pltpu.roll(pull, 32, 1)
        pull = jnp.where(inner, pltpu.roll(pull, 16, 1), pull)
        powers = state * state
        powers = powers + pltpu.roll(powers, 32, 1)
        denominator = window_count * (jnp.sum(powers, axis=0, keepdims=True) - powers) + DAMPING
        return 0.5 * (state + pull / denominator)

    state = jnp.where((quarter < 2) & (row < STATIONS), 1.0, 0.0)
    state = lax.fori_loop(0, GITERS, iterate, state)
    turned = jnp.transpose(jnp.concatenate([state, jnp.zeros((128 - ROWS, 128), F32)], axis=0))
    index = lax.broadcasted_iota(jnp.int32, (16, 128), 0)
    visible = jnp.zeros((16, 128), F32)
    for t in range(2):
        for s in range(2):
            here = lax.div(index, 4) == t * 2 + s
            visible = jnp.where(here, tracks_ref[s, t].astype(F32), visible)
    gains = [turned[:16] * visible, turned[32:48] * visible]
    for ri in range(2):
        for t in range(2):
            for s in range(2):
                at = t * 8 + s * 4
                gain_ref[ri, s, t] = gains[ri][at:at + 4, :STATIONS]
    both = jnp.concatenate(gains, axis=0)[:, :STATIONS]
    stacked = jnp.concatenate([piece.astype(F32) for piece in split_three(both)], axis=0).astype(BF16)
    ends = []
    for table in (first_ref, second_ref):
        wide = dot(stacked, table[...])
        ends.append((wide[:32] + wide[32:64]) + wide[64:])
    left, right = ends
    lr, li, rr, ri_ = left[:16], left[16:], right[:16], right[16:]
    model = (lr * rr + li * ri_, li * rr - lr * ri_)
    for ri in range(2):
        for t in range(2):
            model_ref[ri, t] = model[ri][t * 8:(t + 1) * 8]


def clean_kernel(width, me_ref, delay_ref, model_ref, vis_ref, out_ref, coarse_s):
    time = pl.program_id(0)
    anchor = me_ref[0].astype(F32) * float(width)
    size = out_ref.shape[4]
    fine = []
    for s in range(2):
        cr, ci, fr, fi = phase_rows(delay_ref[s, pl.ds(time, 1), :], anchor, width)
        spread(coarse_s, s, cr, ci)
        fine.append((fr, fi))
    for tile in range(size // 128):
        cut = slice(tile * 128, tile * 128 + 128)
        lanes = pl.ds(tile * 128, 128)
        near = [(fine[s][0][:, cut], fine[s][1][:, cut]) for s in range(2)]
        model = [[[jnp.broadcast_to(model_ref[ri, 0, s * 4 + k:s * 4 + k + 1, lanes], (8, 128))
                   for ri in range(2)] for k in range(4)] for s in range(2)]

        def step(block, carry):
            rows = pl.ds(pl.multiple_of(block * 16, 16), 16)
            wave = [[], []]
            for half in range(2):
                for s in range(2):
                    fr, fi = near[s]
                    cr = coarse_s[block * 2 + half, 2 * s:2 * s + 1, lanes]
                    ci = coarse_s[block * 2 + half, 2 * s + 1:2 * s + 2, lanes]
                    wave[s].append((cr * fr - ci * fi, cr * fi + ci * fr))
            for k in range(4):
                vr = vis_ref[0, 0, k, rows, lanes].astype(F32)
                vi = vis_ref[1, 0, k, rows, lanes].astype(F32)
                re, im = [], []
                for half in range(2):
                    total_re, total_im = 0.0, 0.0
                    for s in range(2):
                        mr, mi = model[s][k]
                        wr, wi = wave[s][half]
                        total_re = total_re + (mr * wr - mi * wi)
                        total_im = total_im + (mr * wi + mi * wr)
                    re.append(vr[half * 8:half * 8 + 8] - total_re)
                    im.append(vi[half * 8:half * 8 + 8] - total_im)
                out_ref[0, 0, k, rows, lanes] = jnp.concatenate(re, axis=0).astype(BF16)
                out_ref[1, 0, k, rows, lanes] = jnp.concatenate(im, axis=0).astype(BF16)
            return carry

        lax.fori_loop(0, width // 16, step, 0)


def partners(value, axis, stride, radix):
    count = lax.axis_size(axis)
    return [lax.ppermute(value, axis, [(i, i ^ (stride * d)) for i in range(count)]) for d in range(1, radix)]


def radices(count):
    stages, stride = [], 1
    while stride < count:
        radix = 4 if count // stride >= 4 else 2
        stages.append((stride, radix))
        stride *= radix
    return stages


def tables():
    first, second = np.triu_indices(STATIONS, 1)
    pairs = len(first)
    hot = np.zeros((STATIONS, ROWS, pairs), np.float32)
    hot[second, first, np.arange(pairs)] = 1.0
    hot[first, second, np.arange(pairs)] = 1.0
    eye = np.eye(STATIONS, dtype=np.float32)
    as_bf16 = lambda value: jnp.asarray(value, BF16)
    return as_bf16(hot.reshape(STATIONS * ROWS, pairs)), as_bf16(eye[:, first]), as_bf16(eye[:, second])


def smem():
    return pl.BlockSpec(memory_space=pltpu.SMEM)


def local(visibilities, delays, flags, windows, tracks):
    width = visibilities.shape[4]
    pairs = visibilities.shape[3]
    count = lax.axis_size("sub")
    window_count = windows.shape[0]
    turned = jnp.transpose(visibilities, (0, 1, 2, 4, 3))
    me = lax.axis_index("sub").astype(jnp.int32).reshape(1)
    gathered = flags[None]
    for stride, radix in radices(count):
        gathered = jnp.concatenate([gathered] + partners(gathered, "sub", stride, radix), axis=0)
    parts = pl.cdiv(pairs, LANES)
    delay_spec = pl.BlockSpec((2, 2, LANES), lambda t, b: (0, 0, b))
    vis_spec = pl.BlockSpec((2, 1, 4, width, LANES), lambda t, b: (0, t, 0, 0, b))
    rows = 2 * window_count + count
    vmem = lambda *shape: pltpu.VMEM(shape, F32)
    y = pl.pallas_call(
        lambda *refs: sums_kernel(width, *refs),
        grid=(2, parts),
        in_specs=[
            smem(),
            pl.BlockSpec((1, window_count), lambda t, b: (0, 0)),
            pl.BlockSpec((count, 2, width), lambda t, b: (0, 0, 0)),
            delay_spec,
            vis_spec,
        ],
        out_specs=pl.BlockSpec((2, 1, 8, LANES), lambda t, b: (0, t, 0, b)),
        out_shape=jax.ShapeDtypeStruct((2, 2, 8, pairs), F32),
        scratch_shapes=[
            pltpu.VMEM((2, rows, width), BF16),
            pltpu.VMEM((2, width, window_count), BF16),
            vmem(2, width, 128),
            vmem(5, window_count, 128),
            vmem(width // 8, 4, LANES),
            vmem(2, 2, 8, LANES),
            vmem(2, 2, width, LANES),
            pltpu.VMEM((2, 2, width, LANES), BF16),
            vmem(2, width, LANES),
            vmem(2, count, width),
        ],
        compiler_params=pltpu.CompilerParams(vmem_limit_bytes=40 * 2 ** 20),
        name="window_sums",
    )(me, windows.reshape(1, window_count), gathered, delays, turned)
    y = y.reshape(32, pairs)
    stages = radices(count)
    pieces = [y]
    for stride, radix in stages:
        if len(pieces) > 1:
            while len(pieces) > 1:
                pieces = [pieces[i] + pieces[i + 1] for i in range(0, len(pieces), 2)]
        pieces = pieces + partners(pieces[0], "sub", stride, radix)
    hot, first, second = tables()
    gains, model = pl.pallas_call(
        lambda *refs: solve_kernel(float(window_count), *refs),
        in_specs=[smem()] + [pl.BlockSpec(memory_space=pltpu.VMEM)] * (3 + len(pieces)),
        out_specs=[pl.BlockSpec(memory_space=pltpu.VMEM)] * 2,
        out_shape=[
            jax.ShapeDtypeStruct((2, 2, 2, 4, STATIONS), F32),
            jax.ShapeDtypeStruct((2, 2, 8, pairs), F32),
        ],
        scratch_shapes=[vmem(STATIONS * ROWS, 128), vmem(ROWS, 128)],
        compiler_params=pltpu.CompilerParams(vmem_limit_bytes=40 * 2 ** 20),
        name="gain_solve",
    )(tracks, hot, first, second, *pieces)
    cleaned = pl.pallas_call(
        lambda *refs: clean_kernel(width, *refs),
        grid=(2, parts),
        in_specs=[
            smem(),
            delay_spec,
            pl.BlockSpec((2, 1, 8, LANES), lambda t, b: (0, t, 0, b)),
            vis_spec,
        ],
        out_specs=vis_spec,
        out_shape=jax.ShapeDtypeStruct(turned.shape, BF16),
        scratch_shapes=[vmem(width // 8, 4, LANES)],
        compiler_params=pltpu.CompilerParams(vmem_limit_bytes=40 * 2 ** 20),
        name="clean",
    )(me, delays, model, turned)
    return jnp.transpose(cleaned, (0, 1, 2, 4, 3)), gains


def solution(mesh):
    return jax.shard_map(
        local,
        mesh=mesh,
        in_specs=(
            P(None, "obs", None, None, "sub"),
            P(None, "obs", None),
            P("obs", "sub"),
            P(),
            P(None, "obs"),
        ),
        out_specs=(P(None, "obs", None, None, "sub"), P(None, None, "obs", None, None)),
        check_vma=False,
    )
```

```python
import jax
import jax.numpy as jnp
import numpy as np
from jax import lax
from jax.experimental import pallas as pl
from jax.experimental.pallas import tpu as pltpu
from jax.sharding import PartitionSpec as P

STATIONS = 38
GITERS = 8
DAMPING = 1.0
STEPS_PER_TURN = 64.0
ROWS = 40
LANES = 384
SYSTEMS = 16

F32 = jnp.float32
BF16 = jnp.bfloat16


def iota(shape, dim):
    return lax.broadcasted_iota(jnp.int32, shape, dim).astype(F32)


def sincos_turns(turns):
    half = (turns - jnp.floor(turns + 0.5)) * np.float32(np.pi)
    sq = half * half
    sin = np.float32(-1.0 / 39916800)
    for term in (1.0 / 362880, -1.0 / 5040, 1.0 / 120, -1.0 / 6, 1.0):
        sin = sin * sq + np.float32(term)
    sin = sin * half
    cos = np.float32(1.0 / 479001600)
    for term in (-1.0 / 3628800, 1.0 / 40320, -1.0 / 720, 1.0 / 24, -0.5, 1.0):
        cos = cos * sq + np.float32(term)
    return 1.0 - 2.0 * (sin * sin), 2.0 * (sin * cos)


def split_two(value):
    high = value.astype(BF16)
    low = (value - high.astype(F32)).astype(BF16)
    return high, low


def split_three(value):
    high = value.astype(BF16)
    rest = value - high.astype(F32)
    mid = rest.astype(BF16)
    low = (rest - mid.astype(F32)).astype(BF16)
    return high, mid, low


def dot(left, right):
    return jnp.dot(left, right, preferred_element_type=F32)


def phase_rows(delay, anchor, width):
    base = anchor + 8.0 * iota((width // 8, 1), 0)
    fine = iota((8, 1), 0)
    coarse_re, coarse_im = sincos_turns(delay * (base * np.float32(1.0 / STEPS_PER_TURN)))
    fine_re, fine_im = sincos_turns(delay * (fine * np.float32(1.0 / STEPS_PER_TURN)))
    return coarse_re, coarse_im, fine_re, fine_im


def spread(rows_ref, source, real, imag):
    for row in range(real.shape[0]):
        rows_ref[row, 2 * source:2 * source + 1, :] = real[row:row + 1]
        rows_ref[row, 2 * source + 1:2 * source + 2, :] = imag[row:row + 1]


def sums_kernel(width, me_ref, win_ref, flags_ref, delay_ref, vis_ref, y_ref,
                rows_s, member_s, alpha_s, window_s, coarse_s, fine_s, wave_s, mix_s, mexp_s, wt_s):
    time, part = pl.program_id(0), pl.program_id(1)
    me = me_ref[0]
    groups = flags_ref.shape[0]
    windows = win_ref.shape[1]
    anchor = me.astype(F32) * float(width)

    @pl.when((time == 0) & (part == 0))
    def prepare():
        win_row = win_ref[...].astype(F32)
        sub, lane = iota((windows, windows), 0), iota((windows, windows), 1)
        end_c = jnp.sum(jnp.where(lane <= sub, win_row, 0.0), axis=1, keepdims=True)
        start_c = jnp.sum(jnp.where(lane < sub, win_row, 0.0), axis=1, keepdims=True)
        win_c = end_c - start_c
        end_r = jnp.sum(jnp.where(sub <= lane, win_c, 0.0), axis=0, keepdims=True)
        start_r = jnp.sum(jnp.where(sub < lane, win_c, 0.0), axis=0, keepdims=True)
        group = iota((windows, groups), 1)
        low = group * float(width)
        first_hot = jnp.where((low <= start_c) & (start_c < low + float(width)), 1.0, 0.0)
        last_hot = jnp.where((low < end_c) & (end_c <= low + float(width)), 1.0, 0.0)
        first_g = jnp.sum(first_hot * group, axis=1, keepdims=True)
        last_g = jnp.sum(last_hot * group, axis=1, keepdims=True)
        full = jnp.where((group > first_g) & (group < last_g), 1.0, 0.0)
        pick = jnp.concatenate([first_hot, last_hot, full], axis=0).astype(BF16)
        place = iota((windows, width), 1)
        head_at = first_g * float(width) + place
        head_in = (head_at >= start_c) & (head_at < end_c)
        tail_in = (last_g > first_g) & (last_g * float(width) + place < end_c)
        channel = anchor + iota((width, windows), 0)
        member = (channel >= start_r) & (channel < end_r)
        diagonal = iota((width, width), 0) == iota((width, width), 1)
        window_s[0] = jnp.broadcast_to(first_g, (windows, 128))
        window_s[1] = jnp.broadcast_to(last_g, (windows, 128))
        for t in range(2):
            for g in range(groups):
                wt_s[t, g:g + 1, :] = 1.0 - flags_ref[g, t:t + 1, :].astype(F32)
            weights = wt_s[t].astype(BF16)
            picked = dot(pick, weights)
            head = jnp.where(head_in, picked[:windows], 0.0)
            tail = jnp.where(tail_in, picked[windows:2 * windows], 0.0)
            count = jnp.sum(head + tail + picked[2 * windows:], axis=1, keepdims=True)
            scale = 1.0 / jnp.maximum(count, 1.0)
            rows_s[t] = jnp.concatenate([head, tail, wt_s[t]], axis=0).astype(BF16)
            window_s[2 + t] = jnp.broadcast_to(scale, (windows, 128))
            scale_r = jnp.sum(jnp.where(sub == lane, scale, 0.0), axis=0, keepdims=True)
            own = 1.0 - flags_ref[me, t:t + 1, :].astype(F32)
            own_c = jnp.sum(jnp.where(diagonal, own, 0.0), axis=1, keepdims=True)
            chosen = jnp.where(member, own_c, 0.0)
            member_s[t] = chosen.astype(BF16)
            alpha = jnp.sum(chosen * scale_r, axis=1, keepdims=True)
            alpha_s[t] = jnp.broadcast_to(alpha, (width, 128))
        pick_full = full.astype(BF16)
        window_s[4, :, :groups] = pick_full.astype(F32)

    size = y_ref.shape[2]
    delay = [delay_ref[s, pl.ds(time, 1), :] for s in range(2)]
    for s in range(2):
        cr, ci, fr, fi = phase_rows(delay[s], anchor, width)
        spread(coarse_s, s, cr, ci)
        fine_s[s, 0], fine_s[s, 1] = fr, fi

    def waves(block, carry):
        out = []
        for s in range(2):
            fr, fi = fine_s[s, 0], fine_s[s, 1]
            re, im = [], []
            for half in range(2):
                cr = coarse_s[block * 2 + half, 2 * s:2 * s + 1, :]
                ci = coarse_s[block * 2 + half, 2 * s + 1:2 * s + 2, :]
                re.append(cr * fr - ci * fi)
                im.append(cr * fi + ci * fr)
            out.append((jnp.concatenate(re, axis=0), jnp.concatenate(im, axis=0)))
        rows = pl.ds(pl.multiple_of(block * 16, 16), 16)
        (r0, i0), (r1, i1) = out
        for s in range(2):
            wave_s[s, 0, rows, :] = out[s][0]
            wave_s[s, 1, rows, :] = out[s][1]
        for slot, value in enumerate((r1 * r0 + i1 * i0, i1 * r0 - r1 * i0)):
            high, low = split_two(value)
            mix_s[slot, 0, rows, :] = high
            mix_s[slot, 1, rows, :] = low
        return carry

    lax.fori_loop(0, width // 16, waves, 0)

    rows = rows_s[time]
    sums = [dot(rows, mix_s[slot, 0]) + dot(rows, mix_s[slot, 1]) for slot in range(2)]
    gap = delay[1] - delay[0]
    per_group = np.float32(width / STEPS_PER_TURN)
    me_f = me.astype(F32)
    total_re, total_im = 0.0, 0.0
    for which in range(2):
        block = window_s[which][:, :1]
        pr, pi = sincos_turns(gap * ((block - me_f) * per_group))
        hr, hi = (part_sum[which * windows:(which + 1) * windows] for part_sum in sums)
        total_re = total_re + (pr * hr - pi * hi)
        total_im = total_im + (pr * hi + pi * hr)
    pr, pi = sincos_turns(gap * ((iota((groups, 1), 0) - me_f) * per_group))
    gr, gi = (part_sum[2 * windows:] for part_sum in sums)
    pick_full = window_s[4][:, :groups].astype(BF16)
    for slot, value in enumerate((pr * gr - pi * gi, pr * gi + pi * gr)):
        high, low = split_two(value)
        term = dot(pick_full, high) + dot(pick_full, low)
        if slot == 0:
            total_re = total_re + term
        else:
            total_im = total_im + term
    scale = window_s[2 + time][:, :1]
    chosen = member_s[time]
    for slot, value in enumerate((total_re, total_im)):
        high, low = split_two(value * (scale * scale))
        mexp_s[slot] = dot(chosen, high) + dot(chosen, low)

    for tile in range(size // 128):
        lanes = pl.ds(tile * 128, 128)

        def step(block, sums):
            rows = pl.ds(pl.multiple_of(block * 16, 16), 16)
            alpha = alpha_s[time, rows, :]
            mr, mi = mexp_s[0, rows, lanes], mexp_s[1, rows, lanes]
            r0, i0 = wave_s[0, 0, rows, lanes], wave_s[0, 1, rows, lanes]
            r1, i1 = wave_s[1, 0, rows, lanes], wave_s[1, 1, rows, lanes]
            factors = (
                (alpha * r0 - (mr * r1 + mi * i1), (mr * i1 - mi * r1) - alpha * i0),
                (alpha * r1 - (mr * r0 - mi * i0), (mr * i0 + mi * r0) - alpha * i1),
            )
            new = []
            for k in range(4):
                vr = vis_ref[0, 0, k, rows, lanes].astype(F32)
                vi = vis_ref[1, 0, k, rows, lanes].astype(F32)
                for s in range(2):
                    fr, fi = factors[s]
                    re = vr * fr - vi * fi
                    im = vr * fi + vi * fr
                    new.append(sums[len(new)] + (re[:8] + re[8:]))
                    new.append(sums[len(new)] + (im[:8] + im[8:]))
            return tuple(new)

        zero = jnp.zeros((8, 128), F32)
        sums = lax.fori_loop(0, width // 16, step, (zero,) * 16)
        for k in range(4):
            for s in range(2):
                for ri in range(2):
                    y_ref[s * 4 + k, ri:ri + 1, lanes] = jnp.sum(
                        sums[(k * 2 + s) * 2 + ri], axis=0, keepdims=True)


def solve_kernel(window_count, me_ref, tracks_ref, first_ref, second_ref, part_ref, gain_ref):
    system = lax.rem(me_ref[0], SYSTEMS)
    total = part_ref[0]
    for source in range(1, part_ref.shape[0]):
        total = total + part_ref[source]
    rows = []
    hot = first_ref[...]
    other = second_ref[...]
    for table in (hot, other):
        for ri in range(2):
            rows += [table * piece for piece in split_three(total[ri:ri + 1])]
    rows = [row.astype(BF16) for row in rows]
    nt = lambda left, right: lax.dot_general(
        left, right, (((1,), (1,)), ((), ())), preferred_element_type=F32)
    upper = nt(jnp.concatenate(rows[:6], axis=0), other)
    lower = nt(jnp.concatenate(rows[6:], axis=0), hot)
    cut = lambda value, i: value[i * ROWS:(i + 1) * ROWS]
    join = lambda value, i: (cut(value, 3 * i) + cut(value, 3 * i + 1)) + cut(value, 3 * i + 2)
    re = join(upper, 0) + join(lower, 0)
    im = join(upper, 1) - join(lower, 1)
    live_r = iota((1, ROWS), 1) < float(STATIONS)
    live_c = iota((ROWS, 1), 0) < float(STATIONS)
    row_re, row_im = jnp.where(live_r, 1.0, 0.0), jnp.zeros((1, ROWS), F32)
    col_re, col_im = jnp.where(live_c, 1.0, 0.0), jnp.zeros((ROWS, 1), F32)
    for turn in range(GITERS):
        pull_cr = jnp.sum(re * row_re - im * row_im, axis=1, keepdims=True)
        pull_ci = jnp.sum(re * row_im + im * row_re, axis=1, keepdims=True)
        pull_rr = jnp.sum(re * col_re + im * col_im, axis=0, keepdims=True)
        pull_ri = jnp.sum(re * col_im - im * col_re, axis=0, keepdims=True)
        power_r = row_re * row_re + row_im * row_im
        power_c = col_re * col_re + col_im * col_im
        total = jnp.sum(power_c, axis=0, keepdims=True)
        inverse_r = 1.0 / (window_count * (total - power_r) + DAMPING)
        inverse_c = 1.0 / (window_count * (total - power_c) + DAMPING)
        row_re, row_im = 0.5 * (row_re + pull_rr * inverse_r), 0.5 * (row_im + pull_ri * inverse_r)
        col_re, col_im = 0.5 * (col_re + pull_cr * inverse_c), 0.5 * (col_im + pull_ci * inverse_c)
    visible = tracks_ref[lax.rem(lax.div(system, 4), 2), lax.div(system, 8)].astype(F32)
    gains = jnp.concatenate([row_re, row_im], axis=0)[:, :STATIONS] * visible
    for target in range(gain_ref.shape[0]):
        gain_ref[target] = gains


def clean_kernel(width, me_ref, delay_ref, first_ref, second_ref, gain_ref, vis_ref, out_ref, gain_out_ref,
                 coarse_s, split_s):
    time, part = pl.program_id(0), pl.program_id(1)
    anchor = me_ref[0].astype(F32) * float(width)
    size = out_ref.shape[4]

    @pl.when((time == 0) & (part == 0))
    def prepare():
        for t in range(2):
            for s in range(2):
                for k in range(4):
                    pair = gain_ref[t * 8 + s * 4 + k]
                    for ri in range(2):
                        gain_out_ref[ri, s, t, k:k + 1, :] = pair[ri:ri + 1]
        for t in range(2):
            both = jnp.concatenate(
                [jnp.concatenate([gain_out_ref[ri, s, t] for s in range(2)], axis=0) for ri in range(2)], axis=0)
            split_s[t] = jnp.concatenate(split_three(both), axis=0)

    ends = []
    for table in (first_ref, second_ref):
        wide = dot(split_s[time], table[...])
        ends.append((wide[:16] + wide[16:32]) + wide[32:])
    left, right = ends
    model_re = left[:8] * right[:8] + left[8:] * right[8:]
    model_im = left[8:] * right[:8] - left[:8] * right[8:]
    fine = []
    for s in range(2):
        cr, ci, fr, fi = phase_rows(delay_ref[s, pl.ds(time, 1), :], anchor, width)
        spread(coarse_s, s, cr, ci)
        fine.append((fr, fi))
    for tile in range(size // 128):
        cut = slice(tile * 128, tile * 128 + 128)
        lanes = pl.ds(tile * 128, 128)
        near = [(fine[s][0][:, cut], fine[s][1][:, cut]) for s in range(2)]
        model = [[[jnp.broadcast_to(value[s * 4 + k:s * 4 + k + 1, cut], (8, 128))
                   for value in (model_re, model_im)] for k in range(4)] for s in range(2)]

        def step(block, carry):
            rows = pl.ds(pl.multiple_of(block * 16, 16), 16)
            wave = [[], []]
            for half in range(2):
                for s in range(2):
                    fr, fi = near[s]
                    cr = coarse_s[block * 2 + half, 2 * s:2 * s + 1, lanes]
                    ci = coarse_s[block * 2 + half, 2 * s + 1:2 * s + 2, lanes]
                    wave[s].append((cr * fr - ci * fi, cr * fi + ci * fr))
            for k in range(4):
                vr = vis_ref[0, 0, k, rows, lanes].astype(F32)
                vi = vis_ref[1, 0, k, rows, lanes].astype(F32)
                re, im = [], []
                for half in range(2):
                    total_re, total_im = 0.0, 0.0
                    for s in range(2):
                        mr, mi = model[s][k]
                        wr, wi = wave[s][half]
                        total_re = total_re + (mr * wr - mi * wi)
                        total_im = total_im + (mr * wi + mi * wr)
                    re.append(vr[half * 8:half * 8 + 8] - total_re)
                    im.append(vi[half * 8:half * 8 + 8] - total_im)
                out_ref[0, 0, k, rows, lanes] = jnp.concatenate(re, axis=0).astype(BF16)
                out_ref[1, 0, k, rows, lanes] = jnp.concatenate(im, axis=0).astype(BF16)
            return carry

        lax.fori_loop(0, width // 16, step, 0)


def tables():
    first, second = np.triu_indices(STATIONS, 1)
    eye = np.eye(ROWS, dtype=np.float32)
    return jnp.asarray(eye[:, first], BF16), jnp.asarray(eye[:, second], BF16)


def exchange(value):
    return lax.all_to_all(value, "sub", 0, 0)


def smem():
    return pl.BlockSpec(memory_space=pltpu.SMEM)


def local(visibilities, delays, flags, windows, tracks):
    width = visibilities.shape[4]
    pairs = visibilities.shape[3]
    count = lax.axis_size("sub")
    window_count = windows.shape[0]
    turned = jnp.transpose(visibilities, (0, 1, 2, 4, 3))
    me = lax.axis_index("sub").astype(jnp.int32).reshape(1)
    gathered = exchange(jnp.broadcast_to(flags[None], (count,) + flags.shape))
    parts = pl.cdiv(pairs, LANES)
    delay_spec = pl.BlockSpec((2, 2, LANES), lambda t, b: (0, 0, b))
    vis_spec = pl.BlockSpec((2, 1, 4, width, LANES), lambda t, b: (0, t, 0, 0, b))
    rows = 2 * window_count + count
    vmem = lambda *shape: pltpu.VMEM(shape, F32)
    y = pl.pallas_call(
        lambda *refs: sums_kernel(width, *refs),
        grid=(2, parts),
        in_specs=[
            smem(),
            pl.BlockSpec((1, window_count), lambda t, b: (0, 0)),
            pl.BlockSpec((count, 2, width), lambda t, b: (0, 0, 0)),
            delay_spec,
            vis_spec,
        ],
        out_specs=pl.BlockSpec((8, 2, LANES), lambda t, b: (t, 0, b)),
        out_shape=jax.ShapeDtypeStruct((SYSTEMS, 2, pairs), F32),
        scratch_shapes=[
            pltpu.VMEM((2, rows, width), BF16),
            pltpu.VMEM((2, width, window_count), BF16),
            vmem(2, width, 128),
            vmem(5, window_count, 128),
            vmem(width // 8, 4, LANES),
            vmem(2, 2, 8, LANES),
            vmem(2, 2, width, LANES),
            pltpu.VMEM((2, 2, width, LANES), BF16),
            vmem(2, width, LANES),
            vmem(2, count, width),
        ],
        compiler_params=pltpu.CompilerParams(vmem_limit_bytes=60 * 2 ** 20),
        name="window_sums",
    )(me, windows.reshape(1, window_count), gathered, delays, turned)
    if count > SYSTEMS:
        y = jnp.tile(y, (count // SYSTEMS, 1, 1))
    y = exchange(y)
    first, second = tables()
    gains = pl.pallas_call(
        lambda *refs: solve_kernel(float(window_count), *refs),
        in_specs=[smem(), smem()] + [pl.BlockSpec(memory_space=pltpu.VMEM)] * 3,
        out_specs=pl.BlockSpec(memory_space=pltpu.VMEM),
        out_shape=jax.ShapeDtypeStruct((count, 2, STATIONS), F32),
        compiler_params=pltpu.CompilerParams(vmem_limit_bytes=40 * 2 ** 20),
        name="gain_solve",
    )(me, tracks, first, second, y)
    gains = exchange(gains)
    table_spec = pl.BlockSpec((STATIONS, LANES), lambda t, b: (0, b))
    cleaned, gains = pl.pallas_call(
        lambda *refs: clean_kernel(width, *refs),
        grid=(2, parts),
        in_specs=[
            smem(),
            delay_spec,
            table_spec,
            table_spec,
            pl.BlockSpec((count, 2, STATIONS), lambda t, b: (0, 0, 0)),
            vis_spec,
        ],
        out_specs=[vis_spec, pl.BlockSpec((2, 2, 2, 4, STATIONS), lambda t, b: (0, 0, 0, 0, 0))],
        out_shape=[
            jax.ShapeDtypeStruct(turned.shape, BF16),
            jax.ShapeDtypeStruct((2, 2, 2, 4, STATIONS), F32),
        ],
        scratch_shapes=[vmem(width // 8, 4, LANES), pltpu.VMEM((2, 48, STATIONS), BF16)],
        compiler_params=pltpu.CompilerParams(vmem_limit_bytes=60 * 2 ** 20),
        name="clean",
    )(me, delays, first[:STATIONS], second[:STATIONS], gains, turned)
    return jnp.transpose(cleaned, (0, 1, 2, 4, 3)), gains


def solution(mesh):
    return jax.shard_map(
        local,
        mesh=mesh,
        in_specs=(
            P(None, "obs", None, None, "sub"),
            P(None, "obs", None),
            P("obs", "sub"),
            P(),
            P(None, "obs"),
        ),
        out_specs=(P(None, "obs", None, None, "sub"), P(None, None, "obs", None, None)),
        check_vma=False,
    )
```

```python
import jax
import jax.numpy as jnp
import numpy as np
from jax import lax
from jax.experimental import pallas as pl
from jax.experimental.pallas import tpu as pltpu
from jax.sharding import PartitionSpec as P

STATIONS = 38
GITERS = 8
DAMPING = 1.0
STEPS_PER_TURN = 64.0
ROWS = 40
LANES = 384

F32 = jnp.float32
BF16 = jnp.bfloat16


def iota(shape, dim):
    return lax.broadcasted_iota(jnp.int32, shape, dim).astype(F32)


def sincos_turns(turns):
    half = (turns - jnp.floor(turns + 0.5)) * np.float32(np.pi)
    sq = half * half
    sin = np.float32(-1.0 / 39916800)
    for term in (1.0 / 362880, -1.0 / 5040, 1.0 / 120, -1.0 / 6, 1.0):
        sin = sin * sq + np.float32(term)
    sin = sin * half
    cos = np.float32(1.0 / 479001600)
    for term in (-1.0 / 3628800, 1.0 / 40320, -1.0 / 720, 1.0 / 24, -0.5, 1.0):
        cos = cos * sq + np.float32(term)
    return 1.0 - 2.0 * (sin * sin), 2.0 * (sin * cos)


def split_two(value):
    high = value.astype(BF16)
    low = (value - high.astype(F32)).astype(BF16)
    return high, low


def split_three(value):
    high = value.astype(BF16)
    rest = value - high.astype(F32)
    mid = rest.astype(BF16)
    low = (rest - mid.astype(F32)).astype(BF16)
    return high, mid, low


def dot(left, right):
    return jnp.dot(left, right, preferred_element_type=F32)


def phase_rows(delay, anchor, width):
    base = anchor + 8.0 * iota((width // 8, 1), 0)
    fine = iota((8, 1), 0)
    coarse_re, coarse_im = sincos_turns(delay * (base * np.float32(1.0 / STEPS_PER_TURN)))
    fine_re, fine_im = sincos_turns(delay * (fine * np.float32(1.0 / STEPS_PER_TURN)))
    return coarse_re, coarse_im, fine_re, fine_im


def spread(rows_ref, source, real, imag):
    for row in range(real.shape[0]):
        rows_ref[row, 2 * source:2 * source + 1, :] = real[row:row + 1]
        rows_ref[row, 2 * source + 1:2 * source + 2, :] = imag[row:row + 1]


def sums_kernel(width, stages, me_ref, win_ref, *refs):
    flag_refs, refs = refs[:stages], refs[stages:]
    (delay_ref, vis_ref, keep_ref, send_ref,
     rows_s, member_s, alpha_s, window_s, coarse_s, fine_s, wave_s, mix_s, mexp_s, wt_s) = refs
    part, time = pl.program_id(0), pl.program_id(1)
    me = me_ref[0]
    near = flag_refs[0].shape[0]
    groups = near * stages
    windows = win_ref.shape[1]
    anchor = me.astype(F32) * float(width)

    @pl.when((time == 0) & (part == 0))
    def prepare():
        win_row = win_ref[...].astype(F32)
        sub, lane = iota((windows, windows), 0), iota((windows, windows), 1)
        end_c = jnp.sum(jnp.where(lane <= sub, win_row, 0.0), axis=1, keepdims=True)
        start_c = jnp.sum(jnp.where(lane < sub, win_row, 0.0), axis=1, keepdims=True)
        win_c = end_c - start_c
        end_r = jnp.sum(jnp.where(sub <= lane, win_c, 0.0), axis=0, keepdims=True)
        start_r = jnp.sum(jnp.where(sub < lane, win_c, 0.0), axis=0, keepdims=True)
        group = iota((windows, groups), 1)
        low = group * float(width)
        first_hot = jnp.where((low <= start_c) & (start_c < low + float(width)), 1.0, 0.0)
        last_hot = jnp.where((low < end_c) & (end_c <= low + float(width)), 1.0, 0.0)
        first_g = jnp.sum(first_hot * group, axis=1, keepdims=True)
        last_g = jnp.sum(last_hot * group, axis=1, keepdims=True)
        full = jnp.where((group > first_g) & (group < last_g), 1.0, 0.0)
        pick = jnp.concatenate([first_hot, last_hot, full], axis=0).astype(BF16)
        place = iota((windows, width), 1)
        head_at = first_g * float(width) + place
        head_in = (head_at >= start_c) & (head_at < end_c)
        tail_in = (last_g > first_g) & (last_g * float(width) + place < end_c)
        channel = anchor + iota((width, windows), 0)
        member = (channel >= start_r) & (channel < end_r)
        diagonal = iota((width, width), 0) == iota((width, width), 1)
        window_s[0] = jnp.broadcast_to(first_g, (windows, 128))
        window_s[1] = jnp.broadcast_to(last_g, (windows, 128))
        for t in range(2):
            for slot in range(groups):
                row = flag_refs[slot // near][slot % near, t:t + 1, :].astype(F32)
                wt_s[lax.bitwise_xor(me, slot), t:t + 1, :] = 1.0 - row
            weights = wt_s[:, t, :].astype(BF16)
            picked = dot(pick, weights)
            head = jnp.where(head_in, picked[:windows], 0.0)
            tail = jnp.where(tail_in, picked[windows:2 * windows], 0.0)
            count = jnp.sum(head + tail + picked[2 * windows:], axis=1, keepdims=True)
            scale = 1.0 / jnp.maximum(count, 1.0)
            rows_s[t] = jnp.concatenate([head, tail, wt_s[:, t, :]], axis=0).astype(BF16)
            window_s[2 + t] = jnp.broadcast_to(scale, (windows, 128))
            scale_r = jnp.sum(jnp.where(sub == lane, scale, 0.0), axis=0, keepdims=True)
            own = 1.0 - flag_refs[0][0, t:t + 1, :].astype(F32)
            own_c = jnp.sum(jnp.where(diagonal, own, 0.0), axis=1, keepdims=True)
            chosen = jnp.where(member, own_c, 0.0)
            member_s[t] = chosen.astype(BF16)
            alpha = jnp.sum(chosen * scale_r, axis=1, keepdims=True)
            alpha_s[t] = jnp.broadcast_to(alpha, (width, 128))
        pick_full = full.astype(BF16)
        window_s[4, :, :groups] = pick_full.astype(F32)

    size = keep_ref.shape[2]
    delay = [delay_ref[s, pl.ds(time, 1), :] for s in range(2)]
    for s in range(2):
        cr, ci, fr, fi = phase_rows(delay[s], anchor, width)
        spread(coarse_s, s, cr, ci)
        fine_s[s, 0], fine_s[s, 1] = fr, fi

    def waves(block, carry):
        out = []
        for s in range(2):
            fr, fi = fine_s[s, 0], fine_s[s, 1]
            re, im = [], []
            for half in range(2):
                cr = coarse_s[block * 2 + half, 2 * s:2 * s + 1, :]
                ci = coarse_s[block * 2 + half, 2 * s + 1:2 * s + 2, :]
                re.append(cr * fr - ci * fi)
                im.append(cr * fi + ci * fr)
            out.append((jnp.concatenate(re, axis=0), jnp.concatenate(im, axis=0)))
        rows = pl.ds(pl.multiple_of(block * 16, 16), 16)
        (r0, i0), (r1, i1) = out
        for s in range(2):
            wave_s[s, 0, rows, :] = out[s][0]
            wave_s[s, 1, rows, :] = out[s][1]
        for slot, value in enumerate((r1 * r0 + i1 * i0, i1 * r0 - r1 * i0)):
            high, low = split_two(value)
            mix_s[slot, 0, rows, :] = high
            mix_s[slot, 1, rows, :] = low
        return carry

    lax.fori_loop(0, width // 16, waves, 0, unroll=4)

    rows = rows_s[time]
    sums = [dot(rows, mix_s[slot, 0]) + dot(rows, mix_s[slot, 1]) for slot in range(2)]
    gap = delay[1] - delay[0]
    per_group = np.float32(width / STEPS_PER_TURN)
    me_f = me.astype(F32)
    total_re, total_im = 0.0, 0.0
    for which in range(2):
        block = window_s[which][:, :1]
        pr, pi = sincos_turns(gap * ((block - me_f) * per_group))
        hr, hi = (part_sum[which * windows:(which + 1) * windows] for part_sum in sums)
        total_re = total_re + (pr * hr - pi * hi)
        total_im = total_im + (pr * hi + pi * hr)
    pr, pi = sincos_turns(gap * ((iota((groups, 1), 0) - me_f) * per_group))
    gr, gi = (part_sum[2 * windows:] for part_sum in sums)
    pick_full = window_s[4][:, :groups].astype(BF16)
    for slot, value in enumerate((pr * gr - pi * gi, pr * gi + pi * gr)):
        high, low = split_two(value)
        term = dot(pick_full, high) + dot(pick_full, low)
        if slot == 0:
            total_re = total_re + term
        else:
            total_im = total_im + term
    scale = window_s[2 + time][:, :1]
    chosen = member_s[time]
    for slot, value in enumerate((total_re, total_im)):
        high, low = split_two(value * (scale * scale))
        mexp_s[slot] = dot(chosen, high) + dot(chosen, low)

    for tile in range(size // 128):
        lanes = pl.ds(tile * 128, 128)

        def step(block, sums):
            rows = pl.ds(pl.multiple_of(block * 16, 16), 16)
            alpha = alpha_s[time, rows, :]
            mr, mi = mexp_s[0, rows, lanes], mexp_s[1, rows, lanes]
            r0, i0 = wave_s[0, 0, rows, lanes], wave_s[0, 1, rows, lanes]
            r1, i1 = wave_s[1, 0, rows, lanes], wave_s[1, 1, rows, lanes]
            factors = (
                (alpha * r0 - (mr * r1 + mi * i1), (mr * i1 - mi * r1) - alpha * i0),
                (alpha * r1 - (mr * r0 - mi * i0), (mr * i0 + mi * r0) - alpha * i1),
            )
            new = []
            for k in range(4):
                vr = vis_ref[0, 0, k, rows, lanes].astype(F32)
                vi = vis_ref[1, 0, k, rows, lanes].astype(F32)
                for s in range(2):
                    fr, fi = factors[s]
                    re = vr * fr - vi * fi
                    im = vr * fi + vi * fr
                    new.append(sums[len(new)] + (re[:8] + re[8:]))
                    new.append(sums[len(new)] + (im[:8] + im[8:]))
            return tuple(new)

        zero = jnp.zeros((8, 128), F32)
        sums = lax.fori_loop(0, width // 16, step, (zero,) * 16, unroll=4)
        for out_ref, chosen_half in ((keep_ref, 0), (send_ref, 1)):
            @pl.when(lax.bitwise_xor(time, lax.bitwise_and(me, 1)) == chosen_half)
            def write():
                for k in range(4):
                    for s in range(2):
                        place = lax.bitwise_xor(s, lax.bitwise_and(lax.div(me, 2), 1)) * 4 + k
                        for ri in range(2):
                            out_ref[place, ri:ri + 1, lanes] = jnp.sum(
                                sums[(k * 2 + s) * 2 + ri], axis=0, keepdims=True)


def solve_kernel(window_count, me_ref, tracks_ref, first_ref, second_ref, *refs):
    parts, gain_ref = refs[:-1], refs[-1]
    me = me_ref[0]
    systems = gain_ref.shape[0]
    total = parts[0][...]
    for part in parts[1:]:
        total = total + part[...]
    hot = first_ref[...]
    other = second_ref[...]
    nt = lambda left, right: lax.dot_general(
        left, right, (((1,), (1,)), ((), ())), preferred_element_type=F32)
    upper, lower = [], []
    for system in range(systems):
        for ri in range(2):
            for piece in split_two(total[system, ri:ri + 1]):
                upper.append(hot * piece)
                lower.append(other * piece)
    upper = nt(jnp.concatenate(upper, axis=0), other)
    lower = nt(jnp.concatenate(lower, axis=0), hot)
    cut = lambda value, i: value[i * ROWS:(i + 1) * ROWS]
    join = lambda value, i: cut(value, 2 * i) + cut(value, 2 * i + 1)
    live_r = jnp.where(iota((1, ROWS), 1) < float(STATIONS), 1.0, 0.0)
    live_c = jnp.where(iota((ROWS, 1), 0) < float(STATIONS), 1.0, 0.0)
    matrices = [(join(upper, 2 * i) + join(lower, 2 * i), join(upper, 2 * i + 1) - join(lower, 2 * i + 1))
                for i in range(systems)]
    states = [(live_r, 0.0 * live_r, live_c, 0.0 * live_c)] * systems
    for turn in range(GITERS):
        for system in range(systems):
            re, im = matrices[system]
            row_re, row_im, col_re, col_im = states[system]
            pull_cr = jnp.sum(re * row_re - im * row_im, axis=1, keepdims=True)
            pull_ci = jnp.sum(re * row_im + im * row_re, axis=1, keepdims=True)
            pull_rr = jnp.sum(re * col_re + im * col_im, axis=0, keepdims=True)
            pull_ri = jnp.sum(re * col_im - im * col_re, axis=0, keepdims=True)
            power_r = row_re * row_re + row_im * row_im
            power_c = col_re * col_re + col_im * col_im
            total = jnp.sum(power_c, axis=0, keepdims=True)
            inverse_r = 0.5 / (window_count * (total - power_r) + DAMPING)
            inverse_c = 0.5 / (window_count * (total - power_c) + DAMPING)
            states[system] = (0.5 * row_re + pull_rr * inverse_r, 0.5 * row_im + pull_ri * inverse_r,
                              0.5 * col_re + pull_cr * inverse_c, 0.5 * col_im + pull_ci * inverse_c)
    visible = tracks_ref[lax.bitwise_and(lax.div(me, 2), 1), lax.bitwise_and(me, 1)].astype(F32)
    for system in range(systems):
        row_re, row_im = states[system][:2]
        gain_ref[system] = jnp.concatenate([row_re, row_im], axis=0)[:, :STATIONS] * visible


def clean_kernel(width, me_ref, delay_ref, first_ref, second_ref, *refs):
    gain_refs, refs = refs[:4], refs[4:]
    vis_ref, out_ref, gain_out_ref, coarse_s, split_s = refs
    part, time = pl.program_id(0), pl.program_id(1)
    me = me_ref[0]
    anchor = me.astype(F32) * float(width)
    size = out_ref.shape[4]

    @pl.when((time == 0) & (part == 0))
    def prepare():
        mine = lax.bitwise_and(me, 3)
        held = [ref[...] for ref in gain_refs]
        for t in range(2):
            for s in range(2):
                owner = t + 2 * s
                group = held[0]
                for d in range(1, 4):
                    group = jnp.where(lax.bitwise_xor(mine, owner) == d, held[d], group)
                for k in range(4):
                    for ri in range(2):
                        gain_out_ref[ri, s, t, k:k + 1, :] = group[k, ri:ri + 1]
        for t in range(2):
            both = jnp.concatenate(
                [jnp.concatenate([gain_out_ref[ri, s, t] for s in range(2)], axis=0) for ri in range(2)], axis=0)
            split_s[t] = jnp.concatenate(split_three(both), axis=0)

    ends = []
    for table in (first_ref, second_ref):
        wide = dot(split_s[time], table[...])
        ends.append((wide[:16] + wide[16:32]) + wide[32:])
    left, right = ends
    model_re = left[:8] * right[:8] + left[8:] * right[8:]
    model_im = left[8:] * right[:8] - left[:8] * right[8:]
    fine = []
    for s in range(2):
        cr, ci, fr, fi = phase_rows(delay_ref[s, pl.ds(time, 1), :], anchor, width)
        spread(coarse_s, s, cr, ci)
        fine.append((fr, fi))
    for tile in range(size // 128):
        cut = slice(tile * 128, tile * 128 + 128)
        lanes = pl.ds(tile * 128, 128)
        near = [(fine[s][0][:, cut], fine[s][1][:, cut]) for s in range(2)]
        model = [[[jnp.broadcast_to(value[s * 4 + k:s * 4 + k + 1, cut], (8, 128))
                   for value in (model_re, model_im)] for k in range(4)] for s in range(2)]

        def step(block, carry):
            rows = pl.ds(pl.multiple_of(block * 16, 16), 16)
            wave = [[], []]
            for half in range(2):
                for s in range(2):
                    fr, fi = near[s]
                    cr = coarse_s[block * 2 + half, 2 * s:2 * s + 1, lanes]
                    ci = coarse_s[block * 2 + half, 2 * s + 1:2 * s + 2, lanes]
                    wave[s].append((cr * fr - ci * fi, cr * fi + ci * fr))
            for k in range(4):
                vr = vis_ref[0, 0, k, rows, lanes].astype(F32)
                vi = vis_ref[1, 0, k, rows, lanes].astype(F32)
                re, im = [], []
                for half in range(2):
                    total_re, total_im = 0.0, 0.0
                    for s in range(2):
                        mr, mi = model[s][k]
                        wr, wi = wave[s][half]
                        total_re = total_re + (mr * wr - mi * wi)
                        total_im = total_im + (mr * wi + mi * wr)
                    re.append(vr[half * 8:half * 8 + 8] - total_re)
                    im.append(vi[half * 8:half * 8 + 8] - total_im)
                out_ref[0, 0, k, rows, lanes] = jnp.concatenate(re, axis=0).astype(BF16)
                out_ref[1, 0, k, rows, lanes] = jnp.concatenate(im, axis=0).astype(BF16)
            return carry

        lax.fori_loop(0, width // 16, step, 0, unroll=4)


def tables():
    first, second = np.triu_indices(STATIONS, 1)
    eye = np.eye(ROWS, dtype=np.float32)
    return jnp.asarray(eye[:, first], BF16), jnp.asarray(eye[:, second], BF16)


def partner(value, bits):
    count = lax.axis_size("sub")
    return lax.ppermute(value, "sub", [(i, i ^ bits) for i in range(count)])


def smem():
    return pl.BlockSpec(memory_space=pltpu.SMEM)


def local(visibilities, delays, flags, windows, tracks):
    width = visibilities.shape[4]
    pairs = visibilities.shape[3]
    count = lax.axis_size("sub")
    window_count = windows.shape[0]
    turned = jnp.transpose(visibilities, (0, 1, 2, 4, 3))
    me = lax.axis_index("sub").astype(jnp.int32).reshape(1)
    gathered = [flags[None]]
    stride = 1
    while stride < count:
        gathered = [jnp.concatenate(gathered, axis=0)] if len(gathered) > 1 else gathered
        gathered += [partner(gathered[0], stride * d) for d in range(1, min(4, count // stride))]
        stride *= 4
    parts = pl.cdiv(pairs, LANES)
    delay_spec = pl.BlockSpec((2, 2, LANES), lambda b, t: (0, 0, b))
    vis_spec = pl.BlockSpec((2, 1, 4, width, LANES), lambda b, t: (0, t, 0, 0, b))
    rows = 2 * window_count + count
    vmem = lambda *shape: pltpu.VMEM(shape, F32)
    keep, send = pl.pallas_call(
        lambda *refs: sums_kernel(width, len(gathered), *refs),
        grid=(parts, 2),
        in_specs=[
            smem(),
            pl.BlockSpec((1, window_count), lambda b, t: (0, 0)),
        ] + [pl.BlockSpec(piece.shape, lambda b, t: (0, 0, 0)) for piece in gathered] + [
            delay_spec,
            vis_spec,
        ],
        out_specs=[pl.BlockSpec((8, 2, LANES), lambda b, t: (0, 0, b))] * 2,
        out_shape=[jax.ShapeDtypeStruct((8, 2, pairs), F32)] * 2,
        scratch_shapes=[
            pltpu.VMEM((2, rows, width), BF16),
            pltpu.VMEM((2, width, window_count), BF16),
            vmem(2, width, 128),
            vmem(5, window_count, 128),
            vmem(width // 8, 4, LANES),
            vmem(2, 2, 8, LANES),
            vmem(2, 2, width, LANES),
            pltpu.VMEM((2, 2, width, LANES), BF16),
            vmem(2, width, LANES),
            vmem(count, 2, width),
        ],
        compiler_params=pltpu.CompilerParams(vmem_limit_bytes=60 * 2 ** 20),
        name="window_sums",
    )(me, windows.reshape(1, window_count), *gathered, delays, turned)
    got = partner(send, 1)
    send = keep[4:] + got[4:]
    keep = keep[:4] + got[:4]
    pieces = [keep, partner(send, 2)]
    stride = 4
    while stride < count:
        keep = pieces[0] + pieces[1]
        pieces = [keep, partner(keep, stride)]
        stride *= 2
    first, second = tables()
    gains = pl.pallas_call(
        lambda *refs: solve_kernel(float(window_count), *refs),
        in_specs=[smem(), smem()] + [pl.BlockSpec(memory_space=pltpu.VMEM)] * (2 + len(pieces)),
        out_specs=pl.BlockSpec(memory_space=pltpu.VMEM),
        out_shape=jax.ShapeDtypeStruct((4, 2, STATIONS), F32),
        compiler_params=pltpu.CompilerParams(vmem_limit_bytes=40 * 2 ** 20),
        name="gain_solve",
    )(me, tracks, first, second, *pieces)
    gains = [gains] + [partner(gains, d) for d in range(1, 4)]
    table_spec = pl.BlockSpec((STATIONS, LANES), lambda b, t: (0, b))
    cleaned, gains = pl.pallas_call(
        lambda *refs: clean_kernel(width, *refs),
        grid=(parts, 2),
        in_specs=[
            smem(),
            delay_spec,
            table_spec,
            table_spec,
        ] + [pl.BlockSpec((4, 2, STATIONS), lambda b, t: (0, 0, 0))] * 4 + [
            vis_spec,
        ],
        out_specs=[vis_spec, pl.BlockSpec((2, 2, 2, 4, STATIONS), lambda b, t: (0, 0, 0, 0, 0))],
        out_shape=[
            jax.ShapeDtypeStruct(turned.shape, BF16),
            jax.ShapeDtypeStruct((2, 2, 2, 4, STATIONS), F32),
        ],
        scratch_shapes=[vmem(width // 8, 4, LANES), pltpu.VMEM((2, 48, STATIONS), BF16)],
        compiler_params=pltpu.CompilerParams(vmem_limit_bytes=60 * 2 ** 20),
        name="clean",
    )(me, delays, first[:STATIONS], second[:STATIONS], *gains, turned)
    return jnp.transpose(cleaned, (0, 1, 2, 4, 3)), gains


def solution(mesh):
    return jax.shard_map(
        local,
        mesh=mesh,
        in_specs=(
            P(None, "obs", None, None, "sub"),
            P(None, "obs", None),
            P("obs", "sub"),
            P(),
            P(None, "obs"),
        ),
        out_specs=(P(None, "obs", None, None, "sub"), P(None, None, "obs", None, None)),
        check_vma=False,
    )
```

```python
import jax
import jax.numpy as jnp
import numpy as np
from jax import lax
from jax.experimental import pallas as pl
from jax.experimental.pallas import tpu as pltpu
from jax.sharding import PartitionSpec as P

STATIONS = 38
GITERS = 8
DAMPING = 1.0
STEPS_PER_TURN = 64
GAINS_AT = 768
ROWS = 40

F32 = jnp.float32
BF16 = jnp.bfloat16


def iota(shape, dim):
    return lax.broadcasted_iota(jnp.int32, shape, dim).astype(F32)


def sincos_turns(turns):
    half = (turns - jnp.floor(turns + 0.5)) * np.float32(np.pi)
    sq = half * half
    sin = np.float32(-1.0 / 39916800)
    for term in (1.0 / 362880, -1.0 / 5040, 1.0 / 120, -1.0 / 6, 1.0):
        sin = sin * sq + np.float32(term)
    sin = sin * half
    cos = np.float32(1.0 / 479001600)
    for term in (-1.0 / 3628800, 1.0 / 40320, -1.0 / 720, 1.0 / 24, -0.5, 1.0):
        cos = cos * sq + np.float32(term)
    return 1.0 - 2.0 * (sin * sin), 2.0 * (sin * cos)


def split_two(value):
    high = value.astype(BF16)
    low = (value - high.astype(F32)).astype(BF16)
    return high, low


def split_three(value):
    high = value.astype(BF16)
    rest = value - high.astype(F32)
    mid = rest.astype(BF16)
    low = (rest - mid.astype(F32)).astype(BF16)
    return high, mid, low


def dot(left, right):
    return jnp.dot(left, right, preferred_element_type=F32)


def times(left, right):
    (lr, li), (rr, ri) = left, right
    return lr * rr - li * ri, lr * ri + li * rr


def phase_rows(delays, anchor, width):
    place = iota((8, 1), 0)
    second = place >= 4.0
    turns = jnp.where(second, delays[1], delays[0])
    at = anchor + float(STEPS_PER_TURN) * jnp.where(second, place - 4.0, place)
    base = sincos_turns(turns * (at * np.float32(1.0 / STEPS_PER_TURN)))
    fine, coarse = [], []
    for s in range(2):
        low = sincos_turns(delays[s] * (place * np.float32(1.0 / STEPS_PER_TURN)))
        high = low
        for doubling in range(3):
            high = times(high, high)
        rows = [times(tuple(part[4 * s + a:4 * s + a + 1] for part in base), high)
                for a in range(width // STEPS_PER_TURN)]
        fine.append(low)
        coarse.append(rows)
    return fine, coarse


def sums_kernel(width, stages, me_ref, win_ref, *refs):
    flag_refs, refs = refs[:stages], refs[stages:]
    delay_ref, vis_ref, out_refs, coarse_ref, fine_ref = refs[0], refs[1], refs[2:6], refs[6], refs[7]
    rows_s, member_s, pick_s, alpha_s, scale_s, wave_s, mix_s, mexp_s, wt_s = refs[8:]
    time = pl.program_id(0)
    me = me_ref[0]
    near = flag_refs[0].shape[0]
    groups = near * stages
    windows = win_ref.shape[1]
    anchor = me.astype(F32) * float(width)
    size = wave_s.shape[3]

    @pl.when(time == 0)
    def prepare():
        win_row = win_ref[...].astype(F32)
        sub, lane = iota((windows, windows), 0), iota((windows, windows), 1)
        end_c = jnp.sum(jnp.where(lane <= sub, win_row, 0.0), axis=1, keepdims=True)
        start_c = jnp.sum(jnp.where(lane < sub, win_row, 0.0), axis=1, keepdims=True)
        win_c = end_c - start_c
        end_r = jnp.sum(jnp.where(sub <= lane, win_c, 0.0), axis=0, keepdims=True)
        start_r = jnp.sum(jnp.where(sub < lane, win_c, 0.0), axis=0, keepdims=True)
        group = iota((windows, groups), 1)
        low = group * float(width)
        first_hot = jnp.where((low <= start_c) & (start_c < low + float(width)), 1.0, 0.0)
        last_hot = jnp.where((low < end_c) & (end_c <= low + float(width)), 1.0, 0.0)
        first_g = jnp.sum(first_hot * group, axis=1, keepdims=True)
        last_g = jnp.sum(last_hot * group, axis=1, keepdims=True)
        full = jnp.where((group > first_g) & (group < last_g), 1.0, 0.0)
        pick = jnp.concatenate([first_hot, last_hot, full], axis=0).astype(BF16)
        pick_s[...] = pick
        place = iota((windows, width), 1)
        head_at = first_g * float(width) + place
        head_in = (head_at >= start_c) & (head_at < end_c)
        tail_in = (last_g > first_g) & (last_g * float(width) + place < end_c)
        channel = anchor + iota((width, windows), 0)
        member = (channel >= start_r) & (channel < end_r)
        diagonal = iota((width, width), 0) == iota((width, width), 1)
        for t in range(2):
            for slot in range(groups):
                row = flag_refs[slot // near][slot % near, t:t + 1, :].astype(F32)
                wt_s[lax.bitwise_xor(me, slot), t:t + 1, :] = 1.0 - row
        for t in range(2):
            weights = wt_s[:, t, :]
            picked = dot(pick, weights.astype(BF16))
            head = jnp.where(head_in, picked[:windows], 0.0)
            tail = jnp.where(tail_in, picked[windows:2 * windows], 0.0)
            count = jnp.sum(head + tail + picked[2 * windows:], axis=1, keepdims=True)
            scale = 1.0 / jnp.maximum(count, 1.0)
            rows_s[t] = jnp.concatenate([head, tail, weights], axis=0).astype(BF16)
            scale_s[t] = jnp.broadcast_to(scale, (windows, 128))
            scale_r = jnp.sum(jnp.where(sub == lane, scale, 0.0), axis=0, keepdims=True)
            own = 1.0 - flag_refs[0][0, t:t + 1, :].astype(F32)
            own_c = jnp.sum(jnp.where(diagonal, own, 0.0), axis=1, keepdims=True)
            chosen = jnp.where(member, own_c, 0.0)
            member_s[t] = chosen.astype(BF16)
            alpha = jnp.sum(chosen * scale_r, axis=1, keepdims=True)
            alpha_s[t] = jnp.broadcast_to(alpha, (width, 128))

    def waves(tile, carry):
        lanes = pl.ds(pl.multiple_of(tile * 128, 128), 128)
        delays = [jnp.where(time == 0, delay_ref[s, 0:1, lanes], delay_ref[s, 1:2, lanes]) for s in range(2)]
        fine, coarse = phase_rows(delays, anchor, width)
        for s in range(2):
            for ri in range(2):
                fine_ref[0, 2 * s + ri, :, lanes] = fine[s][ri]
                for a, rows in enumerate(coarse[s]):
                    coarse_ref[0, 2 * s + ri, 8 * a:8 * a + 8, lanes] = rows[ri]
        for block in range(width // 16):
            found = []
            for s in range(2):
                halves = []
                for half in range(2):
                    a, b = divmod(2 * block + half, 8)
                    halves.append(times(tuple(part[b:b + 1] for part in coarse[s][a]), fine[s]))
                found.append([jnp.concatenate([h[ri] for h in halves], axis=0) for ri in range(2)])
            rows = slice(block * 16, block * 16 + 16)
            (r0, i0), (r1, i1) = found
            for s in range(2):
                for ri in range(2):
                    wave_s[s, ri, rows, lanes] = found[s][ri]
            for slot, value in enumerate((r1 * r0 + i1 * i0, i1 * r0 - r1 * i0)):
                high, low = split_two(value)
                mix_s[slot, 0, rows, lanes] = high
                mix_s[slot, 1, rows, lanes] = low
        return carry

    lax.fori_loop(0, size // 128, waves, 0)

    pick = pick_s[...]
    gap = delay_ref[1, pl.ds(time, 1), :] - delay_ref[0, pl.ds(time, 1), :]
    apart = iota((groups, 1), 0) - me.astype(F32)
    phase = sincos_turns(gap * (apart * np.float32(width / STEPS_PER_TURN)))
    picked = []
    for value in phase:
        high, low = split_two(value)
        ends = pick[:2 * windows]
        picked.append(dot(ends, high) + dot(ends, low))
    rows = rows_s[time]
    sums = [dot(rows, mix_s[slot, 0]) + dot(rows, mix_s[slot, 1]) for slot in range(2)]
    total = [0.0, 0.0]
    for which in range(2):
        cut = slice(which * windows, (which + 1) * windows)
        terms = times(tuple(value[cut] for value in picked), tuple(value[cut] for value in sums))
        total = [old + new for old, new in zip(total, terms)]
    terms = times(phase, tuple(value[2 * windows:] for value in sums))
    scale = scale_s[time][:, :1]
    chosen = member_s[time]
    for slot in range(2):
        high, low = split_two(terms[slot])
        value = total[slot] + (dot(pick[2 * windows:], high) + dot(pick[2 * windows:], low))
        high, low = split_two(value * (scale * scale))
        mexp_s[slot] = dot(chosen, high) + dot(chosen, low)

    def main(tile, carry):
        lanes = pl.ds(pl.multiple_of(tile * 128, 128), 128)

        def step(block, sums):
            rows = pl.ds(pl.multiple_of(block * 16, 16), 16)
            alpha = alpha_s[time, rows, :]
            mr, mi = mexp_s[0, rows, lanes], mexp_s[1, rows, lanes]
            r0, i0 = wave_s[0, 0, rows, lanes], wave_s[0, 1, rows, lanes]
            r1, i1 = wave_s[1, 0, rows, lanes], wave_s[1, 1, rows, lanes]
            factors = []
            for fr, fi in (
                (alpha * r0 - (mr * r1 + mi * i1), (mr * i1 - mi * r1) - alpha * i0),
                (alpha * r1 - (mr * r0 - mi * i0), (mr * i0 + mi * r0) - alpha * i1),
            ):
                factors.append((fr, fi - fr, fr + fi))
            new = []
            for k in range(4):
                vr = vis_ref[0, 0, k, rows, lanes].astype(F32)
                vi = vis_ref[1, 0, k, rows, lanes].astype(F32)
                vs = vr + vi
                for s in range(2):
                    for v, f in zip((vs, vr, vi), factors[s]):
                        product = v * f
                        new.append(sums[len(new)] + (product[:8] + product[8:]))
            return tuple(new)

        zero = jnp.zeros((8, 128), F32)
        sums = lax.fori_loop(0, width // 16, step, (zero,) * 24, unroll=4)
        for s in range(2):
            owner = lax.bitwise_xor(lax.bitwise_and(me, 3), time + 2 * s)
            found = []
            for k in range(4):
                one, two, three = sums[(k * 2 + s) * 3:(k * 2 + s) * 3 + 3]
                found.append([jnp.sum(value, axis=0, keepdims=True) for value in (one - three, one + two)])
            for d in range(4):
                @pl.when(owner == d)
                def write():
                    for k in range(4):
                        for ri in range(2):
                            out_refs[d][k, ri:ri + 1, lanes] = found[k][ri]
        return carry

    lax.fori_loop(0, size // 128, main, 0)


def solve_kernel(window_count, me_ref, tracks_ref, first_ref, second_ref, *refs):
    parts, gain_ref = refs[:-1], refs[-1]
    me = me_ref[0]
    systems = gain_ref.shape[0]
    total = [part[...] for part in parts]
    while len(total) > 1:
        total = [total[i] + total[i + 1] for i in range(0, len(total), 2)]
    total = total[0]
    hot = first_ref[...]
    other = second_ref[...]
    nt = lambda left, right: lax.dot_general(
        left, right, (((1,), (1,)), ((), ())), preferred_element_type=F32)
    upper, lower = [], []
    for system in range(systems):
        for ri in range(2):
            for piece in split_two(total[system, ri:ri + 1]):
                upper.append(hot * piece)
                lower.append(other * piece)
    upper = nt(jnp.concatenate(upper, axis=0), other)
    lower = nt(jnp.concatenate(lower, axis=0), hot)
    cut = lambda value, i: value[i * ROWS:(i + 1) * ROWS]
    join = lambda value, i: cut(value, 2 * i) + cut(value, 2 * i + 1)
    live_r = jnp.where(iota((1, ROWS), 1) < float(STATIONS), 1.0, 0.0)
    live_c = jnp.where(iota((ROWS, 1), 0) < float(STATIONS), 1.0, 0.0)
    matrices = [(join(upper, 2 * i) + join(lower, 2 * i), join(upper, 2 * i + 1) - join(lower, 2 * i + 1))
                for i in range(systems)]
    states = [(live_r, 0.0 * live_r, live_c, 0.0 * live_c)] * systems
    for turn in range(GITERS):
        for system in range(systems):
            re, im = matrices[system]
            row_re, row_im, col_re, col_im = states[system]
            pull_cr = jnp.sum(re * row_re - im * row_im, axis=1, keepdims=True)
            pull_ci = jnp.sum(re * row_im + im * row_re, axis=1, keepdims=True)
            pull_rr = jnp.sum(re * col_re + im * col_im, axis=0, keepdims=True)
            pull_ri = jnp.sum(re * col_im - im * col_re, axis=0, keepdims=True)
            power_r = row_re * row_re + row_im * row_im
            power_c = col_re * col_re + col_im * col_im
            total = jnp.sum(power_c, axis=0, keepdims=True)
            inverse_r = 0.5 / (window_count * (total - power_r) + DAMPING)
            inverse_c = 0.5 / (window_count * (total - power_c) + DAMPING)
            states[system] = (0.5 * row_re + pull_rr * inverse_r, 0.5 * row_im + pull_ri * inverse_r,
                              0.5 * col_re + pull_cr * inverse_c, 0.5 * col_im + pull_ci * inverse_c)
    visible = tracks_ref[lax.bitwise_and(lax.div(me, 2), 1), lax.bitwise_and(me, 1)].astype(F32)
    gains = [state[ri] * visible for state in states for ri in range(2)]
    gains = jnp.concatenate(gains, axis=0)
    stacked = jnp.concatenate([piece.astype(F32) for piece in split_three(gains)], axis=0).astype(BF16)
    ends = []
    for table in (hot, other):
        wide = dot(stacked, table)
        ends.append((wide[:8] + wide[8:16]) + wide[16:])
    pairs = hot.shape[1]
    for system in range(systems):
        (lr, li), (rr, ri_) = [[end[2 * system + ri:2 * system + ri + 1] for ri in range(2)] for end in ends]
        gain_ref[system, 0:1, :pairs] = lr * rr + li * ri_
        gain_ref[system, 1:2, :pairs] = li * rr - lr * ri_
        gain_ref[system, :, GAINS_AT:] = gains[2 * system:2 * system + 2, :STATIONS]


def clean_kernel(width, me_ref, coarse_ref, fine_ref, *refs):
    piece_refs, (vis_ref, out_ref, gain_out_ref, model_s) = refs[:4], refs[4:]
    time = pl.program_id(0)
    pairs = out_ref.shape[4]
    size = model_s.shape[2]

    @pl.when(time == 0)
    def prepare():
        mine = lax.bitwise_and(me_ref[0], 3)
        for d, piece in enumerate(piece_refs):
            owner = lax.bitwise_xor(mine, d)
            t, s = lax.bitwise_and(owner, 1), lax.div(owner, 2)
            for k in range(4):
                for ri in range(2):
                    gain_out_ref[ri, s, t, k:k + 1, :] = piece[k, ri:ri + 1, GAINS_AT:]
                re, im = piece[k, 0:1, :GAINS_AT], piece[k, 1:2, :GAINS_AT]
                for slot, value in enumerate((re, im - re, re + im)):
                    model_s[owner, 3 * k + slot:3 * k + slot + 1, :] = value

    def main(tile, carry):
        lanes = pl.ds(pl.multiple_of(tile * 128, 128), 128)
        fine = [[fine_ref[0, 2 * s + ri, :, lanes] for ri in range(2)] for s in range(2)]
        for a in range(width // STEPS_PER_TURN):
            coarse = [[coarse_ref[0, 2 * s + ri, 8 * a:8 * a + 8, lanes] for ri in range(2)] for s in range(2)]
            for b in range(0, 8, 2):
                block = (8 * a + b) // 2
                rows = slice(block * 16, block * 16 + 16)
                waves = []
                for s in range(2):
                    halves = [times(tuple(part[b + half:b + half + 1] for part in coarse[s]), fine[s])
                              for half in range(2)]
                    re, im = (jnp.concatenate([h[ri] for h in halves], axis=0) for ri in range(2))
                    waves.append((re + im, re, im))
                for k in range(4):
                    sums = []
                    for slot in range(3):
                        one, two = (waves[s][slot] * model_s[time + 2 * s, 3 * k + slot:3 * k + slot + 1, lanes]
                                    for s in range(2))
                        sums.append(one + two)
                    vr = vis_ref[0, 0, k, rows, lanes].astype(F32)
                    vi = vis_ref[1, 0, k, rows, lanes].astype(F32)
                    out_ref[0, 0, k, rows, lanes] = (vr - (sums[0] - sums[2])).astype(BF16)
                    out_ref[1, 0, k, rows, lanes] = (vi - (sums[0] + sums[1])).astype(BF16)
        return carry

    lax.fori_loop(0, size // 128, main, 0)


def tables():
    first, second = np.triu_indices(STATIONS, 1)
    eye = np.eye(ROWS, dtype=np.float32)
    return jnp.asarray(eye[:, first], BF16), jnp.asarray(eye[:, second], BF16)


def partner(value, bits):
    count = lax.axis_size("sub")
    return lax.ppermute(value, "sub", [(i, i ^ bits) for i in range(count)])


def smem():
    return pl.BlockSpec(memory_space=pltpu.SMEM)


def local(visibilities, delays, flags, windows, tracks):
    width = visibilities.shape[4]
    pairs = visibilities.shape[3]
    count = lax.axis_size("sub")
    window_count = windows.shape[0]
    turned = jnp.transpose(visibilities, (0, 1, 2, 4, 3))
    me = lax.axis_index("sub").astype(jnp.int32).reshape(1)
    gathered = [flags[None]]
    stride = 1
    while stride < count:
        gathered = [jnp.concatenate(gathered, axis=0)] if len(gathered) > 1 else gathered
        gathered += [partner(gathered[0], stride * d) for d in range(1, min(4, count // stride))]
        stride *= 4
    lanes = 128 * pl.cdiv(pairs, 128)
    whole = lambda *shape: pl.BlockSpec(shape, lambda t: (0,) * len(shape))
    phases = lambda rows: pl.BlockSpec((1, 4, rows, lanes), lambda t: (t, 0, 0, 0))
    vis_spec = pl.BlockSpec((2, 1, 4, width, lanes), lambda t: (0, t, 0, 0, 0))
    rows = 2 * window_count + count
    vmem = lambda *shape: pltpu.VMEM(shape, F32)
    params = pltpu.CompilerParams(vmem_limit_bytes=57 * 2 ** 20)
    *quarters, coarse, fine = pl.pallas_call(
        lambda *refs: sums_kernel(width, len(gathered), *refs),
        grid=(2,),
        in_specs=[smem(), whole(1, window_count)] + [whole(*piece.shape) for piece in gathered] + [
            whole(2, 2, lanes), vis_spec],
        out_specs=[whole(4, 2, lanes)] * 4 + [phases(width // 8), phases(8)],
        out_shape=[jax.ShapeDtypeStruct((4, 2, pairs), F32)] * 4 + [
            jax.ShapeDtypeStruct((2, 4, rows, pairs), F32) for rows in (width // 8, 8)],
        scratch_shapes=[
            pltpu.VMEM((2, rows, width), BF16),
            pltpu.VMEM((2, width, window_count), BF16),
            pltpu.VMEM((3 * window_count, count), BF16),
            vmem(2, width, 128),
            vmem(2, window_count, 128),
            vmem(2, 2, width, lanes),
            pltpu.VMEM((2, 2, width, lanes), BF16),
            vmem(2, width, lanes),
            vmem(count, 2, width),
        ],
        compiler_params=params,
        name="window_sums",
    )(me, windows.reshape(1, window_count), *gathered, delays, turned)
    pieces = [quarters[0]] + [partner(quarters[d], d) for d in range(1, 4)]
    stride = 4
    while stride < count:
        while len(pieces) > 1:
            pieces = [pieces[i] + pieces[i + 1] for i in range(0, len(pieces), 2)]
        pieces += [partner(pieces[0], stride * d) for d in range(1, min(4, count // stride))]
        stride *= 4
    first, second = tables()
    model = pl.pallas_call(
        lambda *refs: solve_kernel(float(window_count), *refs),
        in_specs=[smem(), smem()] + [pl.BlockSpec(memory_space=pltpu.VMEM)] * (2 + len(pieces)),
        out_specs=pl.BlockSpec(memory_space=pltpu.VMEM),
        out_shape=jax.ShapeDtypeStruct((4, 2, GAINS_AT + STATIONS), F32),
        compiler_params=params,
        name="gain_solve",
    )(me, tracks, first, second, *pieces)
    model = [model] + [partner(model, d) for d in range(1, 4)]
    cleaned, gains = pl.pallas_call(
        lambda *refs: clean_kernel(width, *refs),
        grid=(2,),
        in_specs=[smem(), phases(width // 8), phases(8)] + [whole(4, 2, GAINS_AT + STATIONS)] * 4 + [vis_spec],
        out_specs=[vis_spec, whole(2, 2, 2, 4, STATIONS)],
        out_shape=[
            jax.ShapeDtypeStruct(turned.shape, BF16),
            jax.ShapeDtypeStruct((2, 2, 2, 4, STATIONS), F32),
        ],
        scratch_shapes=[vmem(4, 16, lanes)],
        compiler_params=params,
        name="clean",
    )(me, coarse, fine, *model, turned)
    return jnp.transpose(cleaned, (0, 1, 2, 4, 3)), gains


def solution(mesh):
    return jax.shard_map(
        local,
        mesh=mesh,
        in_specs=(
            P(None, "obs", None, None, "sub"),
            P(None, "obs", None),
            P("obs", "sub"),
            P(),
            P(None, "obs"),
        ),
        out_specs=(P(None, "obs", None, None, "sub"), P(None, None, "obs", None, None)),
        check_vma=False,
    )
```

```python
import jax
import jax.numpy as jnp
import numpy as np
from jax import lax
from jax.experimental import pallas as pl
from jax.experimental.pallas import tpu as pltpu
from jax.sharding import PartitionSpec as P

STATIONS = 38
GITERS = 8
DAMPING = 1.0
STEPS_PER_TURN = 64
GAINS_AT = 768
CHUNK = 48
ROWS = 40

F32 = jnp.float32
BF16 = jnp.bfloat16


def iota(shape, dim):
    return lax.broadcasted_iota(jnp.int32, shape, dim).astype(F32)


def sincos_turns(turns):
    half = (turns - jnp.floor(turns + 0.5)) * np.float32(np.pi)
    sq = half * half
    sin = np.float32(-1.0 / 39916800)
    for term in (1.0 / 362880, -1.0 / 5040, 1.0 / 120, -1.0 / 6, 1.0):
        sin = sin * sq + np.float32(term)
    sin = sin * half
    cos = np.float32(1.0 / 479001600)
    for term in (-1.0 / 3628800, 1.0 / 40320, -1.0 / 720, 1.0 / 24, -0.5, 1.0):
        cos = cos * sq + np.float32(term)
    return 1.0 - 2.0 * (sin * sin), 2.0 * (sin * cos)


def split_two(value):
    high = value.astype(BF16)
    low = (value - high.astype(F32)).astype(BF16)
    return high, low


def split_three(value):
    high = value.astype(BF16)
    rest = value - high.astype(F32)
    mid = rest.astype(BF16)
    low = (rest - mid.astype(F32)).astype(BF16)
    return high, mid, low


def dot(left, right):
    return jnp.dot(left, right, preferred_element_type=F32)


def times(left, right):
    (lr, li), (rr, ri) = left, right
    return lr * rr - li * ri, lr * ri + li * rr


def phase_rows(delays, anchor, width):
    place = iota((8, 1), 0)
    second = place >= 4.0
    turns = jnp.where(second, delays[1], delays[0])
    at = anchor + float(STEPS_PER_TURN) * jnp.where(second, place - 4.0, place)
    base = sincos_turns(turns * (at * np.float32(1.0 / STEPS_PER_TURN)))
    fine, coarse = [], []
    for s in range(2):
        low = sincos_turns(delays[s] * (place * np.float32(1.0 / STEPS_PER_TURN)))
        high = low
        for doubling in range(3):
            high = times(high, high)
        rows = [times(tuple(part[4 * s + a:4 * s + a + 1] for part in base), high)
                for a in range(width // STEPS_PER_TURN)]
        fine.append(low)
        coarse.append(rows)
    return fine, coarse


def tiles(pairs, body):
    full = pairs // 128

    def step(tile, carry):
        body(pl.ds(pl.multiple_of(tile * 128, 128), 128), 128)
        return carry

    lax.fori_loop(0, full, step, 0)
    if pairs % 128:
        body(pl.ds(full * 128, pairs % 128), pairs % 128)


def phase_kernel(width, me_ref, delay_ref, vis_hbm, vis_ref, wave_ref, mix_ref, sems):
    anchor = me_ref[0].astype(F32) * float(width)
    pairs = delay_ref.shape[2]
    copies = [pltpu.make_async_copy(vis_hbm.at[:, t], vis_ref.at[:, t], sems.at[t]) for t in range(2)]
    for copy in copies:
        copy.start()
    for t in range(2):
        def waves(lanes, count):
            delays = [delay_ref[s, t:t + 1, lanes] for s in range(2)]
            fine, coarse = phase_rows(delays, anchor, width)
            for block in range(width // 16):
                found = []
                for s in range(2):
                    halves = []
                    for half in range(2):
                        a, b = divmod(2 * block + half, 8)
                        halves.append(times(tuple(part[b:b + 1] for part in coarse[s][a]), fine[s]))
                    found.append([jnp.concatenate([h[ri] for h in halves], axis=0) for ri in range(2)])
                rows = slice(block * 16, block * 16 + 16)
                (r0, i0), (r1, i1) = found
                for s in range(2):
                    for ri in range(2):
                        wave_ref[t, s, ri, rows, lanes] = found[s][ri]
                for slot, value in enumerate((r1 * r0 + i1 * i0, i1 * r0 - r1 * i0)):
                    high, low = split_two(value)
                    mix_ref[t, slot, 0, rows, lanes] = high
                    mix_ref[t, slot, 1, rows, lanes] = low

        tiles(pairs, waves)
    for copy in copies:
        copy.wait()


def sums_kernel(width, stages, me_ref, win_ref, *refs):
    flag_refs, refs = refs[:stages], refs[stages:]
    delay_ref, vis_ref, wave_ref, mix_ref = refs[:4]
    out_refs, (alpha_s, mexp_s, wt_s) = refs[4:8], refs[8:]
    me = me_ref[0]
    near = flag_refs[0].shape[0]
    groups = near * stages
    windows = win_ref.shape[1]
    pairs = delay_ref.shape[2]
    anchor = me.astype(F32) * float(width)
    final = anchor + float(width - 1)

    win_row = win_ref[...].astype(F32)
    sub, lane = iota((windows, windows), 0), iota((windows, windows), 1)
    end_c = jnp.sum(jnp.where(lane <= sub, win_row, 0.0), axis=1, keepdims=True)
    start_c = jnp.sum(jnp.where(lane < sub, win_row, 0.0), axis=1, keepdims=True)
    win_c = end_c - start_c
    end_r = jnp.sum(jnp.where(sub <= lane, win_c, 0.0), axis=0, keepdims=True)
    start_r = jnp.sum(jnp.where(sub < lane, win_c, 0.0), axis=0, keepdims=True)
    first_c = jnp.where((start_c <= anchor) & (anchor < end_c), 1.0, 0.0)
    last_c = jnp.where((start_c <= final) & (final < end_c), 1.0, 0.0)
    from_first = jnp.sum(first_c * start_c, axis=0, keepdims=True)
    to_last = jnp.sum(last_c * end_c, axis=0, keepdims=True)
    here = anchor + iota((windows, width), 1)
    member_wc = (here >= start_c) & (here < end_c)
    there = iota((width, windows), 0) + anchor
    member_cw = (there >= start_r) & (there < end_r)
    apart = iota((groups, 1), 0) - me.astype(F32)
    channel = iota((groups, width), 0) * float(width) + iota((groups, width), 1)
    remote = ((channel < anchor) & (channel >= from_first)) | ((channel > final) & (channel < to_last))
    diagonal = iota((width, width), 0) == iota((width, width), 1)

    def both_sides(value):
        return (jnp.sum(jnp.where(apart < 0.0, value, 0.0), axis=0, keepdims=True),
                jnp.sum(jnp.where(apart > 0.0, value, 0.0), axis=0, keepdims=True))

    for t in range(2):
        for slot in range(groups):
            row = flag_refs[slot // near][slot % near, t:t + 1, :].astype(F32)
            wt_s[t, pl.ds(lax.bitwise_xor(me, slot), 1), :] = 1.0 - row
        own = 1.0 - flag_refs[0][0, t:t + 1, :].astype(F32)
        inside = jnp.where(member_wc, own, 0.0)
        outside = jnp.where(remote, wt_s[t], 0.0)
        before, after = both_sides(jnp.sum(outside, axis=1, keepdims=True))
        count = jnp.sum(inside, axis=1, keepdims=True) + first_c * before + last_c * after
        scale = 1.0 / jnp.maximum(count, 1.0)
        rows = jnp.concatenate([inside, outside], axis=0).astype(BF16)
        scale_r = jnp.sum(jnp.where(sub == lane, scale, 0.0), axis=0, keepdims=True)
        own_c = jnp.sum(jnp.where(diagonal, own, 0.0), axis=1, keepdims=True)
        chosen = jnp.where(member_cw, own_c, 0.0)
        alpha_s[t] = jnp.broadcast_to(jnp.sum(chosen * scale_r, axis=1, keepdims=True), (width, 128))
        chosen = chosen.astype(BF16)
        sums = [dot(rows, mix_ref[t, slot, 0]) + dot(rows, mix_ref[t, slot, 1]) for slot in range(2)]
        gap = delay_ref[1, t:t + 1, :] - delay_ref[0, t:t + 1, :]
        phase = sincos_turns(gap * (apart * np.float32(width / STEPS_PER_TURN)))
        away = times(phase, tuple(value[windows:] for value in sums))
        for slot in range(2):
            before, after = both_sides(away[slot])
            total = sums[slot][:windows] + first_c * before + last_c * after
            high, low = split_two(total * (scale * scale))
            mexp_s[t, slot] = dot(chosen, high) + dot(chosen, low)

    for t in range(2):
        def main(lanes, count):
            def step(block, sums):
                rows = pl.ds(pl.multiple_of(block * 16, 16), 16)
                alpha = alpha_s[t, rows, :count]
                mr, mi = mexp_s[t, 0, rows, lanes], mexp_s[t, 1, rows, lanes]
                r0, i0 = wave_ref[t, 0, 0, rows, lanes], wave_ref[t, 0, 1, rows, lanes]
                r1, i1 = wave_ref[t, 1, 0, rows, lanes], wave_ref[t, 1, 1, rows, lanes]
                factors = []
                for fr, fi in (
                    (alpha * r0 - (mr * r1 + mi * i1), (mr * i1 - mi * r1) - alpha * i0),
                    (alpha * r1 - (mr * r0 - mi * i0), (mr * i0 + mi * r0) - alpha * i1),
                ):
                    factors.append((fr, fi - fr, fr + fi))
                new = []
                for k in range(4):
                    vr = vis_ref[0, t, k, rows, lanes].astype(F32)
                    vi = vis_ref[1, t, k, rows, lanes].astype(F32)
                    vs = vr + vi
                    for s in range(2):
                        for v, f in zip((vs, vr, vi), factors[s]):
                            product = v * f
                            new.append(sums[len(new)] + (product[:8] + product[8:]))
                return tuple(new)

            zero = jnp.zeros((8, count), F32)
            sums = lax.fori_loop(0, width // 16, step, (zero,) * 24, unroll=4)
            for s in range(2):
                owner = lax.bitwise_xor(lax.bitwise_and(me, 3), t + 2 * s)
                found = []
                for k in range(4):
                    one, two, three = sums[(k * 2 + s) * 3:(k * 2 + s) * 3 + 3]
                    found.append([jnp.sum(value, axis=0, keepdims=True) for value in (one - three, one + two)])
                for d in range(4):
                    @pl.when(owner == d)
                    def write():
                        for k in range(4):
                            for ri in range(2):
                                out_refs[d][k, ri:ri + 1, lanes] = found[k][ri]

        tiles(pairs, main)


def station_hots(pairs):
    station, baseline = iota((ROWS, 1), 0), iota((1, pairs), 1)
    offset = station * (float(2 * STATIONS - 1) - station) * 0.5
    after = (station + 1.0) * (float(2 * STATIONS - 2) - station) * 0.5
    first = jnp.where((baseline >= offset) & (baseline < after), 1.0, 0.0)
    partner_of = baseline + 1.0 + jnp.sum(first * (station - offset), axis=0, keepdims=True)
    second = jnp.where(partner_of == station, 1.0, 0.0)
    return first.astype(BF16), second.astype(BF16)


def solve_kernel(window_count, me_ref, tracks_ref, *refs):
    parts, gain_ref = refs[:-1], refs[-1]
    me = me_ref[0]
    systems = gain_ref.shape[0]
    total = [part[...] for part in parts]
    while len(total) > 1:
        total = [total[i] + total[i + 1] for i in range(0, len(total), 2)]
    total = total[0]
    hot, other = station_hots(total.shape[2])
    nt = lambda left, right: lax.dot_general(
        left, right, (((1,), (1,)), ((), ())), preferred_element_type=F32)
    upper, lower = [], []
    for system in range(systems):
        for ri in range(2):
            for piece in split_two(total[system, ri:ri + 1]):
                upper.append(hot * piece)
                lower.append(other * piece)
    upper = nt(jnp.concatenate(upper, axis=0), other)
    lower = nt(jnp.concatenate(lower, axis=0), hot)
    cut = lambda value, i: value[i * ROWS:(i + 1) * ROWS]
    join = lambda value, i: cut(value, 2 * i) + cut(value, 2 * i + 1)
    live_r = jnp.where(iota((1, ROWS), 1) < float(STATIONS), 1.0, 0.0)
    live_c = jnp.where(iota((ROWS, 1), 0) < float(STATIONS), 1.0, 0.0)
    matrices = [(join(upper, 2 * i) + join(lower, 2 * i), join(upper, 2 * i + 1) - join(lower, 2 * i + 1))
                for i in range(systems)]
    states = [(live_r, 0.0 * live_r, live_c, 0.0 * live_c)] * systems
    for turn in range(GITERS):
        for system in range(systems):
            re, im = matrices[system]
            row_re, row_im, col_re, col_im = states[system]
            pull_cr = jnp.sum(re * row_re - im * row_im, axis=1, keepdims=True)
            pull_ci = jnp.sum(re * row_im + im * row_re, axis=1, keepdims=True)
            pull_rr = jnp.sum(re * col_re + im * col_im, axis=0, keepdims=True)
            pull_ri = jnp.sum(re * col_im - im * col_re, axis=0, keepdims=True)
            power_r = row_re * row_re + row_im * row_im
            power_c = col_re * col_re + col_im * col_im
            total = jnp.sum(power_c, axis=0, keepdims=True)
            inverse_r = 0.5 / (window_count * (total - power_r) + DAMPING)
            inverse_c = 0.5 / (window_count * (total - power_c) + DAMPING)
            states[system] = (0.5 * row_re + pull_rr * inverse_r, 0.5 * row_im + pull_ri * inverse_r,
                              0.5 * col_re + pull_cr * inverse_c, 0.5 * col_im + pull_ci * inverse_c)
    visible = tracks_ref[lax.bitwise_and(lax.div(me, 2), 1), lax.bitwise_and(me, 1)].astype(F32)
    gains = [state[ri] * visible for state in states for ri in range(2)]
    gains = jnp.concatenate(gains, axis=0)
    stacked = jnp.concatenate([piece.astype(F32) for piece in split_three(gains)], axis=0).astype(BF16)
    ends = []
    for table in (hot, other):
        wide = dot(stacked, table)
        ends.append((wide[:8] + wide[8:16]) + wide[16:])
    pairs = hot.shape[1]
    for system in range(systems):
        (lr, li), (rr, ri_) = [[end[2 * system + ri:2 * system + ri + 1] for ri in range(2)] for end in ends]
        gain_ref[system, 0:1, :pairs] = lr * rr + li * ri_
        gain_ref[system, 1:2, :pairs] = li * rr - lr * ri_
        gain_ref[system, :, GAINS_AT:] = gains[2 * system:2 * system + 2, :STATIONS]


def clean_kernel(width, me_ref, vis_ref, wave_ref, *refs):
    piece_refs, (out_hbm, gain_out_ref, out_s, model_s, sems) = refs[:4], refs[4:]
    pairs = wave_ref.shape[4]
    mine = lax.bitwise_and(me_ref[0], 3)
    for d, piece in enumerate(piece_refs):
        owner = lax.bitwise_xor(mine, d)
        t, s = lax.bitwise_and(owner, 1), lax.div(owner, 2)
        for k in range(4):
            for ri in range(2):
                gain_out_ref[ri, s, t, k:k + 1, :] = piece[k, ri:ri + 1, GAINS_AT:]
            re, im = piece[k, 0:1, :pairs], piece[k, 1:2, :pairs]
            for slot, value in enumerate((re, im - re, re + im)):
                model_s[owner, 3 * k + slot:3 * k + slot + 1, :] = value

    chunks = width // CHUNK

    def copy_out(index):
        t, rows = lax.div(index, chunks), pl.ds(pl.multiple_of(lax.rem(index, chunks) * CHUNK, CHUNK), CHUNK)
        return pltpu.make_async_copy(out_s.at[:, t, :, rows], out_hbm.at[:, t, :, rows], sems.at[index])

    def chunk(index, carry):
        t, base = lax.div(index, chunks), lax.rem(index, chunks) * CHUNK

        def main(lanes, count):
            for block in range(CHUNK // 16):
                rows = pl.ds(pl.multiple_of(base + block * 16, 16), 16)
                waves = []
                for s in range(2):
                    re, im = wave_ref[t, s, 0, rows, lanes], wave_ref[t, s, 1, rows, lanes]
                    waves.append((re + im, re, im))
                for k in range(4):
                    sums = []
                    for slot in range(3):
                        one, two = (waves[s][slot] * model_s[t + 2 * s, 3 * k + slot:3 * k + slot + 1, lanes]
                                    for s in range(2))
                        sums.append(one + two)
                    vr = vis_ref[0, t, k, rows, lanes].astype(F32)
                    vi = vis_ref[1, t, k, rows, lanes].astype(F32)
                    out_s[0, t, k, rows, lanes] = (vr - (sums[0] - sums[2])).astype(BF16)
                    out_s[1, t, k, rows, lanes] = (vi - (sums[0] + sums[1])).astype(BF16)

        tiles(pairs, main)
        copy_out(index).start()
        return carry

    lax.fori_loop(0, 2 * chunks, chunk, 0)
    for index in range(2 * chunks):
        copy_out(index).wait()


def partner(value, bits):
    count = lax.axis_size("sub")
    return lax.ppermute(value, "sub", [(i, i ^ bits) for i in range(count)])


def smem():
    return pl.BlockSpec(memory_space=pltpu.SMEM)


def local(visibilities, delays, flags, windows, tracks):
    width = visibilities.shape[4]
    pairs = visibilities.shape[3]
    count = lax.axis_size("sub")
    window_count = windows.shape[0]
    turned = jnp.transpose(visibilities, (0, 1, 2, 4, 3))
    me = lax.axis_index("sub").astype(jnp.int32).reshape(1)
    gathered = [flags[None]]
    stride = 1
    while stride < count:
        gathered = [jnp.concatenate(gathered, axis=0)] if len(gathered) > 1 else gathered
        gathered += [partner(gathered[0], stride * d) for d in range(1, min(4, count // stride))]
        stride *= 4
    vmem_ref = pl.BlockSpec(memory_space=pltpu.VMEM)
    hbm_ref = pl.BlockSpec(memory_space=pltpu.HBM)
    vmem = lambda *shape: pltpu.VMEM(shape, F32)
    params = pltpu.CompilerParams(vmem_limit_bytes=24 * 2 ** 20)
    held, waves, mixing = pl.pallas_call(
        lambda *refs: phase_kernel(width, *refs),
        in_specs=[smem(), vmem_ref, hbm_ref],
        out_specs=[vmem_ref] * 3,
        out_shape=[
            jax.ShapeDtypeStruct(turned.shape, BF16),
            jax.ShapeDtypeStruct((2, 2, 2, width, pairs), F32),
            jax.ShapeDtypeStruct((2, 2, 2, width, pairs), BF16),
        ],
        scratch_shapes=[pltpu.SemaphoreType.DMA((2,))],
        compiler_params=pltpu.CompilerParams(vmem_limit_bytes=40 * 2 ** 20),
        cost_estimate=pl.CostEstimate(flops=2 * 10 ** 7, bytes_accessed=12 * 2 ** 20, transcendentals=0),
        name="phases",
    )(me, delays, turned)
    quarters = pl.pallas_call(
        lambda *refs: sums_kernel(width, len(gathered), *refs),
        in_specs=[smem()] + [vmem_ref] * (len(gathered) + 5),
        out_specs=[vmem_ref] * 4,
        out_shape=[jax.ShapeDtypeStruct((4, 2, pairs), F32)] * 4,
        scratch_shapes=[vmem(2, width, 128), vmem(2, 2, width, pairs), vmem(2, count, width)],
        compiler_params=params,
        name="window_sums",
    )(me, windows.reshape(1, window_count), *gathered, delays, held, waves, mixing)
    pieces = [quarters[0]] + [partner(quarters[d], d) for d in range(1, 4)]
    stride = 4
    while stride < count:
        while len(pieces) > 1:
            pieces = [pieces[i] + pieces[i + 1] for i in range(0, len(pieces), 2)]
        pieces += [partner(pieces[0], stride * d) for d in range(1, min(4, count // stride))]
        stride *= 4
    model = pl.pallas_call(
        lambda *refs: solve_kernel(float(window_count), *refs),
        in_specs=[smem(), smem()] + [vmem_ref] * len(pieces),
        out_specs=vmem_ref,
        out_shape=jax.ShapeDtypeStruct((4, 2, GAINS_AT + STATIONS), F32),
        compiler_params=params,
        name="gain_solve",
    )(me, tracks, *pieces)
    model = [model] + [partner(model, d) for d in range(1, 4)]
    cleaned, gains = pl.pallas_call(
        lambda *refs: clean_kernel(width, *refs),
        in_specs=[smem()] + [vmem_ref] * 6,
        out_specs=[hbm_ref, vmem_ref],
        out_shape=[
            jax.ShapeDtypeStruct(turned.shape, BF16),
            jax.ShapeDtypeStruct((2, 2, 2, 4, STATIONS), F32),
        ],
        scratch_shapes=[
            pltpu.VMEM(turned.shape, BF16),
            vmem(4, 16, pairs),
            pltpu.SemaphoreType.DMA((2 * (width // CHUNK),)),
        ],
        compiler_params=params,
        name="clean",
    )(me, held, waves, *model)
    return jnp.transpose(cleaned, (0, 1, 2, 4, 3)), gains


def solution(mesh):
    return jax.shard_map(
        local,
        mesh=mesh,
        in_specs=(
            P(None, "obs", None, None, "sub"),
            P(None, "obs", None),
            P("obs", "sub"),
            P(),
            P(None, "obs"),
        ),
        out_specs=(P(None, "obs", None, None, "sub"), P(None, None, "obs", None, None)),
        check_vma=False,
    )
```

```python
import jax
import jax.numpy as jnp
import numpy as np
from jax import lax
from jax.experimental import pallas as pl
from jax.experimental.pallas import tpu as pltpu
from jax.sharding import PartitionSpec as P

STATIONS = 38
GITERS = 8
DAMPING = 1.0
STEPS_PER_TURN = 64
GAINS_AT = 768
CHUNK = 48
GRANTS = (50, 42)
ROWS = 40

F32 = jnp.float32
BF16 = jnp.bfloat16


def iota(shape, dim):
    return lax.broadcasted_iota(jnp.int32, shape, dim).astype(F32)


def sincos_turns(turns):
    half = (turns - jnp.floor(turns + 0.5)) * np.float32(np.pi)
    sq = half * half
    sin = np.float32(-1.0 / 39916800)
    for term in (1.0 / 362880, -1.0 / 5040, 1.0 / 120, -1.0 / 6, 1.0):
        sin = sin * sq + np.float32(term)
    sin = sin * half
    cos = np.float32(1.0 / 479001600)
    for term in (-1.0 / 3628800, 1.0 / 40320, -1.0 / 720, 1.0 / 24, -0.5, 1.0):
        cos = cos * sq + np.float32(term)
    return 1.0 - 2.0 * (sin * sin), 2.0 * (sin * cos)


def split_two(value):
    high = value.astype(BF16)
    low = (value - high.astype(F32)).astype(BF16)
    return high, low


def split_three(value):
    high = value.astype(BF16)
    rest = value - high.astype(F32)
    mid = rest.astype(BF16)
    low = (rest - mid.astype(F32)).astype(BF16)
    return high, mid, low


def dot(left, right):
    return jnp.dot(left, right, preferred_element_type=F32)


def times(left, right):
    (lr, li), (rr, ri) = left, right
    return lr * rr - li * ri, lr * ri + li * rr


def phase_rows(delays, anchor, width):
    place = iota((8, 1), 0)
    second = place >= 4.0
    turns = jnp.where(second, delays[1], delays[0])
    at = anchor + float(STEPS_PER_TURN) * jnp.where(second, place - 4.0, place)
    base = sincos_turns(turns * (at * np.float32(1.0 / STEPS_PER_TURN)))
    fine, coarse = [], []
    for s in range(2):
        low = sincos_turns(delays[s] * (place * np.float32(1.0 / STEPS_PER_TURN)))
        high = low
        for doubling in range(3):
            high = times(high, high)
        rows = [times(tuple(part[4 * s + a:4 * s + a + 1] for part in base), high)
                for a in range(width // STEPS_PER_TURN)]
        fine.append(low)
        coarse.append(rows)
    return fine, coarse


def tiles(pairs, body):
    full = pairs // 128

    def step(tile, carry):
        body(pl.ds(pl.multiple_of(tile * 128, 128), 128), 128)
        return carry

    lax.fori_loop(0, full, step, 0)
    if pairs % 128:
        body(pl.ds(full * 128, pairs % 128), pairs % 128)


def phase_kernel(width, t, me_ref, delay_ref, *refs):
    if t == 0:
        flag_ref, wave_ref, mix_ref, own_ref = refs
        own_ref[...] = flag_ref[...]
    else:
        vis_hbm, wave_ref, mix_ref, vis_ref, sem = refs
        copy = pltpu.make_async_copy(vis_hbm, vis_ref, sem)
        copy.start()
    anchor = me_ref[0].astype(F32) * float(width)
    pairs = delay_ref.shape[2]
    def waves(lanes, count):
        delays = [delay_ref[s, t:t + 1, lanes] for s in range(2)]
        fine, coarse = phase_rows(delays, anchor, width)
        for block in range(width // 16):
            found = []
            for s in range(2):
                halves = []
                for half in range(2):
                    a, b = divmod(2 * block + half, 8)
                    halves.append(times(tuple(part[b:b + 1] for part in coarse[s][a]), fine[s]))
                found.append([jnp.concatenate([h[ri] for h in halves], axis=0) for ri in range(2)])
            rows = slice(block * 16, block * 16 + 16)
            (r0, i0), (r1, i1) = found
            for s in range(2):
                for ri in range(2):
                    wave_ref[s, ri, rows, lanes] = found[s][ri]
            for slot, value in enumerate((r1 * r0 + i1 * i0, i1 * r0 - r1 * i0)):
                high, low = split_two(value)
                mix_ref[slot, 0, rows, lanes] = high
                mix_ref[slot, 1, rows, lanes] = low

    tiles(pairs, waves)
    if t == 1:
        copy.wait()


def sums_kernel(width, stages, me_ref, win_ref, *refs):
    flag_refs, refs = refs[:stages], refs[stages:]
    delay_ref, vis_ref, wave_refs, mix_refs = refs[0], refs[1], refs[2:4], refs[4:6]
    out_ref, alpha_s, mexp_s, wt_s = refs[6:]
    me = me_ref[0]
    near = flag_refs[0].shape[0]
    groups = near * stages
    windows = win_ref.shape[1]
    pairs = delay_ref.shape[2]
    anchor = me.astype(F32) * float(width)
    final = anchor + float(width - 1)

    win_row = win_ref[...].astype(F32)
    sub, lane = iota((windows, windows), 0), iota((windows, windows), 1)
    end_c = jnp.sum(jnp.where(lane <= sub, win_row, 0.0), axis=1, keepdims=True)
    start_c = jnp.sum(jnp.where(lane < sub, win_row, 0.0), axis=1, keepdims=True)
    win_c = end_c - start_c
    end_r = jnp.sum(jnp.where(sub <= lane, win_c, 0.0), axis=0, keepdims=True)
    start_r = jnp.sum(jnp.where(sub < lane, win_c, 0.0), axis=0, keepdims=True)
    first_c = jnp.where((start_c <= anchor) & (anchor < end_c), 1.0, 0.0)
    last_c = jnp.where((start_c <= final) & (final < end_c), 1.0, 0.0)
    from_first = jnp.sum(first_c * start_c, axis=0, keepdims=True)
    to_last = jnp.sum(last_c * end_c, axis=0, keepdims=True)
    here = anchor + iota((windows, width), 1)
    member_wc = (here >= start_c) & (here < end_c)
    there = iota((width, windows), 0) + anchor
    member_cw = (there >= start_r) & (there < end_r)
    apart = iota((groups, 1), 0) - me.astype(F32)
    channel = iota((groups, width), 0) * float(width) + iota((groups, width), 1)
    remote = ((channel < anchor) & (channel >= from_first)) | ((channel > final) & (channel < to_last))
    diagonal = iota((width, width), 0) == iota((width, width), 1)

    def both_sides(value):
        return (jnp.sum(jnp.where(apart < 0.0, value, 0.0), axis=0, keepdims=True),
                jnp.sum(jnp.where(apart > 0.0, value, 0.0), axis=0, keepdims=True))

    for t in range(2):
        for slot in range(groups):
            row = flag_refs[slot // near][slot % near, t:t + 1, :].astype(F32)
            wt_s[t, pl.ds(lax.bitwise_xor(me, slot), 1), :] = 1.0 - row
        own = 1.0 - flag_refs[0][0, t:t + 1, :].astype(F32)
        inside = jnp.where(member_wc, own, 0.0)
        outside = jnp.where(remote, wt_s[t], 0.0)
        before, after = both_sides(jnp.sum(outside, axis=1, keepdims=True))
        count = jnp.sum(inside, axis=1, keepdims=True) + first_c * before + last_c * after
        scale = 1.0 / jnp.maximum(count, 1.0)
        rows = jnp.concatenate([inside, outside], axis=0).astype(BF16)
        scale_r = jnp.sum(jnp.where(sub == lane, scale, 0.0), axis=0, keepdims=True)
        own_c = jnp.sum(jnp.where(diagonal, own, 0.0), axis=1, keepdims=True)
        chosen = jnp.where(member_cw, own_c, 0.0)
        alpha_s[t] = jnp.broadcast_to(jnp.sum(chosen * scale_r, axis=1, keepdims=True), (width, 128))
        chosen = chosen.astype(BF16)
        sums = [dot(rows, mix_refs[t][slot, 0]) + dot(rows, mix_refs[t][slot, 1]) for slot in range(2)]
        gap = delay_ref[1, t:t + 1, :] - delay_ref[0, t:t + 1, :]
        phase = sincos_turns(gap * (apart * np.float32(width / STEPS_PER_TURN)))
        away = times(phase, tuple(value[windows:] for value in sums))
        for slot in range(2):
            before, after = both_sides(away[slot])
            total = sums[slot][:windows] + first_c * before + last_c * after
            high, low = split_two(total * (scale * scale))
            mexp_s[t, slot] = dot(chosen, high) + dot(chosen, low)

    for t in range(2):
        def main(lanes, count):
            def step(block, sums):
                rows = pl.ds(pl.multiple_of(block * 16, 16), 16)
                alpha = alpha_s[t, rows, :count]
                mr, mi = mexp_s[t, 0, rows, lanes], mexp_s[t, 1, rows, lanes]
                r0, i0 = wave_refs[t][0, 0, rows, lanes], wave_refs[t][0, 1, rows, lanes]
                r1, i1 = wave_refs[t][1, 0, rows, lanes], wave_refs[t][1, 1, rows, lanes]
                factors = []
                for fr, fi in (
                    (alpha * r0 - (mr * r1 + mi * i1), (mr * i1 - mi * r1) - alpha * i0),
                    (alpha * r1 - (mr * r0 - mi * i0), (mr * i0 + mi * r0) - alpha * i1),
                ):
                    factors.append((fr, fi - fr, fr + fi))
                new = []
                for k in range(4):
                    vr = vis_ref[0, t, k, rows, lanes].astype(F32)
                    vi = vis_ref[1, t, k, rows, lanes].astype(F32)
                    vs = vr + vi
                    for s in range(2):
                        for v, f in zip((vs, vr, vi), factors[s]):
                            product = v * f
                            new.append(sums[len(new)] + (product[:8] + product[8:]))
                return tuple(new)

            zero = jnp.zeros((8, count), F32)
            sums = lax.fori_loop(0, width // 16, step, (zero,) * 24, unroll=4)
            for s in range(2):
                for k in range(4):
                    one, two, three = sums[(k * 2 + s) * 3:(k * 2 + s) * 3 + 3]
                    for ri, value in enumerate((one - three, one + two)):
                        out_ref[t + 2 * s, k, ri:ri + 1, lanes] = jnp.sum(value, axis=0, keepdims=True)

        tiles(pairs, main)


def station_hots(pairs):
    station, baseline = iota((ROWS, 1), 0), iota((1, pairs), 1)
    offset = station * (float(2 * STATIONS - 1) - station) * 0.5
    after = (station + 1.0) * (float(2 * STATIONS - 2) - station) * 0.5
    first = jnp.where((baseline >= offset) & (baseline < after), 1.0, 0.0)
    partner_of = baseline + 1.0 + jnp.sum(first * (station - offset), axis=0, keepdims=True)
    second = jnp.where(partner_of == station, 1.0, 0.0)
    return first.astype(BF16), second.astype(BF16)


def solve_kernel(window_count, me_ref, tracks_ref, *refs):
    parts, gain_ref = refs[:-1], refs[-1]
    me = me_ref[0]
    systems = gain_ref.shape[1]
    total = [part[...] for part in parts]
    while len(total) > 1:
        total = [total[i] + total[i + 1] for i in range(0, len(total), 2)]
    total = total[0]
    hot, other = station_hots(total.shape[2])
    nt = lambda left, right: lax.dot_general(
        left, right, (((1,), (1,)), ((), ())), preferred_element_type=F32)
    upper, lower = [], []
    for system in range(systems):
        for ri in range(2):
            for piece in split_two(total[system, ri:ri + 1]):
                upper.append(hot * piece)
                lower.append(other * piece)
    upper = nt(jnp.concatenate(upper, axis=0), other)
    lower = nt(jnp.concatenate(lower, axis=0), hot)
    cut = lambda value, i: value[i * ROWS:(i + 1) * ROWS]
    join = lambda value, i: cut(value, 2 * i) + cut(value, 2 * i + 1)
    live_r = jnp.where(iota((1, ROWS), 1) < float(STATIONS), 1.0, 0.0)
    live_c = jnp.where(iota((ROWS, 1), 0) < float(STATIONS), 1.0, 0.0)
    matrices = [(join(upper, 2 * i) + join(lower, 2 * i), join(upper, 2 * i + 1) - join(lower, 2 * i + 1))
                for i in range(systems)]
    states = [(live_r, 0.0 * live_r, live_c, 0.0 * live_c)] * systems
    for turn in range(GITERS):
        for system in range(systems):
            re, im = matrices[system]
            row_re, row_im, col_re, col_im = states[system]
            pull_cr = jnp.sum(re * row_re - im * row_im, axis=1, keepdims=True)
            pull_ci = jnp.sum(re * row_im + im * row_re, axis=1, keepdims=True)
            pull_rr = jnp.sum(re * col_re + im * col_im, axis=0, keepdims=True)
            pull_ri = jnp.sum(re * col_im - im * col_re, axis=0, keepdims=True)
            power_r = row_re * row_re + row_im * row_im
            power_c = col_re * col_re + col_im * col_im
            total = jnp.sum(power_c, axis=0, keepdims=True)
            inverse_r = 0.5 / (window_count * (total - power_r) + DAMPING)
            inverse_c = 0.5 / (window_count * (total - power_c) + DAMPING)
            states[system] = (0.5 * row_re + pull_rr * inverse_r, 0.5 * row_im + pull_ri * inverse_r,
                              0.5 * col_re + pull_cr * inverse_c, 0.5 * col_im + pull_ci * inverse_c)
    visible = tracks_ref[lax.bitwise_and(lax.div(me, 2), 1), lax.bitwise_and(me, 1)].astype(F32)
    gains = [state[ri] * visible for state in states for ri in range(2)]
    gains = jnp.concatenate(gains, axis=0)
    stacked = jnp.concatenate([piece.astype(F32) for piece in split_three(gains)], axis=0).astype(BF16)
    ends = []
    for table in (hot, other):
        wide = dot(stacked, table)
        ends.append((wide[:8] + wide[8:16]) + wide[16:])
    pairs = hot.shape[1]
    for system in range(systems):
        (lr, li), (rr, ri_) = [[end[2 * system + ri:2 * system + ri + 1] for ri in range(2)] for end in ends]
        for copy in range(4):
            gain_ref[copy, system, 0:1, :pairs] = lr * rr + li * ri_
            gain_ref[copy, system, 1:2, :pairs] = li * rr - lr * ri_
            gain_ref[copy, system, :, GAINS_AT:] = gains[2 * system:2 * system + 2, :STATIONS]


def clean_kernel(width, *refs):
    vis_ref, wave_refs = refs[0], refs[1:3]
    piece_ref, out_hbm, gain_out_ref, out_s, model_s, sems = refs[3:]
    pairs = wave_refs[0].shape[3]
    for owner in range(4):
        t, s = owner % 2, owner // 2
        for k in range(4):
            for ri in range(2):
                gain_out_ref[ri, s, t, k:k + 1, :] = piece_ref[owner, k, ri:ri + 1, GAINS_AT:]
            re, im = piece_ref[owner, k, 0:1, :pairs], piece_ref[owner, k, 1:2, :pairs]
            for slot, value in enumerate((re, im - re, re + im)):
                model_s[owner, 3 * k + slot:3 * k + slot + 1, :] = value

    chunks = width // CHUNK

    def copy_out(t, index):
        rows = pl.ds(pl.multiple_of(index * CHUNK, CHUNK), CHUNK)
        return pltpu.make_async_copy(out_s.at[:, t, :, rows], out_hbm.at[:, t, :, rows], sems.at[t, index])

    for t in range(2):
        def chunk(index, carry):
            def main(lanes, count):
                for block in range(CHUNK // 16):
                    rows = pl.ds(pl.multiple_of(index * CHUNK + block * 16, 16), 16)
                    waves = []
                    for s in range(2):
                        re, im = (wave_refs[t][s, ri, rows, lanes] for ri in range(2))
                        waves.append((re + im, re, im))
                    for k in range(4):
                        sums = []
                        for slot in range(3):
                            one, two = (waves[s][slot] * model_s[t + 2 * s, 3 * k + slot:3 * k + slot + 1, lanes]
                                        for s in range(2))
                            sums.append(one + two)
                        vr = vis_ref[0, t, k, rows, lanes].astype(F32)
                        vi = vis_ref[1, t, k, rows, lanes].astype(F32)
                        out_s[0, t, k, rows, lanes] = (vr - (sums[0] - sums[2])).astype(BF16)
                        out_s[1, t, k, rows, lanes] = (vi - (sums[0] + sums[1])).astype(BF16)

            tiles(pairs, main)
            copy_out(t, index).start()
            return carry

        lax.fori_loop(0, chunks, chunk, 0)
    for t in range(2):
        for index in range(chunks):
            copy_out(t, index).wait()


def partner(value, bits):
    count = lax.axis_size("sub")
    return lax.ppermute(value, "sub", [(i, i ^ bits) for i in range(count)])


def smem():
    return pl.BlockSpec(memory_space=pltpu.SMEM)


def local(visibilities, delays, flags, windows, tracks):
    width = visibilities.shape[4]
    pairs = visibilities.shape[3]
    count = lax.axis_size("sub")
    window_count = windows.shape[0]
    turned = jnp.transpose(visibilities, (0, 1, 2, 4, 3))
    me = lax.axis_index("sub").astype(jnp.int32).reshape(1)
    fours = [[base + d for d in range(4)] for base in range(0, count, 4)]
    vmem_ref = pl.BlockSpec(memory_space=pltpu.VMEM)
    hbm_ref = pl.BlockSpec(memory_space=pltpu.HBM)
    vmem = lambda *shape: pltpu.VMEM(shape, F32)
    params = pltpu.CompilerParams(vmem_limit_bytes=24 * 2 ** 20)
    waves, mixing = [], []
    own = flags[None]
    gathered = [own]
    stride = 1
    for t, grant in enumerate(GRANTS):
        if stride < count:
            got = [partner(gathered[0], stride * d) for d in range(1, min(4, count // stride))]
        made = pl.pallas_call(
            lambda *refs: phase_kernel(width, t, *refs),
            in_specs=[smem(), vmem_ref, hbm_ref if t else vmem_ref],
            out_specs=[vmem_ref] * 3,
            out_shape=[
                jax.ShapeDtypeStruct((2, 2, width, pairs), F32),
                jax.ShapeDtypeStruct((2, 2, width, pairs), BF16),
                jax.ShapeDtypeStruct(turned.shape, BF16) if t else jax.ShapeDtypeStruct(own.shape, own.dtype),
            ],
            scratch_shapes=[pltpu.SemaphoreType.DMA] * t,
            compiler_params=pltpu.CompilerParams(vmem_limit_bytes=grant * 2 ** 20),
            cost_estimate=pl.CostEstimate(flops=10 ** 7, bytes_accessed=6 * 2 ** 20, transcendentals=0),
            name="phases",
        )(me, delays, turned if t else own)
        waves.append(made[0])
        mixing.append(made[1])
        if t == 0:
            own = made[2]
        else:
            held = made[2]
        if stride < count:
            gathered = [own if t == 0 else gathered[0]] + got
            stride *= 4
            if stride < count:
                gathered = [jnp.concatenate(gathered, axis=0)]
    while stride < count:
        got = [partner(gathered[0], stride * d) for d in range(1, min(4, count // stride))]
        gathered = gathered + got
        stride *= 4
        if stride < count:
            gathered = [jnp.concatenate(gathered, axis=0)]
    shares = pl.pallas_call(
        lambda *refs: sums_kernel(width, len(gathered), *refs),
        in_specs=[smem()] + [vmem_ref] * (len(gathered) + 7),
        out_specs=vmem_ref,
        out_shape=jax.ShapeDtypeStruct((4, 4, 2, pairs), F32),
        scratch_shapes=[vmem(2, width, 128), vmem(2, 2, width, pairs), vmem(2, count, width)],
        compiler_params=params,
        name="window_sums",
    )(me, windows.reshape(1, window_count), *gathered, delays, held, *waves, *mixing)
    shares = lax.all_to_all(shares, "sub", 0, 0, axis_index_groups=fours)
    pieces = [shares[d] for d in range(4)]
    stride = 4
    while stride < count:
        while len(pieces) > 1:
            pieces = [pieces[i] + pieces[i + 1] for i in range(0, len(pieces), 2)]
        pieces += [partner(pieces[0], stride * d) for d in range(1, min(4, count // stride))]
        stride *= 4
    model = pl.pallas_call(
        lambda *refs: solve_kernel(float(window_count), *refs),
        in_specs=[smem(), smem()] + [vmem_ref] * len(pieces),
        out_specs=vmem_ref,
        out_shape=jax.ShapeDtypeStruct((4, 4, 2, GAINS_AT + STATIONS), F32),
        compiler_params=params,
        name="gain_solve",
    )(me, tracks, *pieces)
    model = lax.all_to_all(model, "sub", 0, 0, axis_index_groups=fours)
    cleaned, gains = pl.pallas_call(
        lambda *refs: clean_kernel(width, *refs),
        in_specs=[vmem_ref] * 4,
        out_specs=[hbm_ref, vmem_ref],
        out_shape=[
            jax.ShapeDtypeStruct(turned.shape, BF16),
            jax.ShapeDtypeStruct((2, 2, 2, 4, STATIONS), F32),
        ],
        scratch_shapes=[
            pltpu.VMEM(turned.shape, BF16),
            vmem(4, 16, pairs),
            pltpu.SemaphoreType.DMA((2, width // CHUNK)),
        ],
        compiler_params=params,
        name="clean",
    )(held, *waves, model)
    return jnp.transpose(cleaned, (0, 1, 2, 4, 3)), gains


def solution(mesh):
    return jax.shard_map(
        local,
        mesh=mesh,
        in_specs=(
            P(None, "obs", None, None, "sub"),
            P(None, "obs", None),
            P("obs", "sub"),
            P(),
            P(None, "obs"),
        ),
        out_specs=(P(None, "obs", None, None, "sub"), P(None, None, "obs", None, None)),
        check_vma=False,
    )
```

```python
import jax
import jax.numpy as jnp
import numpy as np
from jax import lax
from jax.experimental import pallas as pl
from jax.experimental.pallas import tpu as pltpu
from jax.sharding import PartitionSpec as P

STATIONS = 38
GITERS = 8
DAMPING = 1.0
STEPS_PER_TURN = 64
GAINS_AT = 768
CHUNK = 48
GRANTS = (45, 45)
ROWS = 40

F32 = jnp.float32
BF16 = jnp.bfloat16


def iota(shape, dim):
    return lax.broadcasted_iota(jnp.int32, shape, dim).astype(F32)


def sincos_turns(turns):
    half = (turns - jnp.floor(turns + 0.5)) * np.float32(np.pi)
    sq = half * half
    sin = np.float32(-1.0 / 39916800)
    for term in (1.0 / 362880, -1.0 / 5040, 1.0 / 120, -1.0 / 6, 1.0):
        sin = sin * sq + np.float32(term)
    sin = sin * half
    cos = np.float32(1.0 / 479001600)
    for term in (-1.0 / 3628800, 1.0 / 40320, -1.0 / 720, 1.0 / 24, -0.5, 1.0):
        cos = cos * sq + np.float32(term)
    return 1.0 - 2.0 * (sin * sin), 2.0 * (sin * cos)


def split_two(value):
    high = value.astype(BF16)
    low = (value - high.astype(F32)).astype(BF16)
    return high, low


def split_three(value):
    high = value.astype(BF16)
    rest = value - high.astype(F32)
    mid = rest.astype(BF16)
    low = (rest - mid.astype(F32)).astype(BF16)
    return high, mid, low


def dot(left, right):
    return jnp.dot(left, right, preferred_element_type=F32)


def times(left, right):
    (lr, li), (rr, ri) = left, right
    return lr * rr - li * ri, lr * ri + li * rr


def phase_rows(delays, anchor, width):
    place = iota((8, 1), 0)
    second = place >= 4.0
    turns = jnp.where(second, delays[1], delays[0])
    at = anchor + float(STEPS_PER_TURN) * jnp.where(second, place - 4.0, place)
    base = sincos_turns(turns * (at * np.float32(1.0 / STEPS_PER_TURN)))
    fine, coarse = [], []
    for s in range(2):
        low = sincos_turns(delays[s] * (place * np.float32(1.0 / STEPS_PER_TURN)))
        high = low
        for doubling in range(3):
            high = times(high, high)
        rows = [times(tuple(part[4 * s + a:4 * s + a + 1] for part in base), high)
                for a in range(width // STEPS_PER_TURN)]
        fine.append(low)
        coarse.append(rows)
    return fine, coarse


def tiles(pairs, body):
    full = pairs // 128

    def step(tile, carry):
        body(pl.ds(pl.multiple_of(tile * 128, 128), 128), 128)
        return carry

    lax.fori_loop(0, full, step, 0)
    if pairs % 128:
        body(pl.ds(full * 128, pairs % 128), pairs % 128)


def phase_kernel(width, t, reach, me_ref, *refs):
    anchor = me_ref[0].astype(F32) * float(width)
    vis_hbm, *refs, sem = refs
    if t == 0:
        delay_ref, flag_ref, wave_ref, mix_ref, vis_ref, own_ref, hot_ref = refs
    else:
        delay_ref, win_ref, wave_ref, mix_ref, vis_ref, *mask_refs = refs
    copy = pltpu.make_async_copy(vis_hbm.at[:, t], vis_ref, sem)
    copy.start()
    if t == 0:
        own_ref[...] = flag_ref[...]
        hot_ref[0], hot_ref[1] = station_hots(delay_ref.shape[2])
    else:
        window_masks(width, reach, me_ref[0], win_ref, *mask_refs)
    pairs = delay_ref.shape[2]

    def waves(lanes, count):
        delays = [delay_ref[s, t:t + 1, lanes] for s in range(2)]
        fine, coarse = phase_rows(delays, anchor, width)
        for block in range(width // 16):
            found = []
            for s in range(2):
                halves = []
                for half in range(2):
                    a, b = divmod(2 * block + half, 8)
                    halves.append(times(tuple(part[b:b + 1] for part in coarse[s][a]), fine[s]))
                found.append([jnp.concatenate([h[ri] for h in halves], axis=0) for ri in range(2)])
            rows = slice(block * 16, block * 16 + 16)
            (r0, i0), (r1, i1) = found
            for s in range(2):
                for ri in range(2):
                    wave_ref[s, ri, rows, lanes] = found[s][ri]
            for slot, value in enumerate((r1 * r0 + i1 * i0, i1 * r0 - r1 * i0)):
                high, low = split_two(value)
                mix_ref[slot, 0, rows, lanes] = high
                mix_ref[slot, 1, rows, lanes] = low

    tiles(pairs, waves)
    copy.wait()


def window_masks(width, reach, me, win_ref, inside_ref, chosen_ref, outside_ref, ends_ref):
    anchor = me.astype(F32) * float(width)
    lowest = (me - lax.rem(me, reach) - reach).astype(F32)
    windows = win_ref.shape[1]
    final = anchor + float(width - 1)
    win_row = win_ref[...].astype(F32)
    sub, lane = iota((windows, windows), 0), iota((windows, windows), 1)
    end_c = jnp.sum(jnp.where(lane <= sub, win_row, 0.0), axis=1, keepdims=True)
    start_c = jnp.sum(jnp.where(lane < sub, win_row, 0.0), axis=1, keepdims=True)
    win_c = end_c - start_c
    end_r = jnp.sum(jnp.where(sub <= lane, win_c, 0.0), axis=0, keepdims=True)
    start_r = jnp.sum(jnp.where(sub < lane, win_c, 0.0), axis=0, keepdims=True)
    first_c = jnp.where((start_c <= anchor) & (anchor < end_c), 1.0, 0.0)
    last_c = jnp.where((start_c <= final) & (final < end_c), 1.0, 0.0)
    from_first = jnp.sum(first_c * start_c, axis=0, keepdims=True)
    to_last = jnp.sum(last_c * end_c, axis=0, keepdims=True)
    here = anchor + iota((windows, width), 1)
    inside_ref[...] = jnp.where((here >= start_c) & (here < end_c), 1.0, 0.0)
    there = anchor + iota((width, windows), 0)
    chosen_ref[...] = jnp.where((there >= start_r) & (there < end_r), 1.0, 0.0)
    shape = outside_ref.shape
    channel = (lowest + iota(shape, 0)) * float(width) + iota(shape, 1)
    remote = ((channel < anchor) & (channel >= from_first)) | ((channel > final) & (channel < to_last))
    outside_ref[...] = jnp.where(remote, 1.0, 0.0)
    ends_ref[0] = jnp.broadcast_to(first_c, ends_ref.shape[1:])
    ends_ref[1] = jnp.broadcast_to(last_c, ends_ref.shape[1:])


def sums_kernel(width, reach, me_ref, *refs):
    flag_refs, refs = refs[:3], refs[3:]
    inside_ref, chosen_ref, outside_ref, ends_ref, delay_ref = refs[:5]
    vis_refs, wave_refs, mix_refs, refs = refs[5:7], refs[7:9], refs[9:11], refs[11:]
    out_refs, (alpha_s, mexp_s, wt_s) = refs[:4], refs[4:]
    me = me_ref[0]
    place = lax.rem(me, reach)
    windows = inside_ref.shape[0]
    pairs = delay_ref.shape[2]
    sub, lane = iota((windows, windows), 0), iota((windows, windows), 1)
    first_c, last_c = ends_ref[0][:, :1], ends_ref[1][:, :1]
    apart = iota((outside_ref.shape[0], 1), 0) - (place + reach).astype(F32)
    diagonal = iota((width, width), 0) == iota((width, width), 1)
    wt_s[...] = jnp.zeros_like(wt_s)

    def both_sides(value):
        return (jnp.sum(jnp.where(apart < 0.0, value, 0.0), axis=0, keepdims=True),
                jnp.sum(jnp.where(apart > 0.0, value, 0.0), axis=0, keepdims=True))

    for t in range(2):
        for group, side in enumerate((1, 0, 2)):
            for slot in range(reach):
                row = flag_refs[group][slot, t:t + 1, :].astype(F32)
                wt_s[t, pl.ds(side * reach + lax.bitwise_xor(place, slot), 1), :] = 1.0 - row
        own = 1.0 - flag_refs[0][0, t:t + 1, :].astype(F32)
        inside = inside_ref[...] * own
        outside = outside_ref[...] * wt_s[t]
        before, after = both_sides(jnp.sum(outside, axis=1, keepdims=True))
        count = jnp.sum(inside, axis=1, keepdims=True) + first_c * before + last_c * after
        scale = 1.0 / jnp.maximum(count, 1.0)
        rows = jnp.concatenate([inside, outside], axis=0).astype(BF16)
        scale_r = jnp.sum(jnp.where(sub == lane, scale, 0.0), axis=0, keepdims=True)
        own_c = jnp.sum(jnp.where(diagonal, own, 0.0), axis=1, keepdims=True)
        chosen = chosen_ref[...] * own_c
        alpha_s[t] = jnp.broadcast_to(jnp.sum(chosen * scale_r, axis=1, keepdims=True), (width, 128))
        chosen = chosen.astype(BF16)
        sums = [dot(rows, mix_refs[t][slot, 0]) + dot(rows, mix_refs[t][slot, 1]) for slot in range(2)]
        gap = delay_ref[1, t:t + 1, :] - delay_ref[0, t:t + 1, :]
        phase = sincos_turns(gap * (apart * np.float32(width / STEPS_PER_TURN)))
        away = times(phase, tuple(value[windows:] for value in sums))
        for slot in range(2):
            before, after = both_sides(away[slot])
            total = sums[slot][:windows] + first_c * before + last_c * after
            high, low = split_two(total * (scale * scale))
            mexp_s[t, slot] = dot(chosen, high) + dot(chosen, low)

    for t in range(2):
        def main(lanes, count):
            def step(block, sums):
                rows = pl.ds(pl.multiple_of(block * 16, 16), 16)
                alpha = alpha_s[t, rows, :count]
                mr, mi = mexp_s[t, 0, rows, lanes], mexp_s[t, 1, rows, lanes]
                r0, i0 = wave_refs[t][0, 0, rows, lanes], wave_refs[t][0, 1, rows, lanes]
                r1, i1 = wave_refs[t][1, 0, rows, lanes], wave_refs[t][1, 1, rows, lanes]
                factors = []
                for fr, fi in (
                    (alpha * r0 - (mr * r1 + mi * i1), (mr * i1 - mi * r1) - alpha * i0),
                    (alpha * r1 - (mr * r0 - mi * i0), (mr * i0 + mi * r0) - alpha * i1),
                ):
                    factors.append((fr, fi - fr, fr + fi))
                new = []
                for k in range(4):
                    vr = vis_refs[t][0, k, rows, lanes].astype(F32)
                    vi = vis_refs[t][1, k, rows, lanes].astype(F32)
                    vs = vr + vi
                    for s in range(2):
                        for v, f in zip((vs, vr, vi), factors[s]):
                            product = v * f
                            new.append(sums[len(new)] + (product[:8] + product[8:]))
                return tuple(new)

            zero = jnp.zeros((8, count), F32)
            sums = lax.fori_loop(0, width // 16, step, (zero,) * 24, unroll=4)
            for s in range(2):
                owner = lax.bitwise_xor(lax.bitwise_and(me, 3), t + 2 * s)
                found = []
                for k in range(4):
                    one, two, three = sums[(k * 2 + s) * 3:(k * 2 + s) * 3 + 3]
                    found.append([jnp.sum(value, axis=0, keepdims=True) for value in (one - three, one + two)])
                for d in range(4):
                    @pl.when(owner == d)
                    def write():
                        for k in range(4):
                            for ri in range(2):
                                out_refs[d][k, ri:ri + 1, lanes] = found[k][ri]

        tiles(pairs, main)


def station_hots(pairs):
    station, baseline = iota((ROWS, 1), 0), iota((1, pairs), 1)
    offset = station * (float(2 * STATIONS - 1) - station) * 0.5
    after = (station + 1.0) * (float(2 * STATIONS - 2) - station) * 0.5
    first = jnp.where((baseline >= offset) & (baseline < after), 1.0, 0.0)
    partner_of = baseline + 1.0 + jnp.sum(first * (station - offset), axis=0, keepdims=True)
    second = jnp.where(partner_of == station, 1.0, 0.0)
    return first.astype(BF16), second.astype(BF16)


def solve_kernel(window_count, me_ref, tracks_ref, hot_ref, *refs):
    parts, gain_ref = refs[:-1], refs[-1]
    me = me_ref[0]
    systems = gain_ref.shape[0]
    total = [part[...] for part in parts]
    while len(total) > 1:
        total = [total[i] + total[i + 1] for i in range(0, len(total), 2)]
    total = total[0]
    hot, other = hot_ref[0], hot_ref[1]
    nt = lambda left, right: lax.dot_general(
        left, right, (((1,), (1,)), ((), ())), preferred_element_type=F32)
    upper, lower = [], []
    for system in range(systems):
        for ri in range(2):
            for piece in split_two(total[system, ri:ri + 1]):
                upper.append(hot * piece)
                lower.append(other * piece)
    upper = nt(jnp.concatenate(upper, axis=0), other)
    lower = nt(jnp.concatenate(lower, axis=0), hot)
    cut = lambda value, i: value[i * ROWS:(i + 1) * ROWS]
    join = lambda value, i: cut(value, 2 * i) + cut(value, 2 * i + 1)
    live_r = jnp.where(iota((1, ROWS), 1) < float(STATIONS), 1.0, 0.0)
    live_c = jnp.where(iota((ROWS, 1), 0) < float(STATIONS), 1.0, 0.0)
    matrices = [(join(upper, 2 * i) + join(lower, 2 * i), join(upper, 2 * i + 1) - join(lower, 2 * i + 1))
                for i in range(systems)]
    states = [(live_r, 0.0 * live_r, live_c, 0.0 * live_c)] * systems
    for turn in range(GITERS):
        for system in range(systems):
            re, im = matrices[system]
            row_re, row_im, col_re, col_im = states[system]
            pull_cr = jnp.sum(re * row_re - im * row_im, axis=1, keepdims=True)
            pull_ci = jnp.sum(re * row_im + im * row_re, axis=1, keepdims=True)
            pull_rr = jnp.sum(re * col_re + im * col_im, axis=0, keepdims=True)
            pull_ri = jnp.sum(re * col_im - im * col_re, axis=0, keepdims=True)
            power_r = row_re * row_re + row_im * row_im
            power_c = col_re * col_re + col_im * col_im
            total = jnp.sum(power_c, axis=0, keepdims=True)
            inverse_r = 0.5 / (window_count * (total - power_r) + DAMPING)
            inverse_c = 0.5 / (window_count * (total - power_c) + DAMPING)
            states[system] = (0.5 * row_re + pull_rr * inverse_r, 0.5 * row_im + pull_ri * inverse_r,
                              0.5 * col_re + pull_cr * inverse_c, 0.5 * col_im + pull_ci * inverse_c)
    visible = tracks_ref[lax.bitwise_and(lax.div(me, 2), 1), lax.bitwise_and(me, 1)].astype(F32)
    gains = [state[ri] * visible for state in states for ri in range(2)]
    gains = jnp.concatenate(gains, axis=0)
    stacked = jnp.concatenate([piece.astype(F32) for piece in split_three(gains)], axis=0).astype(BF16)
    ends = []
    for table in (hot, other):
        wide = dot(stacked, table)
        ends.append((wide[:8] + wide[8:16]) + wide[16:])
    pairs = hot.shape[1]
    for system in range(systems):
        (lr, li), (rr, ri_) = [[end[2 * system + ri:2 * system + ri + 1] for ri in range(2)] for end in ends]
        gain_ref[system, 0:1, :pairs] = lr * rr + li * ri_
        gain_ref[system, 1:2, :pairs] = li * rr - lr * ri_
        gain_ref[system, :, GAINS_AT:] = gains[2 * system:2 * system + 2, :STATIONS]


def clean_kernel(width, me_ref, *refs):
    vis_refs, wave_refs, piece_refs = refs[:2], refs[2:4], refs[4:8]
    out_hbm, gain_out_ref, out_s, model_s, sems = refs[8:]
    pairs = wave_refs[0].shape[3]
    mine = lax.bitwise_and(me_ref[0], 3)
    for d, piece in enumerate(piece_refs):
        owner = lax.bitwise_xor(mine, d)
        t, s = lax.bitwise_and(owner, 1), lax.div(owner, 2)
        for k in range(4):
            for ri in range(2):
                gain_out_ref[ri, s, t, k:k + 1, :] = piece[k, ri:ri + 1, GAINS_AT:]
            re, im = piece[k, 0:1, :pairs], piece[k, 1:2, :pairs]
            for slot, value in enumerate((re, im - re, re + im)):
                model_s[owner, 3 * k + slot:3 * k + slot + 1, :] = value

    def copy_out(t, index):
        rows = pl.ds(pl.multiple_of(index * CHUNK, CHUNK), CHUNK)
        return pltpu.make_async_copy(out_s.at[:, t, :, rows], out_hbm.at[:, t, :, rows], sems.at[t, index])

    chunks = width // CHUNK
    for t in range(2):
        def chunk(index, carry):
            def main(lanes, count):
                for block in range(CHUNK // 16):
                    rows = pl.ds(pl.multiple_of(index * CHUNK + block * 16, 16), 16)
                    waves = []
                    for s in range(2):
                        re, im = (wave_refs[t][s, ri, rows, lanes] for ri in range(2))
                        waves.append((re + im, re, im))
                    for k in range(4):
                        sums = []
                        for slot in range(3):
                            one, two = (waves[s][slot] * model_s[t + 2 * s, 3 * k + slot:3 * k + slot + 1, lanes]
                                        for s in range(2))
                            sums.append(one + two)
                        vr = vis_refs[t][0, k, rows, lanes].astype(F32)
                        vi = vis_refs[t][1, k, rows, lanes].astype(F32)
                        out_s[0, t, k, rows, lanes] = (vr - (sums[0] - sums[2])).astype(BF16)
                        out_s[1, t, k, rows, lanes] = (vi - (sums[0] + sums[1])).astype(BF16)

            tiles(pairs, main)
            copy_out(t, index).start()
            return carry

        lax.fori_loop(0, chunks, chunk, 0)
    for t in range(2):
        for index in range(chunks):
            copy_out(t, index).wait()


def partner(value, bits):
    count = lax.axis_size("sub")
    return lax.ppermute(value, "sub", [(i, i ^ bits) for i in range(count)])


def from_both_sides(value, shift):
    count = lax.axis_size("sub")
    return [lax.ppermute(value, "sub", [(i, i + move) for i in range(count) if 0 <= i + move < count])
            for move in (shift, -shift)]


def smem():
    return pl.BlockSpec(memory_space=pltpu.SMEM)


def local(visibilities, delays, flags, windows, tracks):
    width = visibilities.shape[4]
    pairs = visibilities.shape[3]
    count = lax.axis_size("sub")
    window_count = windows.shape[0]
    turned = jnp.transpose(visibilities, (0, 1, 2, 4, 3))
    me = lax.axis_index("sub").astype(jnp.int32).reshape(1)
    vmem_ref = pl.BlockSpec(memory_space=pltpu.VMEM)
    hbm_ref = pl.BlockSpec(memory_space=pltpu.HBM)
    vmem = lambda *shape: pltpu.VMEM(shape, F32)
    params = pltpu.CompilerParams(vmem_limit_bytes=24 * 2 ** 20)
    flags = flags[None]

    reach = count // 4
    remote_rows = 16 * pl.cdiv(3 * reach, 16)

    made = []
    beside = [partner(flags, d) for d in range(1, 4)]
    for t in range(2):
        shape = lambda *dims: jax.ShapeDtypeStruct(dims, F32)
        out_shape = [
            shape(2, 2, width, pairs),
            jax.ShapeDtypeStruct((2, 2, width, pairs), BF16),
            jax.ShapeDtypeStruct((2, 4, width, pairs), BF16),
        ]
        if t == 0:
            operands = (me, turned, delays, flags)
            out_shape += [jax.ShapeDtypeStruct(flags.shape, flags.dtype),
                          jax.ShapeDtypeStruct((2, ROWS, pairs), BF16)]
        else:
            operands = (me, turned, delays, windows.reshape(1, window_count))
            out_shape += [shape(window_count, width), shape(width, window_count),
                          shape(remote_rows, width), shape(2, window_count, 128)]
        made.append(pl.pallas_call(
            lambda *refs: phase_kernel(width, t, reach, *refs),
            in_specs=[smem(), hbm_ref] + [vmem_ref] * (len(operands) - 2),
            out_specs=[vmem_ref] * len(out_shape),
            out_shape=out_shape,
            scratch_shapes=[pltpu.SemaphoreType.DMA],
            compiler_params=pltpu.CompilerParams(vmem_limit_bytes=GRANTS[t] * 2 ** 20),
            cost_estimate=pl.CostEstimate(flops=10 ** 7, bytes_accessed=6 * 2 ** 20, transcendentals=0),
            name="phases",
        )(*operands))
        if t == 0:
            gathered = jnp.concatenate([made[0][3]] + beside, axis=0)
            while gathered.shape[0] < reach:
                stride = gathered.shape[0]
                gathered = jnp.concatenate([gathered] + [partner(gathered, stride * d) for d in range(1, 4)], axis=0)
            gathered = [gathered] + from_both_sides(gathered, reach)
    waves, mixing, held = ([part[i] for part in made] for i in range(3))
    masks = made[1][3:]
    hots = made[0][4]
    quarters = pl.pallas_call(
        lambda *refs: sums_kernel(width, reach, *refs),
        in_specs=[smem()] + [vmem_ref] * 14,
        out_specs=[vmem_ref] * 4,
        out_shape=[jax.ShapeDtypeStruct((4, 2, pairs), F32)] * 4,
        scratch_shapes=[vmem(2, width, 128), vmem(2, 2, width, pairs), vmem(2, remote_rows, width)],
        compiler_params=params,
        name="window_sums",
    )(me, *gathered, *masks, delays, *held, *waves, *mixing)
    pieces = [quarters[0]] + [partner(quarters[d], d) for d in range(1, 4)]
    stride = 4
    while stride < count:
        while len(pieces) > 1:
            pieces = [pieces[i] + pieces[i + 1] for i in range(0, len(pieces), 2)]
        pieces += [partner(pieces[0], stride * d) for d in range(1, min(4, count // stride))]
        stride *= 4
    model = pl.pallas_call(
        lambda *refs: solve_kernel(float(window_count), *refs),
        in_specs=[smem(), smem()] + [vmem_ref] * (1 + len(pieces)),
        out_specs=vmem_ref,
        out_shape=jax.ShapeDtypeStruct((4, 2, GAINS_AT + STATIONS), F32),
        compiler_params=params,
        name="gain_solve",
    )(me, tracks, hots, *pieces)
    model = [model] + [partner(model, d) for d in range(1, 4)]
    cleaned, gains = pl.pallas_call(
        lambda *refs: clean_kernel(width, *refs),
        in_specs=[smem()] + [vmem_ref] * 8,
        out_specs=[hbm_ref, vmem_ref],
        out_shape=[
            jax.ShapeDtypeStruct(turned.shape, BF16),
            jax.ShapeDtypeStruct((2, 2, 2, 4, STATIONS), F32),
        ],
        scratch_shapes=[
            pltpu.VMEM(turned.shape, BF16),
            vmem(4, 16, pairs),
            pltpu.SemaphoreType.DMA((2, width // CHUNK)),
        ],
        compiler_params=params,
        name="clean",
    )(me, *held, *waves, *model)
    return jnp.transpose(cleaned, (0, 1, 2, 4, 3)), gains


def solution(mesh):
    return jax.shard_map(
        local,
        mesh=mesh,
        in_specs=(
            P(None, "obs", None, None, "sub"),
            P(None, "obs", None),
            P("obs", "sub"),
            P(),
            P(None, "obs"),
        ),
        out_specs=(P(None, "obs", None, None, "sub"), P(None, None, "obs", None, None)),
        check_vma=False,
    )
```

```python
import jax
import jax.numpy as jnp
import numpy as np
from jax import lax
from jax.experimental import pallas as pl
from jax.experimental.pallas import tpu as pltpu
from jax.sharding import PartitionSpec as P

STATIONS = 38
GITERS = 8
DAMPING = 1.0
STEPS_PER_TURN = 64
GAINS_AT = 768
CHUNK = 48
GRANT = 40
ROWS = 40

F32 = jnp.float32
BF16 = jnp.bfloat16


def iota(shape, dim):
    return lax.broadcasted_iota(jnp.int32, shape, dim).astype(F32)


def sincos_turns(turns):
    half = (turns - jnp.floor(turns + 0.5)) * np.float32(np.pi)
    sq = half * half
    sin = np.float32(-1.0 / 39916800)
    for term in (1.0 / 362880, -1.0 / 5040, 1.0 / 120, -1.0 / 6, 1.0):
        sin = sin * sq + np.float32(term)
    sin = sin * half
    cos = np.float32(1.0 / 479001600)
    for term in (-1.0 / 3628800, 1.0 / 40320, -1.0 / 720, 1.0 / 24, -0.5, 1.0):
        cos = cos * sq + np.float32(term)
    return 1.0 - 2.0 * (sin * sin), 2.0 * (sin * cos)


def split_two(value):
    high = value.astype(BF16)
    low = (value - high.astype(F32)).astype(BF16)
    return high, low


def split_three(value):
    high = value.astype(BF16)
    rest = value - high.astype(F32)
    mid = rest.astype(BF16)
    low = (rest - mid.astype(F32)).astype(BF16)
    return high, mid, low


def dot(left, right):
    return jnp.dot(left, right, preferred_element_type=F32)


def times(left, right):
    (lr, li), (rr, ri) = left, right
    return lr * rr - li * ri, lr * ri + li * rr


def phase_rows(delays, anchor, width):
    place = iota((8, 1), 0)
    second = place >= 4.0
    turns = jnp.where(second, delays[1], delays[0])
    at = anchor + float(STEPS_PER_TURN) * jnp.where(second, place - 4.0, place)
    base = sincos_turns(turns * (at * np.float32(1.0 / STEPS_PER_TURN)))
    fine, coarse = [], []
    for s in range(2):
        low = sincos_turns(delays[s] * (place * np.float32(1.0 / STEPS_PER_TURN)))
        high = low
        for doubling in range(3):
            high = times(high, high)
        rows = [times(tuple(part[4 * s + a:4 * s + a + 1] for part in base), high)
                for a in range(width // STEPS_PER_TURN)]
        fine.append(low)
        coarse.append(rows)
    return fine, coarse


def tiles(pairs, body):
    full = pairs // 128

    def step(tile, carry):
        body(pl.ds(pl.multiple_of(tile * 128, 128), 128), 128)
        return carry

    lax.fori_loop(0, full, step, 0)
    if pairs % 128:
        body(pl.ds(full * 128, pairs % 128), pairs % 128)


def phase_kernel(width, t, reach, me_ref, *refs):
    anchor = me_ref[0].astype(F32) * float(width)
    if t == 0:
        delay_ref, flag_ref, wave_ref, mix_ref, own_ref, hot_ref = refs
    else:
        delay_ref, win_ref, wave_ref, mix_ref, *mask_refs = refs
    if t == 0:
        own_ref[...] = flag_ref[...]
        hot_ref[0], hot_ref[1] = station_hots(delay_ref.shape[2])
    else:
        window_masks(width, reach, me_ref[0], win_ref, *mask_refs)
    pairs = delay_ref.shape[2]

    def waves(lanes, count):
        delays = [delay_ref[s, t:t + 1, lanes] for s in range(2)]
        fine, coarse = phase_rows(delays, anchor, width)
        for block in range(width // 16):
            found = []
            for s in range(2):
                halves = []
                for half in range(2):
                    a, b = divmod(2 * block + half, 8)
                    halves.append(times(tuple(part[b:b + 1] for part in coarse[s][a]), fine[s]))
                found.append([jnp.concatenate([h[ri] for h in halves], axis=0) for ri in range(2)])
            rows = slice(block * 16, block * 16 + 16)
            (r0, i0), (r1, i1) = found
            for s in range(2):
                for ri in range(2):
                    wave_ref[s, ri, rows, lanes] = found[s][ri]
            for slot, value in enumerate((r1 * r0 + i1 * i0, i1 * r0 - r1 * i0)):
                high, low = split_two(value)
                mix_ref[slot, 0, rows, lanes] = high
                mix_ref[slot, 1, rows, lanes] = low

    tiles(pairs, waves)


def window_masks(width, reach, me, win_ref, inside_ref, chosen_ref, outside_ref, ends_ref):
    anchor = me.astype(F32) * float(width)
    lowest = (me - lax.rem(me, reach) - reach).astype(F32)
    windows = win_ref.shape[1]
    final = anchor + float(width - 1)
    win_row = win_ref[...].astype(F32)
    sub, lane = iota((windows, windows), 0), iota((windows, windows), 1)
    end_c = jnp.sum(jnp.where(lane <= sub, win_row, 0.0), axis=1, keepdims=True)
    start_c = jnp.sum(jnp.where(lane < sub, win_row, 0.0), axis=1, keepdims=True)
    win_c = end_c - start_c
    end_r = jnp.sum(jnp.where(sub <= lane, win_c, 0.0), axis=0, keepdims=True)
    start_r = jnp.sum(jnp.where(sub < lane, win_c, 0.0), axis=0, keepdims=True)
    first_c = jnp.where((start_c <= anchor) & (anchor < end_c), 1.0, 0.0)
    last_c = jnp.where((start_c <= final) & (final < end_c), 1.0, 0.0)
    from_first = jnp.sum(first_c * start_c, axis=0, keepdims=True)
    to_last = jnp.sum(last_c * end_c, axis=0, keepdims=True)
    here = anchor + iota((windows, width), 1)
    inside_ref[...] = jnp.where((here >= start_c) & (here < end_c), 1.0, 0.0)
    there = anchor + iota((width, windows), 0)
    chosen_ref[...] = jnp.where((there >= start_r) & (there < end_r), 1.0, 0.0)
    shape = outside_ref.shape
    channel = (lowest + iota(shape, 0)) * float(width) + iota(shape, 1)
    remote = ((channel < anchor) & (channel >= from_first)) | ((channel > final) & (channel < to_last))
    outside_ref[...] = jnp.where(remote, 1.0, 0.0)
    ends_ref[0] = jnp.broadcast_to(first_c, ends_ref.shape[1:])
    ends_ref[1] = jnp.broadcast_to(last_c, ends_ref.shape[1:])


def sums_kernel(width, reach, me_ref, *refs):
    flag_refs, refs = refs[:3], refs[3:]
    inside_ref, chosen_ref, outside_ref, ends_ref, delay_ref = refs[:5]
    vis_hbm, wave_refs, mix_refs, refs = refs[5], refs[6:8], refs[8:10], refs[10:]
    out_refs, (vis_ref, alpha_s, mexp_s, wt_s, sems) = refs[:4], refs[4:]
    copies = [pltpu.make_async_copy(vis_hbm.at[:, t], vis_ref.at[:, t], sems.at[t]) for t in range(2)]
    for copy in copies:
        copy.start()
    me = me_ref[0]
    place = lax.rem(me, reach)
    windows = inside_ref.shape[0]
    pairs = delay_ref.shape[2]
    sub, lane = iota((windows, windows), 0), iota((windows, windows), 1)
    first_c, last_c = ends_ref[0][:, :1], ends_ref[1][:, :1]
    apart = iota((outside_ref.shape[0], 1), 0) - (place + reach).astype(F32)
    diagonal = iota((width, width), 0) == iota((width, width), 1)
    wt_s[...] = jnp.zeros_like(wt_s)

    def both_sides(value):
        return (jnp.sum(jnp.where(apart < 0.0, value, 0.0), axis=0, keepdims=True),
                jnp.sum(jnp.where(apart > 0.0, value, 0.0), axis=0, keepdims=True))

    for t in range(2):
        odd = lax.rem(lax.div(me, reach), 2)
        for group, side in enumerate((1, 2 - 2 * odd, 2 * odd)):
            for slot in range(reach):
                row = flag_refs[group][slot, t:t + 1, :].astype(F32)
                wt_s[t, pl.ds(side * reach + lax.bitwise_xor(place, slot), 1), :] = 1.0 - row
        own = 1.0 - flag_refs[0][0, t:t + 1, :].astype(F32)
        inside = inside_ref[...] * own
        outside = outside_ref[...] * wt_s[t]
        before, after = both_sides(jnp.sum(outside, axis=1, keepdims=True))
        count = jnp.sum(inside, axis=1, keepdims=True) + first_c * before + last_c * after
        scale = 1.0 / jnp.maximum(count, 1.0)
        rows = jnp.concatenate([inside, outside], axis=0).astype(BF16)
        scale_r = jnp.sum(jnp.where(sub == lane, scale, 0.0), axis=0, keepdims=True)
        own_c = jnp.sum(jnp.where(diagonal, own, 0.0), axis=1, keepdims=True)
        chosen = chosen_ref[...] * own_c
        alpha_s[t] = jnp.broadcast_to(jnp.sum(chosen * scale_r, axis=1, keepdims=True), (width, 128))
        chosen = chosen.astype(BF16)
        sums = [dot(rows, mix_refs[t][slot, 0]) + dot(rows, mix_refs[t][slot, 1]) for slot in range(2)]
        gap = delay_ref[1, t:t + 1, :] - delay_ref[0, t:t + 1, :]
        phase = sincos_turns(gap * (apart * np.float32(width / STEPS_PER_TURN)))
        away = times(phase, tuple(value[windows:] for value in sums))
        for slot in range(2):
            before, after = both_sides(away[slot])
            total = sums[slot][:windows] + first_c * before + last_c * after
            high, low = split_two(total * (scale * scale))
            mexp_s[t, slot] = dot(chosen, high) + dot(chosen, low)

    for t in range(2):
        def main(lanes, count):
            def step(block, sums):
                rows = pl.ds(pl.multiple_of(block * 16, 16), 16)
                alpha = alpha_s[t, rows, :count]
                mr, mi = mexp_s[t, 0, rows, lanes], mexp_s[t, 1, rows, lanes]
                r0, i0 = wave_refs[t][0, 0, rows, lanes], wave_refs[t][0, 1, rows, lanes]
                r1, i1 = wave_refs[t][1, 0, rows, lanes], wave_refs[t][1, 1, rows, lanes]
                factors = []
                for fr, fi in (
                    (alpha * r0 - (mr * r1 + mi * i1), (mr * i1 - mi * r1) - alpha * i0),
                    (alpha * r1 - (mr * r0 - mi * i0), (mr * i0 + mi * r0) - alpha * i1),
                ):
                    factors.append((fr, fi - fr, fr + fi))
                new = []
                for k in range(4):
                    vr = vis_ref[0, t, k, rows, lanes].astype(F32)
                    vi = vis_ref[1, t, k, rows, lanes].astype(F32)
                    vs = vr + vi
                    for s in range(2):
                        for v, f in zip((vs, vr, vi), factors[s]):
                            product = v * f
                            new.append(sums[len(new)] + (product[:8] + product[8:]))
                return tuple(new)

            zero = jnp.zeros((8, count), F32)
            sums = lax.fori_loop(0, width // 16, step, (zero,) * 24, unroll=4)
            for s in range(2):
                owner = lax.bitwise_xor(lax.bitwise_and(me, 3), t + 2 * s)
                found = []
                for k in range(4):
                    one, two, three = sums[(k * 2 + s) * 3:(k * 2 + s) * 3 + 3]
                    found.append([jnp.sum(value, axis=0, keepdims=True) for value in (one - three, one + two)])
                for d in range(4):
                    @pl.when(owner == d)
                    def write():
                        for k in range(4):
                            for ri in range(2):
                                out_refs[d][k, ri:ri + 1, lanes] = found[k][ri]

        copies[t].wait()
        tiles(pairs, main)


def station_hots(pairs):
    station, baseline = iota((ROWS, 1), 0), iota((1, pairs), 1)
    offset = station * (float(2 * STATIONS - 1) - station) * 0.5
    after = (station + 1.0) * (float(2 * STATIONS - 2) - station) * 0.5
    first = jnp.where((baseline >= offset) & (baseline < after), 1.0, 0.0)
    partner_of = baseline + 1.0 + jnp.sum(first * (station - offset), axis=0, keepdims=True)
    second = jnp.where(partner_of == station, 1.0, 0.0)
    return first.astype(BF16), second.astype(BF16)


def solve_kernel(window_count, me_ref, tracks_ref, hot_ref, *refs):
    parts, gain_ref = refs[:-1], refs[-1]
    me = me_ref[0]
    systems = gain_ref.shape[0]
    total = [part[...] for part in parts]
    while len(total) > 1:
        total = [total[i] + total[i + 1] for i in range(0, len(total), 2)]
    total = total[0]
    hot, other = hot_ref[0], hot_ref[1]
    nt = lambda left, right: lax.dot_general(
        left, right, (((1,), (1,)), ((), ())), preferred_element_type=F32)
    upper, lower = [], []
    for system in range(systems):
        for ri in range(2):
            for piece in split_two(total[system, ri:ri + 1]):
                upper.append(hot * piece)
                lower.append(other * piece)
    upper = nt(jnp.concatenate(upper, axis=0), other)
    lower = nt(jnp.concatenate(lower, axis=0), hot)
    cut = lambda value, i: value[i * ROWS:(i + 1) * ROWS]
    join = lambda value, i: cut(value, 2 * i) + cut(value, 2 * i + 1)
    live_r = jnp.where(iota((1, ROWS), 1) < float(STATIONS), 1.0, 0.0)
    live_c = jnp.where(iota((ROWS, 1), 0) < float(STATIONS), 1.0, 0.0)
    matrices = [(join(upper, 2 * i) + join(lower, 2 * i), join(upper, 2 * i + 1) - join(lower, 2 * i + 1))
                for i in range(systems)]
    states = [(live_r, 0.0 * live_r, live_c, 0.0 * live_c)] * systems
    for turn in range(GITERS):
        for system in range(systems):
            re, im = matrices[system]
            row_re, row_im, col_re, col_im = states[system]
            pull_cr = jnp.sum(re * row_re - im * row_im, axis=1, keepdims=True)
            pull_ci = jnp.sum(re * row_im + im * row_re, axis=1, keepdims=True)
            pull_rr = jnp.sum(re * col_re + im * col_im, axis=0, keepdims=True)
            pull_ri = jnp.sum(re * col_im - im * col_re, axis=0, keepdims=True)
            power_r = row_re * row_re + row_im * row_im
            power_c = col_re * col_re + col_im * col_im
            total = jnp.sum(power_c, axis=0, keepdims=True)
            inverse_r = 0.5 / (window_count * (total - power_r) + DAMPING)
            inverse_c = 0.5 / (window_count * (total - power_c) + DAMPING)
            states[system] = (0.5 * row_re + pull_rr * inverse_r, 0.5 * row_im + pull_ri * inverse_r,
                              0.5 * col_re + pull_cr * inverse_c, 0.5 * col_im + pull_ci * inverse_c)
    visible = tracks_ref[lax.bitwise_and(lax.div(me, 2), 1), lax.bitwise_and(me, 1)].astype(F32)
    gains = [state[ri] * visible for state in states for ri in range(2)]
    gains = jnp.concatenate(gains, axis=0)
    stacked = jnp.concatenate([piece.astype(F32) for piece in split_three(gains)], axis=0).astype(BF16)
    ends = []
    for table in (hot, other):
        wide = dot(stacked, table)
        ends.append((wide[:8] + wide[8:16]) + wide[16:])
    pairs = hot.shape[1]
    for system in range(systems):
        (lr, li), (rr, ri_) = [[end[2 * system + ri:2 * system + ri + 1] for ri in range(2)] for end in ends]
        gain_ref[system, 0:1, :pairs] = lr * rr + li * ri_
        gain_ref[system, 1:2, :pairs] = li * rr - lr * ri_
        gain_ref[system, :, GAINS_AT:] = gains[2 * system:2 * system + 2, :STATIONS]


def clean_kernel(width, me_ref, *refs):
    vis_ref, wave_refs, piece_refs = refs[0], refs[1:3], refs[3:7]
    out_hbm, gain_out_ref, out_s, model_s, sems = refs[7:]
    pairs = wave_refs[0].shape[3]
    mine = lax.bitwise_and(me_ref[0], 3)
    for d, piece in enumerate(piece_refs):
        owner = lax.bitwise_xor(mine, d)
        t, s = lax.bitwise_and(owner, 1), lax.div(owner, 2)
        for k in range(4):
            for ri in range(2):
                gain_out_ref[ri, s, t, k:k + 1, :] = piece[k, ri:ri + 1, GAINS_AT:]
            re, im = piece[k, 0:1, :pairs], piece[k, 1:2, :pairs]
            for slot, value in enumerate((re, im - re, re + im)):
                model_s[owner, 3 * k + slot:3 * k + slot + 1, :] = value

    def copy_out(t, index):
        rows = pl.ds(pl.multiple_of(index * CHUNK, CHUNK), CHUNK)
        return pltpu.make_async_copy(out_s.at[:, t, :, rows], out_hbm.at[:, t, :, rows], sems.at[t, index])

    chunks = width // CHUNK
    for t in range(2):
        def chunk(index, carry):
            def main(lanes, count):
                for block in range(CHUNK // 16):
                    rows = pl.ds(pl.multiple_of(index * CHUNK + block * 16, 16), 16)
                    waves = []
                    for s in range(2):
                        re, im = (wave_refs[t][s, ri, rows, lanes] for ri in range(2))
                        waves.append((re + im, re, im))
                    for k in range(4):
                        sums = []
                        for slot in range(3):
                            one, two = (waves[s][slot] * model_s[t + 2 * s, 3 * k + slot:3 * k + slot + 1, lanes]
                                        for s in range(2))
                            sums.append(one + two)
                        vr = vis_ref[0, t, k, rows, lanes].astype(F32)
                        vi = vis_ref[1, t, k, rows, lanes].astype(F32)
                        out_s[0, t, k, rows, lanes] = (vr - (sums[0] - sums[2])).astype(BF16)
                        out_s[1, t, k, rows, lanes] = (vi - (sums[0] + sums[1])).astype(BF16)

            tiles(pairs, main)
            copy_out(t, index).start()
            return carry

        lax.fori_loop(0, chunks, chunk, 0)
    for t in range(2):
        for index in range(chunks):
            copy_out(t, index).wait()


def partner(value, bits):
    count = lax.axis_size("sub")
    return lax.ppermute(value, "sub", [(i, i ^ bits) for i in range(count)])


def from_both_sides(value, reach):
    count = lax.axis_size("sub")
    pairings = [[], []]
    for i in range(count):
        for pairing, other in enumerate(((i // reach) ^ 1, ((i // reach + 1) ^ 1) - 1)):
            if 0 <= other < count // reach:
                pairings[pairing].append((i, other * reach + i % reach))
    return [lax.ppermute(value, "sub", pairing) for pairing in pairings]


def smem():
    return pl.BlockSpec(memory_space=pltpu.SMEM)


def local(visibilities, delays, flags, windows, tracks):
    width = visibilities.shape[4]
    pairs = visibilities.shape[3]
    count = lax.axis_size("sub")
    window_count = windows.shape[0]
    turned = jnp.transpose(visibilities, (0, 1, 2, 4, 3))
    me = lax.axis_index("sub").astype(jnp.int32).reshape(1)
    vmem_ref = pl.BlockSpec(memory_space=pltpu.VMEM)
    hbm_ref = pl.BlockSpec(memory_space=pltpu.HBM)
    vmem = lambda *shape: pltpu.VMEM(shape, F32)
    params = pltpu.CompilerParams(vmem_limit_bytes=24 * 2 ** 20)
    flags = flags[None]

    reach = count // 4
    remote_rows = 16 * pl.cdiv(3 * reach, 16)

    made = []
    beside = [partner(flags, d) for d in range(1, 4)]
    for t in range(2):
        shape = lambda *dims: jax.ShapeDtypeStruct(dims, F32)
        out_shape = [
            shape(2, 2, width, pairs),
            jax.ShapeDtypeStruct((2, 2, width, pairs), BF16),
        ]
        if t == 0:
            operands = (me, delays, flags)
            out_shape += [jax.ShapeDtypeStruct(flags.shape, flags.dtype),
                          jax.ShapeDtypeStruct((2, ROWS, pairs), BF16)]
        else:
            operands = (me, delays, windows.reshape(1, window_count))
            out_shape += [shape(window_count, width), shape(width, window_count),
                          shape(remote_rows, width), shape(2, window_count, 128)]
        made.append(pl.pallas_call(
            lambda *refs: phase_kernel(width, t, reach, *refs),
            in_specs=[smem()] + [vmem_ref] * (len(operands) - 1),
            out_specs=[vmem_ref] * len(out_shape),
            out_shape=out_shape,
            compiler_params=params,
            cost_estimate=pl.CostEstimate(flops=10 ** 7, bytes_accessed=6 * 2 ** 20, transcendentals=0),
            name="phases",
        )(*operands))
        if t == 0:
            gathered = jnp.concatenate([made[0][2]] + beside, axis=0)
            while gathered.shape[0] < reach:
                stride = gathered.shape[0]
                gathered = jnp.concatenate([gathered] + [partner(gathered, stride * d) for d in range(1, 4)], axis=0)
            gathered = [gathered] + from_both_sides(gathered, reach)
    waves, mixing = ([part[i] for part in made] for i in range(2))
    masks = made[1][2:]
    hots = made[0][3]
    *quarters, held = pl.pallas_call(
        lambda *refs: sums_kernel(width, reach, *refs),
        in_specs=[smem()] + [vmem_ref] * 8 + [hbm_ref] + [vmem_ref] * 4,
        out_specs=[vmem_ref] * 5,
        out_shape=[jax.ShapeDtypeStruct((4, 2, pairs), F32)] * 4 + [jax.ShapeDtypeStruct(turned.shape, BF16)],
        scratch_shapes=[vmem(2, width, 128), vmem(2, 2, width, pairs), vmem(2, remote_rows, width),
                        pltpu.SemaphoreType.DMA((2,))],
        compiler_params=pltpu.CompilerParams(vmem_limit_bytes=GRANT * 2 ** 20),
        name="window_sums",
    )(me, *gathered, *masks, delays, turned, *waves, *mixing)
    pieces = [quarters[0]] + [partner(quarters[d], d) for d in range(1, 4)]
    stride = 4
    while stride < count:
        while len(pieces) > 1:
            pieces = [pieces[i] + pieces[i + 1] for i in range(0, len(pieces), 2)]
        pieces += [partner(pieces[0], stride * d) for d in range(1, min(4, count // stride))]
        stride *= 4
    model = pl.pallas_call(
        lambda *refs: solve_kernel(float(window_count), *refs),
        in_specs=[smem(), smem()] + [vmem_ref] * (1 + len(pieces)),
        out_specs=vmem_ref,
        out_shape=jax.ShapeDtypeStruct((4, 2, GAINS_AT + STATIONS), F32),
        compiler_params=params,
        name="gain_solve",
    )(me, tracks, hots, *pieces)
    model = [model] + [partner(model, d) for d in range(1, 4)]
    cleaned, gains = pl.pallas_call(
        lambda *refs: clean_kernel(width, *refs),
        in_specs=[smem()] + [vmem_ref] * 7,
        out_specs=[hbm_ref, vmem_ref],
        out_shape=[
            jax.ShapeDtypeStruct(turned.shape, BF16),
            jax.ShapeDtypeStruct((2, 2, 2, 4, STATIONS), F32),
        ],
        scratch_shapes=[
            pltpu.VMEM(turned.shape, BF16),
            vmem(4, 16, pairs),
            pltpu.SemaphoreType.DMA((2, width // CHUNK)),
        ],
        compiler_params=params,
        name="clean",
    )(me, held, *waves, *model)
    return jnp.transpose(cleaned, (0, 1, 2, 4, 3)), gains


def solution(mesh):
    return jax.shard_map(
        local,
        mesh=mesh,
        in_specs=(
            P(None, "obs", None, None, "sub"),
            P(None, "obs", None),
            P("obs", "sub"),
            P(),
            P(None, "obs"),
        ),
        out_specs=(P(None, "obs", None, None, "sub"), P(None, None, "obs", None, None)),
        check_vma=False,
    )
```

```python
import jax
import jax.numpy as jnp
import numpy as np
from jax import lax
from jax.experimental import pallas as pl
from jax.experimental.pallas import tpu as pltpu
from jax.sharding import PartitionSpec as P

STATIONS = 38
GITERS = 8
DAMPING = 1.0
STEPS_PER_TURN = 64
GAINS_AT = 768
CHUNK = 48
GRANT = 40
ROWS = 40

F32 = jnp.float32
BF16 = jnp.bfloat16


def iota(shape, dim):
    return lax.broadcasted_iota(jnp.int32, shape, dim).astype(F32)


def sincos_turns(turns):
    half = (turns - jnp.floor(turns + 0.5)) * np.float32(np.pi)
    sq = half * half
    sin = np.float32(-1.0 / 39916800)
    for term in (1.0 / 362880, -1.0 / 5040, 1.0 / 120, -1.0 / 6, 1.0):
        sin = sin * sq + np.float32(term)
    sin = sin * half
    cos = np.float32(1.0 / 479001600)
    for term in (-1.0 / 3628800, 1.0 / 40320, -1.0 / 720, 1.0 / 24, -0.5, 1.0):
        cos = cos * sq + np.float32(term)
    return 1.0 - 2.0 * (sin * sin), 2.0 * (sin * cos)


def split_two(value):
    high = value.astype(BF16)
    low = (value - high.astype(F32)).astype(BF16)
    return high, low


def split_three(value):
    high = value.astype(BF16)
    rest = value - high.astype(F32)
    mid = rest.astype(BF16)
    low = (rest - mid.astype(F32)).astype(BF16)
    return high, mid, low


def dot(left, right):
    return jnp.dot(left, right, preferred_element_type=F32)


def times(left, right):
    (lr, li), (rr, ri) = left, right
    return lr * rr - li * ri, lr * ri + li * rr


def phase_rows(delays, anchor, width):
    place = iota((8, 1), 0)
    second = place >= 4.0
    turns = jnp.where(second, delays[1], delays[0])
    at = anchor + float(STEPS_PER_TURN) * jnp.where(second, place - 4.0, place)
    base = sincos_turns(turns * (at * np.float32(1.0 / STEPS_PER_TURN)))
    fine, coarse = [], []
    for s in range(2):
        low = sincos_turns(delays[s] * (place * np.float32(1.0 / STEPS_PER_TURN)))
        high = low
        for doubling in range(3):
            high = times(high, high)
        rows = [times(tuple(part[4 * s + a:4 * s + a + 1] for part in base), high)
                for a in range(width // STEPS_PER_TURN)]
        fine.append(low)
        coarse.append(rows)
    return fine, coarse


def tiles(pairs, body):
    full = pairs // 128

    def step(tile, carry):
        body(pl.ds(pl.multiple_of(tile * 128, 128), 128), 128)
        return carry

    lax.fori_loop(0, full, step, 0)
    if pairs % 128:
        body(pl.ds(full * 128, pairs % 128), pairs % 128)


def phase_kernel(width, t, reach, me_ref, *refs):
    anchor = me_ref[0].astype(F32) * float(width)
    if t == 0:
        delay_ref, flag_ref, wave_ref, mix_ref, own_ref = refs
    else:
        delay_ref, win_ref, wave_ref, mix_ref, apart_ref, *mask_refs = refs
    if t == 0:
        own_ref[...] = flag_ref[...]
    else:
        window_masks(width, reach, me_ref[0], win_ref, *mask_refs)
        apart = blocks_apart(me_ref[0], reach, apart_ref.shape[2])
        for time in range(2):
            gap = delay_ref[1, time:time + 1, :] - delay_ref[0, time:time + 1, :]
            phase = sincos_turns(gap * (apart * np.float32(width / STEPS_PER_TURN)))
            apart_ref[time, 0], apart_ref[time, 1] = phase
    pairs = delay_ref.shape[2]

    def waves(lanes, count):
        delays = [delay_ref[s, t:t + 1, lanes] for s in range(2)]
        fine, coarse = phase_rows(delays, anchor, width)
        for block in range(width // 16):
            found = []
            for s in range(2):
                halves = []
                for half in range(2):
                    a, b = divmod(2 * block + half, 8)
                    halves.append(times(tuple(part[b:b + 1] for part in coarse[s][a]), fine[s]))
                found.append([jnp.concatenate([h[ri] for h in halves], axis=0) for ri in range(2)])
            rows = slice(block * 16, block * 16 + 16)
            (r0, i0), (r1, i1) = found
            for s in range(2):
                for ri in range(2):
                    wave_ref[s, ri, rows, lanes] = found[s][ri]
            for slot, value in enumerate((r1 * r0 + i1 * i0, i1 * r0 - r1 * i0)):
                high, low = split_two(value)
                mix_ref[slot, 0, rows, lanes] = high
                mix_ref[slot, 1, rows, lanes] = low

    tiles(pairs, waves)


def blocks_apart(me, reach, rows):
    return iota((rows, 1), 0) - (lax.rem(me, reach) + reach).astype(F32)


def window_masks(width, reach, me, win_ref, inside_ref, chosen_ref, outside_ref, ends_ref):
    anchor = me.astype(F32) * float(width)
    lowest = (me - lax.rem(me, reach) - reach).astype(F32)
    windows = inside_ref.shape[0]
    final = anchor + float(width - 1)
    win_row = win_ref[...].astype(F32)
    sub, lane = iota((windows, windows), 0), iota((windows, windows), 1)
    end_c = jnp.sum(jnp.where(lane <= sub, win_row, 0.0), axis=1, keepdims=True)
    start_c = jnp.sum(jnp.where(lane < sub, win_row, 0.0), axis=1, keepdims=True)
    win_c = end_c - start_c
    end_r = jnp.sum(jnp.where(sub <= lane, win_c, 0.0), axis=0, keepdims=True)
    start_r = jnp.sum(jnp.where(sub < lane, win_c, 0.0), axis=0, keepdims=True)
    first_c = jnp.where((start_c <= anchor) & (anchor < end_c), 1.0, 0.0)
    last_c = jnp.where((start_c <= final) & (final < end_c), 1.0, 0.0)
    from_first = jnp.sum(first_c * start_c, axis=0, keepdims=True)
    to_last = jnp.sum(last_c * end_c, axis=0, keepdims=True)
    here = anchor + iota((windows, width), 1)
    inside_ref[...] = jnp.where((here >= start_c) & (here < end_c), 1.0, 0.0)
    there = anchor + iota((width, windows), 0)
    chosen_ref[...] = jnp.where((there >= start_r) & (there < end_r), 1.0, 0.0)
    shape = outside_ref.shape
    channel = (lowest + iota(shape, 0)) * float(width) + iota(shape, 1)
    remote = ((channel < anchor) & (channel >= from_first)) | ((channel > final) & (channel < to_last))
    outside_ref[...] = jnp.where(remote, 1.0, 0.0)
    ends_ref[0] = jnp.broadcast_to(first_c, ends_ref.shape[1:])
    ends_ref[1] = jnp.broadcast_to(last_c, ends_ref.shape[1:])


def sums_kernel(width, reach, me_ref, *refs):
    flag_refs, refs = refs[:3], refs[3:]
    apart_ref, inside_ref, chosen_ref, outside_ref, ends_ref = refs[:5]
    vis_hbm, wave_refs, mix_refs, refs = refs[5], refs[6:8], refs[8:10], refs[10:]
    out_refs, (vis_ref, alpha_s, mexp_s, wt_s, sems) = refs[:4], refs[4:]
    copies = [pltpu.make_async_copy(vis_hbm.at[:, t], vis_ref.at[:, t], sems.at[t]) for t in range(2)]
    copies[0].start()
    me = me_ref[0]
    place = lax.rem(me, reach)
    windows = inside_ref.shape[0]
    pairs = apart_ref.shape[3]
    sub, lane = iota((windows, windows), 0), iota((windows, windows), 1)
    first_c, last_c = ends_ref[0][:, :1], ends_ref[1][:, :1]
    apart = blocks_apart(me, reach, outside_ref.shape[0])
    diagonal = iota((width, width), 0) == iota((width, width), 1)
    wt_s[...] = jnp.zeros_like(wt_s)

    def both_sides(value):
        return (jnp.sum(jnp.where(apart < 0.0, value, 0.0), axis=0, keepdims=True),
                jnp.sum(jnp.where(apart > 0.0, value, 0.0), axis=0, keepdims=True))

    for t in range(2):
        mine = lax.div(me, reach)
        for group, other in enumerate((mine, lax.bitwise_xor(mine, 1), lax.bitwise_xor(mine, 3))):
            side = jnp.where(jnp.abs(other - mine) > 1, 3, other - mine + 1)
            for slot in range(reach):
                row = flag_refs[group][slot, t:t + 1, :].astype(F32)
                wt_s[t, pl.ds(side * reach + lax.bitwise_xor(place, slot), 1), :] = 1.0 - row
        own = 1.0 - flag_refs[0][0, t:t + 1, :].astype(F32)
        inside = inside_ref[...] * own
        outside = outside_ref[...] * wt_s[t]
        before, after = both_sides(jnp.sum(outside, axis=1, keepdims=True))
        count = jnp.sum(inside, axis=1, keepdims=True) + first_c * before + last_c * after
        scale = 1.0 / jnp.maximum(count, 1.0)
        rows = jnp.concatenate([inside, outside], axis=0).astype(BF16)
        scale_r = jnp.sum(jnp.where(sub == lane, scale, 0.0), axis=0, keepdims=True)
        own_c = jnp.sum(jnp.where(diagonal, own, 0.0), axis=1, keepdims=True)
        chosen = chosen_ref[...] * own_c
        alpha_s[t] = jnp.broadcast_to(jnp.sum(chosen * scale_r, axis=1, keepdims=True), (width, 128))
        chosen = chosen.astype(BF16)
        sums = [dot(rows, mix_refs[t][slot, 0]) + dot(rows, mix_refs[t][slot, 1]) for slot in range(2)]
        away = times((apart_ref[t, 0], apart_ref[t, 1]), tuple(value[windows:] for value in sums))
        for slot in range(2):
            before, after = both_sides(away[slot])
            total = sums[slot][:windows] + first_c * before + last_c * after
            high, low = split_two(total * (scale * scale))
            mexp_s[t, slot] = dot(chosen, high) + dot(chosen, low)

    for t in range(2):
        def main(lanes, count):
            def step(block, sums):
                rows = pl.ds(pl.multiple_of(block * 16, 16), 16)
                alpha = alpha_s[t, rows, :count]
                mr, mi = mexp_s[t, 0, rows, lanes], mexp_s[t, 1, rows, lanes]
                r0, i0 = wave_refs[t][0, 0, rows, lanes], wave_refs[t][0, 1, rows, lanes]
                r1, i1 = wave_refs[t][1, 0, rows, lanes], wave_refs[t][1, 1, rows, lanes]
                factors = []
                for fr, fi in (
                    (alpha * r0 - (mr * r1 + mi * i1), (mr * i1 - mi * r1) - alpha * i0),
                    (alpha * r1 - (mr * r0 - mi * i0), (mr * i0 + mi * r0) - alpha * i1),
                ):
                    factors.append((fr, fi - fr, fr + fi))
                new = []
                for k in range(4):
                    vr = vis_ref[0, t, k, rows, lanes].astype(F32)
                    vi = vis_ref[1, t, k, rows, lanes].astype(F32)
                    vs = vr + vi
                    for s in range(2):
                        for v, f in zip((vs, vr, vi), factors[s]):
                            product = v * f
                            new.append(sums[len(new)] + (product[:8] + product[8:]))
                return tuple(new)

            zero = jnp.zeros((8, count), F32)
            sums = lax.fori_loop(0, width // 16, step, (zero,) * 24, unroll=4)
            for s in range(2):
                owner = lax.bitwise_xor(lax.bitwise_and(me, 3), t + 2 * s)
                found = []
                for k in range(4):
                    one, two, three = sums[(k * 2 + s) * 3:(k * 2 + s) * 3 + 3]
                    found.append([jnp.sum(value, axis=0, keepdims=True) for value in (one - three, one + two)])
                for d in range(4):
                    @pl.when(owner == d)
                    def write():
                        for k in range(4):
                            for ri in range(2):
                                out_refs[d][k, ri:ri + 1, lanes] = found[k][ri]

        copies[t].wait()
        if t == 0:
            copies[1].start()
        tiles(pairs, main)


def station_hots(pairs):
    station, baseline = iota((ROWS, 1), 0), iota((1, pairs), 1)
    offset = station * (float(2 * STATIONS - 1) - station) * 0.5
    after = (station + 1.0) * (float(2 * STATIONS - 2) - station) * 0.5
    first = jnp.where((baseline >= offset) & (baseline < after), 1.0, 0.0)
    partner_of = baseline + 1.0 + jnp.sum(first * (station - offset), axis=0, keepdims=True)
    second = jnp.where(partner_of == station, 1.0, 0.0)
    return first.astype(BF16), second.astype(BF16)


def hots_kernel(hot_ref):
    hot_ref[0], hot_ref[1] = station_hots(hot_ref.shape[2])


def solve_kernel(window_count, me_ref, tracks_ref, hot_ref, *refs):
    parts, gain_ref = refs[:-1], refs[-1]
    me = me_ref[0]
    systems = gain_ref.shape[0]
    total = [part[...] for part in parts]
    while len(total) > 1:
        total = [total[i] + total[i + 1] for i in range(0, len(total), 2)]
    total = total[0]
    hot, other = hot_ref[0], hot_ref[1]
    nt = lambda left, right: lax.dot_general(
        left, right, (((1,), (1,)), ((), ())), preferred_element_type=F32)
    upper, lower = [], []
    for system in range(systems):
        for ri in range(2):
            for piece in split_two(total[system, ri:ri + 1]):
                upper.append(hot * piece)
                lower.append(other * piece)
    upper = nt(jnp.concatenate(upper, axis=0), other)
    lower = nt(jnp.concatenate(lower, axis=0), hot)
    cut = lambda value, i: value[i * ROWS:(i + 1) * ROWS]
    join = lambda value, i: cut(value, 2 * i) + cut(value, 2 * i + 1)
    live_r = jnp.where(iota((1, ROWS), 1) < float(STATIONS), 1.0, 0.0)
    live_c = jnp.where(iota((ROWS, 1), 0) < float(STATIONS), 1.0, 0.0)
    matrices = [(join(upper, 2 * i) + join(lower, 2 * i), join(upper, 2 * i + 1) - join(lower, 2 * i + 1))
                for i in range(systems)]
    states = [(live_r, 0.0 * live_r, live_c, 0.0 * live_c)] * systems
    for turn in range(GITERS):
        for system in range(systems):
            re, im = matrices[system]
            row_re, row_im, col_re, col_im = states[system]
            pull_cr = jnp.sum(re * row_re - im * row_im, axis=1, keepdims=True)
            pull_ci = jnp.sum(re * row_im + im * row_re, axis=1, keepdims=True)
            pull_rr = jnp.sum(re * col_re + im * col_im, axis=0, keepdims=True)
            pull_ri = jnp.sum(re * col_im - im * col_re, axis=0, keepdims=True)
            power_r = row_re * row_re + row_im * row_im
            power_c = col_re * col_re + col_im * col_im
            total = jnp.sum(power_c, axis=0, keepdims=True)
            inverse_r = 0.5 / (window_count * (total - power_r) + DAMPING)
            inverse_c = 0.5 / (window_count * (total - power_c) + DAMPING)
            states[system] = (0.5 * row_re + pull_rr * inverse_r, 0.5 * row_im + pull_ri * inverse_r,
                              0.5 * col_re + pull_cr * inverse_c, 0.5 * col_im + pull_ci * inverse_c)
    visible = tracks_ref[lax.bitwise_and(lax.div(me, 2), 1), lax.bitwise_and(me, 1)].astype(F32)
    gains = [state[ri] * visible for state in states for ri in range(2)]
    gains = jnp.concatenate(gains, axis=0)
    stacked = jnp.concatenate([piece.astype(F32) for piece in split_three(gains)], axis=0).astype(BF16)
    ends = []
    for table in (hot, other):
        wide = dot(stacked, table)
        ends.append((wide[:8] + wide[8:16]) + wide[16:])
    pairs = hot.shape[1]
    for system in range(systems):
        (lr, li), (rr, ri_) = [[end[2 * system + ri:2 * system + ri + 1] for ri in range(2)] for end in ends]
        gain_ref[system, 0:1, :pairs] = lr * rr + li * ri_
        gain_ref[system, 1:2, :pairs] = li * rr - lr * ri_
        gain_ref[system, :, GAINS_AT:] = gains[2 * system:2 * system + 2, :STATIONS]


def clean_kernel(width, me_ref, *refs):
    vis_ref, wave_refs, piece_refs = refs[0], refs[1:3], refs[3:7]
    out_hbm, gain_out_ref, out_s, model_s, sems = refs[7:]
    pairs = wave_refs[0].shape[3]
    mine = lax.bitwise_and(me_ref[0], 3)
    for d, piece in enumerate(piece_refs):
        owner = lax.bitwise_xor(mine, d)
        t, s = lax.bitwise_and(owner, 1), lax.div(owner, 2)
        for k in range(4):
            for ri in range(2):
                gain_out_ref[ri, s, t, k:k + 1, :] = piece[k, ri:ri + 1, GAINS_AT:]
            re, im = piece[k, 0:1, :pairs], piece[k, 1:2, :pairs]
            for slot, value in enumerate((re, im - re, re + im)):
                model_s[owner, 3 * k + slot:3 * k + slot + 1, :] = value

    def copy_out(t, index):
        rows = pl.ds(pl.multiple_of(index * CHUNK, CHUNK), CHUNK)
        return pltpu.make_async_copy(out_s.at[:, t, :, rows], out_hbm.at[:, t, :, rows], sems.at[t, index])

    chunks = width // CHUNK
    for t in range(2):
        def chunk(index, carry):
            def main(lanes, count):
                for block in range(CHUNK // 16):
                    rows = pl.ds(pl.multiple_of(index * CHUNK + block * 16, 16), 16)
                    waves = []
                    for s in range(2):
                        re, im = (wave_refs[t][s, ri, rows, lanes] for ri in range(2))
                        waves.append((re + im, re, im))
                    for k in range(4):
                        sums = []
                        for slot in range(3):
                            one, two = (waves[s][slot] * model_s[t + 2 * s, 3 * k + slot:3 * k + slot + 1, lanes]
                                        for s in range(2))
                            sums.append(one + two)
                        vr = vis_ref[0, t, k, rows, lanes].astype(F32)
                        vi = vis_ref[1, t, k, rows, lanes].astype(F32)
                        out_s[0, t, k, rows, lanes] = (vr - (sums[0] - sums[2])).astype(BF16)
                        out_s[1, t, k, rows, lanes] = (vi - (sums[0] + sums[1])).astype(BF16)

            tiles(pairs, main)
            copy_out(t, index).start()
            return carry

        lax.fori_loop(0, chunks, chunk, 0)
    for t in range(2):
        for index in range(chunks):
            copy_out(t, index).wait()


def partner(value, bits):
    count = lax.axis_size("sub")
    return lax.ppermute(value, "sub", [(i, i ^ bits) for i in range(count)])


def smem():
    return pl.BlockSpec(memory_space=pltpu.SMEM)


def local(visibilities, delays, flags, windows, tracks):
    width = visibilities.shape[4]
    pairs = visibilities.shape[3]
    count = lax.axis_size("sub")
    window_count = windows.shape[0]
    turned = jnp.transpose(visibilities, (0, 1, 2, 4, 3))
    me = lax.axis_index("sub").astype(jnp.int32).reshape(1)
    vmem_ref = pl.BlockSpec(memory_space=pltpu.VMEM)
    hbm_ref = pl.BlockSpec(memory_space=pltpu.HBM)
    vmem = lambda *shape: pltpu.VMEM(shape, F32)
    params = pltpu.CompilerParams(vmem_limit_bytes=24 * 2 ** 20)
    flags = flags[None]

    reach = count // 4
    remote_rows = 16 * pl.cdiv(4 * reach, 16)

    hots = pl.pallas_call(
        hots_kernel,
        out_specs=vmem_ref,
        out_shape=jax.ShapeDtypeStruct((2, ROWS, pairs), BF16),
        compiler_params=params,
        cost_estimate=pl.CostEstimate(flops=10 ** 7, bytes_accessed=6 * 2 ** 20, transcendentals=0),
        name="station_hots",
    )()
    made = []
    beside = [partner(flags, d) for d in range(1, 4)]
    for t in range(2):
        shape = lambda *dims: jax.ShapeDtypeStruct(dims, F32)
        out_shape = [
            shape(2, 2, width, pairs),
            jax.ShapeDtypeStruct((2, 2, width, pairs), BF16),
        ]
        if t == 0:
            operands = (me, delays, flags)
            out_shape += [jax.ShapeDtypeStruct(flags.shape, flags.dtype)]
        else:
            operands = (me, delays, windows.reshape(1, window_count))
            out_shape += [shape(2, 2, remote_rows, pairs), shape(window_count, width), shape(width, window_count),
                          shape(remote_rows, width), shape(2, window_count, 128)]
        made.append(pl.pallas_call(
            lambda *refs: phase_kernel(width, t, reach, *refs),
            in_specs=[smem()] + [vmem_ref] * (len(operands) - 1),
            out_specs=[vmem_ref] * len(out_shape),
            out_shape=out_shape,
            compiler_params=params,
            cost_estimate=pl.CostEstimate(flops=10 ** 7, bytes_accessed=6 * 2 ** 20, transcendentals=0),
            name="phases",
        )(*operands))
        if t == 0:
            gathered = jnp.concatenate([made[0][2]] + beside, axis=0)
            while gathered.shape[0] < reach:
                stride = gathered.shape[0]
                gathered = jnp.concatenate([gathered] + [partner(gathered, stride * d) for d in range(1, 4)], axis=0)
            gathered = [gathered] + [partner(gathered, d * reach) for d in (1, 3)]
    waves, mixing = ([part[i] for part in made] for i in range(2))
    masks = made[1][2:]
    *quarters, held = pl.pallas_call(
        lambda *refs: sums_kernel(width, reach, *refs),
        in_specs=[smem()] + [vmem_ref] * 8 + [hbm_ref] + [vmem_ref] * 4,
        out_specs=[vmem_ref] * 5,
        out_shape=[jax.ShapeDtypeStruct((4, 2, pairs), F32)] * 4 + [jax.ShapeDtypeStruct(turned.shape, BF16)],
        scratch_shapes=[vmem(2, width, 128), vmem(2, 2, width, pairs), vmem(2, remote_rows, width),
                        pltpu.SemaphoreType.DMA((2,))],
        compiler_params=pltpu.CompilerParams(vmem_limit_bytes=GRANT * 2 ** 20),
        name="window_sums",
    )(me, *gathered, *masks, turned, *waves, *mixing)
    pieces = [quarters[0]] + [partner(quarters[d], d) for d in range(1, 4)]
    stride = 4
    while stride < count:
        while len(pieces) > 1:
            pieces = [pieces[i] + pieces[i + 1] for i in range(0, len(pieces), 2)]
        pieces += [partner(pieces[0], stride * d) for d in range(1, min(4, count // stride))]
        stride *= 4
    model = pl.pallas_call(
        lambda *refs: solve_kernel(float(window_count), *refs),
        in_specs=[smem(), smem()] + [vmem_ref] * (1 + len(pieces)),
        out_specs=vmem_ref,
        out_shape=jax.ShapeDtypeStruct((4, 2, GAINS_AT + STATIONS), F32),
        compiler_params=params,
        name="gain_solve",
    )(me, tracks, hots, *pieces)
    model = [model] + [partner(model, d) for d in range(1, 4)]
    cleaned, gains = pl.pallas_call(
        lambda *refs: clean_kernel(width, *refs),
        in_specs=[smem()] + [vmem_ref] * 7,
        out_specs=[hbm_ref, vmem_ref],
        out_shape=[
            jax.ShapeDtypeStruct(turned.shape, BF16),
            jax.ShapeDtypeStruct((2, 2, 2, 4, STATIONS), F32),
        ],
        scratch_shapes=[
            pltpu.VMEM(turned.shape, BF16),
            vmem(4, 16, pairs),
            pltpu.SemaphoreType.DMA((2, width // CHUNK)),
        ],
        compiler_params=params,
        name="clean",
    )(me, held, *waves, *model)
    return jnp.transpose(cleaned, (0, 1, 2, 4, 3)), gains


def solution(mesh):
    return jax.shard_map(
        local,
        mesh=mesh,
        in_specs=(
            P(None, "obs", None, None, "sub"),
            P(None, "obs", None),
            P("obs", "sub"),
            P(),
            P(None, "obs"),
        ),
        out_specs=(P(None, "obs", None, None, "sub"), P(None, None, "obs", None, None)),
        check_vma=False,
    )
```

```python
import jax
import jax.numpy as jnp
import numpy as np
from jax import lax
from jax.experimental import pallas as pl
from jax.experimental.pallas import tpu as pltpu
from jax.sharding import PartitionSpec as P

STATIONS = 38
GITERS = 8
DAMPING = 1.0
STEPS_PER_TURN = 64
GAINS_AT = 768
CHUNK = 96
GRANT = 40
ROWS = 40

F32 = jnp.float32
BF16 = jnp.bfloat16


def iota(shape, dim):
    return lax.broadcasted_iota(jnp.int32, shape, dim).astype(F32)


def sincos_turns(turns):
    half = (turns - jnp.floor(turns + 0.5)) * np.float32(np.pi)
    sq = half * half
    sin = np.float32(-1.0 / 39916800)
    for term in (1.0 / 362880, -1.0 / 5040, 1.0 / 120, -1.0 / 6, 1.0):
        sin = sin * sq + np.float32(term)
    sin = sin * half
    cos = np.float32(1.0 / 479001600)
    for term in (-1.0 / 3628800, 1.0 / 40320, -1.0 / 720, 1.0 / 24, -0.5, 1.0):
        cos = cos * sq + np.float32(term)
    return 1.0 - 2.0 * (sin * sin), 2.0 * (sin * cos)


def split_two(value):
    high = value.astype(BF16)
    low = (value - high.astype(F32)).astype(BF16)
    return high, low


def split_three(value):
    high = value.astype(BF16)
    rest = value - high.astype(F32)
    mid = rest.astype(BF16)
    low = (rest - mid.astype(F32)).astype(BF16)
    return high, mid, low


def dot(left, right):
    return jnp.dot(left, right, preferred_element_type=F32)


def times(left, right):
    (lr, li), (rr, ri) = left, right
    return lr * rr - li * ri, lr * ri + li * rr


def phase_rows(delays, anchor, width):
    place = iota((8, 1), 0)
    second = place >= 4.0
    turns = jnp.where(second, delays[1], delays[0])
    at = anchor + float(STEPS_PER_TURN) * jnp.where(second, place - 4.0, place)
    base = sincos_turns(turns * (at * np.float32(1.0 / STEPS_PER_TURN)))
    fine, coarse = [], []
    for s in range(2):
        low = sincos_turns(delays[s] * (place * np.float32(1.0 / STEPS_PER_TURN)))
        high = low
        for doubling in range(3):
            high = times(high, high)
        rows = [times(tuple(part[4 * s + a:4 * s + a + 1] for part in base), high)
                for a in range(width // STEPS_PER_TURN)]
        fine.append(low)
        coarse.append(rows)
    return fine, coarse


def tiles(pairs, body):
    full = pairs // 128

    def step(tile, carry):
        body(pl.ds(pl.multiple_of(tile * 128, 128), 128), 128)
        return carry

    lax.fori_loop(0, full, step, 0)
    if pairs % 128:
        body(pl.ds(full * 128, pairs % 128), pairs % 128)


def phase_kernel(width, t, reach, me_ref, *refs):
    anchor = me_ref[0].astype(F32) * float(width)
    if t == 0:
        delay_ref, _, wave_ref, mix_ref = refs
    else:
        delay_ref, win_ref, wave_ref, mix_ref, apart_ref, *mask_refs = refs
    if t == 1:
        window_masks(width, reach, me_ref[0], win_ref, *mask_refs)
        apart = blocks_apart(me_ref[0], reach, apart_ref.shape[2])
        for time in range(2):
            gap = delay_ref[1, time:time + 1, :] - delay_ref[0, time:time + 1, :]
            phase = sincos_turns(gap * (apart * np.float32(width / STEPS_PER_TURN)))
            apart_ref[time, 0], apart_ref[time, 1] = phase
    pairs = delay_ref.shape[2]

    def waves(lanes, count):
        delays = [delay_ref[s, t:t + 1, lanes] for s in range(2)]
        fine, coarse = phase_rows(delays, anchor, width)
        for block in range(width // 16):
            found = []
            for s in range(2):
                halves = []
                for half in range(2):
                    a, b = divmod(2 * block + half, 8)
                    halves.append(times(tuple(part[b:b + 1] for part in coarse[s][a]), fine[s]))
                found.append([jnp.concatenate([h[ri] for h in halves], axis=0) for ri in range(2)])
            rows = slice(block * 16, block * 16 + 16)
            (r0, i0), (r1, i1) = found
            for s in range(2):
                for ri in range(2):
                    wave_ref[s, ri, rows, lanes] = found[s][ri]
            for slot, value in enumerate((r1 * r0 + i1 * i0, i1 * r0 - r1 * i0)):
                high, low = split_two(value)
                mix_ref[slot, 0, rows, lanes] = high
                mix_ref[slot, 1, rows, lanes] = low

    tiles(pairs, waves)


def blocks_apart(me, reach, rows):
    return iota((rows, 1), 0) - (lax.rem(me, reach) + reach).astype(F32)


def window_masks(width, reach, me, win_ref, inside_ref, chosen_ref, outside_ref, ends_ref):
    anchor = me.astype(F32) * float(width)
    lowest = (me - lax.rem(me, reach) - reach).astype(F32)
    windows = inside_ref.shape[0]
    final = anchor + float(width - 1)
    win_row = win_ref[...].astype(F32)
    sub, lane = iota((windows, windows), 0), iota((windows, windows), 1)
    end_c = jnp.sum(jnp.where(lane <= sub, win_row, 0.0), axis=1, keepdims=True)
    start_c = jnp.sum(jnp.where(lane < sub, win_row, 0.0), axis=1, keepdims=True)
    win_c = end_c - start_c
    end_r = jnp.sum(jnp.where(sub <= lane, win_c, 0.0), axis=0, keepdims=True)
    start_r = jnp.sum(jnp.where(sub < lane, win_c, 0.0), axis=0, keepdims=True)
    first_c = jnp.where((start_c <= anchor) & (anchor < end_c), 1.0, 0.0)
    last_c = jnp.where((start_c <= final) & (final < end_c), 1.0, 0.0)
    from_first = jnp.sum(first_c * start_c, axis=0, keepdims=True)
    to_last = jnp.sum(last_c * end_c, axis=0, keepdims=True)
    here = anchor + iota((windows, width), 1)
    inside_ref[...] = jnp.where((here >= start_c) & (here < end_c), 1.0, 0.0)
    there = anchor + iota((width, windows), 0)
    chosen_ref[...] = jnp.where((there >= start_r) & (there < end_r), 1.0, 0.0)
    shape = outside_ref.shape
    channel = (lowest + iota(shape, 0)) * float(width) + iota(shape, 1)
    remote = ((channel < anchor) & (channel >= from_first)) | ((channel > final) & (channel < to_last))
    outside_ref[...] = jnp.where(remote, 1.0, 0.0)
    ends_ref[0] = jnp.broadcast_to(first_c, ends_ref.shape[1:])
    ends_ref[1] = jnp.broadcast_to(last_c, ends_ref.shape[1:])


def sums_kernel(width, reach, me_ref, *refs):
    flag_refs, refs = refs[:3], refs[3:]
    apart_ref, inside_ref, chosen_ref, outside_ref, ends_ref = refs[:5]
    vis_hbm, wave_refs, mix_refs, refs = refs[5], refs[6:8], refs[8:10], refs[10:]
    out_refs, (vis_ref, alpha_s, mexp_s, wt_s, sems) = refs[:4], refs[4:]
    copies = [pltpu.make_async_copy(vis_hbm.at[:, t], vis_ref.at[:, t], sems.at[t]) for t in range(2)]
    copies[0].start()
    me = me_ref[0]
    place = lax.rem(me, reach)
    windows = inside_ref.shape[0]
    pairs = apart_ref.shape[3]
    sub, lane = iota((windows, windows), 0), iota((windows, windows), 1)
    first_c, last_c = ends_ref[0][:, :1], ends_ref[1][:, :1]
    apart = blocks_apart(me, reach, outside_ref.shape[0])
    diagonal = iota((width, width), 0) == iota((width, width), 1)
    wt_s[...] = jnp.zeros_like(wt_s)

    def both_sides(value):
        return (jnp.sum(jnp.where(apart < 0.0, value, 0.0), axis=0, keepdims=True),
                jnp.sum(jnp.where(apart > 0.0, value, 0.0), axis=0, keepdims=True))

    for t in range(2):
        mine = lax.div(me, reach)
        for group, other in enumerate((mine, lax.bitwise_xor(mine, 1), lax.bitwise_xor(mine, 3))):
            side = jnp.where(jnp.abs(other - mine) > 1, 3, other - mine + 1)
            for slot in range(reach):
                row = flag_refs[group][slot, t:t + 1, :].astype(F32)
                wt_s[t, pl.ds(side * reach + lax.bitwise_xor(place, slot), 1), :] = 1.0 - row
        own = 1.0 - flag_refs[0][0, t:t + 1, :].astype(F32)
        inside = inside_ref[...] * own
        outside = outside_ref[...] * wt_s[t]
        before, after = both_sides(jnp.sum(outside, axis=1, keepdims=True))
        count = jnp.sum(inside, axis=1, keepdims=True) + first_c * before + last_c * after
        scale = 1.0 / jnp.maximum(count, 1.0)
        rows = jnp.concatenate([inside, outside], axis=0).astype(BF16)
        scale_r = jnp.sum(jnp.where(sub == lane, scale, 0.0), axis=0, keepdims=True)
        own_c = jnp.sum(jnp.where(diagonal, own, 0.0), axis=1, keepdims=True)
        chosen = chosen_ref[...] * own_c
        alpha_s[t] = jnp.broadcast_to(jnp.sum(chosen * scale_r, axis=1, keepdims=True), (width, 128))
        chosen = chosen.astype(BF16)
        sums = [dot(rows, mix_refs[t][slot, 0]) + dot(rows, mix_refs[t][slot, 1]) for slot in range(2)]
        away = times((apart_ref[t, 0], apart_ref[t, 1]), tuple(value[windows:] for value in sums))
        for slot in range(2):
            before, after = both_sides(away[slot])
            total = sums[slot][:windows] + first_c * before + last_c * after
            high, low = split_two(total * (scale * scale))
            mexp_s[t, slot] = dot(chosen, high) + dot(chosen, low)

    for t in range(2):
        def main(lanes, count):
            def step(block, sums):
                rows = pl.ds(pl.multiple_of(block * 16, 16), 16)
                alpha = alpha_s[t, rows, :count]
                mr, mi = mexp_s[t, 0, rows, lanes], mexp_s[t, 1, rows, lanes]
                r0, i0 = wave_refs[t][0, 0, rows, lanes], wave_refs[t][0, 1, rows, lanes]
                r1, i1 = wave_refs[t][1, 0, rows, lanes], wave_refs[t][1, 1, rows, lanes]
                factors = []
                for fr, fi in (
                    (alpha * r0 - (mr * r1 + mi * i1), (mr * i1 - mi * r1) - alpha * i0),
                    (alpha * r1 - (mr * r0 - mi * i0), (mr * i0 + mi * r0) - alpha * i1),
                ):
                    factors.append((fr, fi - fr, fr + fi))
                new = []
                for k in range(4):
                    vr = vis_ref[0, t, k, rows, lanes].astype(F32)
                    vi = vis_ref[1, t, k, rows, lanes].astype(F32)
                    vs = vr + vi
                    for s in range(2):
                        for v, f in zip((vs, vr, vi), factors[s]):
                            product = v * f
                            new.append(sums[len(new)] + (product[:8] + product[8:]))
                return tuple(new)

            zero = jnp.zeros((8, count), F32)
            sums = lax.fori_loop(0, width // 16, step, (zero,) * 24, unroll=6)
            for s in range(2):
                owner = lax.bitwise_xor(lax.bitwise_and(me, 3), t + 2 * s)
                found = []
                for k in range(4):
                    one, two, three = sums[(k * 2 + s) * 3:(k * 2 + s) * 3 + 3]
                    found.append([jnp.sum(value, axis=0, keepdims=True) for value in (one - three, one + two)])
                for d in range(4):
                    @pl.when(owner == d)
                    def write():
                        for k in range(4):
                            for ri in range(2):
                                out_refs[d][k, ri:ri + 1, lanes] = found[k][ri]

        copies[t].wait()
        if t == 0:
            copies[1].start()
        tiles(pairs, main)


def station_hots(pairs):
    station, baseline = iota((ROWS, 1), 0), iota((1, pairs), 1)
    offset = station * (float(2 * STATIONS - 1) - station) * 0.5
    after = (station + 1.0) * (float(2 * STATIONS - 2) - station) * 0.5
    first = jnp.where((baseline >= offset) & (baseline < after), 1.0, 0.0)
    partner_of = baseline + 1.0 + jnp.sum(first * (station - offset), axis=0, keepdims=True)
    second = jnp.where(partner_of == station, 1.0, 0.0)
    return first.astype(BF16), second.astype(BF16)


def own_kernel(flag_ref, own_ref):
    own_ref[...] = flag_ref[...]


def hots_kernel(hot_ref):
    hot_ref[0], hot_ref[1] = station_hots(hot_ref.shape[2])


def solve_kernel(window_count, me_ref, tracks_ref, hot_ref, *refs):
    parts, gain_ref = refs[:-1], refs[-1]
    me = me_ref[0]
    systems = gain_ref.shape[0]
    total = [part[...] for part in parts]
    while len(total) > 1:
        total = [total[i] + total[i + 1] for i in range(0, len(total), 2)]
    total = total[0]
    hot, other = hot_ref[0], hot_ref[1]
    nt = lambda left, right: lax.dot_general(
        left, right, (((1,), (1,)), ((), ())), preferred_element_type=F32)
    upper, lower = [], []
    for system in range(systems):
        for ri in range(2):
            for piece in split_two(total[system, ri:ri + 1]):
                upper.append(hot * piece)
                lower.append(other * piece)
    upper = nt(jnp.concatenate(upper, axis=0), other)
    lower = nt(jnp.concatenate(lower, axis=0), hot)
    cut = lambda value, i: value[i * ROWS:(i + 1) * ROWS]
    join = lambda value, i: cut(value, 2 * i) + cut(value, 2 * i + 1)
    live_r = jnp.where(iota((1, ROWS), 1) < float(STATIONS), 1.0, 0.0)
    live_c = jnp.where(iota((ROWS, 1), 0) < float(STATIONS), 1.0, 0.0)
    matrices = [(join(upper, 2 * i) + join(lower, 2 * i), join(upper, 2 * i + 1) - join(lower, 2 * i + 1))
                for i in range(systems)]
    states = [(live_r, 0.0 * live_r, live_c, 0.0 * live_c)] * systems
    for turn in range(GITERS):
        for system in range(systems):
            re, im = matrices[system]
            row_re, row_im, col_re, col_im = states[system]
            pull_cr = jnp.sum(re * row_re - im * row_im, axis=1, keepdims=True)
            pull_ci = jnp.sum(re * row_im + im * row_re, axis=1, keepdims=True)
            pull_rr = jnp.sum(re * col_re + im * col_im, axis=0, keepdims=True)
            pull_ri = jnp.sum(re * col_im - im * col_re, axis=0, keepdims=True)
            power_r = row_re * row_re + row_im * row_im
            power_c = col_re * col_re + col_im * col_im
            total = jnp.sum(power_c, axis=0, keepdims=True)
            inverse_r = 0.5 / (window_count * (total - power_r) + DAMPING)
            inverse_c = 0.5 / (window_count * (total - power_c) + DAMPING)
            states[system] = (0.5 * row_re + pull_rr * inverse_r, 0.5 * row_im + pull_ri * inverse_r,
                              0.5 * col_re + pull_cr * inverse_c, 0.5 * col_im + pull_ci * inverse_c)
    visible = tracks_ref[lax.bitwise_and(lax.div(me, 2), 1), lax.bitwise_and(me, 1)].astype(F32)
    gains = [state[ri] * visible for state in states for ri in range(2)]
    gains = jnp.concatenate(gains, axis=0)
    stacked = jnp.concatenate([piece.astype(F32) for piece in split_three(gains)], axis=0).astype(BF16)
    ends = []
    for table in (hot, other):
        wide = dot(stacked, table)
        ends.append((wide[:8] + wide[8:16]) + wide[16:])
    pairs = hot.shape[1]
    for system in range(systems):
        (lr, li), (rr, ri_) = [[end[2 * system + ri:2 * system + ri + 1] for ri in range(2)] for end in ends]
        gain_ref[system, 0:1, :pairs] = lr * rr + li * ri_
        gain_ref[system, 1:2, :pairs] = li * rr - lr * ri_
        gain_ref[system, :, GAINS_AT:] = gains[2 * system:2 * system + 2, :STATIONS]


def clean_kernel(width, me_ref, *refs):
    vis_ref, wave_refs, piece_refs = refs[0], refs[1:3], refs[3:7]
    out_hbm, gain_out_ref, out_s, model_s, sems = refs[7:]
    pairs = wave_refs[0].shape[3]
    mine = lax.bitwise_and(me_ref[0], 3)
    for d, piece in enumerate(piece_refs):
        owner = lax.bitwise_xor(mine, d)
        t, s = lax.bitwise_and(owner, 1), lax.div(owner, 2)
        for k in range(4):
            for ri in range(2):
                gain_out_ref[ri, s, t, k:k + 1, :] = piece[k, ri:ri + 1, GAINS_AT:]
            re, im = piece[k, 0:1, :pairs], piece[k, 1:2, :pairs]
            for slot, value in enumerate((re, im - re, re + im)):
                model_s[owner, 3 * k + slot:3 * k + slot + 1, :] = value

    def copy_out(t, index):
        rows = pl.ds(pl.multiple_of(index * CHUNK, CHUNK), CHUNK)
        return pltpu.make_async_copy(out_s.at[:, t, :, rows], out_hbm.at[:, t, :, rows], sems.at[t, index])

    chunks = width // CHUNK
    for t in range(2):
        def chunk(index, carry):
            def main(lanes, count):
                for block in range(CHUNK // 16):
                    rows = pl.ds(pl.multiple_of(index * CHUNK + block * 16, 16), 16)
                    waves = []
                    for s in range(2):
                        re, im = (wave_refs[t][s, ri, rows, lanes] for ri in range(2))
                        waves.append((re + im, re, im))
                    for k in range(4):
                        sums = []
                        for slot in range(3):
                            one, two = (waves[s][slot] * model_s[t + 2 * s, 3 * k + slot:3 * k + slot + 1, lanes]
                                        for s in range(2))
                            sums.append(one + two)
                        vr = vis_ref[0, t, k, rows, lanes].astype(F32)
                        vi = vis_ref[1, t, k, rows, lanes].astype(F32)
                        out_s[0, t, k, rows, lanes] = (vr - (sums[0] - sums[2])).astype(BF16)
                        out_s[1, t, k, rows, lanes] = (vi - (sums[0] + sums[1])).astype(BF16)

            tiles(pairs, main)
            copy_out(t, index).start()
            return carry

        lax.fori_loop(0, chunks, chunk, 0)
    for t in range(2):
        for index in range(chunks):
            copy_out(t, index).wait()


def partner(value, bits):
    count = lax.axis_size("sub")
    return lax.ppermute(value, "sub", [(i, i ^ bits) for i in range(count)])


def smem():
    return pl.BlockSpec(memory_space=pltpu.SMEM)


def local(visibilities, delays, flags, windows, tracks):
    width = visibilities.shape[4]
    pairs = visibilities.shape[3]
    count = lax.axis_size("sub")
    window_count = windows.shape[0]
    turned = jnp.transpose(visibilities, (0, 1, 2, 4, 3))
    me = lax.axis_index("sub").astype(jnp.int32).reshape(1)
    vmem_ref = pl.BlockSpec(memory_space=pltpu.VMEM)
    hbm_ref = pl.BlockSpec(memory_space=pltpu.HBM)
    vmem = lambda *shape: pltpu.VMEM(shape, F32)
    params = pltpu.CompilerParams(vmem_limit_bytes=24 * 2 ** 20)
    flags = flags[None]

    reach = count // 4
    remote_rows = 16 * pl.cdiv(4 * reach, 16)

    cost = pl.CostEstimate(flops=10 ** 7, bytes_accessed=6 * 2 ** 20, transcendentals=0)
    hots = pl.pallas_call(
        hots_kernel,
        out_specs=vmem_ref,
        out_shape=jax.ShapeDtypeStruct((2, ROWS, pairs), BF16),
        compiler_params=params,
        cost_estimate=cost,
        name="station_hots",
    )()
    beside = [partner(flags, d) for d in range(1, 4)]
    own = pl.pallas_call(
        own_kernel,
        in_specs=[vmem_ref],
        out_specs=vmem_ref,
        out_shape=jax.ShapeDtypeStruct(flags.shape, flags.dtype),
        compiler_params=params,
        cost_estimate=cost,
        name="own_flags",
    )(flags)
    stack = jnp.concatenate([own] + beside, axis=0)
    while stack.shape[0] < reach:
        stride = stack.shape[0]
        stack = jnp.concatenate([stack] + [partner(stack, stride * d) for d in range(1, 4)], axis=0)
    gathered = [stack] + [partner(stack, d * reach) for d in (1, 3)]
    made = []
    for t in range(2):
        shape = lambda *dims: jax.ShapeDtypeStruct(dims, F32)
        out_shape = [shape(2, 2, width, pairs), jax.ShapeDtypeStruct((2, 2, width, pairs), BF16)]
        operands = (me, delays, windows.reshape(1, window_count) if t else stack)
        if t:
            out_shape += [shape(2, 2, remote_rows, pairs), shape(window_count, width), shape(width, window_count),
                          shape(remote_rows, width), shape(2, window_count, 128)]
        made.append(pl.pallas_call(
            lambda *refs: phase_kernel(width, t, reach, *refs),
            in_specs=[smem()] + [vmem_ref] * 2,
            out_specs=[vmem_ref] * len(out_shape),
            out_shape=out_shape,
            compiler_params=params,
            cost_estimate=cost,
            name="phases",
        )(*operands))
    waves, mixing = ([part[i] for part in made] for i in range(2))
    masks = made[1][2:]
    *quarters, held = pl.pallas_call(
        lambda *refs: sums_kernel(width, reach, *refs),
        in_specs=[smem()] + [vmem_ref] * 8 + [hbm_ref] + [vmem_ref] * 4,
        out_specs=[vmem_ref] * 5,
        out_shape=[jax.ShapeDtypeStruct((4, 2, pairs), F32)] * 4 + [jax.ShapeDtypeStruct(turned.shape, BF16)],
        scratch_shapes=[vmem(2, width, 128), vmem(2, 2, width, pairs), vmem(2, remote_rows, width),
                        pltpu.SemaphoreType.DMA((2,))],
        compiler_params=pltpu.CompilerParams(vmem_limit_bytes=GRANT * 2 ** 20),
        name="window_sums",
    )(me, *gathered, *masks, turned, *waves, *mixing)
    pieces = [quarters[0]] + [partner(quarters[d], d) for d in range(1, 4)]
    stride = 4
    while stride < count:
        while len(pieces) > 1:
            pieces = [pieces[i] + pieces[i + 1] for i in range(0, len(pieces), 2)]
        pieces += [partner(pieces[0], stride * d) for d in range(1, min(4, count // stride))]
        stride *= 4
    model = pl.pallas_call(
        lambda *refs: solve_kernel(float(window_count), *refs),
        in_specs=[smem(), smem()] + [vmem_ref] * (1 + len(pieces)),
        out_specs=vmem_ref,
        out_shape=jax.ShapeDtypeStruct((4, 2, GAINS_AT + STATIONS), F32),
        compiler_params=params,
        name="gain_solve",
    )(me, tracks, hots, *pieces)
    model = [model] + [partner(model, d) for d in range(1, 4)]
    cleaned, gains = pl.pallas_call(
        lambda *refs: clean_kernel(width, *refs),
        in_specs=[smem()] + [vmem_ref] * 7,
        out_specs=[hbm_ref, vmem_ref],
        out_shape=[
            jax.ShapeDtypeStruct(turned.shape, BF16),
            jax.ShapeDtypeStruct((2, 2, 2, 4, STATIONS), F32),
        ],
        scratch_shapes=[
            pltpu.VMEM(turned.shape, BF16),
            vmem(4, 16, pairs),
            pltpu.SemaphoreType.DMA((2, width // CHUNK)),
        ],
        compiler_params=params,
        name="clean",
    )(me, held, *waves, *model)
    return jnp.transpose(cleaned, (0, 1, 2, 4, 3)), gains


def solution(mesh):
    return jax.shard_map(
        local,
        mesh=mesh,
        in_specs=(
            P(None, "obs", None, None, "sub"),
            P(None, "obs", None),
            P("obs", "sub"),
            P(),
            P(None, "obs"),
        ),
        out_specs=(P(None, "obs", None, None, "sub"), P(None, None, "obs", None, None)),
        check_vma=False,
    )
```

```python
import jax
import jax.numpy as jnp
import numpy as np
from jax import lax
from jax.experimental import pallas as pl
from jax.experimental.pallas import tpu as pltpu
from jax.sharding import PartitionSpec as P

STATIONS = 38
GITERS = 8
DAMPING = 1.0
STEPS_PER_TURN = 64
GAINS_AT = 768
GRANT = 42
GRANTS = (50, 45)
ROWS = 40

F32 = jnp.float32
BF16 = jnp.bfloat16


def iota(shape, dim):
    return lax.broadcasted_iota(jnp.int32, shape, dim).astype(F32)


def sincos_turns(turns):
    half = (turns - jnp.floor(turns + 0.5)) * np.float32(np.pi)
    sq = half * half
    sin = np.float32(-1.0 / 39916800)
    for term in (1.0 / 362880, -1.0 / 5040, 1.0 / 120, -1.0 / 6, 1.0):
        sin = sin * sq + np.float32(term)
    sin = sin * half
    cos = np.float32(1.0 / 479001600)
    for term in (-1.0 / 3628800, 1.0 / 40320, -1.0 / 720, 1.0 / 24, -0.5, 1.0):
        cos = cos * sq + np.float32(term)
    return 1.0 - 2.0 * (sin * sin), 2.0 * (sin * cos)


def split_two(value):
    high = value.astype(BF16)
    low = (value - high.astype(F32)).astype(BF16)
    return high, low


def split_three(value):
    high = value.astype(BF16)
    rest = value - high.astype(F32)
    mid = rest.astype(BF16)
    low = (rest - mid.astype(F32)).astype(BF16)
    return high, mid, low


def dot(left, right):
    return jnp.dot(left, right, preferred_element_type=F32)


def times(left, right):
    (lr, li), (rr, ri) = left, right
    return lr * rr - li * ri, lr * ri + li * rr


def phase_rows(delays, anchor, width):
    place = iota((8, 1), 0)
    second = place >= 4.0
    turns = jnp.where(second, delays[1], delays[0])
    at = anchor + float(STEPS_PER_TURN) * jnp.where(second, place - 4.0, place)
    base = sincos_turns(turns * (at * np.float32(1.0 / STEPS_PER_TURN)))
    fine, coarse = [], []
    for s in range(2):
        low = sincos_turns(delays[s] * (place * np.float32(1.0 / STEPS_PER_TURN)))
        high = low
        for doubling in range(3):
            high = times(high, high)
        rows = [times(tuple(part[4 * s + a:4 * s + a + 1] for part in base), high)
                for a in range(width // STEPS_PER_TURN)]
        fine.append(low)
        coarse.append(rows)
    return fine, coarse


def tiles(pairs, body):
    full = pairs // 128

    def step(tile, carry):
        body(pl.ds(pl.multiple_of(tile * 128, 128), 128), 128)
        return carry

    lax.fori_loop(0, full, step, 0)
    if pairs % 128:
        body(pl.ds(full * 128, pairs % 128), pairs % 128)


def phase_kernel(width, t, reach, me_ref, *refs):
    anchor = me_ref[0].astype(F32) * float(width)
    if t == 0:
        delay_ref, flag_ref, wave_ref, mix_ref, own_ref = refs
    else:
        vis_hbm, delay_ref, win_ref, wave_ref, mix_ref, vis_ref, apart_ref, *mask_refs, sem = refs
        copy = pltpu.make_async_copy(vis_hbm.at[:, 0], vis_ref, sem)
        copy.start()
    if t == 0:
        own_ref[...] = flag_ref[...]
    else:
        window_masks(width, reach, me_ref[0], win_ref, *mask_refs)
        apart = blocks_apart(me_ref[0], reach, apart_ref.shape[2])
        for time in range(2):
            gap = delay_ref[1, time:time + 1, :] - delay_ref[0, time:time + 1, :]
            phase = sincos_turns(gap * (apart * np.float32(width / STEPS_PER_TURN)))
            apart_ref[time, 0], apart_ref[time, 1] = phase
    pairs = delay_ref.shape[2]

    def waves(lanes, count):
        delays = [delay_ref[s, t:t + 1, lanes] for s in range(2)]
        fine, coarse = phase_rows(delays, anchor, width)
        for block in range(width // 16):
            found = []
            for s in range(2):
                halves = []
                for half in range(2):
                    a, b = divmod(2 * block + half, 8)
                    halves.append(times(tuple(part[b:b + 1] for part in coarse[s][a]), fine[s]))
                found.append([jnp.concatenate([h[ri] for h in halves], axis=0) for ri in range(2)])
            rows = slice(block * 16, block * 16 + 16)
            (r0, i0), (r1, i1) = found
            for s in range(2):
                for ri in range(2):
                    wave_ref[s, ri, rows, lanes] = found[s][ri]
            for slot, value in enumerate((r1 * r0 + i1 * i0, i1 * r0 - r1 * i0)):
                high, low = split_two(value)
                mix_ref[slot, 0, rows, lanes] = high
                mix_ref[slot, 1, rows, lanes] = low

    tiles(pairs, waves)
    if t == 1:
        copy.wait()


def blocks_apart(me, reach, rows):
    return iota((rows, 1), 0) - (lax.rem(me, reach) + reach).astype(F32)


def window_masks(width, reach, me, win_ref, inside_ref, chosen_ref, outside_ref, ends_ref):
    anchor = me.astype(F32) * float(width)
    lowest = (me - lax.rem(me, reach) - reach).astype(F32)
    windows = inside_ref.shape[0]
    final = anchor + float(width - 1)
    win_row = win_ref[...].astype(F32)
    sub, lane = iota((windows, windows), 0), iota((windows, windows), 1)
    end_c = jnp.sum(jnp.where(lane <= sub, win_row, 0.0), axis=1, keepdims=True)
    start_c = jnp.sum(jnp.where(lane < sub, win_row, 0.0), axis=1, keepdims=True)
    win_c = end_c - start_c
    end_r = jnp.sum(jnp.where(sub <= lane, win_c, 0.0), axis=0, keepdims=True)
    start_r = jnp.sum(jnp.where(sub < lane, win_c, 0.0), axis=0, keepdims=True)
    first_c = jnp.where((start_c <= anchor) & (anchor < end_c), 1.0, 0.0)
    last_c = jnp.where((start_c <= final) & (final < end_c), 1.0, 0.0)
    from_first = jnp.sum(first_c * start_c, axis=0, keepdims=True)
    to_last = jnp.sum(last_c * end_c, axis=0, keepdims=True)
    here = anchor + iota((windows, width), 1)
    inside_ref[...] = jnp.where((here >= start_c) & (here < end_c), 1.0, 0.0)
    there = anchor + iota((width, windows), 0)
    chosen_ref[...] = jnp.where((there >= start_r) & (there < end_r), 1.0, 0.0)
    shape = outside_ref.shape
    channel = (lowest + iota(shape, 0)) * float(width) + iota(shape, 1)
    remote = ((channel < anchor) & (channel >= from_first)) | ((channel > final) & (channel < to_last))
    outside_ref[...] = jnp.where(remote, 1.0, 0.0)
    ends_ref[0] = jnp.broadcast_to(first_c, ends_ref.shape[1:])
    ends_ref[1] = jnp.broadcast_to(last_c, ends_ref.shape[1:])


def sums_kernel(width, reach, me_ref, *refs):
    flag_refs, refs = refs[:3], refs[3:]
    apart_ref, inside_ref, chosen_ref, outside_ref, ends_ref = refs[:5]
    vis_hbm, first_ref, wave_refs, mix_refs, refs = refs[5], refs[6], refs[7:9], refs[9:11], refs[11:]
    out_refs, (second_ref, alpha_s, mexp_s, wt_s, sem) = refs[:4], refs[4:]
    vis_refs = (first_ref, second_ref)
    copy = pltpu.make_async_copy(vis_hbm.at[:, 1], second_ref, sem)
    copy.start()
    me = me_ref[0]
    place = lax.rem(me, reach)
    windows = inside_ref.shape[0]
    pairs = apart_ref.shape[3]
    sub, lane = iota((windows, windows), 0), iota((windows, windows), 1)
    first_c, last_c = ends_ref[0][:, :1], ends_ref[1][:, :1]
    apart = blocks_apart(me, reach, outside_ref.shape[0])
    diagonal = iota((width, width), 0) == iota((width, width), 1)
    wt_s[...] = jnp.zeros_like(wt_s)

    def both_sides(value):
        return (jnp.sum(jnp.where(apart < 0.0, value, 0.0), axis=0, keepdims=True),
                jnp.sum(jnp.where(apart > 0.0, value, 0.0), axis=0, keepdims=True))

    for t in range(2):
        mine = lax.div(me, reach)
        for group, other in enumerate((mine, lax.bitwise_xor(mine, 1), lax.bitwise_xor(mine, 3))):
            side = jnp.where(jnp.abs(other - mine) > 1, 3, other - mine + 1)
            for slot in range(reach):
                row = flag_refs[group][slot, t:t + 1, :].astype(F32)
                wt_s[t, pl.ds(side * reach + lax.bitwise_xor(place, slot), 1), :] = 1.0 - row
        own = 1.0 - flag_refs[0][0, t:t + 1, :].astype(F32)
        inside = inside_ref[...] * own
        outside = outside_ref[...] * wt_s[t]
        before, after = both_sides(jnp.sum(outside, axis=1, keepdims=True))
        count = jnp.sum(inside, axis=1, keepdims=True) + first_c * before + last_c * after
        scale = 1.0 / jnp.maximum(count, 1.0)
        rows = jnp.concatenate([inside, outside], axis=0).astype(BF16)
        scale_r = jnp.sum(jnp.where(sub == lane, scale, 0.0), axis=0, keepdims=True)
        own_c = jnp.sum(jnp.where(diagonal, own, 0.0), axis=1, keepdims=True)
        chosen = chosen_ref[...] * own_c
        alpha_s[t] = jnp.broadcast_to(jnp.sum(chosen * scale_r, axis=1, keepdims=True), (width, 128))
        chosen = chosen.astype(BF16)
        sums = [dot(rows, mix_refs[t][slot, 0]) + dot(rows, mix_refs[t][slot, 1]) for slot in range(2)]
        away = times((apart_ref[t, 0], apart_ref[t, 1]), tuple(value[windows:] for value in sums))
        for slot in range(2):
            before, after = both_sides(away[slot])
            total = sums[slot][:windows] + first_c * before + last_c * after
            high, low = split_two(total * (scale * scale))
            mexp_s[t, slot] = dot(chosen, high) + dot(chosen, low)

    for t in range(2):
        def main(lanes, count):
            def step(block, sums):
                rows = pl.ds(pl.multiple_of(block * 16, 16), 16)
                alpha = alpha_s[t, rows, :count]
                mr, mi = mexp_s[t, 0, rows, lanes], mexp_s[t, 1, rows, lanes]
                r0, i0 = wave_refs[t][0, 0, rows, lanes], wave_refs[t][0, 1, rows, lanes]
                r1, i1 = wave_refs[t][1, 0, rows, lanes], wave_refs[t][1, 1, rows, lanes]
                factors = []
                for fr, fi in (
                    (alpha * r0 - (mr * r1 + mi * i1), (mr * i1 - mi * r1) - alpha * i0),
                    (alpha * r1 - (mr * r0 - mi * i0), (mr * i0 + mi * r0) - alpha * i1),
                ):
                    factors.append((fr, fi - fr, fr + fi))
                new = []
                for k in range(4):
                    vr = vis_refs[t][0, k, rows, lanes].astype(F32)
                    vi = vis_refs[t][1, k, rows, lanes].astype(F32)
                    vs = vr + vi
                    for s in range(2):
                        for v, f in zip((vs, vr, vi), factors[s]):
                            product = v * f
                            new.append(sums[len(new)] + (product[:8] + product[8:]))
                return tuple(new)

            zero = jnp.zeros((8, count), F32)
            sums = lax.fori_loop(0, width // 16, step, (zero,) * 24, unroll=6)
            for s in range(2):
                owner = lax.bitwise_xor(lax.bitwise_and(me, 3), t + 2 * s)
                found = []
                for k in range(4):
                    one, two, three = sums[(k * 2 + s) * 3:(k * 2 + s) * 3 + 3]
                    found.append([jnp.sum(value, axis=0, keepdims=True) for value in (one - three, one + two)])
                for d in range(4):
                    @pl.when(owner == d)
                    def write():
                        for k in range(4):
                            for ri in range(2):
                                out_refs[d][k, ri:ri + 1, lanes] = found[k][ri]

        if t == 1:
            copy.wait()
        tiles(pairs, main)


def station_hots(pairs):
    station, baseline = iota((ROWS, 1), 0), iota((1, pairs), 1)
    offset = station * (float(2 * STATIONS - 1) - station) * 0.5
    after = (station + 1.0) * (float(2 * STATIONS - 2) - station) * 0.5
    first = jnp.where((baseline >= offset) & (baseline < after), 1.0, 0.0)
    partner_of = baseline + 1.0 + jnp.sum(first * (station - offset), axis=0, keepdims=True)
    second = jnp.where(partner_of == station, 1.0, 0.0)
    return first.astype(BF16), second.astype(BF16)


def hots_kernel(hot_ref):
    hot_ref[0], hot_ref[1] = station_hots(hot_ref.shape[2])


def solve_kernel(window_count, me_ref, tracks_ref, hot_ref, *refs):
    parts, gain_ref = refs[:-1], refs[-1]
    me = me_ref[0]
    systems = gain_ref.shape[0]
    total = [part[...] for part in parts]
    while len(total) > 1:
        total = [total[i] + total[i + 1] for i in range(0, len(total), 2)]
    total = total[0]
    hot, other = hot_ref[0], hot_ref[1]
    nt = lambda left, right: lax.dot_general(
        left, right, (((1,), (1,)), ((), ())), preferred_element_type=F32)
    upper, lower = [], []
    for system in range(systems):
        for ri in range(2):
            for piece in split_two(total[system, ri:ri + 1]):
                upper.append(hot * piece)
                lower.append(other * piece)
    upper = nt(jnp.concatenate(upper, axis=0), other)
    lower = nt(jnp.concatenate(lower, axis=0), hot)
    cut = lambda value, i: value[i * ROWS:(i + 1) * ROWS]
    join = lambda value, i: cut(value, 2 * i) + cut(value, 2 * i + 1)
    live_r = jnp.where(iota((1, ROWS), 1) < float(STATIONS), 1.0, 0.0)
    live_c = jnp.where(iota((ROWS, 1), 0) < float(STATIONS), 1.0, 0.0)
    matrices = [(join(upper, 2 * i) + join(lower, 2 * i), join(upper, 2 * i + 1) - join(lower, 2 * i + 1))
                for i in range(systems)]
    states = [(live_r, 0.0 * live_r, live_c, 0.0 * live_c)] * systems
    for turn in range(GITERS):
        for system in range(systems):
            re, im = matrices[system]
            row_re, row_im, col_re, col_im = states[system]
            pull_cr = jnp.sum(re * row_re - im * row_im, axis=1, keepdims=True)
            pull_ci = jnp.sum(re * row_im + im * row_re, axis=1, keepdims=True)
            pull_rr = jnp.sum(re * col_re + im * col_im, axis=0, keepdims=True)
            pull_ri = jnp.sum(re * col_im - im * col_re, axis=0, keepdims=True)
            power_r = row_re * row_re + row_im * row_im
            power_c = col_re * col_re + col_im * col_im
            total = jnp.sum(power_c, axis=0, keepdims=True)
            inverse_r = 0.5 / (window_count * (total - power_r) + DAMPING)
            inverse_c = 0.5 / (window_count * (total - power_c) + DAMPING)
            states[system] = (0.5 * row_re + pull_rr * inverse_r, 0.5 * row_im + pull_ri * inverse_r,
                              0.5 * col_re + pull_cr * inverse_c, 0.5 * col_im + pull_ci * inverse_c)
    visible = tracks_ref[lax.bitwise_and(lax.div(me, 2), 1), lax.bitwise_and(me, 1)].astype(F32)
    gains = [state[ri] * visible for state in states for ri in range(2)]
    gains = jnp.concatenate(gains, axis=0)
    stacked = jnp.concatenate([piece.astype(F32) for piece in split_three(gains)], axis=0).astype(BF16)
    ends = []
    for table in (hot, other):
        wide = dot(stacked, table)
        ends.append((wide[:8] + wide[8:16]) + wide[16:])
    pairs = hot.shape[1]
    for system in range(systems):
        (lr, li), (rr, ri_) = [[end[2 * system + ri:2 * system + ri + 1] for ri in range(2)] for end in ends]
        gain_ref[system, 0:1, :pairs] = lr * rr + li * ri_
        gain_ref[system, 1:2, :pairs] = li * rr - lr * ri_
        gain_ref[system, :, GAINS_AT:] = gains[2 * system:2 * system + 2, :STATIONS]


def clean_kernel(width, me_ref, *refs):
    vis_refs, wave_refs, piece_refs = refs[:2], refs[2:4], refs[4:8]
    out_hbm, gain_out_ref, out_s, model_s, sems = refs[8:]
    pairs = wave_refs[0].shape[3]
    mine = lax.bitwise_and(me_ref[0], 3)
    for d, piece in enumerate(piece_refs):
        owner = lax.bitwise_xor(mine, d)
        t, s = lax.bitwise_and(owner, 1), lax.div(owner, 2)
        for k in range(4):
            for ri in range(2):
                gain_out_ref[ri, s, t, k:k + 1, :] = piece[k, ri:ri + 1, GAINS_AT:]
            re, im = piece[k, 0:1, :pairs], piece[k, 1:2, :pairs]
            for slot, value in enumerate((re, im - re, re + im)):
                model_s[owner, 3 * k + slot:3 * k + slot + 1, :] = value

    half = width // 32 * 16
    quarter = half // 32 * 16
    pieces = [(0, 0, half), (0, half, width - half),
              (1, 0, half), (1, half, half - quarter), (1, 2 * half - quarter, width - 2 * half + quarter)]
    copies = []
    for t, start, length in pieces:
        def main(lanes, count):
            for block in range(length // 16):
                rows = slice(start + block * 16, start + block * 16 + 16)
                waves = []
                for s in range(2):
                    re, im = (wave_refs[t][s, ri, rows, lanes] for ri in range(2))
                    waves.append((re + im, re, im))
                for k in range(4):
                    sums = []
                    for slot in range(3):
                        one, two = (waves[s][slot] * model_s[t + 2 * s, 3 * k + slot:3 * k + slot + 1, lanes]
                                    for s in range(2))
                        sums.append(one + two)
                    vr = vis_refs[t][0, k, rows, lanes].astype(F32)
                    vi = vis_refs[t][1, k, rows, lanes].astype(F32)
                    out_s[0, t, k, rows, lanes] = (vr - (sums[0] - sums[2])).astype(BF16)
                    out_s[1, t, k, rows, lanes] = (vi - (sums[0] + sums[1])).astype(BF16)

        tiles(pairs, main)
        rows = pl.ds(start, length)
        copies.append(pltpu.make_async_copy(
            out_s.at[:, t, :, rows], out_hbm.at[:, t, :, rows], sems.at[len(copies)]))
        copies[-1].start()
    for copy in copies:
        copy.wait()


def partner(value, bits):
    count = lax.axis_size("sub")
    return lax.ppermute(value, "sub", [(i, i ^ bits) for i in range(count)])


def smem():
    return pl.BlockSpec(memory_space=pltpu.SMEM)


def local(visibilities, delays, flags, windows, tracks):
    width = visibilities.shape[4]
    pairs = visibilities.shape[3]
    count = lax.axis_size("sub")
    window_count = windows.shape[0]
    turned = jnp.transpose(visibilities, (0, 1, 2, 4, 3))
    me = lax.axis_index("sub").astype(jnp.int32).reshape(1)
    vmem_ref = pl.BlockSpec(memory_space=pltpu.VMEM)
    hbm_ref = pl.BlockSpec(memory_space=pltpu.HBM)
    vmem = lambda *shape: pltpu.VMEM(shape, F32)
    params = pltpu.CompilerParams(vmem_limit_bytes=24 * 2 ** 20)
    flags = flags[None]

    reach = count // 4
    remote_rows = 16 * pl.cdiv(4 * reach, 16)

    hots = pl.pallas_call(
        hots_kernel,
        out_specs=vmem_ref,
        out_shape=jax.ShapeDtypeStruct((2, ROWS, pairs), BF16),
        compiler_params=params,
        cost_estimate=pl.CostEstimate(flops=10 ** 7, bytes_accessed=6 * 2 ** 20, transcendentals=0),
        name="station_hots",
    )()
    made = []
    beside = [partner(flags, d) for d in range(1, 4)]
    for t in range(2):
        shape = lambda *dims: jax.ShapeDtypeStruct(dims, F32)
        out_shape = [
            shape(2, 2, width, pairs),
            jax.ShapeDtypeStruct((2, 2, width, pairs), BF16),
        ]
        if t == 0:
            operands = (me, delays, flags)
            in_specs = [smem()] + [vmem_ref] * 2
            out_shape += [jax.ShapeDtypeStruct(flags.shape, flags.dtype)]
        else:
            operands = (me, turned, delays, windows.reshape(1, window_count))
            in_specs = [smem(), hbm_ref] + [vmem_ref] * 2
            out_shape += [jax.ShapeDtypeStruct((2, 4, width, pairs), BF16),
                          shape(2, 2, remote_rows, pairs), shape(window_count, width), shape(width, window_count),
                          shape(remote_rows, width), shape(2, window_count, 128)]
        made.append(pl.pallas_call(
            lambda *refs: phase_kernel(width, t, reach, *refs),
            in_specs=in_specs,
            out_specs=[vmem_ref] * len(out_shape),
            out_shape=out_shape,
            scratch_shapes=[pltpu.SemaphoreType.DMA] * t,
            compiler_params=pltpu.CompilerParams(vmem_limit_bytes=GRANTS[t] * 2 ** 20),
            cost_estimate=pl.CostEstimate(flops=10 ** 7, bytes_accessed=6 * 2 ** 20, transcendentals=0),
            name="phases",
        )(*operands))
        if t == 0:
            gathered = jnp.concatenate([made[0][2]] + beside, axis=0)
            while gathered.shape[0] < reach:
                stride = gathered.shape[0]
                gathered = jnp.concatenate([gathered] + [partner(gathered, stride * d) for d in range(1, 4)], axis=0)
            gathered = [gathered] + [partner(gathered, d * reach) for d in (1, 3)]
    waves, mixing = ([part[i] for part in made] for i in range(2))
    held, *masks = made[1][2:]
    *quarters, held_too = pl.pallas_call(
        lambda *refs: sums_kernel(width, reach, *refs),
        in_specs=[smem()] + [vmem_ref] * 8 + [hbm_ref] + [vmem_ref] * 5,
        out_specs=[vmem_ref] * 5,
        out_shape=[jax.ShapeDtypeStruct((4, 2, pairs), F32)] * 4 + [jax.ShapeDtypeStruct(held.shape, BF16)],
        scratch_shapes=[vmem(2, width, 128), vmem(2, 2, width, pairs), vmem(2, remote_rows, width),
                        pltpu.SemaphoreType.DMA],
        compiler_params=pltpu.CompilerParams(vmem_limit_bytes=GRANT * 2 ** 20),
        name="window_sums",
    )(me, *gathered, *masks, turned, held, *waves, *mixing)
    pieces = [quarters[0]] + [partner(quarters[d], d) for d in range(1, 4)]
    stride = 4
    while stride < count:
        while len(pieces) > 1:
            pieces = [pieces[i] + pieces[i + 1] for i in range(0, len(pieces), 2)]
        pieces += [partner(pieces[0], stride * d) for d in range(1, min(4, count // stride))]
        stride *= 4
    model = pl.pallas_call(
        lambda *refs: solve_kernel(float(window_count), *refs),
        in_specs=[smem(), smem()] + [vmem_ref] * (1 + len(pieces)),
        out_specs=vmem_ref,
        out_shape=jax.ShapeDtypeStruct((4, 2, GAINS_AT + STATIONS), F32),
        compiler_params=params,
        name="gain_solve",
    )(me, tracks, hots, *pieces)
    model = [model] + [partner(model, d) for d in range(1, 4)]
    cleaned, gains = pl.pallas_call(
        lambda *refs: clean_kernel(width, *refs),
        in_specs=[smem()] + [vmem_ref] * 8,
        out_specs=[hbm_ref, vmem_ref],
        out_shape=[
            jax.ShapeDtypeStruct(turned.shape, BF16),
            jax.ShapeDtypeStruct((2, 2, 2, 4, STATIONS), F32),
        ],
        scratch_shapes=[
            pltpu.VMEM(turned.shape, BF16),
            vmem(4, 16, pairs),
            pltpu.SemaphoreType.DMA((5,)),
        ],
        compiler_params=params,
        name="clean",
    )(me, held, held_too, *waves, *model)
    return jnp.transpose(cleaned, (0, 1, 2, 4, 3)), gains


def solution(mesh):
    return jax.shard_map(
        local,
        mesh=mesh,
        in_specs=(
            P(None, "obs", None, None, "sub"),
            P(None, "obs", None),
            P("obs", "sub"),
            P(),
            P(None, "obs"),
        ),
        out_specs=(P(None, "obs", None, None, "sub"), P(None, None, "obs", None, None)),
        check_vma=False,
    )
```

```python
import jax
import jax.numpy as jnp
import numpy as np
from jax import lax
from jax.experimental import pallas as pl
from jax.experimental.pallas import tpu as pltpu
from jax.sharding import PartitionSpec as P

STATIONS = 38
GITERS = 8
DAMPING = 1.0
STEPS_PER_TURN = 64
GAINS_AT = 768
GRANT = 42
GRANTS = (47, 45)
ROWS = 48

F32 = jnp.float32
BF16 = jnp.bfloat16


def iota(shape, dim):
    return lax.broadcasted_iota(jnp.int32, shape, dim).astype(F32)


def sincos_turns(turns):
    half = (turns - jnp.floor(turns + 0.5)) * np.float32(np.pi)
    sq = half * half
    sin = np.float32(-1.0 / 39916800)
    for term in (1.0 / 362880, -1.0 / 5040, 1.0 / 120, -1.0 / 6, 1.0):
        sin = sin * sq + np.float32(term)
    sin = sin * half
    cos = np.float32(1.0 / 479001600)
    for term in (-1.0 / 3628800, 1.0 / 40320, -1.0 / 720, 1.0 / 24, -0.5, 1.0):
        cos = cos * sq + np.float32(term)
    return 1.0 - 2.0 * (sin * sin), 2.0 * (sin * cos)


def split_two(value):
    high = value.astype(BF16)
    low = (value - high.astype(F32)).astype(BF16)
    return high, low


def split_three(value):
    high = value.astype(BF16)
    rest = value - high.astype(F32)
    mid = rest.astype(BF16)
    low = (rest - mid.astype(F32)).astype(BF16)
    return high, mid, low


def dot(left, right):
    return jnp.dot(left, right, preferred_element_type=F32)


def times(left, right):
    (lr, li), (rr, ri) = left, right
    return lr * rr - li * ri, lr * ri + li * rr


def phase_rows(delays, anchor, width):
    place = iota((8, 1), 0)
    second = place >= 4.0
    turns = jnp.where(second, delays[1], delays[0])
    at = anchor + float(STEPS_PER_TURN) * jnp.where(second, place - 4.0, place)
    base = sincos_turns(turns * (at * np.float32(1.0 / STEPS_PER_TURN)))
    fine, coarse = [], []
    for s in range(2):
        low = sincos_turns(delays[s] * (place * np.float32(1.0 / STEPS_PER_TURN)))
        high = low
        for doubling in range(3):
            high = times(high, high)
        rows = [times(tuple(part[4 * s + a:4 * s + a + 1] for part in base), high)
                for a in range(width // STEPS_PER_TURN)]
        fine.append(low)
        coarse.append(rows)
    return fine, coarse


def visibility(vis_refs, ri, t, k, rows, lanes):
    ref, at = (vis_refs[2], k) if t else (vis_refs[k // 2], k % 2)
    return ref[ri, at, rows, lanes].astype(F32)


def tiles(pairs, body):
    full = pairs // 128

    def step(tile, carry):
        body(pl.ds(pl.multiple_of(tile * 128, 128), 128), 128)
        return carry

    lax.fori_loop(0, full, step, 0)
    if pairs % 128:
        body(pl.ds(full * 128, pairs % 128), pairs % 128)


def phase_kernel(width, t, reach, me_ref, *refs):
    anchor = me_ref[0].astype(F32) * float(width)
    if t == 0:
        vis_hbm, delay_ref, flag_ref, win_ref, wave_ref, mix_ref, vis_ref, own_ref, win_out_ref, sem = refs
    else:
        vis_hbm, delay_ref, win_ref, wave_ref, mix_ref, vis_ref, apart_ref, *mask_refs, sem = refs
    copy = pltpu.make_async_copy(vis_hbm.at[:, 0, 2 * t:2 * t + 2], vis_ref, sem)
    copy.start()
    if t == 0:
        own_ref[...] = flag_ref[...]
        win_out_ref[...] = win_ref[...]
    else:
        window_masks(width, reach, me_ref[0], win_ref, *mask_refs)
        apart = blocks_apart(me_ref[0], reach, apart_ref.shape[2])
        for time in range(2):
            gap = delay_ref[1, time:time + 1, :] - delay_ref[0, time:time + 1, :]
            phase = sincos_turns(gap * (apart * np.float32(width / STEPS_PER_TURN)))
            apart_ref[time, 0], apart_ref[time, 1] = phase
    pairs = delay_ref.shape[2]

    def waves(lanes, count):
        delays = [delay_ref[s, t:t + 1, lanes] for s in range(2)]
        fine, coarse = phase_rows(delays, anchor, width)
        for block in range(width // 16):
            found = []
            for s in range(2):
                halves = []
                for half in range(2):
                    a, b = divmod(2 * block + half, 8)
                    halves.append(times(tuple(part[b:b + 1] for part in coarse[s][a]), fine[s]))
                found.append([jnp.concatenate([h[ri] for h in halves], axis=0) for ri in range(2)])
            rows = slice(block * 16, block * 16 + 16)
            (r0, i0), (r1, i1) = found
            for s in range(2):
                for ri in range(2):
                    wave_ref[s, ri, rows, lanes] = found[s][ri]
            for slot, value in enumerate((r1 * r0 + i1 * i0, i1 * r0 - r1 * i0)):
                high, low = split_two(value)
                mix_ref[slot, 0, rows, lanes] = high
                mix_ref[slot, 1, rows, lanes] = low

    tiles(pairs, waves)
    copy.wait()


def blocks_apart(me, reach, rows):
    return iota((rows, 1), 0) - (lax.rem(me, reach) + reach).astype(F32)


def window_masks(width, reach, me, win_ref, inside_ref, chosen_ref, outside_ref, ends_ref):
    anchor = me.astype(F32) * float(width)
    lowest = (me - lax.rem(me, reach) - reach).astype(F32)
    windows = inside_ref.shape[0]
    final = anchor + float(width - 1)
    win_row = win_ref[...].astype(F32)
    sub, lane = iota((windows, windows), 0), iota((windows, windows), 1)
    end_c = jnp.sum(jnp.where(lane <= sub, win_row, 0.0), axis=1, keepdims=True)
    start_c = jnp.sum(jnp.where(lane < sub, win_row, 0.0), axis=1, keepdims=True)
    win_c = end_c - start_c
    end_r = jnp.sum(jnp.where(sub <= lane, win_c, 0.0), axis=0, keepdims=True)
    start_r = jnp.sum(jnp.where(sub < lane, win_c, 0.0), axis=0, keepdims=True)
    first_c = jnp.where((start_c <= anchor) & (anchor < end_c), 1.0, 0.0)
    last_c = jnp.where((start_c <= final) & (final < end_c), 1.0, 0.0)
    from_first = jnp.sum(first_c * start_c, axis=0, keepdims=True)
    to_last = jnp.sum(last_c * end_c, axis=0, keepdims=True)
    here = anchor + iota((windows, width), 1)
    inside_ref[...] = jnp.where((here >= start_c) & (here < end_c), 1.0, 0.0)
    there = anchor + iota((width, windows), 0)
    chosen_ref[...] = jnp.where((there >= start_r) & (there < end_r), 1.0, 0.0)
    shape = outside_ref.shape
    channel = (lowest + iota(shape, 0)) * float(width) + iota(shape, 1)
    remote = ((channel < anchor) & (channel >= from_first)) | ((channel > final) & (channel < to_last))
    outside_ref[...] = jnp.where(remote, 1.0, 0.0)
    ends_ref[0] = jnp.broadcast_to(first_c, ends_ref.shape[1:])
    ends_ref[1] = jnp.broadcast_to(last_c, ends_ref.shape[1:])


def sums_kernel(width, reach, me_ref, *refs):
    flag_refs, refs = refs[:3], refs[3:]
    apart_ref, inside_ref, chosen_ref, outside_ref, ends_ref = refs[:5]
    vis_hbm, first_refs, wave_refs, mix_refs, refs = refs[5], refs[6:8], refs[8:10], refs[10:12], refs[12:]
    out_refs, (second_ref, alpha_s, mexp_s, wt_s, sem) = refs[:4], refs[4:]
    vis_refs = (*first_refs, second_ref)
    copy = pltpu.make_async_copy(vis_hbm.at[:, 1], second_ref, sem)
    copy.start()
    me = me_ref[0]
    place = lax.rem(me, reach)
    windows = inside_ref.shape[0]
    pairs = apart_ref.shape[3]
    sub, lane = iota((windows, windows), 0), iota((windows, windows), 1)
    first_c, last_c = ends_ref[0][:, :1], ends_ref[1][:, :1]
    apart = blocks_apart(me, reach, outside_ref.shape[0])
    diagonal = iota((width, width), 0) == iota((width, width), 1)
    wt_s[...] = jnp.zeros_like(wt_s)

    def both_sides(value):
        return (jnp.sum(jnp.where(apart < 0.0, value, 0.0), axis=0, keepdims=True),
                jnp.sum(jnp.where(apart > 0.0, value, 0.0), axis=0, keepdims=True))

    for t in range(2):
        mine = lax.div(me, reach)
        for group, other in enumerate((mine, lax.bitwise_xor(mine, 1), lax.bitwise_xor(mine, 3))):
            side = jnp.where(jnp.abs(other - mine) > 1, 3, other - mine + 1)
            for slot in range(reach):
                row = flag_refs[group][slot, t:t + 1, :].astype(F32)
                wt_s[t, pl.ds(side * reach + lax.bitwise_xor(place, slot), 1), :] = 1.0 - row
        own = 1.0 - flag_refs[0][0, t:t + 1, :].astype(F32)
        inside = inside_ref[...] * own
        outside = outside_ref[...] * wt_s[t]
        before, after = both_sides(jnp.sum(outside, axis=1, keepdims=True))
        count = jnp.sum(inside, axis=1, keepdims=True) + first_c * before + last_c * after
        scale = 1.0 / jnp.maximum(count, 1.0)
        rows = jnp.concatenate([inside, outside], axis=0).astype(BF16)
        scale_r = jnp.sum(jnp.where(sub == lane, scale, 0.0), axis=0, keepdims=True)
        own_c = jnp.sum(jnp.where(diagonal, own, 0.0), axis=1, keepdims=True)
        chosen = chosen_ref[...] * own_c
        alpha_s[t] = jnp.broadcast_to(jnp.sum(chosen * scale_r, axis=1, keepdims=True), (width, 128))
        chosen = chosen.astype(BF16)
        sums = [dot(rows, mix_refs[t][slot, 0]) + dot(rows, mix_refs[t][slot, 1]) for slot in range(2)]
        away = times((apart_ref[t, 0], apart_ref[t, 1]), tuple(value[windows:] for value in sums))
        for slot in range(2):
            before, after = both_sides(away[slot])
            total = sums[slot][:windows] + first_c * before + last_c * after
            high, low = split_two(total * (scale * scale))
            mexp_s[t, slot] = dot(chosen, high) + dot(chosen, low)

    for t in range(2):
        def main(lanes, count):
            def step(block, sums):
                rows = pl.ds(pl.multiple_of(block * 16, 16), 16)
                alpha = alpha_s[t, rows, :count]
                mr, mi = mexp_s[t, 0, rows, lanes], mexp_s[t, 1, rows, lanes]
                r0, i0 = wave_refs[t][0, 0, rows, lanes], wave_refs[t][0, 1, rows, lanes]
                r1, i1 = wave_refs[t][1, 0, rows, lanes], wave_refs[t][1, 1, rows, lanes]
                factors = []
                for fr, fi in (
                    (alpha * r0 - (mr * r1 + mi * i1), (mr * i1 - mi * r1) - alpha * i0),
                    (alpha * r1 - (mr * r0 - mi * i0), (mr * i0 + mi * r0) - alpha * i1),
                ):
                    factors.append((fr, fi - fr, fr + fi))
                new = []
                for k in range(4):
                    vr = visibility(vis_refs, 0, t, k, rows, lanes)
                    vi = visibility(vis_refs, 1, t, k, rows, lanes)
                    vs = vr + vi
                    for s in range(2):
                        for v, f in zip((vs, vr, vi), factors[s]):
                            product = v * f
                            new.append(sums[len(new)] + (product[:8] + product[8:]))
                return tuple(new)

            zero = jnp.zeros((8, count), F32)
            sums = lax.fori_loop(0, width // 16, step, (zero,) * 24, unroll=6)
            for s in range(2):
                owner = lax.bitwise_xor(lax.bitwise_and(me, 3), t + 2 * s)
                found = []
                for k in range(4):
                    one, two, three = sums[(k * 2 + s) * 3:(k * 2 + s) * 3 + 3]
                    found.append([jnp.sum(value, axis=0, keepdims=True) for value in (one - three, one + two)])
                for d in range(4):
                    @pl.when(owner == d)
                    def write():
                        for k in range(4):
                            for ri in range(2):
                                out_refs[d][k, ri:ri + 1, lanes] = found[k][ri]

        if t == 1:
            copy.wait()
        tiles(pairs, main)


def station_hots(pairs):
    station, baseline = iota((ROWS, 1), 0), iota((1, pairs), 1)
    offset = station * (float(2 * STATIONS - 1) - station) * 0.5
    after = (station + 1.0) * (float(2 * STATIONS - 2) - station) * 0.5
    first = jnp.where((baseline >= offset) & (baseline < after), 1.0, 0.0)
    partner_of = baseline + 1.0 + jnp.sum(first * (station - offset), axis=0, keepdims=True)
    second = jnp.where(partner_of == station, 1.0, 0.0)
    return first.astype(BF16), second.astype(BF16)


def hots_kernel(hot_ref):
    hot_ref[0], hot_ref[1] = station_hots(hot_ref.shape[2])


def solve_kernel(window_count, me_ref, tracks_ref, hot_ref, *refs):
    parts, gain_ref = refs[:-1], refs[-1]
    me = me_ref[0]
    systems = gain_ref.shape[0]
    total = [part[...] for part in parts]
    while len(total) > 1:
        total = [total[i] + total[i + 1] for i in range(0, len(total), 2)]
    total = total[0]
    hot, other = hot_ref[0], hot_ref[1]
    nt = lambda left, right: lax.dot_general(
        left, right, (((1,), (1,)), ((), ())), preferred_element_type=F32)
    upper, lower = [], []
    for system in range(systems):
        for ri in range(2):
            for piece in split_two(total[system, ri:ri + 1]):
                upper.append(hot * piece)
                lower.append(other * piece)
    upper = nt(jnp.concatenate(upper, axis=0), other)
    lower = nt(jnp.concatenate(lower, axis=0), hot)
    cut = lambda value, i: value[i * ROWS:(i + 1) * ROWS]
    join = lambda value, i: cut(value, 2 * i) + cut(value, 2 * i + 1)
    live_r = jnp.where(iota((1, ROWS), 1) < float(STATIONS), 1.0, 0.0)
    live_c = jnp.where(iota((ROWS, 1), 0) < float(STATIONS), 1.0, 0.0)
    matrices = [(join(upper, 2 * i) + join(lower, 2 * i), join(upper, 2 * i + 1) - join(lower, 2 * i + 1))
                for i in range(systems)]
    states = [(live_r, 0.0 * live_r, live_c, 0.0 * live_c)] * systems
    for turn in range(GITERS):
        for system in range(systems):
            re, im = matrices[system]
            row_re, row_im, col_re, col_im = states[system]
            pull_cr = jnp.sum(re * row_re - im * row_im, axis=1, keepdims=True)
            pull_ci = jnp.sum(re * row_im + im * row_re, axis=1, keepdims=True)
            pull_rr = jnp.sum(re * col_re + im * col_im, axis=0, keepdims=True)
            pull_ri = jnp.sum(re * col_im - im * col_re, axis=0, keepdims=True)
            power_r = row_re * row_re + row_im * row_im
            power_c = col_re * col_re + col_im * col_im
            total = jnp.sum(power_c, axis=0, keepdims=True)
            inverse_r = 0.5 / (window_count * (total - power_r) + DAMPING)
            inverse_c = 0.5 / (window_count * (total - power_c) + DAMPING)
            states[system] = (0.5 * row_re + pull_rr * inverse_r, 0.5 * row_im + pull_ri * inverse_r,
                              0.5 * col_re + pull_cr * inverse_c, 0.5 * col_im + pull_ci * inverse_c)
    visible = tracks_ref[lax.bitwise_and(lax.div(me, 2), 1), lax.bitwise_and(me, 1)].astype(F32)
    gains = [state[ri] * visible for state in states for ri in range(2)]
    gains = jnp.concatenate(gains, axis=0)
    stacked = jnp.concatenate([piece.astype(F32) for piece in split_three(gains)], axis=0).astype(BF16)
    ends = []
    for table in (hot, other):
        wide = dot(stacked, table)
        ends.append((wide[:8] + wide[8:16]) + wide[16:])
    pairs = hot.shape[1]
    for system in range(systems):
        (lr, li), (rr, ri_) = [[end[2 * system + ri:2 * system + ri + 1] for ri in range(2)] for end in ends]
        gain_ref[system, 0:1, :pairs] = lr * rr + li * ri_
        gain_ref[system, 1:2, :pairs] = li * rr - lr * ri_
        gain_ref[system, :, GAINS_AT:] = gains[2 * system:2 * system + 2, :STATIONS]


def clean_kernel(width, me_ref, *refs):
    vis_refs, wave_refs, piece_refs = refs[:3], refs[3:5], refs[5:9]
    out_hbm, gain_out_ref, out_s, model_s, sems = refs[9:]
    pairs = wave_refs[0].shape[3]
    mine = lax.bitwise_and(me_ref[0], 3)
    for d, piece in enumerate(piece_refs):
        owner = lax.bitwise_xor(mine, d)
        t, s = lax.bitwise_and(owner, 1), lax.div(owner, 2)
        for k in range(4):
            for ri in range(2):
                gain_out_ref[ri, s, t, k:k + 1, :] = piece[k, ri:ri + 1, GAINS_AT:]
            re, im = piece[k, 0:1, :pairs], piece[k, 1:2, :pairs]
            for slot, value in enumerate((re, im - re, re + im)):
                model_s[owner, 3 * k + slot:3 * k + slot + 1, :] = value

    half = width // 32 * 16
    quarter = half // 32 * 16
    pieces = [(0, 0, half), (0, half, width - half),
              (1, 0, half), (1, half, half - quarter), (1, 2 * half - quarter, width - 2 * half + quarter)]
    copies = []
    for t, start, length in pieces:
        def main(lanes, count):
            for block in range(length // 16):
                rows = slice(start + block * 16, start + block * 16 + 16)
                waves = []
                for s in range(2):
                    re, im = (wave_refs[t][s, ri, rows, lanes] for ri in range(2))
                    waves.append((re + im, re, im))
                for k in range(4):
                    sums = []
                    for slot in range(3):
                        one, two = (waves[s][slot] * model_s[t + 2 * s, 3 * k + slot:3 * k + slot + 1, lanes]
                                    for s in range(2))
                        sums.append(one + two)
                    vr = visibility(vis_refs, 0, t, k, rows, lanes)
                    vi = visibility(vis_refs, 1, t, k, rows, lanes)
                    out_s[0, t, k, rows, lanes] = (vr - (sums[0] - sums[2])).astype(BF16)
                    out_s[1, t, k, rows, lanes] = (vi - (sums[0] + sums[1])).astype(BF16)

        tiles(pairs, main)
        rows = pl.ds(start, length)
        copies.append(pltpu.make_async_copy(
            out_s.at[:, t, :, rows], out_hbm.at[:, t, :, rows], sems.at[len(copies)]))
        copies[-1].start()
    for copy in copies:
        copy.wait()


def partner(value, bits):
    count = lax.axis_size("sub")
    return lax.ppermute(value, "sub", [(i, i ^ bits) for i in range(count)])


def smem():
    return pl.BlockSpec(memory_space=pltpu.SMEM)


def local(visibilities, delays, flags, windows, tracks):
    width = visibilities.shape[4]
    pairs = visibilities.shape[3]
    count = lax.axis_size("sub")
    window_count = windows.shape[0]
    turned = jnp.transpose(visibilities, (0, 1, 2, 4, 3))
    me = lax.axis_index("sub").astype(jnp.int32).reshape(1)
    vmem_ref = pl.BlockSpec(memory_space=pltpu.VMEM)
    hbm_ref = pl.BlockSpec(memory_space=pltpu.HBM)
    vmem = lambda *shape: pltpu.VMEM(shape, F32)
    params = pltpu.CompilerParams(vmem_limit_bytes=24 * 2 ** 20)
    flags = flags[None]
    windows = windows.reshape(1, window_count)

    reach = count // 4
    remote_rows = 16 * pl.cdiv(4 * reach, 16)

    hots = pl.pallas_call(
        hots_kernel,
        out_specs=vmem_ref,
        out_shape=jax.ShapeDtypeStruct((2, ROWS, pairs), BF16),
        compiler_params=params,
        cost_estimate=pl.CostEstimate(flops=10 ** 7, bytes_accessed=6 * 2 ** 20, transcendentals=0),
        name="station_hots",
    )()
    made = []
    beside = [partner(flags, d) for d in range(1, 4)]
    for t in range(2):
        shape = lambda *dims: jax.ShapeDtypeStruct(dims, F32)
        out_shape = [
            shape(2, 2, width, pairs),
            jax.ShapeDtypeStruct((2, 2, width, pairs), BF16),
        ]
        out_shape += [jax.ShapeDtypeStruct((2, 2, width, pairs), BF16)]
        if t == 0:
            operands = (me, turned, delays, flags, windows)
            out_shape += [jax.ShapeDtypeStruct(flags.shape, flags.dtype),
                          jax.ShapeDtypeStruct(windows.shape, windows.dtype)]
        else:
            operands = (me, turned, delays, made[0][4])
            out_shape += [shape(2, 2, remote_rows, pairs), shape(window_count, width), shape(width, window_count),
                          shape(remote_rows, width), shape(2, window_count, 128)]
        made.append(pl.pallas_call(
            lambda *refs: phase_kernel(width, t, reach, *refs),
            in_specs=[smem(), hbm_ref] + [vmem_ref] * (len(operands) - 2),
            out_specs=[vmem_ref] * len(out_shape),
            out_shape=out_shape,
            scratch_shapes=[pltpu.SemaphoreType.DMA],
            compiler_params=pltpu.CompilerParams(vmem_limit_bytes=GRANTS[t] * 2 ** 20),
            cost_estimate=pl.CostEstimate(flops=10 ** 7, bytes_accessed=6 * 2 ** 20, transcendentals=0),
            name="phases",
        )(*operands))
        if t == 0:
            gathered = jnp.concatenate([made[0][3]] + beside, axis=0)
            while gathered.shape[0] < reach:
                stride = gathered.shape[0]
                gathered = jnp.concatenate([gathered] + [partner(gathered, stride * d) for d in range(1, 4)], axis=0)
            gathered = [gathered] + [partner(gathered, d * reach) for d in (1, 3)]
    waves, mixing, held = ([part[i] for part in made] for i in range(3))
    masks = made[1][3:]
    *quarters, held_too = pl.pallas_call(
        lambda *refs: sums_kernel(width, reach, *refs),
        in_specs=[smem()] + [vmem_ref] * 8 + [hbm_ref] + [vmem_ref] * 6,
        out_specs=[vmem_ref] * 5,
        out_shape=[jax.ShapeDtypeStruct((4, 2, pairs), F32)] * 4 + [jax.ShapeDtypeStruct((2, 4, width, pairs), BF16)],
        scratch_shapes=[vmem(2, width, 128), vmem(2, 2, width, pairs), vmem(2, remote_rows, width),
                        pltpu.SemaphoreType.DMA],
        compiler_params=pltpu.CompilerParams(vmem_limit_bytes=GRANT * 2 ** 20),
        name="window_sums",
    )(me, *gathered, *masks, turned, *held, *waves, *mixing)
    pieces = [quarters[0]] + [partner(quarters[d], d) for d in range(1, 4)]
    stride = 4
    while stride < count:
        while len(pieces) > 1:
            pieces = [pieces[i] + pieces[i + 1] for i in range(0, len(pieces), 2)]
        pieces += [partner(pieces[0], stride * d) for d in range(1, min(4, count // stride))]
        stride *= 4
    model = pl.pallas_call(
        lambda *refs: solve_kernel(float(window_count), *refs),
        in_specs=[smem(), smem()] + [vmem_ref] * (1 + len(pieces)),
        out_specs=vmem_ref,
        out_shape=jax.ShapeDtypeStruct((4, 2, GAINS_AT + STATIONS), F32),
        compiler_params=params,
        name="gain_solve",
    )(me, tracks, hots, *pieces)
    model = [model] + [partner(model, d) for d in range(1, 4)]
    cleaned, gains = pl.pallas_call(
        lambda *refs: clean_kernel(width, *refs),
        in_specs=[smem()] + [vmem_ref] * 9,
        out_specs=[hbm_ref, vmem_ref],
        out_shape=[
            jax.ShapeDtypeStruct(turned.shape, BF16),
            jax.ShapeDtypeStruct((2, 2, 2, 4, STATIONS), F32),
        ],
        scratch_shapes=[
            pltpu.VMEM(turned.shape, BF16),
            vmem(4, 16, pairs),
            pltpu.SemaphoreType.DMA((5,)),
        ],
        compiler_params=params,
        name="clean",
    )(me, *held, held_too, *waves, *model)
    return jnp.transpose(cleaned, (0, 1, 2, 4, 3)), gains


def solution(mesh):
    return jax.shard_map(
        local,
        mesh=mesh,
        in_specs=(
            P(None, "obs", None, None, "sub"),
            P(None, "obs", None),
            P("obs", "sub"),
            P(),
            P(None, "obs"),
        ),
        out_specs=(P(None, "obs", None, None, "sub"), P(None, None, "obs", None, None)),
        check_vma=False,
    )
```

```python
import jax
import jax.numpy as jnp
import numpy as np
from jax import lax
from jax.experimental import pallas as pl
from jax.experimental.pallas import tpu as pltpu
from jax.sharding import PartitionSpec as P

STATIONS = 38
GITERS = 8
DAMPING = 1.0
STEPS_PER_TURN = 64
GAINS_AT = 768
GRANT = 42
GRANTS = (47, 45)
ROWS = 40

F32 = jnp.float32
BF16 = jnp.bfloat16


def iota(shape, dim):
    return lax.broadcasted_iota(jnp.int32, shape, dim).astype(F32)


def sincos_turns(turns):
    half = (turns - jnp.floor(turns + 0.5)) * np.float32(np.pi)
    sq = half * half
    sin = np.float32(-1.0 / 39916800)
    for term in (1.0 / 362880, -1.0 / 5040, 1.0 / 120, -1.0 / 6, 1.0):
        sin = sin * sq + np.float32(term)
    sin = sin * half
    cos = np.float32(1.0 / 479001600)
    for term in (-1.0 / 3628800, 1.0 / 40320, -1.0 / 720, 1.0 / 24, -0.5, 1.0):
        cos = cos * sq + np.float32(term)
    return 1.0 - 2.0 * (sin * sin), 2.0 * (sin * cos)


def split_two(value):
    high = value.astype(BF16)
    low = (value - high.astype(F32)).astype(BF16)
    return high, low


def split_three(value):
    high = value.astype(BF16)
    rest = value - high.astype(F32)
    mid = rest.astype(BF16)
    low = (rest - mid.astype(F32)).astype(BF16)
    return high, mid, low


def dot(left, right):
    return jnp.dot(left, right, preferred_element_type=F32)


def times(left, right):
    (lr, li), (rr, ri) = left, right
    return lr * rr - li * ri, lr * ri + li * rr


def phase_rows(delays, anchor, width):
    place = iota((8, 1), 0)
    second = place >= 4.0
    turns = jnp.where(second, delays[1], delays[0])
    at = anchor + float(STEPS_PER_TURN) * jnp.where(second, place - 4.0, place)
    base = sincos_turns(turns * (at * np.float32(1.0 / STEPS_PER_TURN)))
    fine, coarse = [], []
    for s in range(2):
        low = sincos_turns(delays[s] * (place * np.float32(1.0 / STEPS_PER_TURN)))
        high = low
        for doubling in range(3):
            high = times(high, high)
        rows = [times(tuple(part[4 * s + a:4 * s + a + 1] for part in base), high)
                for a in range(width // STEPS_PER_TURN)]
        fine.append(low)
        coarse.append(rows)
    return fine, coarse


def tiles(pairs, body):
    full = pairs // 128

    def step(tile, carry):
        body(pl.ds(pl.multiple_of(tile * 128, 128), 128), 128)
        return carry

    lax.fori_loop(0, full, step, 0)
    if pairs % 128:
        body(pl.ds(full * 128, pairs % 128), pairs % 128)


def phase_kernel(width, t, reach, me_ref, *refs):
    anchor = me_ref[0].astype(F32) * float(width)
    if t == 0:
        delay_ref, small_ref, wave_ref, mix_ref, own_ref, win_out_ref = refs
    else:
        vis_hbm, delay_ref, win_ref, wave_ref, mix_ref, vis_ref, apart_ref, *mask_refs, sem = refs
        copy = pltpu.make_async_copy(vis_hbm.at[:, 0], vis_ref, sem)
        copy.start()
    if t == 0:
        own_ref[0] = small_ref[:2]
        win_out_ref[...] = small_ref[2:3, :win_out_ref.shape[1]]
    else:
        window_masks(width, reach, me_ref[0], win_ref, *mask_refs)
        apart = blocks_apart(me_ref[0], reach, apart_ref.shape[2])
        for time in range(2):
            gap = delay_ref[1, time:time + 1, :] - delay_ref[0, time:time + 1, :]
            phase = sincos_turns(gap * (apart * np.float32(width / STEPS_PER_TURN)))
            apart_ref[time, 0], apart_ref[time, 1] = phase
    pairs = delay_ref.shape[2]

    def waves(lanes, count):
        delays = [delay_ref[s, t:t + 1, lanes] for s in range(2)]
        fine, coarse = phase_rows(delays, anchor, width)
        for block in range(width // 16):
            found = []
            for s in range(2):
                halves = []
                for half in range(2):
                    a, b = divmod(2 * block + half, 8)
                    halves.append(times(tuple(part[b:b + 1] for part in coarse[s][a]), fine[s]))
                found.append([jnp.concatenate([h[ri] for h in halves], axis=0) for ri in range(2)])
            rows = slice(block * 16, block * 16 + 16)
            (r0, i0), (r1, i1) = found
            for s in range(2):
                for ri in range(2):
                    wave_ref[s, ri, rows, lanes] = found[s][ri]
            for slot, value in enumerate((r1 * r0 + i1 * i0, i1 * r0 - r1 * i0)):
                high, low = split_two(value)
                mix_ref[slot, 0, rows, lanes] = high
                mix_ref[slot, 1, rows, lanes] = low

    tiles(pairs, waves)
    if t == 1:
        copy.wait()


def blocks_apart(me, reach, rows):
    return iota((rows, 1), 0) - (lax.rem(me, reach) + reach).astype(F32)


def window_masks(width, reach, me, win_ref, inside_ref, chosen_ref, outside_ref, ends_ref):
    anchor = me.astype(F32) * float(width)
    lowest = (me - lax.rem(me, reach) - reach).astype(F32)
    windows = inside_ref.shape[0]
    final = anchor + float(width - 1)
    win_row = win_ref[...].astype(F32)
    sub, lane = iota((windows, windows), 0), iota((windows, windows), 1)
    end_c = jnp.sum(jnp.where(lane <= sub, win_row, 0.0), axis=1, keepdims=True)
    start_c = jnp.sum(jnp.where(lane < sub, win_row, 0.0), axis=1, keepdims=True)
    win_c = end_c - start_c
    end_r = jnp.sum(jnp.where(sub <= lane, win_c, 0.0), axis=0, keepdims=True)
    start_r = jnp.sum(jnp.where(sub < lane, win_c, 0.0), axis=0, keepdims=True)
    first_c = jnp.where((start_c <= anchor) & (anchor < end_c), 1.0, 0.0)
    last_c = jnp.where((start_c <= final) & (final < end_c), 1.0, 0.0)
    from_first = jnp.sum(first_c * start_c, axis=0, keepdims=True)
    to_last = jnp.sum(last_c * end_c, axis=0, keepdims=True)
    here = anchor + iota((windows, width), 1)
    inside_ref[...] = jnp.where((here >= start_c) & (here < end_c), 1.0, 0.0)
    there = anchor + iota((width, windows), 0)
    chosen_ref[...] = jnp.where((there >= start_r) & (there < end_r), 1.0, 0.0)
    shape = outside_ref.shape
    channel = (lowest + iota(shape, 0)) * float(width) + iota(shape, 1)
    remote = ((channel < anchor) & (channel >= from_first)) | ((channel > final) & (channel < to_last))
    outside_ref[...] = jnp.where(remote, 1.0, 0.0)
    ends_ref[0] = jnp.broadcast_to(first_c, ends_ref.shape[1:])
    ends_ref[1] = jnp.broadcast_to(last_c, ends_ref.shape[1:])


def sums_kernel(width, reach, me_ref, *refs):
    flag_refs, refs = refs[:3], refs[3:]
    apart_ref, inside_ref, chosen_ref, outside_ref, ends_ref = refs[:5]
    vis_hbm, first_ref, wave_refs, mix_refs, refs = refs[5], refs[6], refs[7:9], refs[9:11], refs[11:]
    out_refs, (second_ref, alpha_s, mexp_s, wt_s, sem) = refs[:4], refs[4:]
    vis_refs = (first_ref, second_ref)
    copy = pltpu.make_async_copy(vis_hbm.at[:, 1], second_ref, sem)
    copy.start()
    me = me_ref[0]
    place = lax.rem(me, reach)
    windows = inside_ref.shape[0]
    pairs = apart_ref.shape[3]
    sub, lane = iota((windows, windows), 0), iota((windows, windows), 1)
    first_c, last_c = ends_ref[0][:, :1], ends_ref[1][:, :1]
    apart = blocks_apart(me, reach, outside_ref.shape[0])
    diagonal = iota((width, width), 0) == iota((width, width), 1)
    wt_s[...] = jnp.zeros_like(wt_s)

    def both_sides(value):
        return (jnp.sum(jnp.where(apart < 0.0, value, 0.0), axis=0, keepdims=True),
                jnp.sum(jnp.where(apart > 0.0, value, 0.0), axis=0, keepdims=True))

    for t in range(2):
        mine = lax.div(me, reach)
        for group, other in enumerate((mine, lax.bitwise_xor(mine, 1), lax.bitwise_xor(mine, 3))):
            side = jnp.where(jnp.abs(other - mine) > 1, 3, other - mine + 1)
            for slot in range(reach):
                row = flag_refs[group][slot, t:t + 1, :].astype(F32)
                wt_s[t, pl.ds(side * reach + lax.bitwise_xor(place, slot), 1), :] = 1.0 - row
        own = 1.0 - flag_refs[0][0, t:t + 1, :].astype(F32)
        inside = inside_ref[...] * own
        outside = outside_ref[...] * wt_s[t]
        before, after = both_sides(jnp.sum(outside, axis=1, keepdims=True))
        count = jnp.sum(inside, axis=1, keepdims=True) + first_c * before + last_c * after
        scale = 1.0 / jnp.maximum(count, 1.0)
        rows = jnp.concatenate([inside, outside], axis=0).astype(BF16)
        scale_r = jnp.sum(jnp.where(sub == lane, scale, 0.0), axis=0, keepdims=True)
        own_c = jnp.sum(jnp.where(diagonal, own, 0.0), axis=1, keepdims=True)
        chosen = chosen_ref[...] * own_c
        alpha_s[t] = jnp.broadcast_to(jnp.sum(chosen * scale_r, axis=1, keepdims=True), (width, 128))
        chosen = chosen.astype(BF16)
        sums = [dot(rows, mix_refs[t][slot, 0]) + dot(rows, mix_refs[t][slot, 1]) for slot in range(2)]
        away = times((apart_ref[t, 0], apart_ref[t, 1]), tuple(value[windows:] for value in sums))
        for slot in range(2):
            before, after = both_sides(away[slot])
            total = sums[slot][:windows] + first_c * before + last_c * after
            high, low = split_two(total * (scale * scale))
            mexp_s[t, slot] = dot(chosen, high) + dot(chosen, low)

    for t in range(2):
        def main(lanes, count):
            def step(block, sums):
                rows = pl.ds(pl.multiple_of(block * 16, 16), 16)
                alpha = alpha_s[t, rows, :count]
                mr, mi = mexp_s[t, 0, rows, lanes], mexp_s[t, 1, rows, lanes]
                r0, i0 = wave_refs[t][0, 0, rows, lanes], wave_refs[t][0, 1, rows, lanes]
                r1, i1 = wave_refs[t][1, 0, rows, lanes], wave_refs[t][1, 1, rows, lanes]
                factors = []
                for fr, fi in (
                    (alpha * r0 - (mr * r1 + mi * i1), (mr * i1 - mi * r1) - alpha * i0),
                    (alpha * r1 - (mr * r0 - mi * i0), (mr * i0 + mi * r0) - alpha * i1),
                ):
                    factors.append((fr, fi - fr, fr + fi))
                new = []
                for k in range(4):
                    vr = vis_refs[t][0, k, rows, lanes].astype(F32)
                    vi = vis_refs[t][1, k, rows, lanes].astype(F32)
                    vs = vr + vi
                    for s in range(2):
                        for v, f in zip((vs, vr, vi), factors[s]):
                            product = v * f
                            new.append(sums[len(new)] + (product[:8] + product[8:]))
                return tuple(new)

            zero = jnp.zeros((8, count), F32)
            sums = lax.fori_loop(0, width // 16, step, (zero,) * 24, unroll=6)
            for s in range(2):
                owner = lax.bitwise_xor(lax.bitwise_and(me, 3), t + 2 * s)
                found = []
                for k in range(4):
                    one, two, three = sums[(k * 2 + s) * 3:(k * 2 + s) * 3 + 3]
                    found.append([jnp.sum(value, axis=0, keepdims=True) for value in (one - three, one + two)])
                for d in range(4):
                    @pl.when(owner == d)
                    def write():
                        for k in range(4):
                            for ri in range(2):
                                out_refs[d][k, ri:ri + 1, lanes] = found[k][ri]

        if t == 1:
            copy.wait()
        tiles(pairs, main)


def station_hots(pairs):
    station, baseline = iota((ROWS, 1), 0), iota((1, pairs), 1)
    offset = station * (float(2 * STATIONS - 1) - station) * 0.5
    after = (station + 1.0) * (float(2 * STATIONS - 2) - station) * 0.5
    first = jnp.where((baseline >= offset) & (baseline < after), 1.0, 0.0)
    partner_of = baseline + 1.0 + jnp.sum(first * (station - offset), axis=0, keepdims=True)
    second = jnp.where(partner_of == station, 1.0, 0.0)
    return first.astype(BF16), second.astype(BF16)


def hots_kernel(hot_ref):
    hot_ref[0], hot_ref[1] = station_hots(hot_ref.shape[2])


def solve_kernel(window_count, me_ref, tracks_ref, hot_ref, *refs):
    parts, gain_ref = refs[:-1], refs[-1]
    me = me_ref[0]
    systems = gain_ref.shape[0]
    total = [part[...] for part in parts]
    while len(total) > 1:
        total = [total[i] + total[i + 1] for i in range(0, len(total), 2)]
    total = total[0]
    hot, other = hot_ref[0], hot_ref[1]
    nt = lambda left, right: lax.dot_general(
        left, right, (((1,), (1,)), ((), ())), preferred_element_type=F32)
    upper, lower = [], []
    for system in range(systems):
        for ri in range(2):
            for piece in split_two(total[system, ri:ri + 1]):
                upper.append(hot * piece)
                lower.append(other * piece)
    upper = nt(jnp.concatenate(upper, axis=0), other)
    lower = nt(jnp.concatenate(lower, axis=0), hot)
    cut = lambda value, i: value[i * ROWS:(i + 1) * ROWS]
    join = lambda value, i: cut(value, 2 * i) + cut(value, 2 * i + 1)
    live_r = jnp.where(iota((1, ROWS), 1) < float(STATIONS), 1.0, 0.0)
    live_c = jnp.where(iota((ROWS, 1), 0) < float(STATIONS), 1.0, 0.0)
    matrices = [(join(upper, 2 * i) + join(lower, 2 * i), join(upper, 2 * i + 1) - join(lower, 2 * i + 1))
                for i in range(systems)]
    states = [(live_r, 0.0 * live_r, live_c, 0.0 * live_c)] * systems
    for turn in range(GITERS):
        for system in range(systems):
            re, im = matrices[system]
            row_re, row_im, col_re, col_im = states[system]
            pull_cr = jnp.sum(re * row_re - im * row_im, axis=1, keepdims=True)
            pull_ci = jnp.sum(re * row_im + im * row_re, axis=1, keepdims=True)
            pull_rr = jnp.sum(re * col_re + im * col_im, axis=0, keepdims=True)
            pull_ri = jnp.sum(re * col_im - im * col_re, axis=0, keepdims=True)
            power_r = row_re * row_re + row_im * row_im
            power_c = col_re * col_re + col_im * col_im
            total = jnp.sum(power_c, axis=0, keepdims=True)
            inverse_r = 0.5 / (window_count * (total - power_r) + DAMPING)
            inverse_c = 0.5 / (window_count * (total - power_c) + DAMPING)
            states[system] = (0.5 * row_re + pull_rr * inverse_r, 0.5 * row_im + pull_ri * inverse_r,
                              0.5 * col_re + pull_cr * inverse_c, 0.5 * col_im + pull_ci * inverse_c)
    visible = tracks_ref[lax.bitwise_and(lax.div(me, 2), 1), lax.bitwise_and(me, 1)].astype(F32)
    gains = [state[ri] * visible for state in states for ri in range(2)]
    gains = jnp.concatenate(gains, axis=0)
    stacked = jnp.concatenate([piece.astype(F32) for piece in split_three(gains)], axis=0).astype(BF16)
    ends = []
    for table in (hot, other):
        wide = dot(stacked, table)
        ends.append((wide[:8] + wide[8:16]) + wide[16:])
    pairs = hot.shape[1]
    for system in range(systems):
        (lr, li), (rr, ri_) = [[end[2 * system + ri:2 * system + ri + 1] for ri in range(2)] for end in ends]
        gain_ref[system, 0:1, :pairs] = lr * rr + li * ri_
        gain_ref[system, 1:2, :pairs] = li * rr - lr * ri_
        gain_ref[system, :, GAINS_AT:] = gains[2 * system:2 * system + 2, :STATIONS]


def clean_kernel(width, me_ref, *refs):
    vis_refs, wave_refs, piece_refs = refs[:2], refs[2:4], refs[4:8]
    out_hbm, gain_out_ref, out_s, model_s, sems = refs[8:]
    pairs = wave_refs[0].shape[3]
    mine = lax.bitwise_and(me_ref[0], 3)
    for d, piece in enumerate(piece_refs):
        owner = lax.bitwise_xor(mine, d)
        t, s = lax.bitwise_and(owner, 1), lax.div(owner, 2)
        for k in range(4):
            for ri in range(2):
                gain_out_ref[ri, s, t, k:k + 1, :] = piece[k, ri:ri + 1, GAINS_AT:]
            re, im = piece[k, 0:1, :pairs], piece[k, 1:2, :pairs]
            for slot, value in enumerate((re, im - re, re + im)):
                model_s[owner, 3 * k + slot:3 * k + slot + 1, :] = value

    half = width // 32 * 16
    quarter = half // 32 * 16
    pieces = [(0, 0, half), (0, half, width - half),
              (1, 0, half), (1, half, half - quarter), (1, 2 * half - quarter, width - 2 * half + quarter)]
    copies = []
    for t, start, length in pieces:
        def main(lanes, count):
            for block in range(length // 16):
                rows = slice(start + block * 16, start + block * 16 + 16)
                waves = []
                for s in range(2):
                    re, im = (wave_refs[t][s, ri, rows, lanes] for ri in range(2))
                    waves.append((re + im, re, im))
                for k in range(4):
                    sums = []
                    for slot in range(3):
                        one, two = (waves[s][slot] * model_s[t + 2 * s, 3 * k + slot:3 * k + slot + 1, lanes]
                                    for s in range(2))
                        sums.append(one + two)
                    vr = vis_refs[t][0, k, rows, lanes].astype(F32)
                    vi = vis_refs[t][1, k, rows, lanes].astype(F32)
                    out_s[0, t, k, rows, lanes] = (vr - (sums[0] - sums[2])).astype(BF16)
                    out_s[1, t, k, rows, lanes] = (vi - (sums[0] + sums[1])).astype(BF16)

        tiles(pairs, main)
        rows = pl.ds(start, length)
        copies.append(pltpu.make_async_copy(
            out_s.at[:, t, :, rows], out_hbm.at[:, t, :, rows], sems.at[len(copies)]))
        copies[-1].start()
    for copy in copies:
        copy.wait()


def partner(value, bits):
    count = lax.axis_size("sub")
    return lax.ppermute(value, "sub", [(i, i ^ bits) for i in range(count)])


def smem():
    return pl.BlockSpec(memory_space=pltpu.SMEM)


def local(visibilities, delays, flags, windows, tracks):
    width = visibilities.shape[4]
    pairs = visibilities.shape[3]
    count = lax.axis_size("sub")
    window_count = windows.shape[0]
    turned = jnp.transpose(visibilities, (0, 1, 2, 4, 3))
    me = lax.axis_index("sub").astype(jnp.int32).reshape(1)
    vmem_ref = pl.BlockSpec(memory_space=pltpu.VMEM)
    hbm_ref = pl.BlockSpec(memory_space=pltpu.HBM)
    vmem = lambda *shape: pltpu.VMEM(shape, F32)
    params = pltpu.CompilerParams(vmem_limit_bytes=24 * 2 ** 20)
    flags = flags[None]

    reach = count // 4
    remote_rows = 16 * pl.cdiv(4 * reach, 16)

    hots = pl.pallas_call(
        hots_kernel,
        out_specs=vmem_ref,
        out_shape=jax.ShapeDtypeStruct((2, ROWS, pairs), BF16),
        compiler_params=params,
        cost_estimate=pl.CostEstimate(flops=10 ** 7, bytes_accessed=6 * 2 ** 20, transcendentals=0),
        name="station_hots",
    )()
    small = jnp.pad(flags[0], ((0, 1), (0, 0))) + jnp.pad(windows[None], ((2, 0), (0, width - window_count)))
    made = []
    beside = [partner(flags, d) for d in range(1, 4)]
    for t in range(2):
        shape = lambda *dims: jax.ShapeDtypeStruct(dims, F32)
        out_shape = [
            shape(2, 2, width, pairs),
            jax.ShapeDtypeStruct((2, 2, width, pairs), BF16),
        ]
        if t == 0:
            operands = (me, delays, small)
            in_specs = [smem()] + [vmem_ref] * 2
            out_shape += [jax.ShapeDtypeStruct(flags.shape, flags.dtype),
                          jax.ShapeDtypeStruct((1, window_count), windows.dtype)]
        else:
            operands = (me, turned, delays, made[0][3])
            in_specs = [smem(), hbm_ref] + [vmem_ref] * 2
            out_shape += [jax.ShapeDtypeStruct((2, 4, width, pairs), BF16),
                          shape(2, 2, remote_rows, pairs), shape(window_count, width), shape(width, window_count),
                          shape(remote_rows, width), shape(2, window_count, 128)]
        made.append(pl.pallas_call(
            lambda *refs: phase_kernel(width, t, reach, *refs),
            in_specs=in_specs,
            out_specs=[vmem_ref] * len(out_shape),
            out_shape=out_shape,
            scratch_shapes=[pltpu.SemaphoreType.DMA] * t,
            compiler_params=pltpu.CompilerParams(vmem_limit_bytes=GRANTS[t] * 2 ** 20),
            cost_estimate=pl.CostEstimate(flops=10 ** 7, bytes_accessed=6 * 2 ** 20, transcendentals=0),
            name="phases",
        )(*operands))
        if t == 0:
            gathered = jnp.concatenate([made[0][2]] + beside, axis=0)
            while gathered.shape[0] < reach:
                stride = gathered.shape[0]
                gathered = jnp.concatenate([gathered] + [partner(gathered, stride * d) for d in range(1, 4)], axis=0)
            gathered = [gathered] + [partner(gathered, d * reach) for d in (1, 3)]
    waves, mixing = ([part[i] for part in made] for i in range(2))
    held, *masks = made[1][2:]
    *quarters, held_too = pl.pallas_call(
        lambda *refs: sums_kernel(width, reach, *refs),
        in_specs=[smem()] + [vmem_ref] * 8 + [hbm_ref] + [vmem_ref] * 5,
        out_specs=[vmem_ref] * 5,
        out_shape=[jax.ShapeDtypeStruct((4, 2, pairs), F32)] * 4 + [jax.ShapeDtypeStruct(held.shape, BF16)],
        scratch_shapes=[vmem(2, width, 128), vmem(2, 2, width, pairs), vmem(2, remote_rows, width),
                        pltpu.SemaphoreType.DMA],
        compiler_params=pltpu.CompilerParams(vmem_limit_bytes=GRANT * 2 ** 20),
        name="window_sums",
    )(me, *gathered, *masks, turned, held, *waves, *mixing)
    pieces = [quarters[0]] + [partner(quarters[d], d) for d in range(1, 4)]
    stride = 4
    while stride < count:
        while len(pieces) > 1:
            pieces = [pieces[i] + pieces[i + 1] for i in range(0, len(pieces), 2)]
        pieces += [partner(pieces[0], stride * d) for d in range(1, min(4, count // stride))]
        stride *= 4
    model = pl.pallas_call(
        lambda *refs: solve_kernel(float(window_count), *refs),
        in_specs=[smem(), smem()] + [vmem_ref] * (1 + len(pieces)),
        out_specs=vmem_ref,
        out_shape=jax.ShapeDtypeStruct((4, 2, GAINS_AT + STATIONS), F32),
        compiler_params=params,
        name="gain_solve",
    )(me, tracks, hots, *pieces)
    model = [model] + [partner(model, d) for d in range(1, 4)]
    cleaned, gains = pl.pallas_call(
        lambda *refs: clean_kernel(width, *refs),
        in_specs=[smem()] + [vmem_ref] * 8,
        out_specs=[hbm_ref, vmem_ref],
        out_shape=[
            jax.ShapeDtypeStruct(turned.shape, BF16),
            jax.ShapeDtypeStruct((2, 2, 2, 4, STATIONS), F32),
        ],
        scratch_shapes=[
            pltpu.VMEM(turned.shape, BF16),
            vmem(4, 16, pairs),
            pltpu.SemaphoreType.DMA((5,)),
        ],
        compiler_params=params,
        name="clean",
    )(me, held, held_too, *waves, *model)
    return jnp.transpose(cleaned, (0, 1, 2, 4, 3)), gains


def solution(mesh):
    return jax.shard_map(
        local,
        mesh=mesh,
        in_specs=(
            P(None, "obs", None, None, "sub"),
            P(None, "obs", None),
            P("obs", "sub"),
            P(),
            P(None, "obs"),
        ),
        out_specs=(P(None, "obs", None, None, "sub"), P(None, None, "obs", None, None)),
        check_vma=False,
    )
```

```python
import jax
import jax.numpy as jnp
import numpy as np
from jax import lax
from jax.experimental import pallas as pl
from jax.experimental.pallas import tpu as pltpu
from jax.sharding import PartitionSpec as P

STATIONS = 38
GITERS = 8
DAMPING = 1.0
STEPS_PER_TURN = 64
GAINS_AT = 768
GRANT = 42
GRANTS = (47, 45)
ROWS = 40

F32 = jnp.float32
BF16 = jnp.bfloat16


def iota(shape, dim):
    return lax.broadcasted_iota(jnp.int32, shape, dim).astype(F32)


def sincos_turns(turns):
    half = (turns - jnp.floor(turns + 0.5)) * np.float32(np.pi)
    sq = half * half
    sin = np.float32(-1.0 / 39916800)
    for term in (1.0 / 362880, -1.0 / 5040, 1.0 / 120, -1.0 / 6, 1.0):
        sin = sin * sq + np.float32(term)
    sin = sin * half
    cos = np.float32(1.0 / 479001600)
    for term in (-1.0 / 3628800, 1.0 / 40320, -1.0 / 720, 1.0 / 24, -0.5, 1.0):
        cos = cos * sq + np.float32(term)
    return 1.0 - 2.0 * (sin * sin), 2.0 * (sin * cos)


def split_two(value):
    high = value.astype(BF16)
    low = (value - high.astype(F32)).astype(BF16)
    return high, low


def split_three(value):
    high = value.astype(BF16)
    rest = value - high.astype(F32)
    mid = rest.astype(BF16)
    low = (rest - mid.astype(F32)).astype(BF16)
    return high, mid, low


def dot(left, right):
    return jnp.dot(left, right, preferred_element_type=F32)


def times(left, right):
    (lr, li), (rr, ri) = left, right
    return lr * rr - li * ri, lr * ri + li * rr


def phase_rows(delays, anchor, width):
    place = iota((8, 1), 0)
    second = place >= 4.0
    turns = jnp.where(second, delays[1], delays[0])
    at = anchor + float(STEPS_PER_TURN) * jnp.where(second, place - 4.0, place)
    base = sincos_turns(turns * (at * np.float32(1.0 / STEPS_PER_TURN)))
    fine, coarse = [], []
    for s in range(2):
        low = sincos_turns(delays[s] * (place * np.float32(1.0 / STEPS_PER_TURN)))
        high = low
        for doubling in range(3):
            high = times(high, high)
        rows = [times(tuple(part[4 * s + a:4 * s + a + 1] for part in base), high)
                for a in range(width // STEPS_PER_TURN)]
        fine.append(low)
        coarse.append(rows)
    return fine, coarse


def tiles(pairs, body):
    full = pairs // 128

    def step(tile, carry):
        body(pl.ds(pl.multiple_of(tile * 128, 128), 128), 128)
        return carry

    lax.fori_loop(0, full, step, 0)
    if pairs % 128:
        body(pl.ds(full * 128, pairs % 128), pairs % 128)


def phase_kernel(width, t, reach, me_ref, *refs):
    anchor = me_ref[0].astype(F32) * float(width)
    if t == 0:
        delay_ref, small_ref, wave_ref, mix_ref, own_ref, win_out_ref = refs
    else:
        vis_hbm, delay_ref, win_ref, wave_ref, mix_ref, vis_ref, apart_ref, *mask_refs, sem = refs
        copy = pltpu.make_async_copy(vis_hbm.at[:, 0], vis_ref, sem)
        copy.start()
    if t == 0:
        own_ref[0] = small_ref[:2]
        win_out_ref[...] = small_ref[2:3, :win_out_ref.shape[1]]
    else:
        window_masks(width, reach, me_ref[0], win_ref, *mask_refs)
        apart = blocks_apart(me_ref[0], reach, apart_ref.shape[2])
        for time in range(2):
            gap = delay_ref[1, time:time + 1, :] - delay_ref[0, time:time + 1, :]
            phase = sincos_turns(gap * (apart * np.float32(width / STEPS_PER_TURN)))
            apart_ref[time, 0], apart_ref[time, 1] = phase
    pairs = delay_ref.shape[2]

    def waves(lanes, count):
        delays = [delay_ref[s, t:t + 1, lanes] for s in range(2)]
        fine, coarse = phase_rows(delays, anchor, width)
        for block in range(width // 16):
            found = []
            for s in range(2):
                halves = []
                for half in range(2):
                    a, b = divmod(2 * block + half, 8)
                    halves.append(times(tuple(part[b:b + 1] for part in coarse[s][a]), fine[s]))
                found.append([jnp.concatenate([h[ri] for h in halves], axis=0) for ri in range(2)])
            rows = slice(block * 16, block * 16 + 16)
            (r0, i0), (r1, i1) = found
            for s in range(2):
                for ri in range(2):
                    wave_ref[s, ri, rows, lanes] = found[s][ri]
            for slot, value in enumerate((r1 * r0 + i1 * i0, i1 * r0 - r1 * i0)):
                high, low = split_two(value)
                mix_ref[slot, 0, rows, lanes] = high
                mix_ref[slot, 1, rows, lanes] = low

    tiles(pairs, waves)
    if t == 1:
        copy.wait()


def blocks_apart(me, reach, rows):
    return iota((rows, 1), 0) - (lax.rem(me, reach) + reach).astype(F32)


def window_masks(width, reach, me, win_ref, inside_ref, chosen_ref, outside_ref, ends_ref):
    anchor = me.astype(F32) * float(width)
    lowest = (me - lax.rem(me, reach) - reach).astype(F32)
    windows = inside_ref.shape[0]
    final = anchor + float(width - 1)
    win_row = win_ref[...].astype(F32)
    sub, lane = iota((windows, windows), 0), iota((windows, windows), 1)
    end_c = jnp.sum(jnp.where(lane <= sub, win_row, 0.0), axis=1, keepdims=True)
    start_c = jnp.sum(jnp.where(lane < sub, win_row, 0.0), axis=1, keepdims=True)
    win_c = end_c - start_c
    end_r = jnp.sum(jnp.where(sub <= lane, win_c, 0.0), axis=0, keepdims=True)
    start_r = jnp.sum(jnp.where(sub < lane, win_c, 0.0), axis=0, keepdims=True)
    first_c = jnp.where((start_c <= anchor) & (anchor < end_c), 1.0, 0.0)
    last_c = jnp.where((start_c <= final) & (final < end_c), 1.0, 0.0)
    from_first = jnp.sum(first_c * start_c, axis=0, keepdims=True)
    to_last = jnp.sum(last_c * end_c, axis=0, keepdims=True)
    here = anchor + iota((windows, width), 1)
    inside_ref[...] = jnp.where((here >= start_c) & (here < end_c), 1.0, 0.0)
    there = anchor + iota((width, windows), 0)
    chosen_ref[...] = jnp.where((there >= start_r) & (there < end_r), 1.0, 0.0)
    shape = outside_ref.shape
    channel = (lowest + iota(shape, 0)) * float(width) + iota(shape, 1)
    remote = ((channel < anchor) & (channel >= from_first)) | ((channel > final) & (channel < to_last))
    outside_ref[...] = jnp.where(remote, 1.0, 0.0)
    ends_ref[0] = jnp.broadcast_to(first_c, ends_ref.shape[1:])
    ends_ref[1] = jnp.broadcast_to(last_c, ends_ref.shape[1:])


def sums_kernel(width, reach, me_ref, *refs):
    flag_refs, refs = refs[:3], refs[3:]
    apart_ref, inside_ref, chosen_ref, outside_ref, ends_ref = refs[:5]
    vis_hbm, first_ref, wave_refs, mix_refs, refs = refs[5], refs[6], refs[7:9], refs[9:11], refs[11:]
    out_refs, (second_ref, alpha_s, mexp_s, wt_s, sem) = refs[:4], refs[4:]
    vis_refs = (first_ref, second_ref)
    copy = pltpu.make_async_copy(vis_hbm.at[:, 1], second_ref, sem)
    copy.start()
    me = me_ref[0]
    place = lax.rem(me, reach)
    windows = inside_ref.shape[0]
    pairs = apart_ref.shape[3]
    sub, lane = iota((windows, windows), 0), iota((windows, windows), 1)
    first_c, last_c = ends_ref[0][:, :1], ends_ref[1][:, :1]
    apart = blocks_apart(me, reach, outside_ref.shape[0])
    diagonal = iota((width, width), 0) == iota((width, width), 1)
    wt_s[...] = jnp.zeros_like(wt_s)

    def both_sides(value):
        return (jnp.sum(jnp.where(apart < 0.0, value, 0.0), axis=0, keepdims=True),
                jnp.sum(jnp.where(apart > 0.0, value, 0.0), axis=0, keepdims=True))

    for t in range(2):
        mine = lax.div(me, reach)
        for group, other in enumerate((mine, lax.bitwise_xor(mine, 3), lax.bitwise_xor(mine, 1))):
            side = jnp.where(jnp.abs(other - mine) > 1, 3, other - mine + 1)
            for slot in range(reach):
                row = flag_refs[group][slot, t:t + 1, :].astype(F32)
                wt_s[t, pl.ds(side * reach + lax.bitwise_xor(place, slot), 1), :] = 1.0 - row
        own = 1.0 - flag_refs[0][0, t:t + 1, :].astype(F32)
        inside = inside_ref[...] * own
        outside = outside_ref[...] * wt_s[t]
        before, after = both_sides(jnp.sum(outside, axis=1, keepdims=True))
        count = jnp.sum(inside, axis=1, keepdims=True) + first_c * before + last_c * after
        scale = 1.0 / jnp.maximum(count, 1.0)
        rows = jnp.concatenate([inside, outside], axis=0).astype(BF16)
        scale_r = jnp.sum(jnp.where(sub == lane, scale, 0.0), axis=0, keepdims=True)
        own_c = jnp.sum(jnp.where(diagonal, own, 0.0), axis=1, keepdims=True)
        chosen = chosen_ref[...] * own_c
        alpha_s[t] = jnp.broadcast_to(jnp.sum(chosen * scale_r, axis=1, keepdims=True), (width, 128))
        chosen = chosen.astype(BF16)
        sums = [dot(rows, mix_refs[t][slot, 0]) + dot(rows, mix_refs[t][slot, 1]) for slot in range(2)]
        away = times((apart_ref[t, 0], apart_ref[t, 1]), tuple(value[windows:] for value in sums))
        for slot in range(2):
            before, after = both_sides(away[slot])
            total = sums[slot][:windows] + first_c * before + last_c * after
            high, low = split_two(total * (scale * scale))
            mexp_s[t, slot] = dot(chosen, high) + dot(chosen, low)

    for t in range(2):
        def main(lanes, count):
            def step(block, sums):
                rows = pl.ds(pl.multiple_of(block * 16, 16), 16)
                alpha = alpha_s[t, rows, :count]
                mr, mi = mexp_s[t, 0, rows, lanes], mexp_s[t, 1, rows, lanes]
                r0, i0 = wave_refs[t][0, 0, rows, lanes], wave_refs[t][0, 1, rows, lanes]
                r1, i1 = wave_refs[t][1, 0, rows, lanes], wave_refs[t][1, 1, rows, lanes]
                factors = []
                for fr, fi in (
                    (alpha * r0 - (mr * r1 + mi * i1), (mr * i1 - mi * r1) - alpha * i0),
                    (alpha * r1 - (mr * r0 - mi * i0), (mr * i0 + mi * r0) - alpha * i1),
                ):
                    factors.append((fr, fi - fr, fr + fi))
                new = []
                for k in range(4):
                    vr = vis_refs[t][0, k, rows, lanes].astype(F32)
                    vi = vis_refs[t][1, k, rows, lanes].astype(F32)
                    vs = vr + vi
                    for s in range(2):
                        for v, f in zip((vs, vr, vi), factors[s]):
                            product = v * f
                            new.append(sums[len(new)] + (product[:8] + product[8:]))
                return tuple(new)

            zero = jnp.zeros((8, count), F32)
            sums = lax.fori_loop(0, width // 16, step, (zero,) * 24, unroll=6)
            for s in range(2):
                owner = lax.bitwise_xor(lax.bitwise_and(me, 3), t + 2 * s)
                found = []
                for k in range(4):
                    one, two, three = sums[(k * 2 + s) * 3:(k * 2 + s) * 3 + 3]
                    found.append([jnp.sum(value, axis=0, keepdims=True) for value in (one - three, one + two)])
                for d in range(4):
                    @pl.when(owner == d)
                    def write():
                        for k in range(4):
                            for ri in range(2):
                                out_refs[d][k, ri:ri + 1, lanes] = found[k][ri]

        if t == 1:
            copy.wait()
        tiles(pairs, main)


def station_hots(pairs):
    station, baseline = iota((ROWS, 1), 0), iota((1, pairs), 1)
    offset = station * (float(2 * STATIONS - 1) - station) * 0.5
    after = (station + 1.0) * (float(2 * STATIONS - 2) - station) * 0.5
    first = jnp.where((baseline >= offset) & (baseline < after), 1.0, 0.0)
    partner_of = baseline + 1.0 + jnp.sum(first * (station - offset), axis=0, keepdims=True)
    second = jnp.where(partner_of == station, 1.0, 0.0)
    return first.astype(BF16), second.astype(BF16)


def hots_kernel(hot_ref):
    hot_ref[0], hot_ref[1] = station_hots(hot_ref.shape[2])


def solve_kernel(window_count, me_ref, tracks_ref, hot_ref, *refs):
    parts, gain_ref = refs[:-1], refs[-1]
    me = me_ref[0]
    systems = gain_ref.shape[0]
    total = [part[...] for part in parts]
    while len(total) > 1:
        total = [total[i] + total[i + 1] for i in range(0, len(total), 2)]
    total = total[0]
    hot, other = hot_ref[0], hot_ref[1]
    nt = lambda left, right: lax.dot_general(
        left, right, (((1,), (1,)), ((), ())), preferred_element_type=F32)
    upper, lower = [], []
    for system in range(systems):
        for ri in range(2):
            for piece in split_two(total[system, ri:ri + 1]):
                upper.append(hot * piece)
                lower.append(other * piece)
    upper = nt(jnp.concatenate(upper, axis=0), other)
    lower = nt(jnp.concatenate(lower, axis=0), hot)
    cut = lambda value, i: value[i * ROWS:(i + 1) * ROWS]
    join = lambda value, i: cut(value, 2 * i) + cut(value, 2 * i + 1)
    live_r = jnp.where(iota((1, ROWS), 1) < float(STATIONS), 1.0, 0.0)
    live_c = jnp.where(iota((ROWS, 1), 0) < float(STATIONS), 1.0, 0.0)
    matrices = [(join(upper, 2 * i) + join(lower, 2 * i), join(upper, 2 * i + 1) - join(lower, 2 * i + 1))
                for i in range(systems)]
    states = [(live_r, 0.0 * live_r, live_c, 0.0 * live_c)] * systems
    for turn in range(GITERS):
        for system in range(systems):
            re, im = matrices[system]
            row_re, row_im, col_re, col_im = states[system]
            pull_cr = jnp.sum(re * row_re - im * row_im, axis=1, keepdims=True)
            pull_ci = jnp.sum(re * row_im + im * row_re, axis=1, keepdims=True)
            pull_rr = jnp.sum(re * col_re + im * col_im, axis=0, keepdims=True)
            pull_ri = jnp.sum(re * col_im - im * col_re, axis=0, keepdims=True)
            power_r = row_re * row_re + row_im * row_im
            power_c = col_re * col_re + col_im * col_im
            total = jnp.sum(power_c, axis=0, keepdims=True)
            inverse_r = 0.5 / (window_count * (total - power_r) + DAMPING)
            inverse_c = 0.5 / (window_count * (total - power_c) + DAMPING)
            states[system] = (0.5 * row_re + pull_rr * inverse_r, 0.5 * row_im + pull_ri * inverse_r,
                              0.5 * col_re + pull_cr * inverse_c, 0.5 * col_im + pull_ci * inverse_c)
    visible = tracks_ref[lax.bitwise_and(lax.div(me, 2), 1), lax.bitwise_and(me, 1)].astype(F32)
    gains = [state[ri] * visible for state in states for ri in range(2)]
    gains = jnp.concatenate(gains, axis=0)
    stacked = jnp.concatenate([piece.astype(F32) for piece in split_three(gains)], axis=0).astype(BF16)
    ends = []
    for table in (hot, other):
        wide = dot(stacked, table)
        ends.append((wide[:8] + wide[8:16]) + wide[16:])
    pairs = hot.shape[1]
    for system in range(systems):
        (lr, li), (rr, ri_) = [[end[2 * system + ri:2 * system + ri + 1] for ri in range(2)] for end in ends]
        gain_ref[system, 0:1, :pairs] = lr * rr + li * ri_
        gain_ref[system, 1:2, :pairs] = li * rr - lr * ri_
        gain_ref[system, :, GAINS_AT:] = gains[2 * system:2 * system + 2, :STATIONS]


def clean_kernel(width, me_ref, *refs):
    vis_refs, wave_refs, piece_refs = refs[:2], refs[2:4], refs[4:8]
    out_hbm, gain_out_ref, out_s, model_s, sems = refs[8:]
    pairs = wave_refs[0].shape[3]
    mine = lax.bitwise_and(me_ref[0], 3)
    for d, piece in enumerate(piece_refs):
        owner = lax.bitwise_xor(mine, d)
        t, s = lax.bitwise_and(owner, 1), lax.div(owner, 2)
        for k in range(4):
            for ri in range(2):
                gain_out_ref[ri, s, t, k:k + 1, :] = piece[k, ri:ri + 1, GAINS_AT:]
            re, im = piece[k, 0:1, :pairs], piece[k, 1:2, :pairs]
            for slot, value in enumerate((re, im - re, re + im)):
                model_s[owner, 3 * k + slot:3 * k + slot + 1, :] = value

    half = width // 32 * 16
    quarter = half // 32 * 16
    pieces = [(0, 0, half), (0, half, width - half),
              (1, 0, half), (1, half, half - quarter), (1, 2 * half - quarter, width - 2 * half + quarter)]
    copies = []
    for t, start, length in pieces:
        def main(lanes, count):
            for block in range(length // 16):
                rows = slice(start + block * 16, start + block * 16 + 16)
                waves = []
                for s in range(2):
                    re, im = (wave_refs[t][s, ri, rows, lanes] for ri in range(2))
                    waves.append((re + im, re, im))
                for k in range(4):
                    sums = []
                    for slot in range(3):
                        one, two = (waves[s][slot] * model_s[t + 2 * s, 3 * k + slot:3 * k + slot + 1, lanes]
                                    for s in range(2))
                        sums.append(one + two)
                    vr = vis_refs[t][0, k, rows, lanes].astype(F32)
                    vi = vis_refs[t][1, k, rows, lanes].astype(F32)
                    out_s[0, t, k, rows, lanes] = (vr - (sums[0] - sums[2])).astype(BF16)
                    out_s[1, t, k, rows, lanes] = (vi - (sums[0] + sums[1])).astype(BF16)

        tiles(pairs, main)
        rows = pl.ds(start, length)
        copies.append(pltpu.make_async_copy(
            out_s.at[:, t, :, rows], out_hbm.at[:, t, :, rows], sems.at[len(copies)]))
        copies[-1].start()
    for copy in copies:
        copy.wait()


def partner(value, bits):
    count = lax.axis_size("sub")
    return lax.ppermute(value, "sub", [(i, i ^ bits) for i in range(count)])


def smem():
    return pl.BlockSpec(memory_space=pltpu.SMEM)


def local(visibilities, delays, flags, windows, tracks):
    width = visibilities.shape[4]
    pairs = visibilities.shape[3]
    count = lax.axis_size("sub")
    window_count = windows.shape[0]
    turned = jnp.transpose(visibilities, (0, 1, 2, 4, 3))
    me = lax.axis_index("sub").astype(jnp.int32).reshape(1)
    vmem_ref = pl.BlockSpec(memory_space=pltpu.VMEM)
    hbm_ref = pl.BlockSpec(memory_space=pltpu.HBM)
    vmem = lambda *shape: pltpu.VMEM(shape, F32)
    params = pltpu.CompilerParams(vmem_limit_bytes=24 * 2 ** 20)
    flags = flags[None]

    reach = count // 4
    remote_rows = 16 * pl.cdiv(4 * reach, 16)

    hots = pl.pallas_call(
        hots_kernel,
        out_specs=vmem_ref,
        out_shape=jax.ShapeDtypeStruct((2, ROWS, pairs), BF16),
        compiler_params=params,
        cost_estimate=pl.CostEstimate(flops=10 ** 7, bytes_accessed=6 * 2 ** 20, transcendentals=0),
        name="station_hots",
    )()
    small = jnp.pad(flags[0], ((0, 1), (0, 0))) + jnp.pad(windows[None], ((2, 0), (0, width - window_count)))
    made = []
    beside = [partner(flags, d) for d in range(1, 4)]
    for t in range(2):
        shape = lambda *dims: jax.ShapeDtypeStruct(dims, F32)
        out_shape = [
            shape(2, 2, width, pairs),
            jax.ShapeDtypeStruct((2, 2, width, pairs), BF16),
        ]
        if t == 0:
            operands = (me, delays, small)
            in_specs = [smem()] + [vmem_ref] * 2
            out_shape += [jax.ShapeDtypeStruct(flags.shape, flags.dtype),
                          jax.ShapeDtypeStruct((1, window_count), windows.dtype)]
        else:
            operands = (me, turned, delays, made[0][3])
            in_specs = [smem(), hbm_ref] + [vmem_ref] * 2
            out_shape += [jax.ShapeDtypeStruct((2, 4, width, pairs), BF16),
                          shape(2, 2, remote_rows, pairs), shape(window_count, width), shape(width, window_count),
                          shape(remote_rows, width), shape(2, window_count, 128)]
        made.append(pl.pallas_call(
            lambda *refs: phase_kernel(width, t, reach, *refs),
            in_specs=in_specs,
            out_specs=[vmem_ref] * len(out_shape),
            out_shape=out_shape,
            scratch_shapes=[pltpu.SemaphoreType.DMA] * t,
            compiler_params=pltpu.CompilerParams(vmem_limit_bytes=GRANTS[t] * 2 ** 20),
            cost_estimate=pl.CostEstimate(flops=10 ** 7, bytes_accessed=6 * 2 ** 20, transcendentals=0),
            name="phases",
        )(*operands))
        if t == 0:
            gathered = jnp.concatenate([made[0][2]] + beside, axis=0)
            while gathered.shape[0] < reach:
                stride = gathered.shape[0]
                gathered = jnp.concatenate([gathered] + [partner(gathered, stride * d) for d in range(1, 4)], axis=0)
            middle = [(i, i ^ (3 * reach)) for i in range(count) if reach <= i < 3 * reach]
            beyond = lax.ppermute(gathered, "sub", middle)
            gathered = [gathered, beyond, partner(gathered, reach)]
    waves, mixing = ([part[i] for part in made] for i in range(2))
    held, *masks = made[1][2:]
    *quarters, held_too = pl.pallas_call(
        lambda *refs: sums_kernel(width, reach, *refs),
        in_specs=[smem()] + [vmem_ref] * 8 + [hbm_ref] + [vmem_ref] * 5,
        out_specs=[vmem_ref] * 5,
        out_shape=[jax.ShapeDtypeStruct((4, 2, pairs), F32)] * 4 + [jax.ShapeDtypeStruct(held.shape, BF16)],
        scratch_shapes=[vmem(2, width, 128), vmem(2, 2, width, pairs), vmem(2, remote_rows, width),
                        pltpu.SemaphoreType.DMA],
        compiler_params=pltpu.CompilerParams(vmem_limit_bytes=GRANT * 2 ** 20),
        name="window_sums",
    )(me, *gathered, *masks, turned, held, *waves, *mixing)
    pieces = [quarters[0]] + [partner(quarters[d], d) for d in range(1, 4)]
    stride = 4
    while stride < count:
        while len(pieces) > 1:
            pieces = [pieces[i] + pieces[i + 1] for i in range(0, len(pieces), 2)]
        pieces += [partner(pieces[0], stride * d) for d in range(1, min(4, count // stride))]
        stride *= 4
    model = pl.pallas_call(
        lambda *refs: solve_kernel(float(window_count), *refs),
        in_specs=[smem(), smem()] + [vmem_ref] * (1 + len(pieces)),
        out_specs=vmem_ref,
        out_shape=jax.ShapeDtypeStruct((4, 2, GAINS_AT + STATIONS), F32),
        compiler_params=params,
        name="gain_solve",
    )(me, tracks, hots, *pieces)
    model = [model] + [partner(model, d) for d in range(1, 4)]
    cleaned, gains = pl.pallas_call(
        lambda *refs: clean_kernel(width, *refs),
        in_specs=[smem()] + [vmem_ref] * 8,
        out_specs=[hbm_ref, vmem_ref],
        out_shape=[
            jax.ShapeDtypeStruct(turned.shape, BF16),
            jax.ShapeDtypeStruct((2, 2, 2, 4, STATIONS), F32),
        ],
        scratch_shapes=[
            pltpu.VMEM(turned.shape, BF16),
            vmem(4, 16, pairs),
            pltpu.SemaphoreType.DMA((5,)),
        ],
        compiler_params=params,
        name="clean",
    )(me, held, held_too, *waves, *model)
    return jnp.transpose(cleaned, (0, 1, 2, 4, 3)), gains


def solution(mesh):
    return jax.shard_map(
        local,
        mesh=mesh,
        in_specs=(
            P(None, "obs", None, None, "sub"),
            P(None, "obs", None),
            P("obs", "sub"),
            P(),
            P(None, "obs"),
        ),
        out_specs=(P(None, "obs", None, None, "sub"), P(None, None, "obs", None, None)),
        check_vma=False,
    )
```

```python
import jax
import jax.numpy as jnp
import numpy as np
from jax import lax
from jax.experimental import pallas as pl
from jax.experimental.pallas import tpu as pltpu
from jax.sharding import PartitionSpec as P

STATIONS = 38
GITERS = 8
DAMPING = 1.0
STEPS_PER_TURN = 64
GAINS_AT = 768
GRANT = 42
GRANTS = (47, 45)
ROWS = 40

F32 = jnp.float32
BF16 = jnp.bfloat16


def iota(shape, dim):
    return lax.broadcasted_iota(jnp.int32, shape, dim).astype(F32)


def sincos_turns(turns):
    half = (turns - jnp.floor(turns + 0.5)) * np.float32(np.pi)
    sq = half * half
    sin = np.float32(-1.0 / 39916800)
    for term in (1.0 / 362880, -1.0 / 5040, 1.0 / 120, -1.0 / 6, 1.0):
        sin = sin * sq + np.float32(term)
    sin = sin * half
    cos = np.float32(1.0 / 479001600)
    for term in (-1.0 / 3628800, 1.0 / 40320, -1.0 / 720, 1.0 / 24, -0.5, 1.0):
        cos = cos * sq + np.float32(term)
    return 1.0 - 2.0 * (sin * sin), 2.0 * (sin * cos)


def split_two(value):
    high = value.astype(BF16)
    low = (value - high.astype(F32)).astype(BF16)
    return high, low


def split_three(value):
    high = value.astype(BF16)
    rest = value - high.astype(F32)
    mid = rest.astype(BF16)
    low = (rest - mid.astype(F32)).astype(BF16)
    return high, mid, low


def dot(left, right):
    return jnp.dot(left, right, preferred_element_type=F32)


def times(left, right):
    (lr, li), (rr, ri) = left, right
    return lr * rr - li * ri, lr * ri + li * rr


def phase_rows(delays, anchor, width):
    place = iota((8, 1), 0)
    second = place >= 4.0
    turns = jnp.where(second, delays[1], delays[0])
    at = anchor + float(STEPS_PER_TURN) * jnp.where(second, place - 4.0, place)
    base = sincos_turns(turns * (at * np.float32(1.0 / STEPS_PER_TURN)))
    fine, coarse = [], []
    for s in range(2):
        low = sincos_turns(delays[s] * (place * np.float32(1.0 / STEPS_PER_TURN)))
        high = low
        for doubling in range(3):
            high = times(high, high)
        rows = [times(tuple(part[4 * s + a:4 * s + a + 1] for part in base), high)
                for a in range(width // STEPS_PER_TURN)]
        fine.append(low)
        coarse.append(rows)
    return fine, coarse


def tiles(pairs, body):
    full = pairs // 128

    def step(tile, carry):
        body(pl.ds(pl.multiple_of(tile * 128, 128), 128), 128)
        return carry

    lax.fori_loop(0, full, step, 0)
    if pairs % 128:
        body(pl.ds(full * 128, pairs % 128), pairs % 128)


def phase_kernel(width, t, reach, me_ref, *refs):
    anchor = me_ref[0].astype(F32) * float(width)
    if t == 0:
        delay_ref, small_ref, wave_ref, mix_ref, own_ref, win_out_ref = refs
    else:
        vis_hbm, delay_ref, win_ref, wave_ref, mix_ref, vis_ref, apart_ref, *mask_refs, sem = refs
        copy = pltpu.make_async_copy(vis_hbm.at[:, 0], vis_ref, sem)
        copy.start()
    if t == 0:
        own_ref[0] = small_ref[:2]
        win_out_ref[...] = small_ref[2:3, :win_out_ref.shape[1]]
    else:
        window_masks(width, reach, me_ref[0], win_ref, *mask_refs)
        apart = blocks_apart(me_ref[0], reach, apart_ref.shape[2])
        for time in range(2):
            gap = delay_ref[1, time:time + 1, :] - delay_ref[0, time:time + 1, :]
            phase = sincos_turns(gap * (apart * np.float32(width / STEPS_PER_TURN)))
            apart_ref[time, 0], apart_ref[time, 1] = phase
    pairs = delay_ref.shape[2]

    def waves(lanes, count):
        delays = [delay_ref[s, t:t + 1, lanes] for s in range(2)]
        fine, coarse = phase_rows(delays, anchor, width)
        for block in range(width // 16):
            found = []
            for s in range(2):
                halves = []
                for half in range(2):
                    a, b = divmod(2 * block + half, 8)
                    halves.append(times(tuple(part[b:b + 1] for part in coarse[s][a]), fine[s]))
                found.append([jnp.concatenate([h[ri] for h in halves], axis=0) for ri in range(2)])
            rows = slice(block * 16, block * 16 + 16)
            (r0, i0), (r1, i1) = found
            for s in range(2):
                for ri in range(2):
                    wave_ref[s, ri, rows, lanes] = found[s][ri]
            for slot, value in enumerate((r1 * r0 + i1 * i0, i1 * r0 - r1 * i0)):
                high, low = split_two(value)
                mix_ref[slot, 0, rows, lanes] = high
                mix_ref[slot, 1, rows, lanes] = low

    tiles(pairs, waves)
    if t == 1:
        copy.wait()


def blocks_apart(me, reach, rows):
    return iota((rows, 1), 0) - (lax.rem(me, reach) + reach).astype(F32)


def window_masks(width, reach, me, win_ref, inside_ref, chosen_ref, outside_ref, ends_ref):
    anchor = me.astype(F32) * float(width)
    lowest = (me - lax.rem(me, reach) - reach).astype(F32)
    windows = inside_ref.shape[0]
    final = anchor + float(width - 1)
    win_row = win_ref[...].astype(F32)
    sub, lane = iota((windows, windows), 0), iota((windows, windows), 1)
    end_c = jnp.sum(jnp.where(lane <= sub, win_row, 0.0), axis=1, keepdims=True)
    start_c = jnp.sum(jnp.where(lane < sub, win_row, 0.0), axis=1, keepdims=True)
    win_c = end_c - start_c
    end_r = jnp.sum(jnp.where(sub <= lane, win_c, 0.0), axis=0, keepdims=True)
    start_r = jnp.sum(jnp.where(sub < lane, win_c, 0.0), axis=0, keepdims=True)
    first_c = jnp.where((start_c <= anchor) & (anchor < end_c), 1.0, 0.0)
    last_c = jnp.where((start_c <= final) & (final < end_c), 1.0, 0.0)
    from_first = jnp.sum(first_c * start_c, axis=0, keepdims=True)
    to_last = jnp.sum(last_c * end_c, axis=0, keepdims=True)
    here = anchor + iota((windows, width), 1)
    inside_ref[...] = jnp.where((here >= start_c) & (here < end_c), 1.0, 0.0)
    there = anchor + iota((width, windows), 0)
    chosen_ref[...] = jnp.where((there >= start_r) & (there < end_r), 1.0, 0.0)
    shape = outside_ref.shape
    channel = (lowest + iota(shape, 0)) * float(width) + iota(shape, 1)
    remote = ((channel < anchor) & (channel >= from_first)) | ((channel > final) & (channel < to_last))
    outside_ref[...] = jnp.where(remote, 1.0, 0.0)
    ends_ref[0] = jnp.broadcast_to(first_c, ends_ref.shape[1:])
    ends_ref[1] = jnp.broadcast_to(last_c, ends_ref.shape[1:])


def sums_kernel(width, reach, me_ref, *refs):
    flag_refs, refs = refs[:3], refs[3:]
    apart_ref, inside_ref, chosen_ref, outside_ref, ends_ref = refs[:5]
    vis_hbm, first_ref, wave_refs, mix_refs, refs = refs[5], refs[6], refs[7:9], refs[9:11], refs[11:]
    out_refs, (second_ref, alpha_s, mexp_s, wt_s, sem) = refs[:4], refs[4:]
    vis_refs = (first_ref, second_ref)
    copy = pltpu.make_async_copy(vis_hbm.at[:, 1], second_ref, sem)
    copy.start()
    me = me_ref[0]
    place = lax.rem(me, reach)
    windows = inside_ref.shape[0]
    pairs = apart_ref.shape[3]
    sub, lane = iota((windows, windows), 0), iota((windows, windows), 1)
    first_c, last_c = ends_ref[0][:, :1], ends_ref[1][:, :1]
    apart = blocks_apart(me, reach, outside_ref.shape[0])
    diagonal = iota((width, width), 0) == iota((width, width), 1)
    wt_s[...] = jnp.zeros_like(wt_s)

    def both_sides(value):
        return (jnp.sum(jnp.where(apart < 0.0, value, 0.0), axis=0, keepdims=True),
                jnp.sum(jnp.where(apart > 0.0, value, 0.0), axis=0, keepdims=True))

    for t in range(2):
        mine = lax.div(me, reach)
        for group, other in enumerate((mine, lax.bitwise_xor(mine, 1), lax.bitwise_xor(mine, 3))):
            side = jnp.where(jnp.abs(other - mine) > 1, 3, other - mine + 1)
            for slot in range(reach):
                row = flag_refs[group][slot, t:t + 1, :].astype(F32)
                wt_s[t, pl.ds(side * reach + lax.bitwise_xor(place, slot), 1), :] = 1.0 - row
        own = 1.0 - flag_refs[0][0, t:t + 1, :].astype(F32)
        inside = inside_ref[...] * own
        outside = outside_ref[...] * wt_s[t]
        before, after = both_sides(jnp.sum(outside, axis=1, keepdims=True))
        count = jnp.sum(inside, axis=1, keepdims=True) + first_c * before + last_c * after
        scale = 1.0 / jnp.maximum(count, 1.0)
        rows = jnp.concatenate([inside, outside], axis=0).astype(BF16)
        scale_r = jnp.sum(jnp.where(sub == lane, scale, 0.0), axis=0, keepdims=True)
        own_c = jnp.sum(jnp.where(diagonal, own, 0.0), axis=1, keepdims=True)
        chosen = chosen_ref[...] * own_c
        alpha_s[t] = jnp.broadcast_to(jnp.sum(chosen * scale_r, axis=1, keepdims=True), (width, 128))
        chosen = chosen.astype(BF16)
        sums = [dot(rows, mix_refs[t][slot, 0]) + dot(rows, mix_refs[t][slot, 1]) for slot in range(2)]
        away = times((apart_ref[t, 0], apart_ref[t, 1]), tuple(value[windows:] for value in sums))
        for slot in range(2):
            before, after = both_sides(away[slot])
            total = sums[slot][:windows] + first_c * before + last_c * after
            high, low = split_two(total * (scale * scale))
            mexp_s[t, slot] = dot(chosen, high) + dot(chosen, low)

    for t in range(2):
        def main(lanes, count):
            def step(block, sums):
                rows = pl.ds(pl.multiple_of(block * 16, 16), 16)
                alpha = alpha_s[t, rows, :count]
                mr, mi = mexp_s[t, 0, rows, lanes], mexp_s[t, 1, rows, lanes]
                r0, i0 = wave_refs[t][0, 0, rows, lanes], wave_refs[t][0, 1, rows, lanes]
                r1, i1 = wave_refs[t][1, 0, rows, lanes], wave_refs[t][1, 1, rows, lanes]
                factors = []
                for fr, fi in (
                    (alpha * r0 - (mr * r1 + mi * i1), (mr * i1 - mi * r1) - alpha * i0),
                    (alpha * r1 - (mr * r0 - mi * i0), (mr * i0 + mi * r0) - alpha * i1),
                ):
                    factors.append((fr, fi - fr, fr + fi))
                new = []
                for k in range(4):
                    vr = vis_refs[t][0, k, rows, lanes].astype(F32)
                    vi = vis_refs[t][1, k, rows, lanes].astype(F32)
                    vs = vr + vi
                    for s in range(2):
                        for v, f in zip((vs, vr, vi), factors[s]):
                            product = v * f
                            new.append(sums[len(new)] + (product[:8] + product[8:]))
                return tuple(new)

            zero = jnp.zeros((8, count), F32)
            sums = lax.fori_loop(0, width // 16, step, (zero,) * 24, unroll=6)
            for s in range(2):
                owner = lax.bitwise_xor(lax.bitwise_and(me, 3), t + 2 * s)
                found = []
                for k in range(4):
                    one, two, three = sums[(k * 2 + s) * 3:(k * 2 + s) * 3 + 3]
                    found.append([jnp.sum(value, axis=0, keepdims=True) for value in (one - three, one + two)])
                for d in range(4):
                    @pl.when(owner == d)
                    def write():
                        for k in range(4):
                            for ri in range(2):
                                out_refs[d][k, ri:ri + 1, lanes] = found[k][ri]

        if t == 1:
            copy.wait()
        tiles(pairs, main)


def station_hots(pairs):
    station, baseline = iota((ROWS, 1), 0), iota((1, pairs), 1)
    offset = station * (float(2 * STATIONS - 1) - station) * 0.5
    after = (station + 1.0) * (float(2 * STATIONS - 2) - station) * 0.5
    first = jnp.where((baseline >= offset) & (baseline < after), 1.0, 0.0)
    partner_of = baseline + 1.0 + jnp.sum(first * (station - offset), axis=0, keepdims=True)
    second = jnp.where(partner_of == station, 1.0, 0.0)
    return first.astype(BF16), second.astype(BF16)


def hots_kernel(hot_ref):
    hot_ref[0], hot_ref[1] = station_hots(hot_ref.shape[2])


def solve_kernel(window_count, me_ref, tracks_ref, hot_ref, *refs):
    parts, gain_ref = refs[:-1], refs[-1]
    me = me_ref[0]
    systems = gain_ref.shape[0]
    total = [part[...] for part in parts]
    while len(total) > 1:
        total = [total[i] + total[i + 1] for i in range(0, len(total), 2)]
    total = total[0]
    hot, other = hot_ref[0], hot_ref[1]
    nt = lambda left, right: lax.dot_general(
        left, right, (((1,), (1,)), ((), ())), preferred_element_type=F32)
    upper, lower = [], []
    for system in range(systems):
        for ri in range(2):
            for piece in split_two(total[system, ri:ri + 1]):
                upper.append(hot * piece)
                lower.append(other * piece)
    upper = nt(jnp.concatenate(upper, axis=0), other)
    lower = nt(jnp.concatenate(lower, axis=0), hot)
    cut = lambda value, i: value[i * ROWS:(i + 1) * ROWS]
    join = lambda value, i: cut(value, 2 * i) + cut(value, 2 * i + 1)
    live_r = jnp.where(iota((1, ROWS), 1) < float(STATIONS), 1.0, 0.0)
    live_c = jnp.where(iota((ROWS, 1), 0) < float(STATIONS), 1.0, 0.0)
    matrices = [(join(upper, 2 * i) + join(lower, 2 * i), join(upper, 2 * i + 1) - join(lower, 2 * i + 1))
                for i in range(systems)]
    states = [(live_r, 0.0 * live_r, live_c, 0.0 * live_c)] * systems
    for turn in range(GITERS):
        for system in range(systems):
            re, im = matrices[system]
            row_re, row_im, col_re, col_im = states[system]
            pull_cr = jnp.sum(re * row_re - im * row_im, axis=1, keepdims=True)
            pull_ci = jnp.sum(re * row_im + im * row_re, axis=1, keepdims=True)
            pull_rr = jnp.sum(re * col_re + im * col_im, axis=0, keepdims=True)
            pull_ri = jnp.sum(re * col_im - im * col_re, axis=0, keepdims=True)
            power_r = row_re * row_re + row_im * row_im
            power_c = col_re * col_re + col_im * col_im
            total = jnp.sum(power_c, axis=0, keepdims=True)
            inverse_r = 0.5 / (window_count * (total - power_r) + DAMPING)
            inverse_c = 0.5 / (window_count * (total - power_c) + DAMPING)
            states[system] = (0.5 * row_re + pull_rr * inverse_r, 0.5 * row_im + pull_ri * inverse_r,
                              0.5 * col_re + pull_cr * inverse_c, 0.5 * col_im + pull_ci * inverse_c)
    visible = tracks_ref[lax.bitwise_and(lax.div(me, 2), 1), lax.bitwise_and(me, 1)].astype(F32)
    gains = [state[ri] * visible for state in states for ri in range(2)]
    gains = jnp.concatenate(gains, axis=0)
    stacked = jnp.concatenate([piece.astype(F32) for piece in split_three(gains)], axis=0).astype(BF16)
    ends = []
    for table in (hot, other):
        wide = dot(stacked, table)
        ends.append((wide[:8] + wide[8:16]) + wide[16:])
    pairs = hot.shape[1]
    for system in range(systems):
        (lr, li), (rr, ri_) = [[end[2 * system + ri:2 * system + ri + 1] for ri in range(2)] for end in ends]
        gain_ref[system, 0:1, :pairs] = lr * rr + li * ri_
        gain_ref[system, 1:2, :pairs] = li * rr - lr * ri_
        gain_ref[system, :, GAINS_AT:] = gains[2 * system:2 * system + 2, :STATIONS]


def clean_kernel(width, me_ref, *refs):
    vis_refs, wave_refs, piece_refs = refs[:2], refs[2:4], refs[4:8]
    out_hbm, gain_out_ref, out_s, model_s, sems = refs[8:]
    pairs = wave_refs[0].shape[3]
    mine = lax.bitwise_and(me_ref[0], 3)
    for d, piece in enumerate(piece_refs):
        owner = lax.bitwise_xor(mine, d)
        t, s = lax.bitwise_and(owner, 1), lax.div(owner, 2)
        for k in range(4):
            for ri in range(2):
                gain_out_ref[ri, s, t, k:k + 1, :] = piece[k, ri:ri + 1, GAINS_AT:]
            re, im = piece[k, 0:1, :pairs], piece[k, 1:2, :pairs]
            for slot, value in enumerate((re, im - re, re + im)):
                model_s[owner, 3 * k + slot:3 * k + slot + 1, :] = value

    half = width // 32 * 16
    quarter = half // 32 * 16
    pieces = [(0, 0, half), (0, half, width - half),
              (1, 0, half), (1, half, half - quarter), (1, 2 * half - quarter, width - 2 * half + quarter)]
    copies = []
    for t, start, length in pieces:
        def main(lanes, count):
            for block in range(length // 16):
                rows = slice(start + block * 16, start + block * 16 + 16)
                waves = []
                for s in range(2):
                    re, im = (wave_refs[t][s, ri, rows, lanes] for ri in range(2))
                    waves.append((re + im, re, im))
                for k in range(4):
                    sums = []
                    for slot in range(3):
                        one, two = (waves[s][slot] * model_s[t + 2 * s, 3 * k + slot:3 * k + slot + 1, lanes]
                                    for s in range(2))
                        sums.append(one + two)
                    vr = vis_refs[t][0, k, rows, lanes].astype(F32)
                    vi = vis_refs[t][1, k, rows, lanes].astype(F32)
                    out_s[0, t, k, rows, lanes] = (vr - (sums[0] - sums[2])).astype(BF16)
                    out_s[1, t, k, rows, lanes] = (vi - (sums[0] + sums[1])).astype(BF16)

        tiles(pairs, main)
        rows = pl.ds(start, length)
        copies.append(pltpu.make_async_copy(
            out_s.at[:, t, :, rows], out_hbm.at[:, t, :, rows], sems.at[len(copies)]))
        copies[-1].start()
    for copy in copies:
        copy.wait()


def partner(value, bits):
    count = lax.axis_size("sub")
    return lax.ppermute(value, "sub", [(i, i ^ bits) for i in range(count)])


def smem():
    return pl.BlockSpec(memory_space=pltpu.SMEM)


def local(visibilities, delays, flags, windows, tracks):
    width = visibilities.shape[4]
    pairs = visibilities.shape[3]
    count = lax.axis_size("sub")
    window_count = windows.shape[0]
    turned = jnp.transpose(visibilities, (0, 1, 2, 4, 3))
    me = lax.axis_index("sub").astype(jnp.int32).reshape(1)
    vmem_ref = pl.BlockSpec(memory_space=pltpu.VMEM)
    hbm_ref = pl.BlockSpec(memory_space=pltpu.HBM)
    vmem = lambda *shape: pltpu.VMEM(shape, F32)
    params = pltpu.CompilerParams(vmem_limit_bytes=24 * 2 ** 20)
    flags = flags[None]

    reach = count // 4
    remote_rows = 16 * pl.cdiv(4 * reach, 16)

    hots = pl.pallas_call(
        hots_kernel,
        out_specs=vmem_ref,
        out_shape=jax.ShapeDtypeStruct((2, ROWS, pairs), BF16),
        compiler_params=params,
        cost_estimate=pl.CostEstimate(flops=10 ** 7, bytes_accessed=6 * 2 ** 20, transcendentals=0),
        name="station_hots",
    )()
    small = jnp.pad(flags[0], ((0, 1), (0, 0))) + jnp.pad(windows[None], ((2, 0), (0, width - window_count)))
    made = []
    beside = [partner(flags, d) for d in range(1, 4)]
    for t in range(2):
        shape = lambda *dims: jax.ShapeDtypeStruct(dims, F32)
        out_shape = [
            shape(2, 2, width, pairs),
            jax.ShapeDtypeStruct((2, 2, width, pairs), BF16),
        ]
        if t == 0:
            operands = (me, delays, small)
            in_specs = [smem()] + [vmem_ref] * 2
            out_shape += [jax.ShapeDtypeStruct(flags.shape, flags.dtype),
                          jax.ShapeDtypeStruct((1, window_count), windows.dtype)]
        else:
            operands = (me, turned, delays, made[0][3])
            in_specs = [smem(), hbm_ref] + [vmem_ref] * 2
            out_shape += [jax.ShapeDtypeStruct((2, 4, width, pairs), BF16),
                          shape(2, 2, remote_rows, pairs), shape(window_count, width), shape(width, window_count),
                          shape(remote_rows, width), shape(2, window_count, 128)]
        made.append(pl.pallas_call(
            lambda *refs: phase_kernel(width, t, reach, *refs),
            in_specs=in_specs,
            out_specs=[vmem_ref] * len(out_shape),
            out_shape=out_shape,
            scratch_shapes=[pltpu.SemaphoreType.DMA] * t,
            compiler_params=pltpu.CompilerParams(vmem_limit_bytes=GRANTS[t] * 2 ** 20),
            cost_estimate=pl.CostEstimate(flops=10 ** 7, bytes_accessed=6 * 2 ** 20, transcendentals=0),
            name="phases",
        )(*operands))
        if t == 0:
            gathered = jnp.concatenate([made[0][2]] + beside, axis=0)
            while gathered.shape[0] < reach:
                stride = gathered.shape[0]
                gathered = jnp.concatenate([gathered] + [partner(gathered, stride * d) for d in range(1, 4)], axis=0)
            middle = [(i, i ^ (3 * reach)) for i in range(count) if reach <= i < 3 * reach]
            beyond = lax.ppermute(gathered, "sub", middle)
            gathered = [gathered, partner(gathered, reach), beyond]
    waves, mixing = ([part[i] for part in made] for i in range(2))
    held, *masks = made[1][2:]
    *quarters, held_too = pl.pallas_call(
        lambda *refs: sums_kernel(width, reach, *refs),
        in_specs=[smem()] + [vmem_ref] * 8 + [hbm_ref] + [vmem_ref] * 5,
        out_specs=[vmem_ref] * 5,
        out_shape=[jax.ShapeDtypeStruct((4, 2, pairs), F32)] * 4 + [jax.ShapeDtypeStruct(held.shape, BF16)],
        scratch_shapes=[vmem(2, width, 128), vmem(2, 2, width, pairs), vmem(2, remote_rows, width),
                        pltpu.SemaphoreType.DMA],
        compiler_params=pltpu.CompilerParams(vmem_limit_bytes=GRANT * 2 ** 20),
        name="window_sums",
    )(me, *gathered, *masks, turned, held, *waves, *mixing)
    pieces = [quarters[0]] + [partner(quarters[d], d) for d in range(1, 4)]
    stride = 4
    while stride < count:
        while len(pieces) > 1:
            pieces = [pieces[i] + pieces[i + 1] for i in range(0, len(pieces), 2)]
        pieces += [partner(pieces[0], stride * d) for d in range(1, min(4, count // stride))]
        stride *= 4
    model = pl.pallas_call(
        lambda *refs: solve_kernel(float(window_count), *refs),
        in_specs=[smem(), smem()] + [vmem_ref] * (1 + len(pieces)),
        out_specs=vmem_ref,
        out_shape=jax.ShapeDtypeStruct((4, 2, GAINS_AT + STATIONS), F32),
        compiler_params=params,
        name="gain_solve",
    )(me, tracks, hots, *pieces)
    model = [model] + [partner(model, d) for d in range(1, 4)]
    cleaned, gains = pl.pallas_call(
        lambda *refs: clean_kernel(width, *refs),
        in_specs=[smem()] + [vmem_ref] * 8,
        out_specs=[hbm_ref, vmem_ref],
        out_shape=[
            jax.ShapeDtypeStruct(turned.shape, BF16),
            jax.ShapeDtypeStruct((2, 2, 2, 4, STATIONS), F32),
        ],
        scratch_shapes=[
            pltpu.VMEM(turned.shape, BF16),
            vmem(4, 16, pairs),
            pltpu.SemaphoreType.DMA((5,)),
        ],
        compiler_params=params,
        name="clean",
    )(me, held, held_too, *waves, *model)
    return jnp.transpose(cleaned, (0, 1, 2, 4, 3)), gains


def solution(mesh):
    return jax.shard_map(
        local,
        mesh=mesh,
        in_specs=(
            P(None, "obs", None, None, "sub"),
            P(None, "obs", None),
            P("obs", "sub"),
            P(),
            P(None, "obs"),
        ),
        out_specs=(P(None, "obs", None, None, "sub"), P(None, None, "obs", None, None)),
        check_vma=False,
    )
```

```python
import jax
import jax.numpy as jnp
import numpy as np
from jax import lax
from jax.experimental import pallas as pl
from jax.experimental.pallas import tpu as pltpu
from jax.sharding import PartitionSpec as P

STATIONS = 38
GITERS = 8
DAMPING = 1.0
STEPS_PER_TURN = 64
GAINS_AT = 768
GRANT = 42
GRANTS = (47, 45)
ROWS = 40

F32 = jnp.float32
BF16 = jnp.bfloat16


def iota(shape, dim):
    return lax.broadcasted_iota(jnp.int32, shape, dim).astype(F32)


def sincos_turns(turns):
    half = (turns - jnp.floor(turns + 0.5)) * np.float32(np.pi)
    sq = half * half
    sin = np.float32(-1.0 / 39916800)
    for term in (1.0 / 362880, -1.0 / 5040, 1.0 / 120, -1.0 / 6, 1.0):
        sin = sin * sq + np.float32(term)
    sin = sin * half
    cos = np.float32(1.0 / 479001600)
    for term in (-1.0 / 3628800, 1.0 / 40320, -1.0 / 720, 1.0 / 24, -0.5, 1.0):
        cos = cos * sq + np.float32(term)
    return 1.0 - 2.0 * (sin * sin), 2.0 * (sin * cos)


def split_two(value):
    high = value.astype(BF16)
    low = (value - high.astype(F32)).astype(BF16)
    return high, low


def split_three(value):
    high = value.astype(BF16)
    rest = value - high.astype(F32)
    mid = rest.astype(BF16)
    low = (rest - mid.astype(F32)).astype(BF16)
    return high, mid, low


def dot(left, right):
    return jnp.dot(left, right, preferred_element_type=F32)


def times(left, right):
    (lr, li), (rr, ri) = left, right
    return lr * rr - li * ri, lr * ri + li * rr


def phase_rows(delays, anchor, width):
    place = iota((8, 1), 0)
    second = place >= 4.0
    turns = jnp.where(second, delays[1], delays[0])
    at = anchor + float(STEPS_PER_TURN) * jnp.where(second, place - 4.0, place)
    base = sincos_turns(turns * (at * np.float32(1.0 / STEPS_PER_TURN)))
    fine, coarse = [], []
    for s in range(2):
        low = sincos_turns(delays[s] * (place * np.float32(1.0 / STEPS_PER_TURN)))
        high = low
        for doubling in range(3):
            high = times(high, high)
        rows = [times(tuple(part[4 * s + a:4 * s + a + 1] for part in base), high)
                for a in range(width // STEPS_PER_TURN)]
        fine.append(low)
        coarse.append(rows)
    return fine, coarse


def tiles(pairs, body):
    full = pairs // 128

    def step(tile, carry):
        body(pl.ds(pl.multiple_of(tile * 128, 128), 128), 128)
        return carry

    lax.fori_loop(0, full, step, 0)
    if pairs % 128:
        body(pl.ds(full * 128, pairs % 128), pairs % 128)


def phase_kernel(width, t, reach, me_ref, *refs):
    anchor = me_ref[0].astype(F32) * float(width)
    if t == 0:
        delay_ref, small_ref, wave_ref, mix_ref, own_ref, win_out_ref = refs
    else:
        vis_hbm, delay_ref, win_ref, wave_ref, mix_ref, vis_ref, apart_ref, *mask_refs, sem = refs
        copy = pltpu.make_async_copy(vis_hbm.at[:, 0], vis_ref, sem)
        copy.start()
    if t == 0:
        own_ref[0] = small_ref[:2]
        win_out_ref[...] = small_ref[2:3, :win_out_ref.shape[1]]
    else:
        window_masks(width, reach, me_ref[0], win_ref, *mask_refs)
        apart = blocks_apart(me_ref[0], reach, apart_ref.shape[2])
        for time in range(2):
            gap = delay_ref[1, time:time + 1, :] - delay_ref[0, time:time + 1, :]
            phase = sincos_turns(gap * (apart * np.float32(width / STEPS_PER_TURN)))
            apart_ref[time, 0], apart_ref[time, 1] = phase
    pairs = delay_ref.shape[2]

    def waves(lanes, count):
        delays = [delay_ref[s, t:t + 1, lanes] for s in range(2)]
        fine, coarse = phase_rows(delays, anchor, width)
        for block in range(width // 16):
            found = []
            for s in range(2):
                halves = []
                for half in range(2):
                    a, b = divmod(2 * block + half, 8)
                    halves.append(times(tuple(part[b:b + 1] for part in coarse[s][a]), fine[s]))
                found.append([jnp.concatenate([h[ri] for h in halves], axis=0) for ri in range(2)])
            rows = slice(block * 16, block * 16 + 16)
            (r0, i0), (r1, i1) = found
            for s in range(2):
                for ri in range(2):
                    wave_ref[s, ri, rows, lanes] = found[s][ri]
            for slot, value in enumerate((r1 * r0 + i1 * i0, i1 * r0 - r1 * i0)):
                high, low = split_two(value)
                mix_ref[slot, 0, rows, lanes] = high
                mix_ref[slot, 1, rows, lanes] = low

    tiles(pairs, waves)
    if t == 1:
        copy.wait()


def blocks_apart(me, reach, rows):
    return iota((rows, 1), 0) - (lax.rem(me, reach) + reach).astype(F32)


def window_masks(width, reach, me, win_ref, inside_ref, chosen_ref, outside_ref, ends_ref):
    anchor = me.astype(F32) * float(width)
    lowest = (me - lax.rem(me, reach) - reach).astype(F32)
    windows = inside_ref.shape[0]
    final = anchor + float(width - 1)
    win_row = win_ref[...].astype(F32)
    sub, lane = iota((windows, windows), 0), iota((windows, windows), 1)
    end_c = jnp.sum(jnp.where(lane <= sub, win_row, 0.0), axis=1, keepdims=True)
    start_c = jnp.sum(jnp.where(lane < sub, win_row, 0.0), axis=1, keepdims=True)
    win_c = end_c - start_c
    end_r = jnp.sum(jnp.where(sub <= lane, win_c, 0.0), axis=0, keepdims=True)
    start_r = jnp.sum(jnp.where(sub < lane, win_c, 0.0), axis=0, keepdims=True)
    first_c = jnp.where((start_c <= anchor) & (anchor < end_c), 1.0, 0.0)
    last_c = jnp.where((start_c <= final) & (final < end_c), 1.0, 0.0)
    from_first = jnp.sum(first_c * start_c, axis=0, keepdims=True)
    to_last = jnp.sum(last_c * end_c, axis=0, keepdims=True)
    here = anchor + iota((windows, width), 1)
    inside_ref[...] = jnp.where((here >= start_c) & (here < end_c), 1.0, 0.0)
    there = anchor + iota((width, windows), 0)
    chosen_ref[...] = jnp.where((there >= start_r) & (there < end_r), 1.0, 0.0)
    shape = outside_ref.shape
    channel = (lowest + iota(shape, 0)) * float(width) + iota(shape, 1)
    remote = ((channel < anchor) & (channel >= from_first)) | ((channel > final) & (channel < to_last))
    outside_ref[...] = jnp.where(remote, 1.0, 0.0)
    ends_ref[0] = jnp.broadcast_to(first_c, ends_ref.shape[1:])
    ends_ref[1] = jnp.broadcast_to(last_c, ends_ref.shape[1:])


def sums_kernel(width, reach, me_ref, *refs):
    flag_refs, refs = refs[:3], refs[3:]
    apart_ref, inside_ref, chosen_ref, outside_ref, ends_ref = refs[:5]
    vis_hbm, first_ref, wave_refs, mix_refs, refs = refs[5], refs[6], refs[7:9], refs[9:11], refs[11:]
    out_refs, (second_ref, alpha_s, mexp_s, wt_s, sem) = refs[:4], refs[4:]
    vis_refs = (first_ref, second_ref)
    copy = pltpu.make_async_copy(vis_hbm.at[:, 1], second_ref, sem)
    copy.start()
    me = me_ref[0]
    place = lax.rem(me, reach)
    windows = inside_ref.shape[0]
    pairs = apart_ref.shape[3]
    sub, lane = iota((windows, windows), 0), iota((windows, windows), 1)
    first_c, last_c = ends_ref[0][:, :1], ends_ref[1][:, :1]
    apart = blocks_apart(me, reach, outside_ref.shape[0])
    diagonal = iota((width, width), 0) == iota((width, width), 1)
    wt_s[...] = jnp.zeros_like(wt_s)

    def both_sides(value):
        return (jnp.sum(jnp.where(apart < 0.0, value, 0.0), axis=0, keepdims=True),
                jnp.sum(jnp.where(apart > 0.0, value, 0.0), axis=0, keepdims=True))

    for t in range(2):
        mine = lax.div(me, reach)
        for group, other in enumerate((mine, lax.bitwise_xor(mine, 3), lax.bitwise_xor(mine, 1))):
            side = jnp.where(jnp.abs(other - mine) > 1, 3, other - mine + 1)
            for slot in range(reach):
                row = flag_refs[group][slot, t:t + 1, :].astype(F32)
                wt_s[t, pl.ds(side * reach + lax.bitwise_xor(place, slot), 1), :] = 1.0 - row
        own = 1.0 - flag_refs[0][0, t:t + 1, :].astype(F32)
        inside = inside_ref[...] * own
        outside = outside_ref[...] * wt_s[t]
        before, after = both_sides(jnp.sum(outside, axis=1, keepdims=True))
        count = jnp.sum(inside, axis=1, keepdims=True) + first_c * before + last_c * after
        scale = 1.0 / jnp.maximum(count, 1.0)
        rows = jnp.concatenate([inside, outside], axis=0).astype(BF16)
        scale_r = jnp.sum(jnp.where(sub == lane, scale, 0.0), axis=0, keepdims=True)
        own_c = jnp.sum(jnp.where(diagonal, own, 0.0), axis=1, keepdims=True)
        chosen = chosen_ref[...] * own_c
        alpha_s[t] = jnp.broadcast_to(jnp.sum(chosen * scale_r, axis=1, keepdims=True), (width, 128))
        chosen = chosen.astype(BF16)
        sums = [dot(rows, mix_refs[t][slot, 0]) + dot(rows, mix_refs[t][slot, 1]) for slot in range(2)]
        away = times((apart_ref[t, 0], apart_ref[t, 1]), tuple(value[windows:] for value in sums))
        for slot in range(2):
            before, after = both_sides(away[slot])
            total = sums[slot][:windows] + first_c * before + last_c * after
            high, low = split_two(total * (scale * scale))
            mexp_s[t, slot] = dot(chosen, high) + dot(chosen, low)

    for t in range(2):
        def main(lanes, count):
            def step(block, sums):
                rows = pl.ds(pl.multiple_of(block * 16, 16), 16)
                alpha = alpha_s[t, rows, :count]
                mr, mi = mexp_s[t, 0, rows, lanes], mexp_s[t, 1, rows, lanes]
                r0, i0 = wave_refs[t][0, 0, rows, lanes], wave_refs[t][0, 1, rows, lanes]
                r1, i1 = wave_refs[t][1, 0, rows, lanes], wave_refs[t][1, 1, rows, lanes]
                factors = []
                for fr, fi in (
                    (alpha * r0 - (mr * r1 + mi * i1), (mr * i1 - mi * r1) - alpha * i0),
                    (alpha * r1 - (mr * r0 - mi * i0), (mr * i0 + mi * r0) - alpha * i1),
                ):
                    factors.append((fr, fi - fr, fr + fi))
                new = []
                for k in range(4):
                    vr = vis_refs[t][0, k, rows, lanes].astype(F32)
                    vi = vis_refs[t][1, k, rows, lanes].astype(F32)
                    vs = vr + vi
                    for s in range(2):
                        for v, f in zip((vs, vr, vi), factors[s]):
                            product = v * f
                            new.append(sums[len(new)] + (product[:8] + product[8:]))
                return tuple(new)

            zero = jnp.zeros((8, count), F32)
            sums = lax.fori_loop(0, width // 16, step, (zero,) * 24, unroll=12)
            for s in range(2):
                owner = lax.bitwise_xor(lax.bitwise_and(me, 3), t + 2 * s)
                found = []
                for k in range(4):
                    one, two, three = sums[(k * 2 + s) * 3:(k * 2 + s) * 3 + 3]
                    found.append([jnp.sum(value, axis=0, keepdims=True) for value in (one - three, one + two)])
                for d in range(4):
                    @pl.when(owner == d)
                    def write():
                        for k in range(4):
                            for ri in range(2):
                                out_refs[d][k, ri:ri + 1, lanes] = found[k][ri]

        if t == 1:
            copy.wait()
        tiles(pairs, main)


def station_hots(pairs):
    station, baseline = iota((ROWS, 1), 0), iota((1, pairs), 1)
    offset = station * (float(2 * STATIONS - 1) - station) * 0.5
    after = (station + 1.0) * (float(2 * STATIONS - 2) - station) * 0.5
    first = jnp.where((baseline >= offset) & (baseline < after), 1.0, 0.0)
    partner_of = baseline + 1.0 + jnp.sum(first * (station - offset), axis=0, keepdims=True)
    second = jnp.where(partner_of == station, 1.0, 0.0)
    return first.astype(BF16), second.astype(BF16)


def hots_kernel(hot_ref):
    hot_ref[0], hot_ref[1] = station_hots(hot_ref.shape[2])


def solve_kernel(window_count, me_ref, tracks_ref, hot_ref, *refs):
    parts, gain_ref = refs[:-1], refs[-1]
    me = me_ref[0]
    systems = gain_ref.shape[0]
    total = [part[...] for part in parts]
    while len(total) > 1:
        total = [total[i] + total[i + 1] for i in range(0, len(total), 2)]
    total = total[0]
    hot, other = hot_ref[0], hot_ref[1]
    nt = lambda left, right: lax.dot_general(
        left, right, (((1,), (1,)), ((), ())), preferred_element_type=F32)
    upper, lower = [], []
    for system in range(systems):
        for ri in range(2):
            for piece in split_two(total[system, ri:ri + 1]):
                upper.append(hot * piece)
                lower.append(other * piece)
    upper = nt(jnp.concatenate(upper, axis=0), other)
    lower = nt(jnp.concatenate(lower, axis=0), hot)
    cut = lambda value, i: value[i * ROWS:(i + 1) * ROWS]
    join = lambda value, i: cut(value, 2 * i) + cut(value, 2 * i + 1)
    live_r = jnp.where(iota((1, ROWS), 1) < float(STATIONS), 1.0, 0.0)
    live_c = jnp.where(iota((ROWS, 1), 0) < float(STATIONS), 1.0, 0.0)
    matrices = [(join(upper, 2 * i) + join(lower, 2 * i), join(upper, 2 * i + 1) - join(lower, 2 * i + 1))
                for i in range(systems)]
    states = [(live_r, 0.0 * live_r, live_c, 0.0 * live_c)] * systems
    for turn in range(GITERS):
        for system in range(systems):
            re, im = matrices[system]
            row_re, row_im, col_re, col_im = states[system]
            pull_cr = jnp.sum(re * row_re - im * row_im, axis=1, keepdims=True)
            pull_ci = jnp.sum(re * row_im + im * row_re, axis=1, keepdims=True)
            pull_rr = jnp.sum(re * col_re + im * col_im, axis=0, keepdims=True)
            pull_ri = jnp.sum(re * col_im - im * col_re, axis=0, keepdims=True)
            power_r = row_re * row_re + row_im * row_im
            power_c = col_re * col_re + col_im * col_im
            total = jnp.sum(power_c, axis=0, keepdims=True)
            inverse_r = 0.5 / (window_count * (total - power_r) + DAMPING)
            inverse_c = 0.5 / (window_count * (total - power_c) + DAMPING)
            states[system] = (0.5 * row_re + pull_rr * inverse_r, 0.5 * row_im + pull_ri * inverse_r,
                              0.5 * col_re + pull_cr * inverse_c, 0.5 * col_im + pull_ci * inverse_c)
    visible = tracks_ref[lax.bitwise_and(lax.div(me, 2), 1), lax.bitwise_and(me, 1)].astype(F32)
    gains = [state[ri] * visible for state in states for ri in range(2)]
    gains = jnp.concatenate(gains, axis=0)
    stacked = jnp.concatenate([piece.astype(F32) for piece in split_three(gains)], axis=0).astype(BF16)
    ends = []
    for table in (hot, other):
        wide = dot(stacked, table)
        ends.append((wide[:8] + wide[8:16]) + wide[16:])
    pairs = hot.shape[1]
    for system in range(systems):
        (lr, li), (rr, ri_) = [[end[2 * system + ri:2 * system + ri + 1] for ri in range(2)] for end in ends]
        gain_ref[system, 0:1, :pairs] = lr * rr + li * ri_
        gain_ref[system, 1:2, :pairs] = li * rr - lr * ri_
        gain_ref[system, :, GAINS_AT:] = gains[2 * system:2 * system + 2, :STATIONS]


def clean_kernel(width, me_ref, *refs):
    vis_refs, wave_refs, piece_refs = refs[:2], refs[2:4], refs[4:8]
    out_hbm, gain_out_ref, out_s, model_s, sems = refs[8:]
    pairs = wave_refs[0].shape[3]
    mine = lax.bitwise_and(me_ref[0], 3)
    for d, piece in enumerate(piece_refs):
        owner = lax.bitwise_xor(mine, d)
        t, s = lax.bitwise_and(owner, 1), lax.div(owner, 2)
        for k in range(4):
            for ri in range(2):
                gain_out_ref[ri, s, t, k:k + 1, :] = piece[k, ri:ri + 1, GAINS_AT:]
            re, im = piece[k, 0:1, :pairs], piece[k, 1:2, :pairs]
            for slot, value in enumerate((re, im - re, re + im)):
                model_s[owner, 3 * k + slot:3 * k + slot + 1, :] = value

    half = width // 32 * 16
    quarter = half // 32 * 16
    pieces = [(0, 0, half), (0, half, width - half),
              (1, 0, half), (1, half, half - quarter), (1, 2 * half - quarter, width - 2 * half + quarter)]
    copies = []
    for t, start, length in pieces:
        def main(lanes, count):
            for block in range(length // 16):
                rows = slice(start + block * 16, start + block * 16 + 16)
                waves = []
                for s in range(2):
                    re, im = (wave_refs[t][s, ri, rows, lanes] for ri in range(2))
                    waves.append((re + im, re, im))
                for k in range(4):
                    sums = []
                    for slot in range(3):
                        one, two = (waves[s][slot] * model_s[t + 2 * s, 3 * k + slot:3 * k + slot + 1, lanes]
                                    for s in range(2))
                        sums.append(one + two)
                    vr = vis_refs[t][0, k, rows, lanes].astype(F32)
                    vi = vis_refs[t][1, k, rows, lanes].astype(F32)
                    out_s[0, t, k, rows, lanes] = (vr - (sums[0] - sums[2])).astype(BF16)
                    out_s[1, t, k, rows, lanes] = (vi - (sums[0] + sums[1])).astype(BF16)

        tiles(pairs, main)
        rows = pl.ds(start, length)
        copies.append(pltpu.make_async_copy(
            out_s.at[:, t, :, rows], out_hbm.at[:, t, :, rows], sems.at[len(copies)]))
        copies[-1].start()
    for copy in copies:
        copy.wait()


def partner(value, bits):
    count = lax.axis_size("sub")
    return lax.ppermute(value, "sub", [(i, i ^ bits) for i in range(count)])


def smem():
    return pl.BlockSpec(memory_space=pltpu.SMEM)


def local(visibilities, delays, flags, windows, tracks):
    width = visibilities.shape[4]
    pairs = visibilities.shape[3]
    count = lax.axis_size("sub")
    window_count = windows.shape[0]
    turned = jnp.transpose(visibilities, (0, 1, 2, 4, 3))
    me = lax.axis_index("sub").astype(jnp.int32).reshape(1)
    vmem_ref = pl.BlockSpec(memory_space=pltpu.VMEM)
    hbm_ref = pl.BlockSpec(memory_space=pltpu.HBM)
    vmem = lambda *shape: pltpu.VMEM(shape, F32)
    params = pltpu.CompilerParams(vmem_limit_bytes=24 * 2 ** 20)
    flags = flags[None]

    reach = count // 4
    remote_rows = 16 * pl.cdiv(4 * reach, 16)

    hots = pl.pallas_call(
        hots_kernel,
        out_specs=vmem_ref,
        out_shape=jax.ShapeDtypeStruct((2, ROWS, pairs), BF16),
        compiler_params=params,
        cost_estimate=pl.CostEstimate(flops=10 ** 7, bytes_accessed=6 * 2 ** 20, transcendentals=0),
        name="station_hots",
    )()
    small = jnp.pad(flags[0], ((0, 1), (0, 0))) + jnp.pad(windows[None], ((2, 0), (0, width - window_count)))
    made = []
    beside = [partner(flags, d) for d in range(1, 4)]
    for t in range(2):
        shape = lambda *dims: jax.ShapeDtypeStruct(dims, F32)
        out_shape = [
            shape(2, 2, width, pairs),
            jax.ShapeDtypeStruct((2, 2, width, pairs), BF16),
        ]
        if t == 0:
            operands = (me, delays, small)
            in_specs = [smem()] + [vmem_ref] * 2
            out_shape += [jax.ShapeDtypeStruct(flags.shape, flags.dtype),
                          jax.ShapeDtypeStruct((1, window_count), windows.dtype)]
        else:
            operands = (me, turned, delays, made[0][3])
            in_specs = [smem(), hbm_ref] + [vmem_ref] * 2
            out_shape += [jax.ShapeDtypeStruct((2, 4, width, pairs), BF16),
                          shape(2, 2, remote_rows, pairs), shape(window_count, width), shape(width, window_count),
                          shape(remote_rows, width), shape(2, window_count, 128)]
        made.append(pl.pallas_call(
            lambda *refs: phase_kernel(width, t, reach, *refs),
            in_specs=in_specs,
            out_specs=[vmem_ref] * len(out_shape),
            out_shape=out_shape,
            scratch_shapes=[pltpu.SemaphoreType.DMA] * t,
            compiler_params=pltpu.CompilerParams(vmem_limit_bytes=GRANTS[t] * 2 ** 20),
            cost_estimate=pl.CostEstimate(flops=10 ** 7, bytes_accessed=6 * 2 ** 20, transcendentals=0),
            name="phases",
        )(*operands))
        if t == 0:
            gathered = jnp.concatenate([made[0][2]] + beside, axis=0)
            while gathered.shape[0] < reach:
                stride = gathered.shape[0]
                gathered = jnp.concatenate([gathered] + [partner(gathered, stride * d) for d in range(1, 4)], axis=0)
            middle = [(i, i ^ (3 * reach)) for i in range(count) if reach <= i < 3 * reach]
            beyond = lax.ppermute(gathered, "sub", middle)
            gathered = [gathered, beyond, partner(gathered, reach)]
    waves, mixing = ([part[i] for part in made] for i in range(2))
    held, *masks = made[1][2:]
    *quarters, held_too = pl.pallas_call(
        lambda *refs: sums_kernel(width, reach, *refs),
        in_specs=[smem()] + [vmem_ref] * 8 + [hbm_ref] + [vmem_ref] * 5,
        out_specs=[vmem_ref] * 5,
        out_shape=[jax.ShapeDtypeStruct((4, 2, pairs), F32)] * 4 + [jax.ShapeDtypeStruct(held.shape, BF16)],
        scratch_shapes=[vmem(2, width, 128), vmem(2, 2, width, pairs), vmem(2, remote_rows, width),
                        pltpu.SemaphoreType.DMA],
        compiler_params=pltpu.CompilerParams(vmem_limit_bytes=GRANT * 2 ** 20),
        name="window_sums",
    )(me, *gathered, *masks, turned, held, *waves, *mixing)
    pieces = [quarters[0]] + [partner(quarters[d], d) for d in range(1, 4)]
    stride = 4
    while stride < count:
        while len(pieces) > 1:
            pieces = [pieces[i] + pieces[i + 1] for i in range(0, len(pieces), 2)]
        pieces += [partner(pieces[0], stride * d) for d in range(1, min(4, count // stride))]
        stride *= 4
    model = pl.pallas_call(
        lambda *refs: solve_kernel(float(window_count), *refs),
        in_specs=[smem(), smem()] + [vmem_ref] * (1 + len(pieces)),
        out_specs=vmem_ref,
        out_shape=jax.ShapeDtypeStruct((4, 2, GAINS_AT + STATIONS), F32),
        compiler_params=params,
        name="gain_solve",
    )(me, tracks, hots, *pieces)
    model = [model] + [partner(model, d) for d in range(1, 4)]
    cleaned, gains = pl.pallas_call(
        lambda *refs: clean_kernel(width, *refs),
        in_specs=[smem()] + [vmem_ref] * 8,
        out_specs=[hbm_ref, vmem_ref],
        out_shape=[
            jax.ShapeDtypeStruct(turned.shape, BF16),
            jax.ShapeDtypeStruct((2, 2, 2, 4, STATIONS), F32),
        ],
        scratch_shapes=[
            pltpu.VMEM(turned.shape, BF16),
            vmem(4, 16, pairs),
            pltpu.SemaphoreType.DMA((5,)),
        ],
        compiler_params=params,
        name="clean",
    )(me, held, held_too, *waves, *model)
    return jnp.transpose(cleaned, (0, 1, 2, 4, 3)), gains


def solution(mesh):
    return jax.shard_map(
        local,
        mesh=mesh,
        in_specs=(
            P(None, "obs", None, None, "sub"),
            P(None, "obs", None),
            P("obs", "sub"),
            P(),
            P(None, "obs"),
        ),
        out_specs=(P(None, "obs", None, None, "sub"), P(None, None, "obs", None, None)),
        check_vma=False,
    )
```

```python
import jax
import jax.numpy as jnp
import numpy as np
from jax import lax
from jax.experimental import pallas as pl
from jax.experimental.pallas import tpu as pltpu
from jax.sharding import PartitionSpec as P

STATIONS = 38
GITERS = 8
DAMPING = 1.0
STEPS_PER_TURN = 64
GAINS_AT = 768
GRANT = 42
GRANTS = (47, 45)
ROWS = 40

F32 = jnp.float32
BF16 = jnp.bfloat16


def iota(shape, dim):
    return lax.broadcasted_iota(jnp.int32, shape, dim).astype(F32)


def sincos_turns(turns):
    half = (turns - jnp.floor(turns + 0.5)) * np.float32(np.pi)
    sq = half * half
    sin = np.float32(-1.0 / 39916800)
    for term in (1.0 / 362880, -1.0 / 5040, 1.0 / 120, -1.0 / 6, 1.0):
        sin = sin * sq + np.float32(term)
    sin = sin * half
    cos = np.float32(1.0 / 479001600)
    for term in (-1.0 / 3628800, 1.0 / 40320, -1.0 / 720, 1.0 / 24, -0.5, 1.0):
        cos = cos * sq + np.float32(term)
    return 1.0 - 2.0 * (sin * sin), 2.0 * (sin * cos)


def split_two(value):
    high = value.astype(BF16)
    low = (value - high.astype(F32)).astype(BF16)
    return high, low


def split_three(value):
    high = value.astype(BF16)
    rest = value - high.astype(F32)
    mid = rest.astype(BF16)
    low = (rest - mid.astype(F32)).astype(BF16)
    return high, mid, low


def dot(left, right):
    return jnp.dot(left, right, preferred_element_type=F32)


def times(left, right):
    (lr, li), (rr, ri) = left, right
    return lr * rr - li * ri, lr * ri + li * rr


def phase_rows(delays, anchor, width):
    place = iota((8, 1), 0)
    second = place >= 4.0
    turns = jnp.where(second, delays[1], delays[0])
    at = anchor + float(STEPS_PER_TURN) * jnp.where(second, place - 4.0, place)
    base = sincos_turns(turns * (at * np.float32(1.0 / STEPS_PER_TURN)))
    fine, coarse = [], []
    for s in range(2):
        low = sincos_turns(delays[s] * (place * np.float32(1.0 / STEPS_PER_TURN)))
        high = low
        for doubling in range(3):
            high = times(high, high)
        rows = [times(tuple(part[4 * s + a:4 * s + a + 1] for part in base), high)
                for a in range(width // STEPS_PER_TURN)]
        fine.append(low)
        coarse.append(rows)
    return fine, coarse


def tiles(pairs, body):
    full = pairs // 128

    def step(tile, carry):
        body(pl.ds(pl.multiple_of(tile * 128, 128), 128), 128)
        return carry

    lax.fori_loop(0, full, step, 0)
    if pairs % 128:
        body(pl.ds(full * 128, pairs % 128), pairs % 128)


def phase_kernel(width, t, reach, me_ref, *refs):
    anchor = me_ref[0].astype(F32) * float(width)
    if t == 0:
        delay_ref, small_ref, wave_ref, mix_ref, own_ref, win_out_ref = refs
    else:
        vis_hbm, delay_ref, win_ref, wave_ref, mix_ref, vis_ref, apart_ref, *mask_refs, sem = refs
        copy = pltpu.make_async_copy(vis_hbm.at[:, 0], vis_ref, sem)
        copy.start()
    if t == 0:
        own_ref[0] = small_ref[:2]
        win_out_ref[...] = small_ref[2:3, :win_out_ref.shape[1]]
    else:
        window_masks(width, reach, me_ref[0], win_ref, *mask_refs)
        apart = blocks_apart(me_ref[0], reach, apart_ref.shape[2])
        for time in range(2):
            gap = delay_ref[1, time:time + 1, :] - delay_ref[0, time:time + 1, :]
            phase = sincos_turns(gap * (apart * np.float32(width / STEPS_PER_TURN)))
            apart_ref[time, 0], apart_ref[time, 1] = phase
    pairs = delay_ref.shape[2]

    def waves(lanes, count):
        delays = [delay_ref[s, t:t + 1, lanes] for s in range(2)]
        fine, coarse = phase_rows(delays, anchor, width)
        for block in range(width // 16):
            found = []
            for s in range(2):
                halves = []
                for half in range(2):
                    a, b = divmod(2 * block + half, 8)
                    halves.append(times(tuple(part[b:b + 1] for part in coarse[s][a]), fine[s]))
                found.append([jnp.concatenate([h[ri] for h in halves], axis=0) for ri in range(2)])
            rows = slice(block * 16, block * 16 + 16)
            (r0, i0), (r1, i1) = found
            for s in range(2):
                for ri in range(2):
                    wave_ref[s, ri, rows, lanes] = found[s][ri]
            for slot, value in enumerate((r1 * r0 + i1 * i0, i1 * r0 - r1 * i0)):
                high, low = split_two(value)
                mix_ref[slot, 0, rows, lanes] = high
                mix_ref[slot, 1, rows, lanes] = low

    tiles(pairs, waves)
    if t == 1:
        copy.wait()


def blocks_apart(me, reach, rows):
    return iota((rows, 1), 0) - (lax.rem(me, reach) + reach).astype(F32)


def window_masks(width, reach, me, win_ref, inside_ref, chosen_ref, outside_ref, ends_ref):
    anchor = me.astype(F32) * float(width)
    lowest = (me - lax.rem(me, reach) - reach).astype(F32)
    windows = inside_ref.shape[0]
    final = anchor + float(width - 1)
    win_row = win_ref[...].astype(F32)
    sub, lane = iota((windows, windows), 0), iota((windows, windows), 1)
    end_c = jnp.sum(jnp.where(lane <= sub, win_row, 0.0), axis=1, keepdims=True)
    start_c = jnp.sum(jnp.where(lane < sub, win_row, 0.0), axis=1, keepdims=True)
    win_c = end_c - start_c
    end_r = jnp.sum(jnp.where(sub <= lane, win_c, 0.0), axis=0, keepdims=True)
    start_r = jnp.sum(jnp.where(sub < lane, win_c, 0.0), axis=0, keepdims=True)
    first_c = jnp.where((start_c <= anchor) & (anchor < end_c), 1.0, 0.0)
    last_c = jnp.where((start_c <= final) & (final < end_c), 1.0, 0.0)
    from_first = jnp.sum(first_c * start_c, axis=0, keepdims=True)
    to_last = jnp.sum(last_c * end_c, axis=0, keepdims=True)
    here = anchor + iota((windows, width), 1)
    inside_ref[...] = jnp.where((here >= start_c) & (here < end_c), 1.0, 0.0)
    there = anchor + iota((width, windows), 0)
    chosen_ref[...] = jnp.where((there >= start_r) & (there < end_r), 1.0, 0.0)
    shape = outside_ref.shape
    channel = (lowest + iota(shape, 0)) * float(width) + iota(shape, 1)
    remote = ((channel < anchor) & (channel >= from_first)) | ((channel > final) & (channel < to_last))
    outside_ref[...] = jnp.where(remote, 1.0, 0.0)
    ends_ref[0] = jnp.broadcast_to(first_c, ends_ref.shape[1:])
    ends_ref[1] = jnp.broadcast_to(last_c, ends_ref.shape[1:])


def sums_kernel(width, reach, me_ref, *refs):
    flag_refs, refs = refs[:3], refs[3:]
    apart_ref, inside_ref, chosen_ref, outside_ref, ends_ref = refs[:5]
    vis_hbm, first_ref, wave_refs, mix_refs, refs = refs[5], refs[6], refs[7:9], refs[9:11], refs[11:]
    out_refs, (second_ref, alpha_s, mexp_s, wt_s, sem) = refs[:4], refs[4:]
    vis_refs = (first_ref, second_ref)
    copy = pltpu.make_async_copy(vis_hbm.at[:, 1], second_ref, sem)
    copy.start()
    me = me_ref[0]
    place = lax.rem(me, reach)
    windows = inside_ref.shape[0]
    pairs = apart_ref.shape[3]
    sub, lane = iota((windows, windows), 0), iota((windows, windows), 1)
    first_c, last_c = ends_ref[0][:, :1], ends_ref[1][:, :1]
    apart = blocks_apart(me, reach, outside_ref.shape[0])
    diagonal = iota((width, width), 0) == iota((width, width), 1)
    wt_s[...] = jnp.zeros_like(wt_s)

    def both_sides(value):
        return (jnp.sum(jnp.where(apart < 0.0, value, 0.0), axis=0, keepdims=True),
                jnp.sum(jnp.where(apart > 0.0, value, 0.0), axis=0, keepdims=True))

    for t in range(2):
        mine = lax.div(me, reach)
        for group, other in enumerate((mine, lax.bitwise_xor(mine, 3), lax.bitwise_xor(mine, 1))):
            side = jnp.where(jnp.abs(other - mine) > 1, 3, other - mine + 1)
            for slot in range(reach):
                row = flag_refs[group][slot, t:t + 1, :].astype(F32)
                wt_s[t, pl.ds(side * reach + lax.bitwise_xor(place, slot), 1), :] = 1.0 - row
        own = 1.0 - flag_refs[0][0, t:t + 1, :].astype(F32)
        inside = inside_ref[...] * own
        outside = outside_ref[...] * wt_s[t]
        before, after = both_sides(jnp.sum(outside, axis=1, keepdims=True))
        count = jnp.sum(inside, axis=1, keepdims=True) + first_c * before + last_c * after
        scale = 1.0 / jnp.maximum(count, 1.0)
        rows = jnp.concatenate([inside, outside], axis=0).astype(BF16)
        scale_r = jnp.sum(jnp.where(sub == lane, scale, 0.0), axis=0, keepdims=True)
        own_c = jnp.sum(jnp.where(diagonal, own, 0.0), axis=1, keepdims=True)
        chosen = chosen_ref[...] * own_c
        alpha_s[t] = jnp.broadcast_to(jnp.sum(chosen * scale_r, axis=1, keepdims=True), (width, 128))
        chosen = chosen.astype(BF16)
        sums = [dot(rows, mix_refs[t][slot, 0]) + dot(rows, mix_refs[t][slot, 1]) for slot in range(2)]
        away = times((apart_ref[t, 0], apart_ref[t, 1]), tuple(value[windows:] for value in sums))
        for slot in range(2):
            before, after = both_sides(away[slot])
            total = sums[slot][:windows] + first_c * before + last_c * after
            high, low = split_two(total * (scale * scale))
            mexp_s[t, slot] = dot(chosen, high) + dot(chosen, low)

    for t in range(2):
        def main(lanes, count):
            def step(block, sums):
                rows = pl.ds(pl.multiple_of(block * 16, 16), 16)
                alpha = alpha_s[t, rows, :count]
                mr, mi = mexp_s[t, 0, rows, lanes], mexp_s[t, 1, rows, lanes]
                r0, i0 = wave_refs[t][0, 0, rows, lanes], wave_refs[t][0, 1, rows, lanes]
                r1, i1 = wave_refs[t][1, 0, rows, lanes], wave_refs[t][1, 1, rows, lanes]
                factors = []
                for fr, fi in (
                    (alpha * r0 - (mr * r1 + mi * i1), (mr * i1 - mi * r1) - alpha * i0),
                    (alpha * r1 - (mr * r0 - mi * i0), (mr * i0 + mi * r0) - alpha * i1),
                ):
                    factors.append((fr, fi - fr, fr + fi))
                new = []
                for k in range(4):
                    vr = vis_refs[t][0, k, rows, lanes].astype(F32)
                    vi = vis_refs[t][1, k, rows, lanes].astype(F32)
                    vs = vr + vi
                    for s in range(2):
                        for v, f in zip((vs, vr, vi), factors[s]):
                            product = v * f
                            new.append(sums[len(new)] + (product[:8] + product[8:]))
                return tuple(new)

            zero = jnp.zeros((8, count), F32)
            sums = lax.fori_loop(0, width // 16, step, (zero,) * 24, unroll=12)
            for s in range(2):
                owner = lax.bitwise_xor(lax.bitwise_and(me, 3), t + 2 * s)
                found = []
                for k in range(4):
                    one, two, three = sums[(k * 2 + s) * 3:(k * 2 + s) * 3 + 3]
                    found.append([jnp.sum(value, axis=0, keepdims=True) for value in (one - three, one + two)])
                for d in range(4):
                    @pl.when(owner == d)
                    def write():
                        for k in range(4):
                            for ri in range(2):
                                out_refs[d][k, ri:ri + 1, lanes] = found[k][ri]

        if t == 1:
            copy.wait()
        tiles(pairs, main)


def station_hots(pairs):
    station, baseline = iota((ROWS, 1), 0), iota((1, pairs), 1)
    offset = station * (float(2 * STATIONS - 1) - station) * 0.5
    after = (station + 1.0) * (float(2 * STATIONS - 2) - station) * 0.5
    first = jnp.where((baseline >= offset) & (baseline < after), 1.0, 0.0)
    partner_of = baseline + 1.0 + jnp.sum(first * (station - offset), axis=0, keepdims=True)
    second = jnp.where(partner_of == station, 1.0, 0.0)
    return first.astype(BF16), second.astype(BF16)


def hots_kernel(hot_ref):
    hot_ref[0], hot_ref[1] = station_hots(hot_ref.shape[2])


def solve_kernel(window_count, me_ref, tracks_ref, hot_ref, *refs):
    parts, gain_ref = refs[:-1], refs[-1]
    me = me_ref[0]
    systems = gain_ref.shape[0]
    total = [part[...] for part in parts]
    while len(total) > 1:
        total = [total[i] + total[i + 1] for i in range(0, len(total), 2)]
    total = total[0]
    hot, other = hot_ref[0], hot_ref[1]
    nt = lambda left, right: lax.dot_general(
        left, right, (((1,), (1,)), ((), ())), preferred_element_type=F32)
    upper, lower = [], []
    for system in range(systems):
        for ri in range(2):
            for piece in split_two(total[system, ri:ri + 1]):
                upper.append(hot * piece)
                lower.append(other * piece)
    upper = nt(jnp.concatenate(upper, axis=0), other)
    lower = nt(jnp.concatenate(lower, axis=0), hot)
    cut = lambda value, i: value[i * ROWS:(i + 1) * ROWS]
    join = lambda value, i: cut(value, 2 * i) + cut(value, 2 * i + 1)
    live_r = jnp.where(iota((1, ROWS), 1) < float(STATIONS), 1.0, 0.0)
    live_c = jnp.where(iota((ROWS, 1), 0) < float(STATIONS), 1.0, 0.0)
    matrices = [(join(upper, 2 * i) + join(lower, 2 * i), join(upper, 2 * i + 1) - join(lower, 2 * i + 1))
                for i in range(systems)]
    states = [(live_r, 0.0 * live_r, live_c, 0.0 * live_c)] * systems
    for turn in range(GITERS):
        for system in range(systems):
            re, im = matrices[system]
            row_re, row_im, col_re, col_im = states[system]
            pull_cr = jnp.sum(re * row_re - im * row_im, axis=1, keepdims=True)
            pull_ci = jnp.sum(re * row_im + im * row_re, axis=1, keepdims=True)
            pull_rr = jnp.sum(re * col_re + im * col_im, axis=0, keepdims=True)
            pull_ri = jnp.sum(re * col_im - im * col_re, axis=0, keepdims=True)
            power_r = row_re * row_re + row_im * row_im
            power_c = col_re * col_re + col_im * col_im
            total = jnp.sum(power_c, axis=0, keepdims=True)
            inverse_r = 0.5 / (window_count * (total - power_r) + DAMPING)
            inverse_c = 0.5 / (window_count * (total - power_c) + DAMPING)
            states[system] = (0.5 * row_re + pull_rr * inverse_r, 0.5 * row_im + pull_ri * inverse_r,
                              0.5 * col_re + pull_cr * inverse_c, 0.5 * col_im + pull_ci * inverse_c)
    visible = tracks_ref[lax.bitwise_and(lax.div(me, 2), 1), lax.bitwise_and(me, 1)].astype(F32)
    gains = [state[ri] * visible for state in states for ri in range(2)]
    gains = jnp.concatenate(gains, axis=0)
    stacked = jnp.concatenate([piece.astype(F32) for piece in split_three(gains)], axis=0).astype(BF16)
    ends = []
    for table in (hot, other):
        wide = dot(stacked, table)
        ends.append((wide[:8] + wide[8:16]) + wide[16:])
    pairs = hot.shape[1]
    for system in range(systems):
        (lr, li), (rr, ri_) = [[end[2 * system + ri:2 * system + ri + 1] for ri in range(2)] for end in ends]
        gain_ref[system, 0:1, :pairs] = lr * rr + li * ri_
        gain_ref[system, 1:2, :pairs] = li * rr - lr * ri_
        gain_ref[system, :, GAINS_AT:] = gains[2 * system:2 * system + 2, :STATIONS]


def clean_kernel(width, me_ref, *refs):
    vis_refs, wave_refs, piece_refs = refs[:2], refs[2:4], refs[4:8]
    out_hbm, gain_out_ref, out_s, model_s, sems = refs[8:]
    pairs = wave_refs[0].shape[3]
    mine = lax.bitwise_and(me_ref[0], 3)
    for d, piece in enumerate(piece_refs):
        owner = lax.bitwise_xor(mine, d)
        t, s = lax.bitwise_and(owner, 1), lax.div(owner, 2)
        for k in range(4):
            for ri in range(2):
                gain_out_ref[ri, s, t, k:k + 1, :] = piece[k, ri:ri + 1, GAINS_AT:]
            re, im = piece[k, 0:1, :pairs], piece[k, 1:2, :pairs]
            for slot, value in enumerate((re, im - re, re + im)):
                model_s[owner, 3 * k + slot:3 * k + slot + 1, :] = value

    half = width // 32 * 16
    quarter = half // 32 * 16
    pieces = [(0, 0, half), (0, half, width - half),
              (1, 0, half), (1, half, half - quarter), (1, 2 * half - quarter, width - 2 * half + quarter)]
    copies = []
    for t, start, length in pieces:
        def main(lanes, count):
            for block in range(length // 16):
                rows = slice(start + block * 16, start + block * 16 + 16)
                waves = []
                for s in range(2):
                    re, im = (wave_refs[t][s, ri, rows, lanes] for ri in range(2))
                    waves.append((re + im, re, im))
                for k in range(4):
                    sums = []
                    for slot in range(3):
                        one, two = (waves[s][slot] * model_s[t + 2 * s, 3 * k + slot:3 * k + slot + 1, lanes]
                                    for s in range(2))
                        sums.append(one + two)
                    vr = vis_refs[t][0, k, rows, lanes].astype(F32)
                    vi = vis_refs[t][1, k, rows, lanes].astype(F32)
                    out_s[0, t, k, rows, lanes] = (vr - (sums[0] - sums[2])).astype(BF16)
                    out_s[1, t, k, rows, lanes] = (vi - (sums[0] + sums[1])).astype(BF16)

        tiles(pairs, main)
        rows = pl.ds(start, length)
        copies.append(pltpu.make_async_copy(
            out_s.at[:, t, :, rows], out_hbm.at[:, t, :, rows], sems.at[len(copies)]))
        copies[-1].start()
    for copy in copies:
        copy.wait()


def partner(value, bits):
    count = lax.axis_size("sub")
    return lax.ppermute(value, "sub", [(i, i ^ bits) for i in range(count)])


def smem():
    return pl.BlockSpec(memory_space=pltpu.SMEM)


def local(visibilities, delays, flags, windows, tracks):
    width = visibilities.shape[4]
    pairs = visibilities.shape[3]
    count = lax.axis_size("sub")
    window_count = windows.shape[0]
    turned = jnp.transpose(visibilities, (0, 1, 2, 4, 3))
    me = lax.axis_index("sub").astype(jnp.int32).reshape(1)
    vmem_ref = pl.BlockSpec(memory_space=pltpu.VMEM)
    hbm_ref = pl.BlockSpec(memory_space=pltpu.HBM)
    vmem = lambda *shape: pltpu.VMEM(shape, F32)
    params = pltpu.CompilerParams(vmem_limit_bytes=24 * 2 ** 20)
    flags = flags[None]

    reach = count // 4
    remote_rows = 16 * pl.cdiv(4 * reach, 16)

    hots = pl.pallas_call(
        hots_kernel,
        out_specs=vmem_ref,
        out_shape=jax.ShapeDtypeStruct((2, ROWS, pairs), BF16),
        compiler_params=params,
        cost_estimate=pl.CostEstimate(flops=10 ** 7, bytes_accessed=6 * 2 ** 20, transcendentals=0),
        name="station_hots",
    )()
    small = jnp.pad(flags[0], ((0, 1), (0, 0))) + jnp.pad(windows[None], ((2, 0), (0, width - window_count)))
    made = []
    beside = [partner(flags, d) for d in range(1, 4)]
    for t in range(2):
        shape = lambda *dims: jax.ShapeDtypeStruct(dims, F32)
        out_shape = [
            shape(2, 2, width, pairs),
            jax.ShapeDtypeStruct((2, 2, width, pairs), BF16),
        ]
        if t == 0:
            operands = (me, delays, small)
            in_specs = [smem()] + [vmem_ref] * 2
            out_shape += [jax.ShapeDtypeStruct(flags.shape, flags.dtype),
                          jax.ShapeDtypeStruct((1, window_count), windows.dtype)]
        else:
            operands = (me, turned, delays, made[0][3])
            in_specs = [smem(), hbm_ref] + [vmem_ref] * 2
            out_shape += [jax.ShapeDtypeStruct((2, 4, width, pairs), BF16),
                          shape(2, 2, remote_rows, pairs), shape(window_count, width), shape(width, window_count),
                          shape(remote_rows, width), shape(2, window_count, 128)]
        made.append(pl.pallas_call(
            lambda *refs: phase_kernel(width, t, reach, *refs),
            in_specs=in_specs,
            out_specs=[vmem_ref] * len(out_shape),
            out_shape=out_shape,
            scratch_shapes=[pltpu.SemaphoreType.DMA] * t,
            compiler_params=pltpu.CompilerParams(vmem_limit_bytes=GRANTS[t] * 2 ** 20),
            cost_estimate=pl.CostEstimate(flops=10 ** 7, bytes_accessed=6 * 2 ** 20, transcendentals=0),
            name="phases",
        )(*operands))
        if t == 0:
            gathered = jnp.concatenate([made[0][2]] + beside, axis=0)
            while gathered.shape[0] < reach:
                stride = gathered.shape[0]
                gathered = jnp.concatenate([gathered] + [partner(gathered, stride * d) for d in range(1, 4)], axis=0)
            middle = [(i, i ^ (3 * reach)) for i in range(count) if reach <= i < 3 * reach]
            beyond = lax.ppermute(gathered, "sub", middle)
            gathered = [gathered, beyond, partner(gathered, reach)]
    waves, mixing = ([part[i] for part in made] for i in range(2))
    held, *masks = made[1][2:]
    *quarters, held_too = pl.pallas_call(
        lambda *refs: sums_kernel(width, reach, *refs),
        in_specs=[smem()] + [vmem_ref] * 8 + [hbm_ref] + [vmem_ref] * 5,
        out_specs=[vmem_ref] * 5,
        out_shape=[jax.ShapeDtypeStruct((4, 2, pairs), F32)] * 4 + [jax.ShapeDtypeStruct(held.shape, BF16)],
        scratch_shapes=[vmem(2, width, 128), vmem(2, 2, width, pairs), vmem(2, remote_rows, width),
                        pltpu.SemaphoreType.DMA],
        compiler_params=pltpu.CompilerParams(vmem_limit_bytes=GRANT * 2 ** 20),
        name="window_sums",
    )(me, *gathered, *masks, turned, held, *waves, *mixing)
    pieces = [quarters[0]] + [partner(quarters[d], d) for d in range(1, 4)]
    stride = 4
    while stride < count:
        while len(pieces) > 1:
            pieces = [pieces[i] + pieces[i + 1] for i in range(0, len(pieces), 2)]
        pieces += [partner(pieces[0], stride * d) for d in range(1, min(4, count // stride))]
        stride *= 4
    model = pl.pallas_call(
        lambda *refs: solve_kernel(float(window_count), *refs),
        in_specs=[smem(), smem()] + [vmem_ref] * (1 + len(pieces)),
        out_specs=vmem_ref,
        out_shape=jax.ShapeDtypeStruct((4, 2, GAINS_AT + STATIONS), F32),
        compiler_params=params,
        name="gain_solve",
    )(me, tracks, hots, pieces[0], *pieces[:0:-1])
    model = [model] + [partner(model, d) for d in range(1, 4)]
    cleaned, gains = pl.pallas_call(
        lambda *refs: clean_kernel(width, *refs),
        in_specs=[smem()] + [vmem_ref] * 8,
        out_specs=[hbm_ref, vmem_ref],
        out_shape=[
            jax.ShapeDtypeStruct(turned.shape, BF16),
            jax.ShapeDtypeStruct((2, 2, 2, 4, STATIONS), F32),
        ],
        scratch_shapes=[
            pltpu.VMEM(turned.shape, BF16),
            vmem(4, 16, pairs),
            pltpu.SemaphoreType.DMA((5,)),
        ],
        compiler_params=params,
        name="clean",
    )(me, held, held_too, *waves, *model)
    return jnp.transpose(cleaned, (0, 1, 2, 4, 3)), gains


def solution(mesh):
    return jax.shard_map(
        local,
        mesh=mesh,
        in_specs=(
            P(None, "obs", None, None, "sub"),
            P(None, "obs", None),
            P("obs", "sub"),
            P(),
            P(None, "obs"),
        ),
        out_specs=(P(None, "obs", None, None, "sub"), P(None, None, "obs", None, None)),
        check_vma=False,
    )
```
